32 devices in a mesh: fsdp: 4 (over y, x), context: 4 (over z), tensor: 2 (over core).
Axes of the slice: x: 2, y: 2, z: 4, core: 2. Of those that a mesh axis runs over, the one named last changes fastest.
Arguments:
- tokens: bfloat16 [4, 2560, 768], P('fsdp', 'context'), may hold values from -6 to 6
- attn_gain: bfloat16 [768], P('fsdp'), may hold values from 0.5 to 1.5
- w_qkv: bfloat16 [768, 3, 768], P('fsdp', None, 'tensor'), may hold values from -0.21875 to 0.21875
- w_out: bfloat16 [768, 768], P('tensor', 'fsdp'), may hold values from -0.875 to 0.875
- ffn_gain: bfloat16 [768], P('fsdp'), may hold values from 0.5 to 1.5
- w_gu: bfloat16 [768, 2, 2048], P('fsdp', None, 'tensor'), may hold values from -0.21875 to 0.21875
- w_dn: bfloat16 [2048, 768], P('tensor', 'fsdp'), may hold values from -0.125 to 0.125
- w_egu: bfloat16 [8, 768, 2, 2048], P('fsdp', None, None, 'tensor'), may hold values from -0.21875 to 0.21875
- w_edn: bfloat16 [8, 2048, 768], P('fsdp', 'tensor'), may hold values from -0.125 to 0.125
- adapters: bfloat16 [8, 233472], P('fsdp', ('context', 'tensor')), may hold values from -0.29882812 to 0.29882812
- adapter_ids: int32 [4], P('fsdp'), may hold values from 0 to 7
- parents: int32 [4, 13], P('fsdp'), may hold values from 0 to 4, as said below
- seg_lengths: int32 [4, 13], P('fsdp'), may hold values from 64 to 1024, as said below
- routes: int32 [4, 2560, 2], P('fsdp', 'context'), may hold values from 0 to 7, as said below
- route_weights: bfloat16 [4, 2560, 2], P('fsdp', 'context'), may hold values from 0.25 to 0.75
- cotangent: bfloat16 [4, 2560, 768], P('fsdp', 'context'), may hold values from -6 to 6
Outputs:
- block_out: float32 [4, 2560, 768], P('fsdp', 'context')
- input_grad: float32 [4, 2560, 768], P('fsdp', 'context')
- adapter_grads: float32 [8, 233472], P('fsdp', ('context', 'tensor'))
The draws below stay inside these ranges and needn't reach their ends.
Inputs may be any that keep to these rules, and one draw needn't show every extreme that they name: Segment 0 is the root with parent 0; segments 1 to 4 have parent 0; segments 5 to 12 have parents among 1 to 4, two each. `seg_lengths`: segment 0 has 1024 tokens; every other segment has 64 to 192; a tree's lengths sum to 2560. `routes`: a token's two experts differ; among the rows that one device holds (640 rows of each of its 1 trees) no expert is named more than 320 times, and one expert is named exactly 320 times.
All inputs are finite; a program needn't handle non-finite values.
Results may differ from the reference program's by a relative error of at most 0.02.
The reference program's roundings to bfloat16 on the way count: a program that leaves them out, or rounds other values in their place, can miss the bound.
Values may be sent and summed in bfloat16 or wider, within the bound.
A program may use at most 320 MiB of HBM per device.

```python
import jax
import jax.numpy as jnp
from jax import lax

D = 768
HEADS = 12
HEAD_DIM = 64
FF = 2048
FFE = 2048
EXPERTS = 8
TOPK = 2
RANK = 16
ADAPTERS = 8
SEGS = 13
TREES = 1
TREE_LEN = 2560
ROWS = 640
LEAF = 128
N_TREES = 4
CAP = 320
PARAMS = 233472


def draw_routes(key, part):
    key = jax.random.fold_in(key, 11)
    block_count = N_TREES // TREES * (TREE_LEN // ROWS)
    block_rows = TREES * ROWS
    other_count = EXPERTS - 1
    rest_total = 2 * block_rows - CAP
    base_load = rest_total // other_count
    extra_count = rest_total - base_load * other_count
    pair_count = other_count // 2

    def one_block(block_key):
        key_list = jax.random.split(block_key, 3)
        shift_sizes = jax.random.randint(key_list[0], (pair_count,), 0, base_load // 2 + 1)
        signed_shifts = jnp.stack([shift_sizes, -shift_sizes], axis=1).reshape(2 * pair_count)
        signed_shifts = jnp.concatenate([signed_shifts, jnp.zeros((other_count - 2 * pair_count,), jnp.int32)])
        load_counts = base_load + (jnp.arange(other_count) < extra_count).astype(jnp.int32) + signed_shifts
        load_counts = jnp.concatenate([jnp.full((1,), CAP, jnp.int32), load_counts.astype(jnp.int32)])
        expert_order = jax.random.permutation(key_list[1], EXPERTS).astype(jnp.int32)
        run_ends = jnp.cumsum(load_counts)
        positions = jnp.arange(2 * block_rows)
        run_index = jnp.sum((positions[:, None] >= run_ends[None, :]).astype(jnp.int32), axis=1)
        expert_named = expert_order[run_index]
        pair_rows = jnp.stack([expert_named[:block_rows], expert_named[block_rows:]], axis=1)
        row_order = jax.random.permutation(key_list[2], block_rows)
        return pair_rows[row_order]
    route_table = jax.vmap(one_block)(jax.random.split(key, block_count))
    route_table = route_table.reshape(N_TREES // TREES, TREE_LEN // ROWS, TREES, ROWS, 2)
    return route_table.transpose(0, 2, 1, 3, 4).reshape(N_TREES, TREE_LEN, 2).astype(jnp.int32)


def draw_parents(key, part):
    key = jax.random.fold_in(key, 23)

    def one_tree(tree_key):
        leaf_parents = 1 + jax.random.permutation(tree_key, SEGS - 5) // 2
        return jnp.concatenate([jnp.zeros((5,), jnp.int32), leaf_parents.astype(jnp.int32)])
    return jax.vmap(one_tree)(jax.random.split(key, N_TREES))


def draw_seg_lengths(key, part):
    key = jax.random.fold_in(key, 37)
    half_leaf = LEAF // 2

    def one_tree(tree_key):
        key_list = jax.random.split(tree_key, 2)
        shift_sizes = jax.random.randint(key_list[0], (6,), 0, half_leaf + 1)
        shift_sizes = shift_sizes.at[0].set(half_leaf)
        signed_shifts = jnp.stack([shift_sizes, -shift_sizes], axis=1).reshape(12)
        branch_sizes = LEAF + signed_shifts[jax.random.permutation(key_list[1], 12)]
        return jnp.concatenate([jnp.full((1,), 8 * LEAF, jnp.int32), branch_sizes.astype(jnp.int32)])
    return jax.vmap(one_tree)(jax.random.split(key, N_TREES))


def with_ends(array, key, least, top_value):
    longest = array.shape.index(max(array.shape))
    spots = []
    for shift in (0, 1):
        where = [jax.random.randint(jax.random.fold_in(key, axis), (), 0, length) for axis, length in enumerate(array.shape)]
        where[longest] = (where[longest] + shift) % array.shape[longest]
        spots.append(tuple(where))
    return array.at[spots[0]].set(least).at[spots[1]].set(top_value)


def steps_of(key, dims, shards, least, top_value):
    loudness, own = 1.0, jax.random.fold_in(key, 6)
    for dim, blocks in shards:
        draws = jnp.exp(jax.random.uniform(jax.random.fold_in(own, dim), (blocks,), jnp.float32, least / len(shards), top_value / len(shards)))
        loudness = loudness * jnp.repeat(draws, dims[dim] // blocks).reshape([-1 if axis == dim else 1 for axis in range(len(dims))])
    return loudness


def centred(stream_key, shape, spread, bound, cuts=(), kind=jnp.bfloat16):
    drawn = jax.random.normal(stream_key, shape, jnp.float32) * spread
    if len(cuts) > 0:
        drawn = steps_of(stream_key, shape, cuts, -0.22, 0.18) * drawn
    return jnp.clip(drawn, min=-bound, max=bound).astype(kind)


def setup_inputs(seed: int = 0) -> dict:
    seeds = jax.random.split(jax.random.key(seed), 17)
    tokens = centred(seeds[0], (N_TREES, TREE_LEN, D), 1.0, 6.0, ((0, 4), (1, 4)))
    attn_gain = jnp.clip(1.0 + 0.1 * jax.random.normal(seeds[1], (D,), jnp.float32), 0.5, 1.5).astype(jnp.bfloat16)
    w_qkv = centred(seeds[2], (D, 3, D), D ** -0.5, 0.21875, ((0, 4), (2, 2)))
    w_out = centred(seeds[3], (D, D), (D // 16) ** -0.5, 0.875, ((0, 2), (1, 4)))
    ffn_gain = jnp.clip(1.0 + 0.1 * jax.random.normal(seeds[4], (D,), jnp.float32), 0.5, 1.5).astype(jnp.bfloat16)
    w_gu = centred(seeds[5], (D, 2, FF), D ** -0.5, 0.21875, ((0, 4), (2, 2)))
    w_dn = centred(seeds[6], (FF, D), FF ** -0.5, 0.125, ((0, 2), (1, 4)))
    w_egu = centred(seeds[7], (EXPERTS, D, 2, FFE), D ** -0.5, 0.21875, ((0, 4), (3, 2)))
    w_edn = centred(seeds[8], (EXPERTS, FFE, D), FFE ** -0.5, 0.125, ((0, 4), (1, 2)))
    adapters = centred(seeds[9], (ADAPTERS, PARAMS), 0.05, 0.29882812, ((0, 4), (1, 8)))
    adapter_ids = with_ends(jax.random.randint(seeds[10], (N_TREES,), 0, ADAPTERS), jax.random.fold_in(seeds[10], 1), 0, ADAPTERS - 1).astype(jnp.int32)
    parents = draw_parents(jax.random.fold_in(seeds[16], 71), 0)
    seg_lengths = draw_seg_lengths(jax.random.fold_in(seeds[16], 71), 0)
    routes = draw_routes(jax.random.fold_in(seeds[16], 71), 0)
    route_weights = jnp.clip(0.25 + 0.5 * jax.random.uniform(seeds[14], (N_TREES, TREE_LEN, TOPK), jnp.float32) ** steps_of(seeds[14], (N_TREES, TREE_LEN, TOPK), ((0, 4), (1, 4)), -0.2, 0.2), 0.25, 0.75).astype(jnp.bfloat16)
    cotangent = centred(seeds[15], (N_TREES, TREE_LEN, D), 1.0, 6.0, ((0, 4), (1, 4)))
    return {"tokens": tokens, "attn_gain": attn_gain, "w_qkv": w_qkv, "w_out": w_out, "ffn_gain": ffn_gain, "w_gu": w_gu, "w_dn": w_dn, "w_egu": w_egu, "w_edn": w_edn, "adapters": adapters, "adapter_ids": adapter_ids, "parents": parents, "seg_lengths": seg_lengths, "routes": routes, "route_weights": route_weights, "cotangent": cotangent}


@jax.custom_vjp
def low(v):
    return lax.optimization_barrier(v.astype(jnp.bfloat16)).astype(jnp.float32)

@jax.custom_vjp
def lowrank_backward(v):
    return v

def low_keep(v):
    return (low(v), None)

def low_pass(kept, grad):
    return (grad,)

def back_keep(v):
    return (v, None)

def back_low(kept, grad):
    return (low(grad),)
low.defvjp(low_keep, low_pass)
lowrank_backward.defvjp(back_keep, back_low)
epsilon = 1e-06
adapter_scale = 2.0
rope_base = 10000.0
masked_score = -1e+30
highest_precision = lax.Precision.HIGHEST

def unpack(flat_params):
    leading = flat_params.shape[:-1]
    block_shapes = [(D, 3 * RANK), (3, RANK, D), (D, RANK), (RANK, D), (D, 2 * RANK), (2, RANK, FF), (FF, RANK), (RANK, D)]
    pieces = []
    offset = 0
    for block_shape in block_shapes:
        extent = 1
        for factor in block_shape:
            extent = extent * factor
        pieces.append(flat_params[..., offset:offset + extent].reshape(leading + block_shape))
        offset = offset + extent
    return pieces

def silu_of(values):
    return values * jax.nn.sigmoid(values)

def rms_scale(values):
    return lax.rsqrt(lax.optimization_barrier(jnp.mean(values * values, axis=-1, keepdims=True)) + epsilon)

def rotate(values, cosine, sinus):
    half_dim = values.shape[-1] // 2
    front_half = values[..., :half_dim]
    back_half = values[..., half_dim:]
    return jnp.concatenate([front_half * cosine - back_half * sinus, back_half * cosine + front_half * sinus], axis=-1)

def angles(positions):
    half_dim = HEAD_DIM // 2
    frequency = rope_base ** (-(jnp.arange(half_dim, dtype=jnp.float32) * 2.0) / HEAD_DIM)
    turned = positions.astype(jnp.float32)[..., None] * frequency
    return (jnp.cos(turned)[..., None, :], jnp.sin(turned)[..., None, :])

def tree_layout(lengths, parent_ids):
    seg_count = lengths.shape[0]
    seg_ids = jnp.arange(seg_count, dtype=jnp.int32)
    parent_hot = (parent_ids[:, None] == seg_ids[None, :]).astype(jnp.int32)
    grand_hot = jnp.dot(parent_hot, parent_hot).astype(jnp.int32)
    same_seg = (seg_ids[:, None] == seg_ids[None, :]).astype(jnp.int32)
    ancestry = (same_seg + parent_hot + grand_hot > 0).astype(jnp.int32)
    starts = (jnp.cumsum(lengths) - lengths).astype(jnp.int32)
    offsets = lax.optimization_barrier(jnp.sum((ancestry - same_seg) * lengths[None, :], axis=1)).astype(jnp.int32)
    return (ancestry, starts, offsets)

def locate(row_ids, starts, offsets):
    segment = (lax.optimization_barrier(jnp.sum((row_ids[:, None] >= starts[None, :]).astype(jnp.int32), axis=1)) - 1).astype(jnp.int32)
    seg_hot = (segment[:, None] == jnp.arange(starts.shape[0], dtype=jnp.int32)[None, :]).astype(jnp.int32)
    positions = row_ids - lax.optimization_barrier(jnp.sum(seg_hot * starts[None, :], axis=1)) + lax.optimization_barrier(jnp.sum(seg_hot * offsets[None, :], axis=1))
    return (seg_hot, positions.astype(jnp.int32))

def reference(tokens, attn_gain, w_qkv, w_out, ffn_gain, w_gu, w_dn, w_egu, w_edn, adapters, adapter_ids, parents, seg_lengths, routes, route_weights, cotangent):
    gain_one = attn_gain.astype(jnp.float32)
    gain_two = ffn_gain.astype(jnp.float32)
    qkv_weight = w_qkv.astype(jnp.float32)
    output_matrix = w_out.astype(jnp.float32)
    gu_weight = w_gu.astype(jnp.float32)
    down_matrix = w_dn.astype(jnp.float32)
    egu_weight = w_egu.astype(jnp.float32)
    edn_weight = w_edn.astype(jnp.float32)
    tree_len = TREE_LEN
    block_rows = 512 if tree_len % 512 == 0 else tree_len
    group_cap = CAP * (TREE_LEN // ROWS)
    group_count = N_TREES // TREES
    head_shape = (tree_len, HEADS, HEAD_DIM)

    def attention_tree(inputs):
        tree_tokens, chosen, lengths, parent_ids = inputs
        a_qkv, query_key_value_adapter_up, a_out, output_adapter_up, a_gu, gate_up_adapter_up, a_dn, down_adapter_up = unpack(chosen)
        normed = low(tree_tokens * rms_scale(tree_tokens) * gain_one)
        query_key_value_rank = jnp.dot(normed, a_qkv, precision=highest_precision).reshape(tree_len, 3, RANK)
        projected_rows = jnp.einsum('ld,djc->ljc', normed, qkv_weight, precision=highest_precision)
        projected_rows = lowrank_backward(projected_rows + adapter_scale * jnp.einsum('utn,tny->uty', query_key_value_rank, query_key_value_adapter_up, precision=highest_precision))
        ancestry, starts, offsets = tree_layout(lengths, parent_ids)
        row_ids = jnp.arange(tree_len, dtype=jnp.int32)
        seg_hot, positions = locate(row_ids, starts, offsets)
        cosine, sinus = angles(positions)
        queries = low(rotate(projected_rows[:, 0].reshape(head_shape), cosine, sinus))
        key_rows = low(rotate(projected_rows[:, 1].reshape(head_shape), cosine, sinus))
        value_rows = low(projected_rows[:, 2].reshape(head_shape))
        reach = (jnp.dot(seg_hot, ancestry) > 0).astype(jnp.float32)
        key_hot = seg_hot.astype(jnp.float32)

        def attend_block(start):
            query_block = lax.dynamic_slice_in_dim(queries, start, block_rows, 0)
            reach_block = lax.dynamic_slice_in_dim(reach, start, block_rows, 0)
            block_ids = start + jnp.arange(block_rows, dtype=jnp.int32)
            visible = (jnp.dot(reach_block, key_hot.T, precision=highest_precision) > 0.5) & (row_ids[None, :] <= block_ids[:, None])
            scores = lowrank_backward(jnp.einsum('rhd,khd->hrk', query_block, key_rows, precision=highest_precision) * 0.125)
            scores = jnp.where(visible[None], scores, masked_score)
            shifted = scores - lax.optimization_barrier(jnp.max(scores, axis=-1, keepdims=True))
            weights = jnp.exp(shifted)
            probabilities = weights / lax.optimization_barrier(jnp.sum(weights, axis=-1, keepdims=True))
            mixed_block = jnp.einsum('hrk,khd->rhd', low(probabilities), value_rows, precision=highest_precision)
            return mixed_block.reshape(block_rows, D)
        block_starts = jnp.arange(tree_len // block_rows, dtype=jnp.int32) * block_rows
        mixed_row_values = lax.map(jax.checkpoint(attend_block), block_starts).reshape(tree_len, D)
        mixed_row_values = low(lowrank_backward(mixed_row_values))
        output_rank_rows = jnp.dot(mixed_row_values, a_out, precision=highest_precision)
        branch_node = jnp.dot(mixed_row_values, output_matrix, precision=highest_precision) + adapter_scale * jnp.dot(output_rank_rows, output_adapter_up, precision=highest_precision)
        return tree_tokens + lowrank_backward(branch_node)

    def group_fn(inputs):
        group_tokens, chosen, lengths, parent_ids, group_routes, group_gates = inputs
        residual = lax.map(jax.checkpoint(attention_tree), (group_tokens, chosen, lengths, parent_ids))
        a_qkv, query_key_value_adapter_up, a_out, output_adapter_up, a_gu, gate_up_adapter_up, a_dn, down_adapter_up = unpack(chosen)
        normed = low(residual * rms_scale(residual) * gain_two)
        gate_up_rank_rows = jnp.einsum('tld,tdm->tlm', normed, a_gu, precision=highest_precision).reshape(TREES, tree_len, 2, RANK)
        gate_up_matrix = jnp.einsum('tld,djf->tljf', normed, gu_weight, precision=highest_precision)
        gate_up_matrix = lowrank_backward(gate_up_matrix + adapter_scale * jnp.einsum('yuwk,ywkh->yuwh', gate_up_rank_rows, gate_up_adapter_up, precision=highest_precision))
        hidden_state = low(silu_of(gate_up_matrix[:, :, 0]) * gate_up_matrix[:, :, 1])
        down_rank_rows = jnp.einsum('tlf,tfr->tlr', hidden_state, a_dn, precision=highest_precision)
        shared_weights = jnp.einsum('zjb,ba->zja', hidden_state, down_matrix, precision=highest_precision) + adapter_scale * jnp.einsum('cpg,cgo->cpo', down_rank_rows, down_adapter_up, precision=highest_precision)
        token_count = TREES * tree_len
        flat_routes = group_routes.reshape(token_count * TOPK).astype(jnp.int32)
        route_hot = (flat_routes[:, None] == jnp.arange(EXPERTS, dtype=jnp.int32)[None, :]).astype(jnp.int32)
        slot_place = lax.optimization_barrier(jnp.sum((jnp.cumsum(route_hot, axis=0) - route_hot) * route_hot, axis=1))
        slot_index = (flat_routes * group_cap + slot_place).astype(jnp.int32)
        slot_owner = jnp.full((EXPERTS * group_cap,), token_count, jnp.int32).at[slot_index].set(jnp.arange(token_count * TOPK, dtype=jnp.int32) // TOPK)
        padded = jnp.concatenate([normed.reshape(token_count, D), jnp.zeros((1, D), normed.dtype)], axis=0)

        def expert_fn(expert_inputs):
            rows_taken, gate_weight_one, down_weight_one = expert_inputs
            taken = padded[rows_taken]
            pre = lowrank_backward(jnp.einsum('cd,djf->cjf', taken, gate_weight_one, precision=highest_precision))
            active = low(silu_of(pre[:, 0]) * pre[:, 1])
            return jnp.dot(active, down_weight_one, precision=highest_precision)
        expert_out = lax.map(jax.checkpoint(expert_fn), (slot_owner.reshape(EXPERTS, group_cap), egu_weight, edn_weight))
        picked = expert_out.reshape(EXPERTS * group_cap, D)[slot_index].reshape(token_count, TOPK, D)
        moe = lax.optimization_barrier(jnp.sum(picked * group_gates.reshape(token_count, TOPK, 1), axis=1))
        branch_node = lowrank_backward(shared_weights.reshape(token_count, D) + moe)
        return residual + branch_node.reshape(TREES, tree_len, D)

    def forward(tokens_f, adapters_f):
        chosen = adapters_f[adapter_ids]

        def regroup(values):
            return values.reshape((group_count, TREES) + values.shape[1:])
        result = lax.map(jax.checkpoint(group_fn), (regroup(tokens_f), regroup(chosen), regroup(seg_lengths), regroup(parents), regroup(routes), regroup(route_weights.astype(jnp.float32))))
        return result.reshape(N_TREES, TREE_LEN, D)
    block_out, pullback = jax.vjp(forward, tokens.astype(jnp.float32), adapters.astype(jnp.float32))
    input_grad, adapter_grads = pullback(cotangent.astype(jnp.float32))
    return (block_out, input_grad, adapter_grads)
```

```python
import jax
import jax.numpy as jnp
import functools

from jax import lax
from jax.experimental import pallas as pl
from jax.experimental.pallas import tpu as pltpu
from jax.sharding import PartitionSpec as P

D = 768
HEADS = 12
HEAD_DIM = 64
FF = 2048
EXPERTS = 8
TOPK = 2
RANK = 16
ADAPTERS = 8
PARAMS = 233472


epsilon = 1e-06
adapter_scale = 2.0
rope_base = 10000.0
masked_score = -1e30
highest_precision = lax.Precision.HIGHEST


def unpack(flat_params):
    leading = flat_params.shape[:-1]
    block_shapes = [
        (D, 3 * RANK),
        (3, RANK, D),
        (D, RANK),
        (RANK, D),
        (D, 2 * RANK),
        (2, RANK, FF),
        (FF, RANK),
        (RANK, D),
    ]
    pieces = []
    offset = 0
    for block_shape in block_shapes:
        extent = 1
        for factor in block_shape:
            extent = extent * factor
        pieces.append(flat_params[..., offset : offset + extent].reshape(leading + block_shape))
        offset = offset + extent
    return pieces


def silu_of(values):
    return values * jax.nn.sigmoid(values)


def rms_scale(values):
    return lax.rsqrt(jnp.mean(values * values, axis=-1, keepdims=True) + epsilon)


def norm_back(values, scaling, gain_values, gradient):
    weighted = gradient * gain_values
    inner_mean = jnp.mean(values * weighted, axis=-1, keepdims=True)
    return scaling * weighted - values * (scaling * scaling * scaling) * inner_mean


def rotate(values, cosine, sinus):
    half_dim = values.shape[-1] // 2
    front_half = values[..., :half_dim]
    back_half = values[..., half_dim:]
    return jnp.concatenate(
        [front_half * cosine - back_half * sinus, back_half * cosine + front_half * sinus], axis=-1
    )


def unrotate(gradient, cosine, sinus):
    half_dim = gradient.shape[-1] // 2
    front_half = gradient[..., :half_dim]
    back_half = gradient[..., half_dim:]
    return jnp.concatenate(
        [front_half * cosine + back_half * sinus, back_half * cosine - front_half * sinus], axis=-1
    )


def angles(positions):
    half_dim = HEAD_DIM // 2
    frequency = rope_base ** (-(jnp.arange(half_dim, dtype=jnp.float32) * 2.0) / HEAD_DIM)
    turned = positions.astype(jnp.float32)[..., None] * frequency
    return (jnp.cos(turned)[..., None, :], jnp.sin(turned)[..., None, :])


def tree_layout(lengths, parent_ids):
    seg_count = lengths.shape[0]
    seg_ids = jnp.arange(seg_count, dtype=jnp.int32)
    parent_hot = (parent_ids[:, None] == seg_ids[None, :]).astype(jnp.int32)
    grand_hot = jnp.dot(parent_hot, parent_hot)
    same_seg = (seg_ids[:, None] == seg_ids[None, :]).astype(jnp.int32)
    ancestry = (same_seg + parent_hot + grand_hot > 0).astype(jnp.int32)
    starts = jnp.cumsum(lengths) - lengths
    offsets = jnp.sum((ancestry - same_seg) * lengths[None, :], axis=1)
    return (ancestry, starts, offsets)


def locate(row_ids, starts, offsets):
    segment = jnp.sum((row_ids[:, None] >= starts[None, :]).astype(jnp.int32), axis=1) - 1
    seg_hot = (segment[:, None] == jnp.arange(starts.shape[0], dtype=jnp.int32)[None, :]).astype(
        jnp.int32
    )
    positions = (
        row_ids
        - jnp.sum(seg_hot * starts[None, :], axis=1)
        + jnp.sum(seg_hot * offsets[None, :], axis=1)
    )
    return (seg_hot, positions)


SLOT_TILE = 256
TOKEN_TILE = 256


def nt_dot(left, right):
    return lax.dot_general(left, right, (((1,), (1,)), ((), ())), preferred_element_type=jnp.float32)


def tn_dot(left, right):
    return lax.dot_general(left, right, (((0,), (0,)), ((), ())), preferred_element_type=jnp.float32)


def nn_dot(left, right):
    return jnp.dot(left, right, preferred_element_type=jnp.float32)


def moe_kernel(
    spans,
    place_row,
    weight_row,
    place_col,
    weight_col,
    rows_ref,
    grads_ref,
    egu_hbm,
    edn_hbm,
    out_ref,
    back_ref,
    egu_ref,
    edn_ref,
    out_sum,
    back_sum,
    taken,
    taken_grad,
    slot_weight,
    sems,
):
    experts = egu_hbm.shape[0]
    copies = []
    for e in range(experts):
        copies.append(
            (
                pltpu.make_async_copy(egu_hbm.at[e], egu_ref.at[e], sems.at[e, 0]),
                pltpu.make_async_copy(edn_hbm.at[e], edn_ref.at[e], sems.at[e, 1]),
            )
        )
        copies[e][0].start()
        copies[e][1].start()
    out_sum[...] = jnp.zeros_like(out_sum)
    back_sum[...] = jnp.zeros_like(back_sum)
    slot_rows = lax.broadcasted_iota(jnp.int32, (SLOT_TILE, TOKEN_TILE), 0)
    slot_cols = lax.broadcasted_iota(jnp.int32, (TOKEN_TILE, SLOT_TILE), 1)
    for e in range(experts):
        copies[e][0].wait()
        copies[e][1].wait()

        def tile_step(i, carry, e=e):
            low = spans[e, 1 + 2 * i]
            high = spans[e, 2 + 2 * i]
            first = i * SLOT_TILE
            taken[...] = jnp.zeros_like(taken)
            taken_grad[...] = jnp.zeros_like(taken_grad)
            slot_weight[...] = jnp.zeros_like(slot_weight)

            def fetch(b, c):
                start = pl.multiple_of(b * TOKEN_TILE, TOKEN_TILE)
                hit = place_row[e, :, pl.ds(start, TOKEN_TILE)] == slot_rows + first
                pick = jnp.where(hit, 1.0, 0.0).astype(jnp.bfloat16)
                taken[...] += nn_dot(pick, rows_ref[pl.ds(start, TOKEN_TILE), :])
                taken_grad[...] += nn_dot(pick, grads_ref[pl.ds(start, TOKEN_TILE), :])
                slot_weight[...] += jnp.sum(
                    jnp.where(hit, weight_row[e, :, pl.ds(start, TOKEN_TILE)], 0.0),
                    axis=1,
                    keepdims=True,
                )
                return c

            lax.fori_loop(low, high, fetch, 0)
            inputs = taken[...].astype(jnp.bfloat16)
            gate_pre = nn_dot(inputs, egu_ref[e, 0])
            up_pre = nn_dot(inputs, egu_ref[e, 1])
            sigmoid_gate = jax.nn.sigmoid(gate_pre)
            silu = gate_pre * sigmoid_gate
            active = (silu * up_pre).astype(jnp.bfloat16)
            result = nn_dot(active, edn_ref[e]).astype(jnp.bfloat16)
            grad_active = nt_dot(taken_grad[...].astype(jnp.bfloat16), edn_ref[e])
            grad_active = grad_active * slot_weight[...]
            grad_gate = (
                grad_active * up_pre * sigmoid_gate * (1.0 + gate_pre * (1.0 - sigmoid_gate))
            ).astype(jnp.bfloat16)
            grad_up = (grad_active * silu).astype(jnp.bfloat16)
            grad_rows = (
                nt_dot(grad_gate, egu_ref[e, 0]) + nt_dot(grad_up, egu_ref[e, 1])
            ).astype(jnp.bfloat16)

            def give(b, c):
                start = pl.multiple_of(b * TOKEN_TILE, TOKEN_TILE)
                block = pl.ds(start, TOKEN_TILE)
                hit = place_col[block, e : e + 1] == slot_cols + first
                pick = jnp.where(hit, 1.0, 0.0).astype(jnp.bfloat16)
                out_sum[block, :] += nn_dot(pick, result) * weight_col[block, e : e + 1]
                back_sum[block, :] += nn_dot(pick, grad_rows)
                return c

            lax.fori_loop(low, high, give, 0)
            return carry

        lax.fori_loop(0, spans[e, 0], tile_step, 0)
    out_ref[...] = out_sum[...].astype(jnp.bfloat16)
    back_ref[...] = back_sum[...].astype(jnp.bfloat16)


def moe_layout(routes, weights, first_expert, experts):
    total = routes.shape[0]
    blocks = total // TOKEN_TILE
    ids = first_expert + jnp.arange(experts, dtype=jnp.int32)
    hits = routes[None] == ids[:, None, None]
    hit = jnp.any(hits, axis=-1)
    weight = jnp.sum(jnp.where(hits, weights.astype(jnp.float32)[None], 0.0), axis=-1)
    counted = hit.astype(jnp.int32)
    upto = jnp.cumsum(counted, axis=1)
    place = jnp.where(hit, upto - 1, -1)
    ends = upto.reshape(experts, blocks, TOKEN_TILE)[:, :, -1]
    begins = jnp.concatenate([jnp.zeros((experts, 1), jnp.int32), ends[:, :-1]], axis=1)
    count = ends[:, -1]
    tiles = total // SLOT_TILE
    tile_start = jnp.arange(tiles, dtype=jnp.int32) * SLOT_TILE
    low = jnp.sum((ends[:, None, :] <= tile_start[None, :, None]).astype(jnp.int32), axis=2)
    tile_end = jnp.minimum(tile_start[None] + SLOT_TILE, count[:, None])
    high = jnp.sum((begins[:, None, :] < tile_end[:, :, None]).astype(jnp.int32), axis=2)
    spans = jnp.stack([low, high], axis=2).reshape(experts, 2 * tiles)
    spans = jnp.concatenate([((count + SLOT_TILE - 1) // SLOT_TILE)[:, None], spans], axis=1)
    return spans, place, weight


def moe_call(spans, place, weight, rows, grads, egu, edn):
    total, width = rows.shape
    experts, _, _, units = egu.shape
    vmem = pl.BlockSpec(memory_space=pltpu.VMEM)
    hbm = pl.BlockSpec(memory_space=pl.ANY)
    shape = jax.ShapeDtypeStruct((total, width), jnp.bfloat16)
    return pl.pallas_call(
        moe_kernel,
        grid_spec=pltpu.PrefetchScalarGridSpec(
            num_scalar_prefetch=1,
            grid=(),
            in_specs=[vmem] * 6 + [hbm] * 2,
            out_specs=[vmem, vmem],
            scratch_shapes=[
                pltpu.VMEM(egu.shape, jnp.bfloat16),
                pltpu.VMEM(edn.shape, jnp.bfloat16),
                pltpu.VMEM((total, width), jnp.float32),
                pltpu.VMEM((total, width), jnp.float32),
                pltpu.VMEM((SLOT_TILE, width), jnp.float32),
                pltpu.VMEM((SLOT_TILE, width), jnp.float32),
                pltpu.VMEM((SLOT_TILE, 1), jnp.float32),
                pltpu.SemaphoreType.DMA((experts, 2)),
            ],
        ),
        out_shape=[shape, shape],
        name="experts",
        compiler_params=pltpu.CompilerParams(vmem_limit_bytes=60 << 20),
    )(spans, place[:, None, :], weight[:, None, :], place.T, weight.T, rows, grads, egu, edn)


def shards(
    tokens,
    attn_gain,
    w_qkv,
    w_out,
    ffn_gain,
    w_gu,
    w_dn,
    w_egu,
    w_edn,
    adapters,
    adapter_ids,
    parents,
    seg_lengths,
    routes,
    route_weights,
    cotangent,
):
    tree_count = tokens.shape[0]
    row_count = tokens.shape[1]
    contexts = lax.axis_size("context")
    tensors = lax.axis_size("tensor")
    fsdp_size = lax.axis_size("fsdp")
    tree_len = row_count * contexts
    token_count = tree_count * row_count
    local_heads = HEADS // tensors
    local_width = local_heads * HEAD_DIM
    local_ff = FF // tensors
    part_index = lax.axis_index("tensor")
    row_start = lax.axis_index("context") * row_count
    width_start = part_index * local_width
    ff_start = part_index * local_ff
    head_shape = (tree_count, row_count, local_heads, HEAD_DIM)
    wide_shape = (tree_count, tree_len, local_heads, HEAD_DIM)
    qkv_weight, output_matrix, gu_weight, down_matrix, gain_one, gain_two, adapter_cols = (
        lax.all_gather(w_qkv, "fsdp", axis=0, tiled=True),
        lax.all_gather(w_out, "fsdp", axis=1, tiled=True),
        lax.all_gather(w_gu, "fsdp", axis=0, tiled=True),
        lax.all_gather(w_dn, "fsdp", axis=1, tiled=True),
        lax.all_gather(attn_gain, "fsdp", axis=0, tiled=True),
        lax.all_gather(ffn_gain, "fsdp", axis=0, tiled=True),
        lax.all_gather(adapters, "fsdp", axis=0, tiled=True),
    )
    id_hot = (adapter_ids[:, None] == jnp.arange(ADAPTERS, dtype=jnp.int32)[None, :]).astype(
        jnp.bfloat16
    )
    own_cols = jnp.dot(id_hot, adapter_cols, preferred_element_type=jnp.float32)
    chosen = lax.all_gather(
        own_cols.astype(jnp.bfloat16), ("context", "tensor"), axis=1, tiled=True
    ).astype(jnp.float32)
    (
        a_qkv,
        query_key_value_adapter_up,
        a_out,
        output_adapter_up,
        a_gu,
        gate_up_adapter_up,
        a_dn,
        down_adapter_up,
    ) = unpack(chosen)
    b_qkv_part = lax.dynamic_slice_in_dim(query_key_value_adapter_up, width_start, local_width, 3)
    a_out_part = lax.dynamic_slice_in_dim(a_out, width_start, local_width, 1)
    b_gu_part = lax.dynamic_slice_in_dim(gate_up_adapter_up, ff_start, local_ff, 3)
    down_adapter_slice = lax.dynamic_slice_in_dim(a_dn, ff_start, local_ff, 1)
    ancestry, starts, offsets = jax.vmap(tree_layout)(seg_lengths, parents)
    ancestry_f = ancestry.astype(jnp.float32)
    key_ids = jnp.arange(tree_len, dtype=jnp.int32)
    query_ids = row_start + jnp.arange(row_count, dtype=jnp.int32)
    key_hot, key_positions = jax.vmap(locate, in_axes=(None, 0, 0))(key_ids, starts, offsets)
    key_hot = key_hot.astype(jnp.float32)
    query_hot = lax.dynamic_slice_in_dim(key_hot, row_start, row_count, 1)
    positions = lax.dynamic_slice_in_dim(key_positions, row_start, row_count, 1)
    reach = (jnp.einsum("trs,tsu->tru", query_hot, ancestry_f) > 0.5).astype(jnp.float32)
    visible = (jnp.einsum("tru,tku->trk", reach, key_hot) > 0.5) & (
        key_ids[None, None, :] <= query_ids[None, :, None]
    )
    cosine, sinus = angles(positions)
    tokens_f = tokens.astype(jnp.float32)
    scale_one = rms_scale(tokens_f)
    normed_one = (tokens_f * scale_one * gain_one.astype(jnp.float32)).astype(jnp.bfloat16)
    query_key_value_rank = jnp.einsum(
        "trd,tdm->trm", normed_one, a_qkv.astype(jnp.bfloat16), preferred_element_type=jnp.float32
    )
    rank_split = query_key_value_rank.reshape(tree_count, row_count, 3, RANK)
    projected_rows = jnp.einsum(
        "trd,djc->trjc", normed_one, qkv_weight, preferred_element_type=jnp.float32
    )
    projected_rows = projected_rows + adapter_scale * jnp.einsum(
        "trjk,tjkc->trjc", rank_split, b_qkv_part, precision=highest_precision
    )
    queries = rotate(projected_rows[:, :, 0].reshape(head_shape), cosine, sinus).astype(
        jnp.bfloat16
    )
    key_rows = (
        rotate(projected_rows[:, :, 1].reshape(head_shape), cosine, sinus)
        .astype(jnp.bfloat16)
        .reshape(tree_count, row_count, local_width)
    )
    value_rows = projected_rows[:, :, 2].astype(jnp.bfloat16)
    key_all, value_all = (
        lax.all_gather(key_rows, "context", axis=1, tiled=True),
        lax.all_gather(value_rows, "context", axis=1, tiled=True),
    )
    key_heads = key_all.reshape(wide_shape)
    value_heads = value_all.reshape(wide_shape)

    def attend(inputs):
        query_rows, key_block, value_block, visible_rows = inputs
        scores = (
            jnp.einsum("rhd,khd->hrk", query_rows, key_block, preferred_element_type=jnp.float32)
            * 0.125
        )
        scores = jnp.where(visible_rows[None], scores, masked_score)
        row_max = jnp.max(scores, axis=-1, keepdims=True)
        weights = jnp.exp(scores - row_max)
        totals = jnp.sum(weights, axis=-1, keepdims=True)
        probabilities = (weights / totals).astype(jnp.bfloat16)
        mixed_block = jnp.einsum(
            "hrk,khd->rhd", probabilities, value_block, preferred_element_type=jnp.float32
        )
        return (mixed_block.astype(jnp.bfloat16), (row_max + jnp.log(totals))[..., 0])

    mixed_heads, log_totals = lax.map(attend, (queries, key_heads, value_heads, visible))
    mixed_row_values = mixed_heads.reshape(tree_count, row_count, local_width)
    output_rank_rows = jnp.einsum(
        "trc,tck->trk",
        mixed_row_values,
        a_out_part.astype(jnp.bfloat16),
        preferred_element_type=jnp.float32,
    )
    attention_slice = jnp.einsum(
        "trc,cd->trd", mixed_row_values, output_matrix, preferred_element_type=jnp.float32
    )
    attention_slice = attention_slice + adapter_scale * jnp.einsum(
        "trk,tkd->trd", output_rank_rows, output_adapter_up, precision=highest_precision
    )
    attn_total = lax.psum(attention_slice, "tensor")
    residual = tokens_f + attn_total
    scale_two = rms_scale(residual)
    normed_two = (residual * scale_two * gain_two.astype(jnp.float32)).astype(jnp.bfloat16)
    gate_up_rank_rows = jnp.einsum(
        "trd,tdm->trm", normed_two, a_gu.astype(jnp.bfloat16), preferred_element_type=jnp.float32
    ).reshape(tree_count, row_count, 2, RANK)
    gate_up_matrix = jnp.einsum(
        "trd,djf->trjf", normed_two, gu_weight, preferred_element_type=jnp.float32
    )
    gate_up_matrix = gate_up_matrix + adapter_scale * jnp.einsum(
        "trjk,tjkf->trjf", gate_up_rank_rows, b_gu_part, precision=highest_precision
    )
    gate_pre = gate_up_matrix[:, :, 0]
    up_pre = gate_up_matrix[:, :, 1]
    hidden_state = (silu_of(gate_pre) * up_pre).astype(jnp.bfloat16)
    down_rank_rows = jnp.einsum(
        "xbw,xwz->xbz",
        hidden_state,
        down_adapter_slice.astype(jnp.bfloat16),
        preferred_element_type=jnp.float32,
    )
    shared_slice = jnp.einsum(
        "wmg,gh->wmh", hidden_state, down_matrix, preferred_element_type=jnp.float32
    )
    shared_slice = shared_slice + adapter_scale * jnp.einsum(
        "trk,tkd->trd", down_rank_rows, down_adapter_up, precision=highest_precision
    )
    routes_all = lax.all_gather(routes[0], "fsdp", axis=0, tiled=True)
    route_weights_all = lax.all_gather(route_weights[0], "fsdp", axis=0, tiled=True)
    cotangent_all = lax.all_gather(cotangent[0], "fsdp", axis=0, tiled=True)
    normed_all = lax.all_gather(normed_two[0], "fsdp", axis=0, tiled=True)
    own_experts = EXPERTS // fsdp_size
    spans, place, weight = moe_layout(
        routes_all, route_weights_all, lax.axis_index("fsdp") * own_experts, own_experts
    )
    moe_all, moe_back_all = moe_call(
        spans, place, weight, normed_all, cotangent_all, w_egu.transpose(0, 2, 1, 3), w_edn
    )
    moe_part = lax.psum_scatter(moe_all, "fsdp", scatter_dimension=0, tiled=True).astype(jnp.float32)
    moe_grad = lax.psum_scatter(moe_back_all, "fsdp", scatter_dimension=0, tiled=True).astype(
        jnp.float32
    )
    ffn_total = lax.psum(
        (shared_slice + moe_part.reshape(tree_count, row_count, D)).astype(jnp.bfloat16), "tensor"
    ).astype(jnp.float32)
    block_out = residual + ffn_total
    output_gradient = cotangent.astype(jnp.float32)
    grad_hidden = jnp.einsum(
        "boz,kz->bok", cotangent, down_matrix, preferred_element_type=jnp.float32
    )
    down_rank_gradient = adapter_scale * jnp.einsum(
        "trd,tkd->trk",
        cotangent,
        down_adapter_up.astype(jnp.bfloat16),
        preferred_element_type=jnp.float32,
    )
    grad_hidden = grad_hidden + jnp.einsum(
        "jax,jnx->jan", down_rank_gradient, down_adapter_slice, precision=highest_precision
    )
    sigmoid_gate = jax.nn.sigmoid(gate_pre)
    grad_gate = grad_hidden * up_pre * sigmoid_gate * (1.0 + gate_pre * (1.0 - sigmoid_gate))
    grad_up = grad_hidden * gate_pre * sigmoid_gate
    grad_gu = jnp.stack([grad_gate, grad_up], axis=2).astype(jnp.bfloat16)
    grad_normed_two = jnp.einsum(
        "trjf,djf->trd", grad_gu, gu_weight, preferred_element_type=jnp.float32
    )
    gate_up_rank_gradient = adapter_scale * jnp.einsum(
        "trjf,tjkf->trjk",
        grad_gu,
        b_gu_part.astype(jnp.bfloat16),
        preferred_element_type=jnp.float32,
    )
    rank_gu_flat = gate_up_rank_gradient.reshape(tree_count, row_count, 2 * RANK)
    grad_normed_two = grad_normed_two + jnp.einsum(
        "trm,tdm->trd", rank_gu_flat, a_gu, precision=highest_precision
    )
    grad_normed_two = grad_normed_two + moe_grad.reshape(tree_count, row_count, D)
    grad_normed_two = lax.psum(grad_normed_two, "tensor")
    grad_residual = output_gradient + norm_back(
        residual, scale_two, gain_two.astype(jnp.float32), grad_normed_two
    )
    grad_attn = grad_residual.astype(jnp.bfloat16)
    grad_mixed = jnp.einsum(
        "trd,cd->trc", grad_attn, output_matrix, preferred_element_type=jnp.float32
    )
    output_rank_gradient = adapter_scale * jnp.einsum(
        "trd,tkd->trk",
        grad_attn,
        output_adapter_up.astype(jnp.bfloat16),
        preferred_element_type=jnp.float32,
    )
    grad_mixed = grad_mixed + jnp.einsum(
        "trk,tck->trc", output_rank_gradient, a_out_part, precision=highest_precision
    )
    grad_mixed_heads = grad_mixed.astype(jnp.bfloat16).reshape(head_shape)

    def attend_back(inputs):
        query_rows, key_block, value_block, visible_rows, log_total, grad_rows = inputs
        scores = (
            jnp.einsum("rhd,khd->hrk", query_rows, key_block, preferred_element_type=jnp.float32)
            * 0.125
        )
        scores = jnp.where(visible_rows[None], scores, masked_score)
        probabilities = jnp.exp(scores - log_total[..., None])
        grad_values = jnp.einsum(
            "hrk,rhd->khd",
            probabilities.astype(jnp.bfloat16),
            grad_rows,
            preferred_element_type=jnp.float32,
        )
        grad_probs = jnp.einsum(
            "rhd,khd->hrk", grad_rows, value_block, preferred_element_type=jnp.float32
        )
        inner_sum = jnp.sum(probabilities * grad_probs, axis=-1, keepdims=True)
        grad_scores = (probabilities * (grad_probs - inner_sum)).astype(jnp.bfloat16)
        grad_query = (
            jnp.einsum("hrk,khd->rhd", grad_scores, key_block, preferred_element_type=jnp.float32)
            * 0.125
        )
        grad_keys = (
            jnp.einsum("hrk,rhd->khd", grad_scores, query_rows, preferred_element_type=jnp.float32)
            * 0.125
        )
        span = key_block.shape[0]
        return (
            grad_query,
            jnp.concatenate([grad_keys.reshape(span, -1), grad_values.reshape(span, -1)], axis=1),
        )

    grad_query_rot, grad_key_value = lax.map(
        attend_back, (queries, key_heads, value_heads, visible, log_totals, grad_mixed_heads)
    )
    own_grads = lax.psum_scatter(
        grad_key_value.astype(jnp.bfloat16), "context", scatter_dimension=1, tiled=True
    ).astype(jnp.float32)
    grad_query = unrotate(grad_query_rot, cosine, sinus).reshape(tree_count, row_count, local_width)
    grad_key = unrotate(own_grads[..., :local_width].reshape(head_shape), cosine, sinus).reshape(
        tree_count, row_count, local_width
    )
    grad_qkv = jnp.stack([grad_query, grad_key, own_grads[..., local_width:]], axis=2).astype(
        jnp.bfloat16
    )
    grad_normed_one = jnp.einsum(
        "trjc,djc->trd", grad_qkv, qkv_weight, preferred_element_type=jnp.float32
    )
    query_key_value_rank_gradient = adapter_scale * jnp.einsum(
        "trjc,tjkc->trjk",
        grad_qkv,
        b_qkv_part.astype(jnp.bfloat16),
        preferred_element_type=jnp.float32,
    )
    rank_qkv_flat = query_key_value_rank_gradient.reshape(tree_count, row_count, 3 * RANK)
    grad_normed_one = grad_normed_one + jnp.einsum(
        "trm,tdm->trd", rank_qkv_flat, a_qkv, precision=highest_precision
    )
    grad_normed_one = lax.psum(grad_normed_one.astype(jnp.bfloat16), "tensor").astype(jnp.float32)
    input_grad = grad_residual + norm_back(
        tokens_f, scale_one, gain_one.astype(jnp.float32), grad_normed_one
    )
    grad_qkv_f = grad_qkv.astype(jnp.float32)
    grad_gu_f = grad_gu.astype(jnp.float32)
    grad_a_qkv = jnp.einsum(
        "trd,trm->tdm", normed_one.astype(jnp.float32), rank_qkv_flat, precision=highest_precision
    )
    query_key_value_gradient_slice = adapter_scale * jnp.einsum(
        "trjk,trjc->tjkc", rank_split, grad_qkv_f, precision=highest_precision
    )
    grad_b_qkv = lax.dynamic_update_slice_in_dim(
        jnp.zeros((tree_count, 3, RANK, D), jnp.float32),
        query_key_value_gradient_slice,
        width_start,
        3,
    )
    grad_a_out_part = jnp.einsum(
        "trc,trk->tck",
        mixed_row_values.astype(jnp.float32),
        output_rank_gradient,
        precision=highest_precision,
    )
    grad_a_out = lax.dynamic_update_slice_in_dim(
        jnp.zeros((tree_count, D, RANK), jnp.float32), grad_a_out_part, width_start, 1
    )
    output_adapter_up_gradient = adapter_scale * jnp.einsum(
        "ags,agh->ash", output_rank_rows, grad_attn.astype(jnp.float32), precision=highest_precision
    )
    grad_a_gu = jnp.einsum(
        "trd,trm->tdm", normed_two.astype(jnp.float32), rank_gu_flat, precision=highest_precision
    )
    gate_up_adapter_gradient_slice = adapter_scale * jnp.einsum(
        "trjk,trjf->tjkf", gate_up_rank_rows, grad_gu_f, precision=highest_precision
    )
    grad_b_gu = lax.dynamic_update_slice_in_dim(
        jnp.zeros((tree_count, 2, RANK, FF), jnp.float32),
        gate_up_adapter_gradient_slice,
        ff_start,
        3,
    )
    grad_a_dn_part = jnp.einsum(
        "uya,uye->uae",
        hidden_state.astype(jnp.float32),
        down_rank_gradient,
        precision=highest_precision,
    )
    grad_a_dn = lax.dynamic_update_slice_in_dim(
        jnp.zeros((tree_count, FF, RANK), jnp.float32), grad_a_dn_part, ff_start, 1
    )
    down_adapter_up_gradient = adapter_scale * jnp.einsum(
        "ags,agh->ash", down_rank_rows, output_gradient, precision=highest_precision
    )
    grad_pieces = [
        grad_a_qkv,
        grad_b_qkv,
        grad_a_out,
        output_adapter_up_gradient,
        grad_a_gu,
        grad_b_gu,
        grad_a_dn,
        down_adapter_up_gradient,
    ]
    packed = jnp.concatenate([piece.reshape(tree_count, -1) for piece in grad_pieces], axis=1)
    own_part = lax.psum_scatter(
        packed[0], ("context", "tensor"), scatter_dimension=0, tiled=True
    )
    part_all = lax.all_gather(own_part[None], "fsdp", axis=0, tiled=True)
    ids_all = lax.all_gather(adapter_ids, "fsdp", axis=0, tiled=True)
    rows_own = ADAPTERS // fsdp_size
    own_ids = lax.axis_index("fsdp") * rows_own + jnp.arange(rows_own, dtype=jnp.int32)
    own_hot = (own_ids[:, None] == ids_all[None, :]).astype(jnp.float32)
    adapter_grads = jnp.sum(own_hot[:, :, None] * part_all[None], axis=1)
    return (block_out, input_grad, adapter_grads)


def solution(mesh):
    return jax.shard_map(
        shards,
        mesh=mesh,
        in_specs=(
            P("fsdp", "context", None),
            P("fsdp"),
            P("fsdp", None, "tensor"),
            P("tensor", "fsdp"),
            P("fsdp"),
            P("fsdp", None, "tensor"),
            P("tensor", "fsdp"),
            P("fsdp", None, None, "tensor"),
            P("fsdp", "tensor", None),
            P("fsdp", ("context", "tensor")),
            P("fsdp"),
            P("fsdp", None),
            P("fsdp", None),
            P("fsdp", "context", None),
            P("fsdp", "context", None),
            P("fsdp", "context", None),
        ),
        out_specs=(
            P("fsdp", "context", None),
            P("fsdp", "context", None),
            P("fsdp", ("context", "tensor")),
        ),
        check_vma=False,
    )
```

```python
import jax
import jax.numpy as jnp
import functools

from jax import lax
from jax.experimental import pallas as pl
from jax.experimental.pallas import tpu as pltpu
from jax.sharding import PartitionSpec as P

D = 768
HEADS = 12
HEAD_DIM = 64
FF = 2048
EXPERTS = 8
TOPK = 2
RANK = 16
ADAPTERS = 8
PARAMS = 233472


epsilon = 1e-06
adapter_scale = 2.0
rope_base = 10000.0
masked_score = -1e30
highest_precision = lax.Precision.HIGHEST


def unpack(flat_params):
    leading = flat_params.shape[:-1]
    block_shapes = [
        (D, 3 * RANK),
        (3, RANK, D),
        (D, RANK),
        (RANK, D),
        (D, 2 * RANK),
        (2, RANK, FF),
        (FF, RANK),
        (RANK, D),
    ]
    pieces = []
    offset = 0
    for block_shape in block_shapes:
        extent = 1
        for factor in block_shape:
            extent = extent * factor
        pieces.append(flat_params[..., offset : offset + extent].reshape(leading + block_shape))
        offset = offset + extent
    return pieces


def silu_of(values):
    return values * jax.nn.sigmoid(values)


def rms_scale(values):
    return lax.rsqrt(jnp.mean(values * values, axis=-1, keepdims=True) + epsilon)


def norm_back(values, scaling, gain_values, gradient):
    weighted = gradient * gain_values
    inner_mean = jnp.mean(values * weighted, axis=-1, keepdims=True)
    return scaling * weighted - values * (scaling * scaling * scaling) * inner_mean


def rotate(values, cosine, sinus):
    half_dim = values.shape[-1] // 2
    front_half = values[..., :half_dim]
    back_half = values[..., half_dim:]
    return jnp.concatenate(
        [front_half * cosine - back_half * sinus, back_half * cosine + front_half * sinus], axis=-1
    )


def unrotate(gradient, cosine, sinus):
    half_dim = gradient.shape[-1] // 2
    front_half = gradient[..., :half_dim]
    back_half = gradient[..., half_dim:]
    return jnp.concatenate(
        [front_half * cosine + back_half * sinus, back_half * cosine - front_half * sinus], axis=-1
    )


def angles(positions):
    half_dim = HEAD_DIM // 2
    frequency = rope_base ** (-(jnp.arange(half_dim, dtype=jnp.float32) * 2.0) / HEAD_DIM)
    turned = positions.astype(jnp.float32)[..., None] * frequency
    return (jnp.cos(turned)[..., None, :], jnp.sin(turned)[..., None, :])


def tree_layout(lengths, parent_ids):
    seg_count = lengths.shape[0]
    seg_ids = jnp.arange(seg_count, dtype=jnp.int32)
    parent_hot = (parent_ids[:, None] == seg_ids[None, :]).astype(jnp.int32)
    grand_hot = jnp.dot(parent_hot, parent_hot)
    same_seg = (seg_ids[:, None] == seg_ids[None, :]).astype(jnp.int32)
    ancestry = (same_seg + parent_hot + grand_hot > 0).astype(jnp.int32)
    starts = jnp.cumsum(lengths) - lengths
    offsets = jnp.sum((ancestry - same_seg) * lengths[None, :], axis=1)
    return (ancestry, starts, offsets)


def locate(row_ids, starts, offsets):
    segment = jnp.sum((row_ids[:, None] >= starts[None, :]).astype(jnp.int32), axis=1) - 1
    seg_hot = (segment[:, None] == jnp.arange(starts.shape[0], dtype=jnp.int32)[None, :]).astype(
        jnp.int32
    )
    positions = (
        row_ids
        - jnp.sum(seg_hot * starts[None, :], axis=1)
        + jnp.sum(seg_hot * offsets[None, :], axis=1)
    )
    return (seg_hot, positions)


SLOT_TILE = 256
TOKEN_TILE = 256


def nt_dot(left, right):
    return lax.dot_general(left, right, (((1,), (1,)), ((), ())), preferred_element_type=jnp.float32)


def tn_dot(left, right):
    return lax.dot_general(left, right, (((0,), (0,)), ((), ())), preferred_element_type=jnp.float32)


def nn_dot(left, right):
    return jnp.dot(left, right, preferred_element_type=jnp.float32)


def moe_kernel(
    spans,
    place_row,
    weight_row,
    place_col,
    weight_col,
    rows_ref,
    grads_ref,
    egu_hbm,
    edn_hbm,
    out_ref,
    back_ref,
    egu_ref,
    edn_ref,
    out_sum,
    back_sum,
    taken,
    taken_grad,
    slot_weight,
    sems,
):
    experts = egu_hbm.shape[0]
    copies = []
    for e in range(experts):
        copies.append(
            (
                pltpu.make_async_copy(egu_hbm.at[e], egu_ref.at[e], sems.at[e, 0]),
                pltpu.make_async_copy(edn_hbm.at[e], edn_ref.at[e], sems.at[e, 1]),
            )
        )
        copies[e][0].start()
        copies[e][1].start()
    out_sum[...] = jnp.zeros_like(out_sum)
    back_sum[...] = jnp.zeros_like(back_sum)
    slot_rows = lax.broadcasted_iota(jnp.int32, (SLOT_TILE, TOKEN_TILE), 0)
    slot_cols = lax.broadcasted_iota(jnp.int32, (TOKEN_TILE, SLOT_TILE), 1)
    for e in range(experts):
        copies[e][0].wait()
        copies[e][1].wait()

        def tile_step(i, carry, e=e):
            low = spans[e, 1 + 2 * i]
            high = spans[e, 2 + 2 * i]
            first = i * SLOT_TILE
            taken[...] = jnp.zeros_like(taken)
            taken_grad[...] = jnp.zeros_like(taken_grad)
            slot_weight[...] = jnp.zeros_like(slot_weight)

            def fetch(b, c):
                start = pl.multiple_of(b * TOKEN_TILE, TOKEN_TILE)
                hit = place_row[e, :, pl.ds(start, TOKEN_TILE)] == slot_rows + first
                pick = jnp.where(hit, 1.0, 0.0).astype(jnp.bfloat16)
                taken[...] += nn_dot(pick, rows_ref[pl.ds(start, TOKEN_TILE), :])
                taken_grad[...] += nn_dot(pick, grads_ref[pl.ds(start, TOKEN_TILE), :])
                slot_weight[...] += jnp.sum(
                    jnp.where(hit, weight_row[e, :, pl.ds(start, TOKEN_TILE)], 0.0),
                    axis=1,
                    keepdims=True,
                )
                return c

            lax.fori_loop(low, high, fetch, 0)
            inputs = taken[...].astype(jnp.bfloat16)
            gate_pre = nn_dot(inputs, egu_ref[e, 0])
            up_pre = nn_dot(inputs, egu_ref[e, 1])
            sigmoid_gate = jax.nn.sigmoid(gate_pre)
            silu = gate_pre * sigmoid_gate
            active = (silu * up_pre).astype(jnp.bfloat16)
            result = nn_dot(active, edn_ref[e]).astype(jnp.bfloat16)
            grad_active = nt_dot(taken_grad[...].astype(jnp.bfloat16), edn_ref[e])
            grad_active = grad_active * slot_weight[...]
            grad_gate = (
                grad_active * up_pre * sigmoid_gate * (1.0 + gate_pre * (1.0 - sigmoid_gate))
            ).astype(jnp.bfloat16)
            grad_up = (grad_active * silu).astype(jnp.bfloat16)
            grad_rows = (
                nt_dot(grad_gate, egu_ref[e, 0]) + nt_dot(grad_up, egu_ref[e, 1])
            ).astype(jnp.bfloat16)

            def give(b, c):
                start = pl.multiple_of(b * TOKEN_TILE, TOKEN_TILE)
                block = pl.ds(start, TOKEN_TILE)
                hit = place_col[block, e : e + 1] == slot_cols + first
                pick = jnp.where(hit, 1.0, 0.0).astype(jnp.bfloat16)
                out_sum[block, :] += nn_dot(pick, result) * weight_col[block, e : e + 1]
                back_sum[block, :] += nn_dot(pick, grad_rows)
                return c

            lax.fori_loop(low, high, give, 0)
            return carry

        lax.fori_loop(0, spans[e, 0], tile_step, 0)
    out_ref[...] = out_sum[...].astype(jnp.bfloat16)
    back_ref[...] = back_sum[...].astype(jnp.bfloat16)


def moe_layout(routes, weights, first_expert, experts):
    total = routes.shape[0]
    blocks = total // TOKEN_TILE
    ids = first_expert + jnp.arange(experts, dtype=jnp.int32)
    hits = routes[None] == ids[:, None, None]
    hit = jnp.any(hits, axis=-1)
    weight = jnp.sum(jnp.where(hits, weights.astype(jnp.float32)[None], 0.0), axis=-1)
    counted = hit.astype(jnp.int32)
    upto = jnp.cumsum(counted, axis=1)
    place = jnp.where(hit, upto - 1, -1)
    ends = upto.reshape(experts, blocks, TOKEN_TILE)[:, :, -1]
    begins = jnp.concatenate([jnp.zeros((experts, 1), jnp.int32), ends[:, :-1]], axis=1)
    count = ends[:, -1]
    tiles = total // SLOT_TILE
    tile_start = jnp.arange(tiles, dtype=jnp.int32) * SLOT_TILE
    low = jnp.sum((ends[:, None, :] <= tile_start[None, :, None]).astype(jnp.int32), axis=2)
    tile_end = jnp.minimum(tile_start[None] + SLOT_TILE, count[:, None])
    high = jnp.sum((begins[:, None, :] < tile_end[:, :, None]).astype(jnp.int32), axis=2)
    spans = jnp.stack([low, high], axis=2).reshape(experts, 2 * tiles)
    spans = jnp.concatenate([((count + SLOT_TILE - 1) // SLOT_TILE)[:, None], spans], axis=1)
    return spans, place, weight


def moe_call(spans, place, weight, rows, grads, egu, edn):
    total, width = rows.shape
    experts, _, _, units = egu.shape
    vmem = pl.BlockSpec(memory_space=pltpu.VMEM)
    hbm = pl.BlockSpec(memory_space=pl.ANY)
    shape = jax.ShapeDtypeStruct((total, width), jnp.bfloat16)
    return pl.pallas_call(
        moe_kernel,
        grid_spec=pltpu.PrefetchScalarGridSpec(
            num_scalar_prefetch=1,
            grid=(),
            in_specs=[vmem] * 6 + [hbm] * 2,
            out_specs=[vmem, vmem],
            scratch_shapes=[
                pltpu.VMEM(egu.shape, jnp.bfloat16),
                pltpu.VMEM(edn.shape, jnp.bfloat16),
                pltpu.VMEM((total, width), jnp.float32),
                pltpu.VMEM((total, width), jnp.float32),
                pltpu.VMEM((SLOT_TILE, width), jnp.float32),
                pltpu.VMEM((SLOT_TILE, width), jnp.float32),
                pltpu.VMEM((SLOT_TILE, 1), jnp.float32),
                pltpu.SemaphoreType.DMA((experts, 2)),
            ],
        ),
        out_shape=[shape, shape],
        name="experts",
        compiler_params=pltpu.CompilerParams(vmem_limit_bytes=60 << 20),
    )(spans, place[:, None, :], weight[:, None, :], place.T, weight.T, rows, grads, egu, edn)


MESH = pl.DeviceIdType.MESH


def place_of():
    return lax.axis_index("fsdp"), lax.axis_index("context"), lax.axis_index("tensor")


def greet(devices):
    barrier = pltpu.get_barrier_semaphore()
    for device in devices:
        pl.semaphore_signal(barrier, inc=1, device_id=device, device_id_type=MESH)
    pl.semaphore_wait(barrier, len(devices))


def send(source, target, send_sem, recv_sem, device):
    return pltpu.make_async_remote_copy(
        src_ref=source,
        dst_ref=target,
        send_sem=send_sem,
        recv_sem=recv_sem,
        device_id=device,
        device_id_type=MESH,
    )


def small_kernel(
    sizes,
    ids_ref,
    adapters_ref,
    gains_ref,
    table_ref,
    chosen_ref,
    gains_all,
    table_all,
    adapters_all,
    send_sems,
    recv_sems,
):
    fsdp, contexts, _ = sizes
    f, c, t = place_of()
    peers = [(lax.rem(f + k, fsdp), c, t) for k in range(1, fsdp)]
    stacked = [(f, lax.rem(c + k, contexts), t) for k in range(1, contexts)]
    sibling = (f, c, 1 - t)
    greet(peers + stacked + [sibling])
    first = []
    for k, peer in enumerate(peers):
        for j, (source, target) in enumerate(
            ((adapters_ref, adapters_all), (gains_ref, gains_all), (table_ref, table_all))
        ):
            copy = send(source, target.at[f], send_sems.at[j, k], recv_sems.at[j, k], peer)
            copy.start()
            first.append(copy)
    adapters_all[f] = adapters_ref[...]
    gains_all[f] = gains_ref[...]
    table_all[f] = table_ref[...]
    for copy in first:
        copy.wait()
    wanted = ids_ref[0]
    rows = RANK
    own = ADAPTERS // fsdp
    total = jnp.zeros((rows, adapters_ref.shape[1]), jnp.float32)
    for a in range(ADAPTERS):
        block = adapters_all[a // own, pl.ds((a % own) * rows, rows), :].astype(jnp.float32)
        total = total + jnp.where(wanted == a, block, 0.0)
    chosen_ref[t, c] = total.astype(jnp.bfloat16)
    second = []
    for k, other in enumerate(stacked):
        copy = send(
            chosen_ref.at[t, c], chosen_ref.at[t, c], send_sems.at[3, k], recv_sems.at[3, k], other
        )
        copy.start()
        second.append(copy)
    for copy in second:
        copy.wait()
    last = send(chosen_ref.at[t], chosen_ref.at[t], send_sems.at[4, 0], recv_sems.at[4, 0], sibling)
    last.start()
    last.wait()


def small_call(sizes, ids, adapters, gains, table):
    fsdp, contexts, tensors = sizes
    slots = max(fsdp, contexts)
    vmem = pl.BlockSpec(memory_space=pltpu.VMEM)
    return pl.pallas_call(
        functools.partial(small_kernel, sizes),
        in_specs=[pl.BlockSpec(memory_space=pltpu.SMEM), vmem, vmem, vmem],
        out_specs=[vmem] * 3,
        out_shape=[
            jax.ShapeDtypeStruct((tensors, contexts, RANK, adapters.shape[1]), jnp.bfloat16),
            jax.ShapeDtypeStruct((fsdp,) + gains.shape, gains.dtype),
            jax.ShapeDtypeStruct((fsdp,) + table.shape, table.dtype),
        ],
        scratch_shapes=[
            pltpu.VMEM((fsdp,) + adapters.shape, adapters.dtype),
            pltpu.SemaphoreType.DMA((5, slots)),
            pltpu.SemaphoreType.DMA((5, slots)),
        ],
        name="small_gather",
        compiler_params=pltpu.CompilerParams(
            collective_id=1, has_side_effects=True, vmem_limit_bytes=60 << 20
        ),
    )(ids, adapters, gains, table)


def shards(
    tokens,
    attn_gain,
    w_qkv,
    w_out,
    ffn_gain,
    w_gu,
    w_dn,
    w_egu,
    w_edn,
    adapters,
    adapter_ids,
    parents,
    seg_lengths,
    routes,
    route_weights,
    cotangent,
):
    tree_count = tokens.shape[0]
    row_count = tokens.shape[1]
    contexts = lax.axis_size("context")
    tensors = lax.axis_size("tensor")
    fsdp_size = lax.axis_size("fsdp")
    tree_len = row_count * contexts
    token_count = tree_count * row_count
    local_heads = HEADS // tensors
    local_width = local_heads * HEAD_DIM
    local_ff = FF // tensors
    part_index = lax.axis_index("tensor")
    row_start = lax.axis_index("context") * row_count
    width_start = part_index * local_width
    ff_start = part_index * local_ff
    head_shape = (tree_count, row_count, local_heads, HEAD_DIM)
    wide_shape = (tree_count, tree_len, local_heads, HEAD_DIM)
    qkv_weight, output_matrix, gu_weight, down_matrix = (
        lax.all_gather(w_qkv, "fsdp", axis=0, tiled=True),
        lax.all_gather(w_out, "fsdp", axis=1, tiled=True),
        lax.all_gather(w_gu, "fsdp", axis=0, tiled=True),
        lax.all_gather(w_dn, "fsdp", axis=1, tiled=True),
    )
    sizes = (fsdp_size, contexts, tensors)
    own_adapters = adapters.shape[0]
    own_width = D // fsdp_size
    gains = jnp.broadcast_to(jnp.concatenate([attn_gain, ffn_gain])[None], (16, 2 * own_width))
    route_table = jnp.concatenate(
        [
            routes[0].astype(jnp.float32).T,
            route_weights[0].astype(jnp.float32).T,
            jnp.zeros((4, row_count), jnp.float32),
        ]
    )
    chosen_parts, gains_all, table_all = small_call(
        sizes, adapter_ids, adapters.reshape(own_adapters * RANK, -1), gains, route_table
    )
    chosen = chosen_parts.transpose(1, 0, 2, 3).reshape(1, PARAMS).astype(jnp.float32)
    gain_one = gains_all[:, 0, :own_width].reshape(D)
    gain_two = gains_all[:, 0, own_width:].reshape(D)
    routes_all = table_all[:, 0:2].transpose(0, 2, 1).reshape(-1, TOPK).astype(jnp.int32)
    route_weights_all = table_all[:, 2:4].transpose(0, 2, 1).reshape(-1, TOPK)
    (
        a_qkv,
        query_key_value_adapter_up,
        a_out,
        output_adapter_up,
        a_gu,
        gate_up_adapter_up,
        a_dn,
        down_adapter_up,
    ) = unpack(chosen)
    b_qkv_part = lax.dynamic_slice_in_dim(query_key_value_adapter_up, width_start, local_width, 3)
    a_out_part = lax.dynamic_slice_in_dim(a_out, width_start, local_width, 1)
    b_gu_part = lax.dynamic_slice_in_dim(gate_up_adapter_up, ff_start, local_ff, 3)
    down_adapter_slice = lax.dynamic_slice_in_dim(a_dn, ff_start, local_ff, 1)
    ancestry, starts, offsets = jax.vmap(tree_layout)(seg_lengths, parents)
    ancestry_f = ancestry.astype(jnp.float32)
    key_ids = jnp.arange(tree_len, dtype=jnp.int32)
    query_ids = row_start + jnp.arange(row_count, dtype=jnp.int32)
    key_hot, key_positions = jax.vmap(locate, in_axes=(None, 0, 0))(key_ids, starts, offsets)
    key_hot = key_hot.astype(jnp.float32)
    query_hot = lax.dynamic_slice_in_dim(key_hot, row_start, row_count, 1)
    positions = lax.dynamic_slice_in_dim(key_positions, row_start, row_count, 1)
    reach = (jnp.einsum("trs,tsu->tru", query_hot, ancestry_f) > 0.5).astype(jnp.float32)
    visible = (jnp.einsum("tru,tku->trk", reach, key_hot) > 0.5) & (
        key_ids[None, None, :] <= query_ids[None, :, None]
    )
    cosine, sinus = angles(positions)
    tokens_f = tokens.astype(jnp.float32)
    scale_one = rms_scale(tokens_f)
    normed_one = (tokens_f * scale_one * gain_one.astype(jnp.float32)).astype(jnp.bfloat16)
    query_key_value_rank = jnp.einsum(
        "trd,tdm->trm", normed_one, a_qkv.astype(jnp.bfloat16), preferred_element_type=jnp.float32
    )
    rank_split = query_key_value_rank.reshape(tree_count, row_count, 3, RANK)
    projected_rows = jnp.einsum(
        "trd,djc->trjc", normed_one, qkv_weight, preferred_element_type=jnp.float32
    )
    projected_rows = projected_rows + adapter_scale * jnp.einsum(
        "trjk,tjkc->trjc", rank_split, b_qkv_part, precision=highest_precision
    )
    queries = rotate(projected_rows[:, :, 0].reshape(head_shape), cosine, sinus).astype(
        jnp.bfloat16
    )
    key_rows = (
        rotate(projected_rows[:, :, 1].reshape(head_shape), cosine, sinus)
        .astype(jnp.bfloat16)
        .reshape(tree_count, row_count, local_width)
    )
    value_rows = projected_rows[:, :, 2].astype(jnp.bfloat16)
    key_all, value_all = (
        lax.all_gather(key_rows, "context", axis=1, tiled=True),
        lax.all_gather(value_rows, "context", axis=1, tiled=True),
    )
    key_heads = key_all.reshape(wide_shape)
    value_heads = value_all.reshape(wide_shape)

    def attend(inputs):
        query_rows, key_block, value_block, visible_rows = inputs
        scores = (
            jnp.einsum("rhd,khd->hrk", query_rows, key_block, preferred_element_type=jnp.float32)
            * 0.125
        )
        scores = jnp.where(visible_rows[None], scores, masked_score)
        row_max = jnp.max(scores, axis=-1, keepdims=True)
        weights = jnp.exp(scores - row_max)
        totals = jnp.sum(weights, axis=-1, keepdims=True)
        probabilities = (weights / totals).astype(jnp.bfloat16)
        mixed_block = jnp.einsum(
            "hrk,khd->rhd", probabilities, value_block, preferred_element_type=jnp.float32
        )
        return (mixed_block.astype(jnp.bfloat16), (row_max + jnp.log(totals))[..., 0])

    mixed_heads, log_totals = lax.map(attend, (queries, key_heads, value_heads, visible))
    mixed_row_values = mixed_heads.reshape(tree_count, row_count, local_width)
    output_rank_rows = jnp.einsum(
        "trc,tck->trk",
        mixed_row_values,
        a_out_part.astype(jnp.bfloat16),
        preferred_element_type=jnp.float32,
    )
    attention_slice = jnp.einsum(
        "trc,cd->trd", mixed_row_values, output_matrix, preferred_element_type=jnp.float32
    )
    attention_slice = attention_slice + adapter_scale * jnp.einsum(
        "trk,tkd->trd", output_rank_rows, output_adapter_up, precision=highest_precision
    )
    attn_total = lax.psum(attention_slice, "tensor")
    residual = tokens_f + attn_total
    scale_two = rms_scale(residual)
    normed_two = (residual * scale_two * gain_two.astype(jnp.float32)).astype(jnp.bfloat16)
    gate_up_rank_rows = jnp.einsum(
        "trd,tdm->trm", normed_two, a_gu.astype(jnp.bfloat16), preferred_element_type=jnp.float32
    ).reshape(tree_count, row_count, 2, RANK)
    gate_up_matrix = jnp.einsum(
        "trd,djf->trjf", normed_two, gu_weight, preferred_element_type=jnp.float32
    )
    gate_up_matrix = gate_up_matrix + adapter_scale * jnp.einsum(
        "trjk,tjkf->trjf", gate_up_rank_rows, b_gu_part, precision=highest_precision
    )
    gate_pre = gate_up_matrix[:, :, 0]
    up_pre = gate_up_matrix[:, :, 1]
    hidden_state = (silu_of(gate_pre) * up_pre).astype(jnp.bfloat16)
    down_rank_rows = jnp.einsum(
        "xbw,xwz->xbz",
        hidden_state,
        down_adapter_slice.astype(jnp.bfloat16),
        preferred_element_type=jnp.float32,
    )
    shared_slice = jnp.einsum(
        "wmg,gh->wmh", hidden_state, down_matrix, preferred_element_type=jnp.float32
    )
    shared_slice = shared_slice + adapter_scale * jnp.einsum(
        "trk,tkd->trd", down_rank_rows, down_adapter_up, precision=highest_precision
    )
    cotangent_all = lax.all_gather(cotangent[0], "fsdp", axis=0, tiled=True)
    normed_all = lax.all_gather(normed_two[0], "fsdp", axis=0, tiled=True)
    own_experts = EXPERTS // fsdp_size
    spans, place, weight = moe_layout(
        routes_all, route_weights_all, lax.axis_index("fsdp") * own_experts, own_experts
    )
    moe_all, moe_back_all = moe_call(
        spans, place, weight, normed_all, cotangent_all, w_egu.transpose(0, 2, 1, 3), w_edn
    )
    moe_part = lax.psum_scatter(moe_all, "fsdp", scatter_dimension=0, tiled=True).astype(jnp.float32)
    moe_grad = lax.psum_scatter(moe_back_all, "fsdp", scatter_dimension=0, tiled=True).astype(
        jnp.float32
    )
    ffn_total = lax.psum(
        (shared_slice + moe_part.reshape(tree_count, row_count, D)).astype(jnp.bfloat16), "tensor"
    ).astype(jnp.float32)
    block_out = residual + ffn_total
    output_gradient = cotangent.astype(jnp.float32)
    grad_hidden = jnp.einsum(
        "boz,kz->bok", cotangent, down_matrix, preferred_element_type=jnp.float32
    )
    down_rank_gradient = adapter_scale * jnp.einsum(
        "trd,tkd->trk",
        cotangent,
        down_adapter_up.astype(jnp.bfloat16),
        preferred_element_type=jnp.float32,
    )
    grad_hidden = grad_hidden + jnp.einsum(
        "jax,jnx->jan", down_rank_gradient, down_adapter_slice, precision=highest_precision
    )
    sigmoid_gate = jax.nn.sigmoid(gate_pre)
    grad_gate = grad_hidden * up_pre * sigmoid_gate * (1.0 + gate_pre * (1.0 - sigmoid_gate))
    grad_up = grad_hidden * gate_pre * sigmoid_gate
    grad_gu = jnp.stack([grad_gate, grad_up], axis=2).astype(jnp.bfloat16)
    grad_normed_two = jnp.einsum(
        "trjf,djf->trd", grad_gu, gu_weight, preferred_element_type=jnp.float32
    )
    gate_up_rank_gradient = adapter_scale * jnp.einsum(
        "trjf,tjkf->trjk",
        grad_gu,
        b_gu_part.astype(jnp.bfloat16),
        preferred_element_type=jnp.float32,
    )
    rank_gu_flat = gate_up_rank_gradient.reshape(tree_count, row_count, 2 * RANK)
    grad_normed_two = grad_normed_two + jnp.einsum(
        "trm,tdm->trd", rank_gu_flat, a_gu, precision=highest_precision
    )
    grad_normed_two = grad_normed_two + moe_grad.reshape(tree_count, row_count, D)
    grad_normed_two = lax.psum(grad_normed_two, "tensor")
    grad_residual = output_gradient + norm_back(
        residual, scale_two, gain_two.astype(jnp.float32), grad_normed_two
    )
    grad_attn = grad_residual.astype(jnp.bfloat16)
    grad_mixed = jnp.einsum(
        "trd,cd->trc", grad_attn, output_matrix, preferred_element_type=jnp.float32
    )
    output_rank_gradient = adapter_scale * jnp.einsum(
        "trd,tkd->trk",
        grad_attn,
        output_adapter_up.astype(jnp.bfloat16),
        preferred_element_type=jnp.float32,
    )
    grad_mixed = grad_mixed + jnp.einsum(
        "trk,tck->trc", output_rank_gradient, a_out_part, precision=highest_precision
    )
    grad_mixed_heads = grad_mixed.astype(jnp.bfloat16).reshape(head_shape)

    def attend_back(inputs):
        query_rows, key_block, value_block, visible_rows, log_total, grad_rows = inputs
        scores = (
            jnp.einsum("rhd,khd->hrk", query_rows, key_block, preferred_element_type=jnp.float32)
            * 0.125
        )
        scores = jnp.where(visible_rows[None], scores, masked_score)
        probabilities = jnp.exp(scores - log_total[..., None])
        grad_values = jnp.einsum(
            "hrk,rhd->khd",
            probabilities.astype(jnp.bfloat16),
            grad_rows,
            preferred_element_type=jnp.float32,
        )
        grad_probs = jnp.einsum(
            "rhd,khd->hrk", grad_rows, value_block, preferred_element_type=jnp.float32
        )
        inner_sum = jnp.sum(probabilities * grad_probs, axis=-1, keepdims=True)
        grad_scores = (probabilities * (grad_probs - inner_sum)).astype(jnp.bfloat16)
        grad_query = (
            jnp.einsum("hrk,khd->rhd", grad_scores, key_block, preferred_element_type=jnp.float32)
            * 0.125
        )
        grad_keys = (
            jnp.einsum("hrk,rhd->khd", grad_scores, query_rows, preferred_element_type=jnp.float32)
            * 0.125
        )
        span = key_block.shape[0]
        return (
            grad_query,
            jnp.concatenate([grad_keys.reshape(span, -1), grad_values.reshape(span, -1)], axis=1),
        )

    grad_query_rot, grad_key_value = lax.map(
        attend_back, (queries, key_heads, value_heads, visible, log_totals, grad_mixed_heads)
    )
    own_grads = lax.psum_scatter(
        grad_key_value.astype(jnp.bfloat16), "context", scatter_dimension=1, tiled=True
    ).astype(jnp.float32)
    grad_query = unrotate(grad_query_rot, cosine, sinus).reshape(tree_count, row_count, local_width)
    grad_key = unrotate(own_grads[..., :local_width].reshape(head_shape), cosine, sinus).reshape(
        tree_count, row_count, local_width
    )
    grad_qkv = jnp.stack([grad_query, grad_key, own_grads[..., local_width:]], axis=2).astype(
        jnp.bfloat16
    )
    grad_normed_one = jnp.einsum(
        "trjc,djc->trd", grad_qkv, qkv_weight, preferred_element_type=jnp.float32
    )
    query_key_value_rank_gradient = adapter_scale * jnp.einsum(
        "trjc,tjkc->trjk",
        grad_qkv,
        b_qkv_part.astype(jnp.bfloat16),
        preferred_element_type=jnp.float32,
    )
    rank_qkv_flat = query_key_value_rank_gradient.reshape(tree_count, row_count, 3 * RANK)
    grad_normed_one = grad_normed_one + jnp.einsum(
        "trm,tdm->trd", rank_qkv_flat, a_qkv, precision=highest_precision
    )
    grad_normed_one = lax.psum(grad_normed_one.astype(jnp.bfloat16), "tensor").astype(jnp.float32)
    input_grad = grad_residual + norm_back(
        tokens_f, scale_one, gain_one.astype(jnp.float32), grad_normed_one
    )
    grad_qkv_f = grad_qkv.astype(jnp.float32)
    grad_gu_f = grad_gu.astype(jnp.float32)
    grad_a_qkv = jnp.einsum(
        "trd,trm->tdm", normed_one.astype(jnp.float32), rank_qkv_flat, precision=highest_precision
    )
    query_key_value_gradient_slice = adapter_scale * jnp.einsum(
        "trjk,trjc->tjkc", rank_split, grad_qkv_f, precision=highest_precision
    )
    grad_b_qkv = lax.dynamic_update_slice_in_dim(
        jnp.zeros((tree_count, 3, RANK, D), jnp.float32),
        query_key_value_gradient_slice,
        width_start,
        3,
    )
    grad_a_out_part = jnp.einsum(
        "trc,trk->tck",
        mixed_row_values.astype(jnp.float32),
        output_rank_gradient,
        precision=highest_precision,
    )
    grad_a_out = lax.dynamic_update_slice_in_dim(
        jnp.zeros((tree_count, D, RANK), jnp.float32), grad_a_out_part, width_start, 1
    )
    output_adapter_up_gradient = adapter_scale * jnp.einsum(
        "ags,agh->ash", output_rank_rows, grad_attn.astype(jnp.float32), precision=highest_precision
    )
    grad_a_gu = jnp.einsum(
        "trd,trm->tdm", normed_two.astype(jnp.float32), rank_gu_flat, precision=highest_precision
    )
    gate_up_adapter_gradient_slice = adapter_scale * jnp.einsum(
        "trjk,trjf->tjkf", gate_up_rank_rows, grad_gu_f, precision=highest_precision
    )
    grad_b_gu = lax.dynamic_update_slice_in_dim(
        jnp.zeros((tree_count, 2, RANK, FF), jnp.float32),
        gate_up_adapter_gradient_slice,
        ff_start,
        3,
    )
    grad_a_dn_part = jnp.einsum(
        "uya,uye->uae",
        hidden_state.astype(jnp.float32),
        down_rank_gradient,
        precision=highest_precision,
    )
    grad_a_dn = lax.dynamic_update_slice_in_dim(
        jnp.zeros((tree_count, FF, RANK), jnp.float32), grad_a_dn_part, ff_start, 1
    )
    down_adapter_up_gradient = adapter_scale * jnp.einsum(
        "ags,agh->ash", down_rank_rows, output_gradient, precision=highest_precision
    )
    grad_pieces = [
        grad_a_qkv,
        grad_b_qkv,
        grad_a_out,
        output_adapter_up_gradient,
        grad_a_gu,
        grad_b_gu,
        grad_a_dn,
        down_adapter_up_gradient,
    ]
    packed = jnp.concatenate([piece.reshape(tree_count, -1) for piece in grad_pieces], axis=1)
    own_part = lax.psum_scatter(
        packed[0], ("context", "tensor"), scatter_dimension=0, tiled=True
    )
    part_all = lax.all_gather(own_part[None], "fsdp", axis=0, tiled=True)
    ids_all = lax.all_gather(adapter_ids, "fsdp", axis=0, tiled=True)
    rows_own = ADAPTERS // fsdp_size
    own_ids = lax.axis_index("fsdp") * rows_own + jnp.arange(rows_own, dtype=jnp.int32)
    own_hot = (own_ids[:, None] == ids_all[None, :]).astype(jnp.float32)
    adapter_grads = jnp.sum(own_hot[:, :, None] * part_all[None], axis=1)
    return (block_out, input_grad, adapter_grads)


def solution(mesh):
    return jax.shard_map(
        shards,
        mesh=mesh,
        in_specs=(
            P("fsdp", "context", None),
            P("fsdp"),
            P("fsdp", None, "tensor"),
            P("tensor", "fsdp"),
            P("fsdp"),
            P("fsdp", None, "tensor"),
            P("tensor", "fsdp"),
            P("fsdp", None, None, "tensor"),
            P("fsdp", "tensor", None),
            P("fsdp", ("context", "tensor")),
            P("fsdp"),
            P("fsdp", None),
            P("fsdp", None),
            P("fsdp", "context", None),
            P("fsdp", "context", None),
            P("fsdp", "context", None),
        ),
        out_specs=(
            P("fsdp", "context", None),
            P("fsdp", "context", None),
            P("fsdp", ("context", "tensor")),
        ),
        check_vma=False,
    )
```

```python
import jax
import jax.numpy as jnp
import functools

from jax import lax
from jax.experimental import pallas as pl
from jax.experimental.pallas import tpu as pltpu
from jax.sharding import PartitionSpec as P

D = 768
HEADS = 12
HEAD_DIM = 64
FF = 2048
EXPERTS = 8
TOPK = 2
RANK = 16
ADAPTERS = 8
PARAMS = 233472


epsilon = 1e-06
adapter_scale = 2.0
rope_base = 10000.0
masked_score = -1e30
highest_precision = lax.Precision.HIGHEST


def unpack(flat_params):
    leading = flat_params.shape[:-1]
    block_shapes = [
        (D, 3 * RANK),
        (3, RANK, D),
        (D, RANK),
        (RANK, D),
        (D, 2 * RANK),
        (2, RANK, FF),
        (FF, RANK),
        (RANK, D),
    ]
    pieces = []
    offset = 0
    for block_shape in block_shapes:
        extent = 1
        for factor in block_shape:
            extent = extent * factor
        pieces.append(flat_params[..., offset : offset + extent].reshape(leading + block_shape))
        offset = offset + extent
    return pieces


def silu_of(values):
    return values * jax.nn.sigmoid(values)


def rms_scale(values):
    return lax.rsqrt(jnp.mean(values * values, axis=-1, keepdims=True) + epsilon)


def norm_back(values, scaling, gain_values, gradient):
    weighted = gradient * gain_values
    inner_mean = jnp.mean(values * weighted, axis=-1, keepdims=True)
    return scaling * weighted - values * (scaling * scaling * scaling) * inner_mean


def rotate(values, cosine, sinus):
    half_dim = values.shape[-1] // 2
    front_half = values[..., :half_dim]
    back_half = values[..., half_dim:]
    return jnp.concatenate(
        [front_half * cosine - back_half * sinus, back_half * cosine + front_half * sinus], axis=-1
    )


def unrotate(gradient, cosine, sinus):
    half_dim = gradient.shape[-1] // 2
    front_half = gradient[..., :half_dim]
    back_half = gradient[..., half_dim:]
    return jnp.concatenate(
        [front_half * cosine + back_half * sinus, back_half * cosine - front_half * sinus], axis=-1
    )


def angles(positions):
    half_dim = HEAD_DIM // 2
    frequency = rope_base ** (-(jnp.arange(half_dim, dtype=jnp.float32) * 2.0) / HEAD_DIM)
    turned = positions.astype(jnp.float32)[..., None] * frequency
    return (jnp.cos(turned)[..., None, :], jnp.sin(turned)[..., None, :])


def tree_layout(lengths, parent_ids):
    seg_count = lengths.shape[0]
    seg_ids = jnp.arange(seg_count, dtype=jnp.int32)
    parent_hot = (parent_ids[:, None] == seg_ids[None, :]).astype(jnp.int32)
    grand_hot = jnp.dot(parent_hot, parent_hot)
    same_seg = (seg_ids[:, None] == seg_ids[None, :]).astype(jnp.int32)
    ancestry = (same_seg + parent_hot + grand_hot > 0).astype(jnp.int32)
    starts = jnp.cumsum(lengths) - lengths
    offsets = jnp.sum((ancestry - same_seg) * lengths[None, :], axis=1)
    return (ancestry, starts, offsets)


def locate(row_ids, starts, offsets):
    segment = jnp.sum((row_ids[:, None] >= starts[None, :]).astype(jnp.int32), axis=1) - 1
    seg_hot = (segment[:, None] == jnp.arange(starts.shape[0], dtype=jnp.int32)[None, :]).astype(
        jnp.int32
    )
    positions = (
        row_ids
        - jnp.sum(seg_hot * starts[None, :], axis=1)
        + jnp.sum(seg_hot * offsets[None, :], axis=1)
    )
    return (seg_hot, positions)


SLOT_TILE = 256
TOKEN_TILE = 256


def nt_dot(left, right):
    return lax.dot_general(left, right, (((1,), (1,)), ((), ())), preferred_element_type=jnp.float32)


def tn_dot(left, right):
    return lax.dot_general(left, right, (((0,), (0,)), ((), ())), preferred_element_type=jnp.float32)


def nn_dot(left, right):
    return jnp.dot(left, right, preferred_element_type=jnp.float32)


def moe_kernel(
    spans,
    place_row,
    weight_row,
    place_col,
    weight_col,
    rows_ref,
    grads_ref,
    egu_hbm,
    edn_hbm,
    out_ref,
    back_ref,
    egu_ref,
    edn_ref,
    out_sum,
    back_sum,
    taken,
    taken_grad,
    slot_weight,
    sems,
):
    experts = egu_hbm.shape[0]
    copies = []
    for e in range(experts):
        copies.append(
            (
                pltpu.make_async_copy(egu_hbm.at[e], egu_ref.at[e], sems.at[e, 0]),
                pltpu.make_async_copy(edn_hbm.at[e], edn_ref.at[e], sems.at[e, 1]),
            )
        )
        copies[e][0].start()
        copies[e][1].start()
    out_sum[...] = jnp.zeros_like(out_sum)
    back_sum[...] = jnp.zeros_like(back_sum)
    slot_rows = lax.broadcasted_iota(jnp.int32, (SLOT_TILE, TOKEN_TILE), 0)
    slot_cols = lax.broadcasted_iota(jnp.int32, (TOKEN_TILE, SLOT_TILE), 1)
    for e in range(experts):
        copies[e][0].wait()
        copies[e][1].wait()

        def tile_step(i, carry, e=e):
            low = spans[e, 1 + 2 * i]
            high = spans[e, 2 + 2 * i]
            first = i * SLOT_TILE
            taken[...] = jnp.zeros_like(taken)
            taken_grad[...] = jnp.zeros_like(taken_grad)
            slot_weight[...] = jnp.zeros_like(slot_weight)

            def fetch(b, c):
                start = pl.multiple_of(b * TOKEN_TILE, TOKEN_TILE)
                hit = place_row[e, :, pl.ds(start, TOKEN_TILE)] == slot_rows + first
                pick = jnp.where(hit, 1.0, 0.0).astype(jnp.bfloat16)
                taken[...] += nn_dot(pick, rows_ref[pl.ds(start, TOKEN_TILE), :])
                taken_grad[...] += nn_dot(pick, grads_ref[pl.ds(start, TOKEN_TILE), :])
                slot_weight[...] += jnp.sum(
                    jnp.where(hit, weight_row[e, :, pl.ds(start, TOKEN_TILE)], 0.0),
                    axis=1,
                    keepdims=True,
                )
                return c

            lax.fori_loop(low, high, fetch, 0)
            inputs = taken[...].astype(jnp.bfloat16)
            gate_pre = nn_dot(inputs, egu_ref[e, 0])
            up_pre = nn_dot(inputs, egu_ref[e, 1])
            sigmoid_gate = jax.nn.sigmoid(gate_pre)
            silu = gate_pre * sigmoid_gate
            active = (silu * up_pre).astype(jnp.bfloat16)
            result = nn_dot(active, edn_ref[e]).astype(jnp.bfloat16)
            grad_active = nt_dot(taken_grad[...].astype(jnp.bfloat16), edn_ref[e])
            grad_active = grad_active * slot_weight[...]
            grad_gate = (
                grad_active * up_pre * sigmoid_gate * (1.0 + gate_pre * (1.0 - sigmoid_gate))
            ).astype(jnp.bfloat16)
            grad_up = (grad_active * silu).astype(jnp.bfloat16)
            grad_rows = (
                nt_dot(grad_gate, egu_ref[e, 0]) + nt_dot(grad_up, egu_ref[e, 1])
            ).astype(jnp.bfloat16)

            def give(b, c):
                start = pl.multiple_of(b * TOKEN_TILE, TOKEN_TILE)
                block = pl.ds(start, TOKEN_TILE)
                hit = place_col[block, e : e + 1] == slot_cols + first
                pick = jnp.where(hit, 1.0, 0.0).astype(jnp.bfloat16)
                out_sum[block, :] += nn_dot(pick, result) * weight_col[block, e : e + 1]
                back_sum[block, :] += nn_dot(pick, grad_rows)
                return c

            lax.fori_loop(low, high, give, 0)
            return carry

        lax.fori_loop(0, spans[e, 0], tile_step, 0)
    out_ref[...] = out_sum[...].astype(jnp.bfloat16)
    back_ref[...] = back_sum[...].astype(jnp.bfloat16)


def moe_layout(routes, weights, first_expert, experts):
    total = routes.shape[0]
    blocks = total // TOKEN_TILE
    ids = first_expert + jnp.arange(experts, dtype=jnp.int32)
    hits = routes[None] == ids[:, None, None]
    hit = jnp.any(hits, axis=-1)
    weight = jnp.sum(jnp.where(hits, weights.astype(jnp.float32)[None], 0.0), axis=-1)
    counted = hit.astype(jnp.int32)
    upto = jnp.cumsum(counted, axis=1)
    place = jnp.where(hit, upto - 1, -1)
    ends = upto.reshape(experts, blocks, TOKEN_TILE)[:, :, -1]
    begins = jnp.concatenate([jnp.zeros((experts, 1), jnp.int32), ends[:, :-1]], axis=1)
    count = ends[:, -1]
    tiles = total // SLOT_TILE
    tile_start = jnp.arange(tiles, dtype=jnp.int32) * SLOT_TILE
    low = jnp.sum((ends[:, None, :] <= tile_start[None, :, None]).astype(jnp.int32), axis=2)
    tile_end = jnp.minimum(tile_start[None] + SLOT_TILE, count[:, None])
    high = jnp.sum((begins[:, None, :] < tile_end[:, :, None]).astype(jnp.int32), axis=2)
    spans = jnp.stack([low, high], axis=2).reshape(experts, 2 * tiles)
    spans = jnp.concatenate([((count + SLOT_TILE - 1) // SLOT_TILE)[:, None], spans], axis=1)
    return spans, place, weight


def moe_call(spans, place, weight, rows, grads, egu, edn):
    total, width = rows.shape
    experts, _, _, units = egu.shape
    vmem = pl.BlockSpec(memory_space=pltpu.VMEM)
    hbm = pl.BlockSpec(memory_space=pl.ANY)
    shape = jax.ShapeDtypeStruct((total, width), jnp.bfloat16)
    return pl.pallas_call(
        moe_kernel,
        grid_spec=pltpu.PrefetchScalarGridSpec(
            num_scalar_prefetch=1,
            grid=(),
            in_specs=[vmem] * 6 + [hbm] * 2,
            out_specs=[vmem, vmem],
            scratch_shapes=[
                pltpu.VMEM(egu.shape, jnp.bfloat16),
                pltpu.VMEM(edn.shape, jnp.bfloat16),
                pltpu.VMEM((total, width), jnp.float32),
                pltpu.VMEM((total, width), jnp.float32),
                pltpu.VMEM((SLOT_TILE, width), jnp.float32),
                pltpu.VMEM((SLOT_TILE, width), jnp.float32),
                pltpu.VMEM((SLOT_TILE, 1), jnp.float32),
                pltpu.SemaphoreType.DMA((experts, 2)),
            ],
        ),
        out_shape=[shape, shape],
        name="experts",
        compiler_params=pltpu.CompilerParams(vmem_limit_bytes=60 << 20),
    )(spans, place[:, None, :], weight[:, None, :], place.T, weight.T, rows, grads, egu, edn)


MESH = pl.DeviceIdType.MESH


def place_of():
    return lax.axis_index("fsdp"), lax.axis_index("context"), lax.axis_index("tensor")


def greet(devices):
    barrier = pltpu.get_barrier_semaphore()
    for device in devices:
        pl.semaphore_signal(barrier, inc=1, device_id=device, device_id_type=MESH)
    pl.semaphore_wait(barrier, len(devices))


def send(source, target, send_sem, recv_sem, device):
    return pltpu.make_async_remote_copy(
        src_ref=source,
        dst_ref=target,
        send_sem=send_sem,
        recv_sem=recv_sem,
        device_id=device,
        device_id_type=MESH,
    )


def flip(index, bit):
    return index + (1 - 2 * lax.rem(index // (1 << bit), 2)) * (1 << bit)


def split_rows(count):
    first = (count // 2 + 15) // 16 * 16
    return ((0, first), (first, count - first))


class Gather:
    def __init__(self, bits, me, device_of, own, buf, stride, base, count, send_sems, recv_sems):
        self.stages = [[] for _ in range(bits)]
        self.arrived = [[] for _ in range(bits)]
        number = 0
        for half, (offset, size) in enumerate(split_rows(count)):
            held = [me]
            for stage in range(bits):
                bit = (stage + half) % bits
                for block in held:
                    rows = self.rows(block * stride + base + offset, size)
                    source = own.at[self.rows(base + offset, size)] if block is me else buf.at[rows]
                    self.stages[stage].append(
                        send(
                            source,
                            buf.at[rows],
                            send_sems.at[number],
                            recv_sems.at[number],
                            device_of(flip(me, bit)),
                        )
                    )
                    self.arrived[stage].append(
                        self.rows(flip(block, bit) * stride + base + offset, size)
                    )
                    number = number + 1
                held = held + [flip(block, bit) for block in held]

    @staticmethod
    def rows(start, size):
        return pl.ds(pl.multiple_of(start, 16), size)

    def start(self, stage):
        for copy in self.stages[stage]:
            copy.start()

    def wait(self, stage):
        for copy in self.stages[stage]:
            copy.wait_recv()

    def finish(self):
        for stage in self.stages:
            for copy in stage:
                copy.wait_send()


def turn(values, cosine, sinus):
    lane = lax.broadcasted_iota(jnp.int32, values.shape, 1)
    first = lax.rem(lane, HEAD_DIM) < HEAD_DIM // 2
    swapped = jnp.where(
        first,
        pltpu.roll(values, 128 - HEAD_DIM // 2, 1),
        pltpu.roll(values, HEAD_DIM // 2, 1),
    )
    return values * cosine + swapped * sinus


def two_parts(values):
    high = values.astype(jnp.bfloat16)
    low = (values - high.astype(jnp.float32)).astype(jnp.bfloat16)
    return jnp.concatenate([high, low], axis=1)


def normed(values, gain):
    scale = lax.rsqrt(jnp.mean(values * values, axis=-1, keepdims=True) + epsilon)
    return (values * scale * gain).astype(jnp.bfloat16)


def fill_bias(bias, hot_rows, reach_t, key_start, query_start):
    seen = nn_dot(hot_rows, reach_t)
    keys = key_start + lax.broadcasted_iota(jnp.int32, seen.shape, 0)
    queries = query_start + lax.broadcasted_iota(jnp.int32, seen.shape, 1)
    bias[...] = jnp.where((seen > 0.5) & (keys <= queries), 0.0, masked_score)


def head_half(shape, axis, odd):
    index = lax.broadcasted_iota(jnp.int32, shape, axis)
    return (index >= HEAD_DIM) if odd else (index < HEAD_DIM)


def forward_kernel(
    sizes,
    x_in,
    g_in,
    wq_in,
    wo_in,
    gu_in,
    dn_in,
    gains,
    cosine,
    sinus,
    hot,
    reach_t,
    a_qkv,
    b_qkv2,
    a_o,
    b_o2,
    a_gu,
    b_gu2,
    a_gu_t2,
    a_dn,
    a_dn_t2,
    b_dn2,
    n1_all,
    k_all,
    v_all,
    wq_all,
    wo_all,
    n2_all,
    g_all,
    q_t,
    q_n,
    mixed,
    o_t,
    lse,
    resid,
    shared_half,
    dn2_half,
    da_gu,
    db_gu,
    da_dn,
    db_dn,
    x_buf,
    wq,
    wo,
    gu,
    dn,
    g_own,
    n1_buf,
    k_buf,
    v_buf,
    v_t,
    peak,
    total,
    bias,
    part_out,
    part_in,
    n2_own,
    shared,
    dn2,
    shared_in,
    dn2_in,
    fs_send,
    fs_recv,
    z_send,
    z_recv,
    core_send,
    core_recv,
    local_sems,
    chunk_sems,
):
    fsdp, contexts, _ = sizes
    bits = fsdp.bit_length() - 1
    f, c, t = place_of()
    rows = x_in.shape[0]
    half = rows // 2
    heads = q_t.shape[0] // HEAD_DIM
    width = q_t.shape[0]
    units = dn_in.shape[1]
    own_n = wq_in.shape[0]
    sibling = (f, c, 1 - t)

    def peer(index):
        return (index, c, t)

    greet(
        [peer(flip(f, bit)) for bit in range(bits)]
        + [sibling, (f, lax.rem(c + 1, contexts), t), (f, lax.rem(c + contexts - 1, contexts), t)]
    )

    def half_rows(chunk, part):
        return pl.ds(pl.multiple_of(chunk * rows + part * half, 16), half)

    def up(chunk, source):
        return send(
            source,
            x_buf.at[half_rows(chunk, t)],
            z_send.at[chunk],
            z_recv.at[chunk],
            (f, c + 1, t),
        )

    def across(chunk):
        block = x_buf.at[half_rows(chunk, t)]
        return send(block, block, core_send.at[chunk], core_recv.at[chunk], sibling)

    @pl.when(c < contexts - 1)
    def _():
        up(c, x_in.at[half_rows(0, t)]).start()

    gathers = []
    for i, (own, buf) in enumerate(((wq_in, wq), (wo_in, wo), (gu_in, gu), (dn_in, dn))):
        gathers.append(
            Gather(bits, f, peer, own, buf, own_n, 0, own_n, fs_send.at[i], fs_recv.at[i])
        )
    g_gather = Gather(
        bits, f, peer, g_in, g_all, rows, t * half, half, fs_send.at[4], fs_recv.at[4]
    )
    n2_gather = Gather(
        bits, f, peer, n2_own, n2_all, rows, t * half, half, fs_send.at[5], fs_recv.at[5]
    )
    wq_gather, wo_gather, gu_gather, dn_gather = gathers
    wq_gather.start(0)
    locals_ = [pltpu.make_async_copy(x_in, x_buf.at[pl.ds(c * rows, rows)], local_sems.at[0])]
    for i, (own, buf) in enumerate(((wq_in, wq), (wo_in, wo), (gu_in, gu), (dn_in, dn))):
        locals_.append(
            pltpu.make_async_copy(own, buf.at[pl.ds(f * own_n, own_n)], local_sems.at[1 + i])
        )
    locals_.append(pltpu.make_async_copy(g_in, g_own, local_sems.at[5]))
    locals_.append(
        pltpu.make_async_copy(g_in, g_all.at[pl.ds(f * rows, rows)], local_sems.at[6])
    )
    for copy in locals_:
        copy.start()

    o_t[...] = jnp.zeros_like(o_t)
    peak[...] = jnp.full_like(peak, masked_score)
    total[...] = jnp.zeros_like(total)
    da_gu[...] = jnp.zeros_like(da_gu)
    db_gu[...] = jnp.zeros_like(db_gu)
    da_dn[...] = jnp.zeros_like(da_dn)
    db_dn[...] = jnp.zeros_like(db_dn)
    gain_one = gains[0:1, :]
    gain_two = gains[1:2, :]

    def receive(step):
        chunk = c - step

        @pl.when(step <= c)
        def _():
            up(chunk, x_buf.at[half_rows(chunk, t)]).wait_recv()

            @pl.when(c < contexts - 1)
            def _():
                up(chunk, x_buf.at[half_rows(chunk, t)]).start()

            across(chunk).start()

    def chunk_rows(chunk):
        return pl.ds(pl.multiple_of(chunk * rows, 16), rows)

    def out_copies(chunk):
        block = chunk_rows(chunk)
        return [
            pltpu.make_async_copy(n1_buf.at[block], n1_all.at[block], chunk_sems.at[0, chunk]),
            pltpu.make_async_copy(k_buf.at[block], k_all.at[block], chunk_sems.at[1, chunk]),
            pltpu.make_async_copy(v_buf.at[block], v_all.at[block], chunk_sems.at[2, chunk]),
        ]

    def project(chunk, own):
        block = chunk_rows(chunk)
        n1 = normed(x_buf[block, :].astype(jnp.float32), gain_one)
        n1_buf[block, :] = n1
        rank = two_parts(nn_dot(n1, a_qkv[...]))
        cos_rows = cosine[block, :]
        sin_rows = sinus[block, :]
        for p in range(width // 128):
            cols = slice(width + 128 * p, width + 128 * p + 128)
            key = nn_dot(n1, wq[:, cols]) + nn_dot(rank, b_qkv2[:, cols])
            k_buf[block, 128 * p : 128 * p + 128] = turn(key, cos_rows, sin_rows).astype(
                jnp.bfloat16
            )
            cols = slice(2 * width + 128 * p, 2 * width + 128 * p + 128)
            value = nn_dot(n1, wq[:, cols]) + nn_dot(rank, b_qkv2[:, cols])
            v_buf[block, 128 * p : 128 * p + 128] = value.astype(jnp.bfloat16)
            v_t[128 * p : 128 * p + 128, :] = value.T.astype(jnp.bfloat16)
            if own:
                cols = slice(128 * p, 128 * p + 128)
                query = nn_dot(n1, wq[:, cols]) + nn_dot(rank, b_qkv2[:, cols])
                query = turn(query, cos_rows, sin_rows) * 0.125
                q_n[:, cols] = query.astype(jnp.bfloat16)
                q_t[cols, :] = query.T.astype(jnp.bfloat16)
        for copy in out_copies(chunk):
            copy.start()

    def attend(chunk):
        block = chunk_rows(chunk)
        fill_bias(bias, hot[block, :], reach_t[...], chunk * rows, c * rows)

        def pair_step(p, carry):
            lanes = pl.ds(pl.multiple_of(p * 128, 128), 128)
            keys = k_buf[block, lanes]
            query = q_t[lanes, :]
            for odd in range(2):
                h = 2 * p + odd
                alone = jnp.where(
                    head_half(query.shape, 0, odd), query, jnp.zeros_like(query)
                )
                scores = nn_dot(keys, alone) + bias[...]
                before = peak[pl.ds(h, 1), :]
                now = jnp.maximum(before, jnp.max(scores, axis=0, keepdims=True))
                weights = jnp.exp(scores - now)
                shrink = jnp.exp(before - now)
                peak[pl.ds(h, 1), :] = now
                total[pl.ds(h, 1), :] = total[pl.ds(h, 1), :] * shrink + jnp.sum(
                    weights, axis=0, keepdims=True
                )
                head = pl.ds(pl.multiple_of(h * HEAD_DIM, HEAD_DIM), HEAD_DIM)
                o_t[head, :] = o_t[head, :] * shrink + nn_dot(
                    v_t[head, :], weights.astype(jnp.bfloat16)
                )
            return carry

        lax.fori_loop(0, heads // 2, pair_step, 0)

    receive(1)
    wq_gather.wait(0)
    for stage in range(1, bits):
        wq_gather.start(stage)
        if stage == 1:
            wo_gather.start(0)
        wq_gather.wait(stage)
    wo_gather.wait(0)
    for stage in range(1, bits):
        wo_gather.start(stage)
        if stage == 1:
            gu_gather.start(0)
        if stage < bits - 1:
            wo_gather.wait(stage)
    locals_[0].wait()
    locals_[1].wait()
    wq_out = pltpu.make_async_copy(wq, wq_all, local_sems.at[10])
    wq_out.start()
    project(c, True)
    attend(c)

    def between(step):
        if step == 1:
            gu_gather.wait(0)
            for stage in range(1, bits):
                gu_gather.start(stage)
                if stage == 1:
                    dn_gather.start(0)
                if stage < bits - 1:
                    gu_gather.wait(stage)
        if step == 2:
            dn_gather.wait(0)
            for stage in range(1, bits):
                dn_gather.start(stage)
                if stage == 1:
                    g_gather.start(0)
                if stage < bits - 1:
                    dn_gather.wait(stage)

    def later(step):
        chunk = c - step

        @pl.when(step <= c)
        def _():
            across(chunk).wait_recv()
            project(chunk, False)
            attend(chunk)

    for step in range(1, 3):
        receive(step + 1)
        between(step)
        later(step)

    def rest(step, carry):
        receive(step + 1)
        later(step)
        return carry

    lax.fori_loop(3, contexts, rest, 0)

    for h in range(heads):
        head = slice(h * HEAD_DIM, h * HEAD_DIM + HEAD_DIM)
        o_t[head, :] = o_t[head, :] / total[h : h + 1, :]
    lse[...] = peak[...] + jnp.log(total[...])
    for p in range(width // 128):
        mixed[:, 128 * p : 128 * p + 128] = o_t[128 * p : 128 * p + 128, :].T.astype(jnp.bfloat16)
    wo_gather.wait(bits - 1)
    locals_[2].wait()
    wo_out = pltpu.make_async_copy(wo, wo_all, local_sems.at[11])
    wo_out.start()

    def local_rows(part):
        return pl.ds(pl.multiple_of(part * half, 16), half)

    mine = local_rows(t)
    theirs = local_rows(1 - t)

    def branch(block):
        values = mixed[block, :]
        rank = two_parts(nn_dot(values, a_o[...]))
        return nt_dot(values, wo[...]) + nn_dot(rank, b_o2[...])

    part_out[...] = branch(theirs)
    number = contexts
    part_copy = send(
        part_out, part_in, core_send.at[number], core_recv.at[number], sibling
    )
    part_copy.start()
    own_part = branch(mine) + x_in_rows(x_buf, c, rows, t, half)
    part_copy.wait_recv()
    resid_half = own_part + part_in[...]
    resid[mine, :] = resid_half
    n2_own[mine, :] = normed(resid_half, gain_two)
    n2_gather.start(0)
    n2_copy = send(
        n2_own.at[mine], n2_own.at[mine], core_send.at[number + 1], core_recv.at[number + 1], sibling
    )
    n2_copy.start()
    resid_copy = send(
        resid.at[mine], resid.at[mine], core_send.at[number + 2], core_recv.at[number + 2], sibling
    )
    resid_copy.start()

    def forwards(gather, buf, first):
        copies = []
        for stage in range(bits):
            group = []
            for block in gather.arrived[stage]:
                index = first + len(copies)
                copies.append(
                    send(
                        buf.at[block],
                        buf.at[block],
                        core_send.at[index],
                        core_recv.at[index],
                        sibling,
                    )
                )
        return copies

    per_stage = [len(stage) for stage in g_gather.arrived]
    g_forward = forwards(g_gather, g_all, number + 5)
    n2_forward = forwards(n2_gather, n2_all, number + 5 + sum(per_stage))

    def pass_on(copies, stage):
        start = sum(per_stage[:stage])
        for copy in copies[start : start + per_stage[stage]]:
            copy.start()

    locals_[5].wait()
    gu_gather.wait(bits - 1)
    locals_[3].wait()
    dn_gather.wait(bits - 1)
    locals_[4].wait()

    def shared_tile(block):
        inputs = n2_own[block, :]
        grads = g_own[block, :]
        rank = nn_dot(inputs, a_gu[...])
        rank2 = two_parts(rank)
        gate = nn_dot(inputs, gu[:, :units]) + nn_dot(rank2, b_gu2[:, :units])
        up_pre = nn_dot(inputs, gu[:, units:]) + nn_dot(rank2, b_gu2[:, units:])
        sigmoid_gate = jax.nn.sigmoid(gate)
        silu = gate * sigmoid_gate
        hidden = (silu * up_pre).astype(jnp.bfloat16)
        down_rank = nn_dot(hidden, a_dn[...])
        shared[block, :] = nt_dot(hidden, dn[...]) + nn_dot(two_parts(down_rank), b_dn2[...])
        down_back = nt_dot(grads, b_dn2[0:RANK, :])
        grad_hidden = nn_dot(grads, dn[...]) + nn_dot(two_parts(down_back), a_dn_t2[...])
        grad_gate = (
            grad_hidden * up_pre * sigmoid_gate * (1.0 + gate * (1.0 - sigmoid_gate))
        ).astype(jnp.bfloat16)
        grad_up = (grad_hidden * silu).astype(jnp.bfloat16)
        rank_back = nt_dot(grad_gate, b_gu2[0 : 2 * RANK, :units]) + nt_dot(
            grad_up, b_gu2[0 : 2 * RANK, units:]
        )
        dn2[block, :] = (
            nt_dot(grad_gate, gu[:, :units])
            + nt_dot(grad_up, gu[:, units:])
            + nn_dot(two_parts(rank_back), a_gu_t2[...])
        )
        rank_low = rank.astype(jnp.bfloat16)
        da_gu[...] += tn_dot(rank_back.astype(jnp.bfloat16), inputs)
        db_gu[0:RANK, :] += 2.0 * tn_dot(rank_low, grad_gate)[0:RANK]
        db_gu[RANK:, :] += 2.0 * tn_dot(rank_low, grad_up)[RANK:]
        da_dn[...] += tn_dot(down_back.astype(jnp.bfloat16), hidden)
        db_dn[...] += 2.0 * tn_dot(down_rank.astype(jnp.bfloat16), grads)

    n2_gather.wait(0)
    for stage in range(1, bits):
        n2_gather.start(stage)
        pass_on(n2_forward, stage - 1)
        if stage < bits - 1:
            n2_gather.wait(stage)
    n2_copy.wait_recv()
    shared_tile(theirs)
    pair_copies = [
        send(
            source.at[theirs], target, core_send.at[number + 3 + i], core_recv.at[number + 3 + i], sibling
        )
        for i, (source, target) in enumerate(((dn2, dn2_in), (shared, shared_in)))
    ]
    for copy in pair_copies:
        copy.start()
    g_gather.wait(0)
    for stage in range(1, bits):
        g_gather.start(stage)
        pass_on(g_forward, stage - 1)
        if stage < bits - 1:
            g_gather.wait(stage)
    n2_out = pltpu.make_async_copy(n2_own, n2_all.at[pl.ds(f * rows, rows)], local_sems.at[12])
    n2_out.start()
    shared_tile(mine)
    for copy in pair_copies:
        copy.wait()
    dn2_half[...] = dn2[mine, :] + dn2_in[...]
    shared_half[...] = shared[mine, :] + shared_in[...]
    n2_gather.wait(bits - 1)
    pass_on(n2_forward, bits - 1)
    g_gather.wait(bits - 1)
    pass_on(g_forward, bits - 1)
    for copy in n2_forward + g_forward:
        copy.wait()
    resid_copy.wait()
    n2_copy.wait_send()
    part_copy.wait_send()
    for gather in gathers + [g_gather, n2_gather]:
        gather.finish()
    n2_out.wait()
    wq_out.wait()
    wo_out.wait()
    locals_[6].wait()

    @pl.when(c < contexts - 1)
    def _():
        up(c, x_in.at[half_rows(0, t)]).wait_send()

    def drain(step, carry):
        chunk = c - step

        @pl.when(c < contexts - 1)
        def _():
            up(chunk, x_buf.at[half_rows(chunk, t)]).wait_send()

        across(chunk).wait_send()
        return carry

    lax.fori_loop(1, c + 1, drain, 0)

    def drain_out(step, carry):
        for copy in out_copies(c - step):
            copy.wait()
        return carry

    lax.fori_loop(0, c + 1, drain_out, 0)


def x_in_rows(x_buf, chunk, rows, part, half):
    block = pl.ds(pl.multiple_of(chunk * rows + part * half, 16), half)
    return x_buf[block, :].astype(jnp.float32)


def forward_call(sizes, sharded, local):
    fsdp, contexts, _ = sizes
    x, g, wq, wo, gu, dn = sharded
    rows = x.shape[0]
    tree = rows * contexts
    width = wo.shape[1]
    units = dn.shape[1]
    bf, f32 = jnp.bfloat16, jnp.float32
    vmem = pl.BlockSpec(memory_space=pltpu.VMEM)
    hbm = pl.BlockSpec(memory_space=pl.ANY)

    def shape(kind, *dims):
        return jax.ShapeDtypeStruct(dims, kind)

    moves = 2 * (fsdp - 1)
    hops = contexts + 5 + 2 * moves
    return pl.pallas_call(
        functools.partial(forward_kernel, sizes),
        in_specs=[hbm] * 6 + [vmem] * len(local),
        out_specs=[hbm] * 7 + [vmem] * 12,
        out_shape=[
            shape(bf, tree, D),
            shape(bf, tree, width),
            shape(bf, tree, width),
            shape(bf, D, 3 * width),
            shape(bf, D, width),
            shape(bf, fsdp * rows, D),
            shape(bf, fsdp * rows, D),
            shape(bf, width, rows),
            shape(bf, rows, width),
            shape(bf, rows, width),
            shape(f32, width, rows),
            shape(f32, 8, rows),
            shape(f32, rows, D),
            shape(f32, rows // 2, D),
            shape(f32, rows // 2, D),
            shape(f32, 2 * RANK, D),
            shape(f32, 2 * RANK, units),
            shape(f32, RANK, units),
            shape(f32, RANK, D),
        ],
        scratch_shapes=[
            pltpu.VMEM((tree, D), bf),
            pltpu.VMEM((D, 3 * width), bf),
            pltpu.VMEM((D, width), bf),
            pltpu.VMEM((D, 2 * units), bf),
            pltpu.VMEM((D, units), bf),
            pltpu.VMEM((rows, D), bf),
            pltpu.VMEM((tree, D), bf),
            pltpu.VMEM((tree, width), bf),
            pltpu.VMEM((tree, width), bf),
            pltpu.VMEM((width, rows), bf),
            pltpu.VMEM((8, rows), f32),
            pltpu.VMEM((8, rows), f32),
            pltpu.VMEM((rows, rows), f32),
            pltpu.VMEM((rows // 2, D), f32),
            pltpu.VMEM((rows // 2, D), f32),
            pltpu.VMEM((rows, D), bf),
            pltpu.VMEM((rows, D), f32),
            pltpu.VMEM((rows, D), f32),
            pltpu.VMEM((rows // 2, D), f32),
            pltpu.VMEM((rows // 2, D), f32),
            pltpu.SemaphoreType.DMA((6, moves)),
            pltpu.SemaphoreType.DMA((6, moves)),
            pltpu.SemaphoreType.DMA((contexts,)),
            pltpu.SemaphoreType.DMA((contexts,)),
            pltpu.SemaphoreType.DMA((hops,)),
            pltpu.SemaphoreType.DMA((hops,)),
            pltpu.SemaphoreType.DMA((13,)),
            pltpu.SemaphoreType.DMA((3, contexts)),
        ],
        name="forward",
        compiler_params=pltpu.CompilerParams(
            collective_id=2, has_side_effects=True, vmem_limit_bytes=62 << 20
        ),
    )(*sharded, *local)


def flips(index, mask, bits):
    for bit in range(bits):
        if mask >> bit & 1:
            index = flip(index, bit)
    return index


class Scatter:
    def __init__(self, bits, me, device_of, work, inbox, count, send_sems, recv_sems):
        self.bits, self.work, self.inbox = bits, work, inbox
        self.copies = [[] for _ in range(bits)]
        self.adds = [[] for _ in range(bits)]
        number = 0
        for half, (offset, size) in enumerate(split_rows(count)):
            alive = list(range(1 << bits))
            slot = 0
            for stage in range(bits):
                bit = (stage + half) % bits
                for mask in alive:
                    if mask >> bit & 1:
                        source = Gather.rows(flips(me, mask, bits) * count + offset, size)
                        target = pl.ds(slot * count + offset, size)
                        kept = Gather.rows(flips(me, mask ^ (1 << bit), bits) * count + offset, size)
                        self.copies[stage].append(
                            send(
                                work.at[source],
                                inbox.at[target],
                                send_sems.at[number],
                                recv_sems.at[number],
                                device_of(flip(me, bit)),
                            )
                        )
                        self.adds[stage].append((kept, target, pl.ds(offset, size)))
                        number = number + 1
                        slot = slot + 1
                alive = [mask for mask in alive if not mask >> bit & 1]

    def start(self, stage):
        for copy in self.copies[stage]:
            copy.start()

    def add(self, stage):
        for copy in self.copies[stage]:
            copy.wait_recv()
        for kept, target, _ in self.adds[stage]:
            total = self.work[kept, :].astype(jnp.float32) + self.inbox[target, :].astype(
                jnp.float32
            )
            self.work[kept, :] = total.astype(jnp.bfloat16)

    def last(self, out, own):
        for copy in self.copies[self.bits - 1]:
            copy.wait_recv()
        for kept, target, rows in self.adds[self.bits - 1]:
            total = self.work[kept, :].astype(jnp.float32) + self.inbox[target, :].astype(
                jnp.float32
            )
            out[rows, :] = (total + own[rows, :]).astype(jnp.bfloat16)

    def finish(self):
        for stage in self.copies:
            for copy in stage:
                copy.wait_send()


def backward_kernel(
    sizes,
    moe_out,
    moe_back,
    n1_hbm,
    k_hbm,
    v_hbm,
    wq_hbm,
    wo_hbm,
    cos_hbm,
    sin_hbm,
    x_in,
    g_in,
    gains,
    hot,
    reach_t,
    resid,
    shared_half,
    dn2_half,
    q_t,
    q_n,
    mixed,
    o_t,
    lse,
    a_qkv,
    b_qkv2,
    a_qkv_t2,
    a_o,
    a_o_t2,
    b_o2,
    block_out,
    input_grad,
    da_qkv,
    db_qkv,
    da_o,
    db_o,
    cosine,
    sinus,
    n1_buf,
    k_buf,
    v_buf,
    wq,
    wo,
    work_back,
    pair_back,
    inbox_back,
    work_out,
    pair_out,
    inbox_out,
    total_half,
    total_full,
    ffn_half,
    ffn_full,
    dy,
    do_n,
    do_t,
    delta,
    k_t,
    dq_t,
    grad_kv,
    bias,
    part,
    part_out,
    part_in,
    z_in,
    z_out,
    dn1_full,
    fs_send,
    fs_recv,
    z_send,
    z_recv,
    core_send,
    core_recv,
    pair_send,
    pair_recv,
    local_sems,
    chunk_sems,
):
    fsdp, contexts, _ = sizes
    bits = fsdp.bit_length() - 1
    f, c, t = place_of()
    rows = x_in.shape[0]
    half = rows // 2
    width = q_t.shape[0]
    heads = width // HEAD_DIM
    sibling = (f, c, 1 - t)
    f32, bf = jnp.float32, jnp.bfloat16

    def peer(index):
        return (index, c, t)

    def local_rows(part_index):
        return pl.ds(pl.multiple_of(part_index * half, 16), half)

    mine = local_rows(t)
    theirs = local_rows(1 - t)

    def block_rows(block, part_index):
        return pl.ds(pl.multiple_of(block * rows + part_index * half, 16), half)

    def work_rows(block):
        return pl.ds(pl.multiple_of(block * half, 16), half)

    masks = list(range(fsdp - 1, -1, -1))

    def exchange(source, work, inbox, which):
        own, sent = [], []
        for mask in masks:
            block = flips(f, mask, bits)
            own.append(
                pltpu.make_async_copy(
                    source.at[block_rows(block, t)],
                    work.at[work_rows(block)],
                    local_sems.at[which, mask],
                )
            )
            sent.append(
                send(
                    source.at[block_rows(block, 1 - t)],
                    inbox.at[work_rows(block)],
                    core_send.at[which, mask],
                    core_recv.at[which, mask],
                    sibling,
                )
            )
        return own, sent

    back_own, back_sent = exchange(moe_back, work_back, pair_back, 0)
    out_own, out_sent = exchange(moe_out, work_out, pair_out, 1)
    for copy in back_own:
        copy.start()
    wo_copy = pltpu.make_async_copy(wo_hbm, wo, local_sems.at[2, 0])
    wq_copy = pltpu.make_async_copy(wq_hbm, wq, local_sems.at[2, 1])
    wo_copy.start()
    greet(
        [peer(flip(f, bit)) for bit in range(bits)]
        + [sibling, (f, lax.rem(c + 1, contexts), t), (f, lax.rem(c + contexts - 1, contexts), t)]
    )
    for copy in back_sent:
        copy.start()
    for copy in out_own:
        copy.start()
    wq_copy.start()

    def chunk_rows(chunk):
        return pl.ds(pl.multiple_of(chunk * rows, 16), rows)

    def loads(chunk):
        block = chunk_rows(chunk)
        return [
            pltpu.make_async_copy(k_hbm.at[block], k_buf.at[block], chunk_sems.at[1, chunk]),
            pltpu.make_async_copy(v_hbm.at[block], v_buf.at[block], chunk_sems.at[2, chunk]),
        ]

    def n1_load(chunk):
        return pltpu.make_async_copy(
            n1_hbm.at[chunk_rows(chunk)], n1_buf, chunk_sems.at[0, chunk]
        )

    def table_loads(chunk):
        block = chunk_rows(chunk)
        return [
            pltpu.make_async_copy(cos_hbm.at[block], cosine, chunk_sems.at[3, chunk]),
            pltpu.make_async_copy(sin_hbm.at[block], sinus, chunk_sems.at[4, chunk]),
        ]

    def start_loads(chunk, carry):
        for copy in loads(chunk):
            copy.start()
        return carry

    lax.fori_loop(0, c + 1, start_loads, 0)

    back = Scatter(
        bits, f, peer, work_back, inbox_back, half, fs_send.at[0], fs_recv.at[0]
    )
    out = Scatter(bits, f, peer, work_out, inbox_out, half, fs_send.at[1], fs_recv.at[1])

    def pair_sum(own, sent, work, inbox):
        for i, mask in enumerate(masks):
            block = work_rows(flips(f, mask, bits))
            own[i].wait()
            sent[i].wait_recv()
            work[block, :] = (
                work[block, :].astype(f32) + inbox[block, :].astype(f32)
            ).astype(bf)

    pair_sum(back_own, back_sent, work_back, pair_back)
    back.start(0)
    for copy in out_sent:
        copy.start()
    for stage in range(1, bits):
        back.add(stage - 1)
        back.start(stage)
    dq_t[...] = jnp.zeros_like(dq_t)
    da_qkv[...] = jnp.zeros_like(da_qkv)
    db_qkv[...] = jnp.zeros_like(db_qkv)
    pair_sum(out_own, out_sent, work_out, pair_out)
    back.last(total_half, dn2_half)
    out.start(0)
    total_full[mine, :] = total_half[...]
    full_copy = send(
        total_half, total_full.at[mine], core_send.at[2, 0], core_recv.at[2, 0], sibling
    )
    full_copy.start()
    gain_one = gains[0:1, :]
    gain_two = gains[1:2, :]
    wo_copy.wait()
    full_copy.wait_recv()

    def attn_tile(i, carry):
        block = local_rows(i)
        values = resid[block, :]
        gradient = g_in[block, :].astype(f32) + norm_back(
            values, rms_scale(values), gain_two, total_full[block, :].astype(f32)
        )
        dy[block, :] = gradient
        low_grad = gradient.astype(bf)
        rank_back = nt_dot(low_grad, b_o2[0:RANK, :])
        do_n[block, :] = (
            nn_dot(low_grad, wo[...]) + nn_dot(two_parts(rank_back), a_o_t2[...])
        ).astype(bf)
        values_o = mixed[block, :]
        rank = nn_dot(values_o, a_o[...])
        first = tn_dot(rank_back.astype(bf), values_o)
        second = 2.0 * tn_dot(rank.astype(bf), low_grad)

        @pl.when(i == 0)
        def _():
            da_o[...] = first
            db_o[...] = second

        @pl.when(i > 0)
        def _():
            da_o[...] += first
            db_o[...] += second

        return carry

    lax.fori_loop(0, 2, attn_tile, 0)
    for p in range(width // 128):
        lanes = slice(128 * p, 128 * p + 128)
        turned = do_n[:, lanes].astype(f32).T
        do_t[lanes, :] = turned.astype(bf)
        product = turned * o_t[lanes, :]
        for odd in range(2):
            delta[2 * p + odd : 2 * p + odd + 1, :] = jnp.sum(
                product[HEAD_DIM * odd : HEAD_DIM * odd + HEAD_DIM, :], axis=0, keepdims=True
            )
    wq_copy.wait()

    def attend_back(chunk):
        block = chunk_rows(chunk)
        n1_load(chunk).start()
        for copy in table_loads(chunk):
            copy.start()
        for copy in loads(chunk) + table_loads(chunk):
            copy.wait()
        fill_bias(bias, hot[block, :], reach_t[...], chunk * rows, c * rows)
        cos_rows = cosine[...]
        sin_rows = -sinus[...]
        for p in range(width // 128):
            lanes = slice(128 * p, 128 * p + 128)
            k_t[lanes, :] = k_buf[block, lanes].astype(f32).T.astype(bf)

        def pair_step(p, carry):
            lanes = pl.ds(pl.multiple_of(p * 128, 128), 128)
            keys = k_buf[block, lanes]
            values = v_buf[block, lanes]
            query_t = q_t[lanes, :]
            grad_t = do_t[lanes, :]
            query = q_n[:, lanes]
            grad = do_n[:, lanes]
            grad_keys = jnp.zeros((rows, 128), f32)
            grad_values = jnp.zeros((rows, 128), f32)
            for odd in range(2):
                h = 2 * p + odd
                upper = head_half(query_t.shape, 0, odd)
                side = head_half(query.shape, 1, odd)
                none_t = jnp.zeros_like(query_t)
                none = jnp.zeros_like(query)
                scores = nn_dot(keys, jnp.where(upper, query_t, none_t)) + bias[...]
                weights = jnp.exp(scores - lse[pl.ds(h, 1), :])
                grad_weights = nn_dot(values, jnp.where(upper, grad_t, none_t))
                grad_scores = (weights * (grad_weights - delta[pl.ds(h, 1), :])).astype(bf)
                grad_values += nn_dot(weights.astype(bf), jnp.where(side, grad, none))
                grad_keys += nn_dot(grad_scores, jnp.where(side, query, none))
                head = pl.ds(pl.multiple_of(h * HEAD_DIM, HEAD_DIM), HEAD_DIM)
                dq_t[head, :] += nn_dot(k_t[head, :], grad_scores)
            grad_kv[:, lanes] = turn(grad_keys, cos_rows, sin_rows).astype(bf)
            grad_kv[:, pl.ds(pl.multiple_of(width + p * 128, 128), 128)] = grad_values.astype(bf)
            return carry

        lax.fori_loop(0, heads // 2, pair_step, 0)

    def project_back(chunk, own):
        block = chunk_rows(chunk)
        grads = grad_kv[...]
        result = nt_dot(grads, wq[:, width:])
        rank_back = nt_dot(grads, b_qkv2[0 : 3 * RANK, width:])
        n1_load(chunk).wait()
        n1 = n1_buf[...]
        rank = nn_dot(n1, a_qkv[...]).astype(bf)
        both = 2.0 * tn_dot(rank, grads)
        db_qkv[RANK : 2 * RANK, :] += both[RANK : 2 * RANK, :width]
        db_qkv[2 * RANK :, :] += both[2 * RANK :, width:]
        if own:
            pieces = []
            for p in range(width // 128):
                lanes = slice(128 * p, 128 * p + 128)
                grad_query = (dq_t[lanes, :] * 0.125).T
                pieces.append(
                    turn(grad_query, cosine[...], -sinus[...]).astype(bf)
                )
            grad_query = jnp.concatenate(pieces, axis=1)
            result += nt_dot(grad_query, wq[:, :width])
            rank_back += nt_dot(grad_query, b_qkv2[0 : 3 * RANK, :width])
            db_qkv[0:RANK, :] += 2.0 * tn_dot(rank, grad_query)[0:RANK, :]
        result += nn_dot(two_parts(rank_back), a_qkv_t2[...])
        da_qkv[...] += tn_dot(rank_back.astype(bf), n1)
        part[...] = result.astype(bf)
        part_out[work_rows(chunk), :] = part[theirs, :]
        z_out[work_rows(chunk), :] = part[mine, :]

    def pair_copy(chunk):
        return send(
            part_out.at[work_rows(chunk)],
            part_in.at[work_rows(chunk)],
            pair_send.at[chunk],
            pair_recv.at[chunk],
            sibling,
        )

    def down(chunk):
        block = work_rows(chunk)
        return send(
            z_out.at[block], z_in.at[block], z_send.at[chunk], z_recv.at[chunk], (f, c - 1, t)
        )

    def chain(chunk):
        block = work_rows(chunk)
        pair_copy(chunk).wait_recv()
        summed = z_out[block, :].astype(f32) + part_in[block, :].astype(f32)
        z_out[block, :] = summed.astype(bf)

        @pl.when(c < contexts - 1)
        def _():
            down(chunk).wait_recv()
            z_out[block, :] = (summed + z_in[block, :].astype(f32)).astype(bf)

    def pass_down(chunk):
        chain(chunk)
        down(chunk).start()

    def step(chunk, carry):
        attend_back(chunk)
        project_back(chunk, False)
        pair_copy(chunk).start()

        @pl.when(c == contexts - 1)
        def _():
            pass_down(chunk)

        @pl.when((c < contexts - 1) & (chunk >= 1))
        def _():
            pass_down(chunk - 1)

        return carry

    lax.fori_loop(0, c, step, 0)
    attend_back(c)
    project_back(c, True)
    pair_copy(c).start()

    @pl.when((c < contexts - 1) & (c >= 1))
    def _():
        pass_down(c - 1)

    for stage in range(1, bits):
        out.add(stage - 1)
        out.start(stage)
    out.last(ffn_half, shared_half)
    ffn_full[mine, :] = ffn_half[...]
    ffn_copy = send(ffn_half, ffn_full.at[mine], core_send.at[2, 1], core_recv.at[2, 1], sibling)
    ffn_copy.start()
    chain(c)
    dn1_full[mine, :] = z_out[work_rows(c), :]
    dn1_copy = send(
        z_out.at[work_rows(c)],
        dn1_full.at[mine],
        core_send.at[2, 2],
        core_recv.at[2, 2],
        sibling,
    )
    dn1_copy.start()
    ffn_copy.wait_recv()
    block_out[...] = resid[...] + ffn_full[...].astype(f32)
    dn1_copy.wait_recv()

    def final_tile(i, carry):
        block = local_rows(i)
        values = x_in[block, :].astype(f32)
        input_grad[block, :] = dy[block, :] + norm_back(
            values, rms_scale(values), gain_one, dn1_full[block, :].astype(f32)
        )
        return carry

    lax.fori_loop(0, 2, final_tile, 0)
    for copy in back_sent + out_sent + [full_copy, ffn_copy, dn1_copy]:
        copy.wait_send()
    back.finish()
    out.finish()

    def drain(chunk, carry):
        pair_copy(chunk).wait_send()

        @pl.when(chunk < c)
        def _():
            down(chunk).wait_send()

        return carry

    lax.fori_loop(0, c + 1, drain, 0)


def backward_call(sizes, remote, local):
    fsdp, contexts, _ = sizes
    rows = local[0].shape[0]
    half = rows // 2
    tree = rows * contexts
    width = remote[6].shape[1]
    bf, f32 = jnp.bfloat16, jnp.float32
    vmem = pl.BlockSpec(memory_space=pltpu.VMEM)
    hbm = pl.BlockSpec(memory_space=pl.ANY)

    def shape(kind, *dims):
        return jax.ShapeDtypeStruct(dims, kind)

    moves = 2 * (fsdp - 1)
    slots = max(fsdp, 4)
    dma = pltpu.SemaphoreType.DMA
    return pl.pallas_call(
        functools.partial(backward_kernel, sizes),
        in_specs=[hbm] * len(remote) + [vmem] * len(local),
        out_specs=[vmem] * 6,
        out_shape=[
            shape(f32, rows, D),
            shape(f32, rows, D),
            shape(f32, 3 * RANK, D),
            shape(f32, 3 * RANK, width),
            shape(f32, RANK, width),
            shape(f32, RANK, D),
        ],
        scratch_shapes=[
            pltpu.VMEM((rows, 128), f32),
            pltpu.VMEM((rows, 128), f32),
            pltpu.VMEM((rows, D), bf),
            pltpu.VMEM((tree, width), bf),
            pltpu.VMEM((tree, width), bf),
            pltpu.VMEM((D, 3 * width), bf),
            pltpu.VMEM((D, width), bf),
            pltpu.VMEM((fsdp * half, D), bf),
            pltpu.VMEM((fsdp * half, D), bf),
            pltpu.VMEM(((fsdp - 1) * half, D), bf),
            pltpu.VMEM((fsdp * half, D), bf),
            pltpu.VMEM((fsdp * half, D), bf),
            pltpu.VMEM(((fsdp - 1) * half, D), bf),
            pltpu.VMEM((half, D), bf),
            pltpu.VMEM((rows, D), bf),
            pltpu.VMEM((half, D), bf),
            pltpu.VMEM((rows, D), bf),
            pltpu.VMEM((rows, D), f32),
            pltpu.VMEM((rows, width), bf),
            pltpu.VMEM((width, rows), bf),
            pltpu.VMEM((8, rows), f32),
            pltpu.VMEM((width, rows), bf),
            pltpu.VMEM((width, rows), f32),
            pltpu.VMEM((rows, 2 * width), bf),
            pltpu.VMEM((rows, rows), f32),
            pltpu.VMEM((rows, D), bf),
            pltpu.VMEM((contexts * half, D), bf),
            pltpu.VMEM((contexts * half, D), bf),
            pltpu.VMEM((contexts * half, D), bf),
            pltpu.VMEM((contexts * half, D), bf),
            pltpu.VMEM((rows, D), bf),
            dma((2, moves)),
            dma((2, moves)),
            dma((contexts,)),
            dma((contexts,)),
            dma((3, slots)),
            dma((3, slots)),
            dma((contexts,)),
            dma((contexts,)),
            dma((3, slots)),
            dma((5, contexts)),
        ],
        name="backward",
        compiler_params=pltpu.CompilerParams(
            collective_id=3, has_side_effects=True, vmem_limit_bytes=62 << 20
        ),
    )(*remote, *local)


def small_kernel(
    sizes,
    ids_ref,
    adapters_ref,
    gains_ref,
    table_ref,
    chosen_ref,
    gains_all,
    table_all,
    adapters_all,
    send_sems,
    recv_sems,
):
    fsdp, contexts, _ = sizes
    f, c, t = place_of()
    peers = [(lax.rem(f + k, fsdp), c, t) for k in range(1, fsdp)]
    stacked = [(f, lax.rem(c + k, contexts), t) for k in range(1, contexts)]
    sibling = (f, c, 1 - t)
    greet(peers + stacked + [sibling])
    first = []
    for k, peer in enumerate(peers):
        for j, (source, target) in enumerate(
            ((adapters_ref, adapters_all), (gains_ref, gains_all), (table_ref, table_all))
        ):
            copy = send(source, target.at[f], send_sems.at[j, k], recv_sems.at[j, k], peer)
            copy.start()
            first.append(copy)
    adapters_all[f] = adapters_ref[...]
    gains_all[f] = gains_ref[...]
    table_all[f] = table_ref[...]
    for copy in first:
        copy.wait()
    wanted = ids_ref[0]
    rows = RANK
    own = ADAPTERS // fsdp
    total = jnp.zeros((rows, adapters_ref.shape[1]), jnp.float32)
    for a in range(ADAPTERS):
        block = adapters_all[a // own, pl.ds((a % own) * rows, rows), :].astype(jnp.float32)
        total = total + jnp.where(wanted == a, block, 0.0)
    chosen_ref[t, c] = total.astype(jnp.bfloat16)
    second = []
    for k, other in enumerate(stacked):
        copy = send(
            chosen_ref.at[t, c], chosen_ref.at[t, c], send_sems.at[3, k], recv_sems.at[3, k], other
        )
        copy.start()
        second.append(copy)
    for copy in second:
        copy.wait()
    last = send(chosen_ref.at[t], chosen_ref.at[t], send_sems.at[4, 0], recv_sems.at[4, 0], sibling)
    last.start()
    last.wait()


def small_call(sizes, ids, adapters, gains, table):
    fsdp, contexts, tensors = sizes
    slots = max(fsdp, contexts)
    vmem = pl.BlockSpec(memory_space=pltpu.VMEM)
    return pl.pallas_call(
        functools.partial(small_kernel, sizes),
        in_specs=[pl.BlockSpec(memory_space=pltpu.SMEM), vmem, vmem, vmem],
        out_specs=[vmem] * 3,
        out_shape=[
            jax.ShapeDtypeStruct((tensors, contexts, RANK, adapters.shape[1]), jnp.bfloat16),
            jax.ShapeDtypeStruct((fsdp,) + gains.shape, gains.dtype),
            jax.ShapeDtypeStruct((fsdp,) + table.shape, table.dtype),
        ],
        scratch_shapes=[
            pltpu.VMEM((fsdp,) + adapters.shape, adapters.dtype),
            pltpu.SemaphoreType.DMA((5, slots)),
            pltpu.SemaphoreType.DMA((5, slots)),
        ],
        name="small_gather",
        compiler_params=pltpu.CompilerParams(
            collective_id=1, has_side_effects=True, vmem_limit_bytes=60 << 20
        ),
    )(ids, adapters, gains, table)


def shards(
    tokens,
    attn_gain,
    w_qkv,
    w_out,
    ffn_gain,
    w_gu,
    w_dn,
    w_egu,
    w_edn,
    adapters,
    adapter_ids,
    parents,
    seg_lengths,
    routes,
    route_weights,
    cotangent,
):
    tree_count = tokens.shape[0]
    row_count = tokens.shape[1]
    contexts = lax.axis_size("context")
    tensors = lax.axis_size("tensor")
    fsdp_size = lax.axis_size("fsdp")
    tree_len = row_count * contexts
    token_count = tree_count * row_count
    local_heads = HEADS // tensors
    local_width = local_heads * HEAD_DIM
    local_ff = FF // tensors
    part_index = lax.axis_index("tensor")
    row_start = lax.axis_index("context") * row_count
    width_start = part_index * local_width
    ff_start = part_index * local_ff
    head_shape = (tree_count, row_count, local_heads, HEAD_DIM)
    wide_shape = (tree_count, tree_len, local_heads, HEAD_DIM)
    sizes = (fsdp_size, contexts, tensors)
    own_adapters = adapters.shape[0]
    own_width = D // fsdp_size
    gains = jnp.broadcast_to(jnp.concatenate([attn_gain, ffn_gain])[None], (16, 2 * own_width))
    route_table = jnp.concatenate(
        [
            routes[0].astype(jnp.float32).T,
            route_weights[0].astype(jnp.float32).T,
            jnp.zeros((4, row_count), jnp.float32),
        ]
    )
    chosen_parts, gains_all, table_all = small_call(
        sizes, adapter_ids, adapters.reshape(own_adapters * RANK, -1), gains, route_table
    )
    chosen = chosen_parts.transpose(1, 0, 2, 3).reshape(1, PARAMS).astype(jnp.float32)
    gain_one = gains_all[:, 0, :own_width].reshape(D)
    gain_two = gains_all[:, 0, own_width:].reshape(D)
    routes_all = table_all[:, 0:2].transpose(0, 2, 1).reshape(-1, TOPK).astype(jnp.int32)
    route_weights_all = table_all[:, 2:4].transpose(0, 2, 1).reshape(-1, TOPK)
    (
        a_qkv,
        query_key_value_adapter_up,
        a_out,
        output_adapter_up,
        a_gu,
        gate_up_adapter_up,
        a_dn,
        down_adapter_up,
    ) = unpack(chosen)
    b_qkv_part = lax.dynamic_slice_in_dim(query_key_value_adapter_up, width_start, local_width, 3)
    a_out_part = lax.dynamic_slice_in_dim(a_out, width_start, local_width, 1)
    b_gu_part = lax.dynamic_slice_in_dim(gate_up_adapter_up, ff_start, local_ff, 3)
    down_adapter_slice = lax.dynamic_slice_in_dim(a_dn, ff_start, local_ff, 1)
    ancestry, starts, offsets = jax.vmap(tree_layout)(seg_lengths, parents)
    ancestry_f = ancestry.astype(jnp.float32)
    key_ids = jnp.arange(tree_len, dtype=jnp.int32)
    query_ids = row_start + jnp.arange(row_count, dtype=jnp.int32)
    key_hot, key_positions = jax.vmap(locate, in_axes=(None, 0, 0))(key_ids, starts, offsets)
    key_hot = key_hot.astype(jnp.float32)
    query_hot = lax.dynamic_slice_in_dim(key_hot, row_start, row_count, 1)
    reach = (jnp.einsum("trs,tsu->tru", query_hot, ancestry_f) > 0.5).astype(jnp.float32)
    visible = (jnp.einsum("tru,tku->trk", reach, key_hot) > 0.5) & (
        key_ids[None, None, :] <= query_ids[None, :, None]
    )
    cos_all, sin_all = angles(key_positions)
    cosine = lax.dynamic_slice_in_dim(cos_all, row_start, row_count, 1)
    sinus = lax.dynamic_slice_in_dim(sin_all, row_start, row_count, 1)
    cos_one = cos_all[0, :, 0, :]
    sin_one = sin_all[0, :, 0, :]
    cos_table = jnp.concatenate([cos_one] * 4, axis=1)
    sin_table = jnp.concatenate([-sin_one, sin_one, -sin_one, sin_one], axis=1)
    pad = 16 - key_hot.shape[2]
    hot_table = jnp.pad(key_hot[0], ((0, 0), (0, pad))).astype(jnp.bfloat16)
    reach_t = jnp.pad(reach[0], ((0, 0), (0, pad))).T.astype(jnp.bfloat16)

    def low(values):
        return values.astype(jnp.bfloat16)

    def blocks(up_rows):
        count, rank, cols = up_rows.shape
        out = jnp.zeros((count, rank, count, cols), jnp.float32)
        for j in range(count):
            out = out.at[j, :, j].set(up_rows[j])
        return out.reshape(count * rank, count * cols)

    def twice(values):
        return low(jnp.concatenate([values, values], axis=0))

    local = (
        jnp.pad(jnp.stack([gain_one, gain_two]).astype(jnp.float32), ((0, 6), (0, 0))),
        cos_table,
        sin_table,
        hot_table,
        reach_t,
        low(a_qkv[0]),
        twice(2.0 * blocks(b_qkv_part[0])),
        low(a_out_part[0]),
        twice(2.0 * output_adapter_up[0]),
        low(a_gu[0]),
        twice(2.0 * blocks(b_gu_part[0])),
        twice(a_gu[0].T),
        low(down_adapter_slice[0]),
        twice(down_adapter_slice[0].T),
        twice(2.0 * down_adapter_up[0]),
    )
    sharded = (
        tokens[0],
        cotangent[0],
        w_qkv.reshape(own_width, 3 * local_width),
        w_out.T,
        w_gu.reshape(own_width, 2 * local_ff),
        w_dn.T,
    )
    (
        n1_all,
        k_all,
        v_all,
        wq_all,
        wo_all,
        normed_all,
        cotangent_all,
        q_t,
        q_n,
        mixed_own,
        o_t,
        lse,
        resid,
        shared_half,
        dn2_half,
        da_gu_t,
        db_gu_own,
        da_dn_t,
        db_dn_own,
    ) = forward_call(sizes, sharded, local)
    own_experts = EXPERTS // fsdp_size
    spans, place, weight = moe_layout(
        routes_all, route_weights_all, lax.axis_index("fsdp") * own_experts, own_experts
    )
    moe_all, moe_back_all = moe_call(
        spans, place, weight, normed_all, cotangent_all, w_egu.transpose(0, 2, 1, 3), w_edn
    )
    remote = (moe_all, moe_back_all, n1_all, k_all, v_all, wq_all, wo_all, local[1], local[2])
    block_out, input_grad, da_qkv_t, db_qkv_own, da_o_t, db_o_own = backward_call(
        sizes,
        remote,
        (tokens[0], cotangent[0])
        + (local[0], local[3], local[4])
        + (resid, shared_half, dn2_half, q_t, q_n, mixed_own, o_t, lse)
        + (local[5], local[6], twice(a_qkv[0].T), local[7], twice(a_out_part[0].T), local[8]),
    )
    block_out = block_out[None]
    input_grad = input_grad[None]
    grad_a_qkv = da_qkv_t.T[None]
    grad_b_qkv = lax.dynamic_update_slice_in_dim(
        jnp.zeros((tree_count, 3, RANK, D), jnp.float32),
        db_qkv_own.reshape(1, 3, RANK, local_width),
        width_start,
        3,
    )
    grad_a_out = lax.dynamic_update_slice_in_dim(
        jnp.zeros((tree_count, D, RANK), jnp.float32), da_o_t.T[None], width_start, 1
    )
    output_adapter_up_gradient = db_o_own[None]
    grad_a_gu = da_gu_t.T[None]
    grad_b_gu = lax.dynamic_update_slice_in_dim(
        jnp.zeros((tree_count, 2, RANK, FF), jnp.float32),
        db_gu_own.reshape(1, 2, RANK, local_ff),
        ff_start,
        3,
    )
    grad_a_dn = lax.dynamic_update_slice_in_dim(
        jnp.zeros((tree_count, FF, RANK), jnp.float32), da_dn_t.T[None], ff_start, 1
    )
    down_adapter_up_gradient = db_dn_own[None]
    grad_pieces = [
        grad_a_qkv,
        grad_b_qkv,
        grad_a_out,
        output_adapter_up_gradient,
        grad_a_gu,
        grad_b_gu,
        grad_a_dn,
        down_adapter_up_gradient,
    ]
    packed = jnp.concatenate([piece.reshape(tree_count, -1) for piece in grad_pieces], axis=1)
    own_part = lax.psum_scatter(
        packed[0], ("context", "tensor"), scatter_dimension=0, tiled=True
    )
    part_all = lax.all_gather(own_part[None], "fsdp", axis=0, tiled=True)
    ids_all = lax.all_gather(adapter_ids, "fsdp", axis=0, tiled=True)
    rows_own = ADAPTERS // fsdp_size
    own_ids = lax.axis_index("fsdp") * rows_own + jnp.arange(rows_own, dtype=jnp.int32)
    own_hot = (own_ids[:, None] == ids_all[None, :]).astype(jnp.float32)
    adapter_grads = jnp.sum(own_hot[:, :, None] * part_all[None], axis=1)
    return (block_out, input_grad, adapter_grads)


def solution(mesh):
    return jax.shard_map(
        shards,
        mesh=mesh,
        in_specs=(
            P("fsdp", "context", None),
            P("fsdp"),
            P("fsdp", None, "tensor"),
            P("tensor", "fsdp"),
            P("fsdp"),
            P("fsdp", None, "tensor"),
            P("tensor", "fsdp"),
            P("fsdp", None, None, "tensor"),
            P("fsdp", "tensor", None),
            P("fsdp", ("context", "tensor")),
            P("fsdp"),
            P("fsdp", None),
            P("fsdp", None),
            P("fsdp", "context", None),
            P("fsdp", "context", None),
            P("fsdp", "context", None),
        ),
        out_specs=(
            P("fsdp", "context", None),
            P("fsdp", "context", None),
            P("fsdp", ("context", "tensor")),
        ),
        check_vma=False,
    )
```

```python
import jax
import jax.numpy as jnp
import functools

from jax import lax
from jax.experimental import pallas as pl
from jax.experimental.pallas import tpu as pltpu
from jax.sharding import PartitionSpec as P

D = 768
HEADS = 12
HEAD_DIM = 64
FF = 2048
EXPERTS = 8
TOPK = 2
RANK = 16
ADAPTERS = 8
PARAMS = 233472


epsilon = 1e-06
adapter_scale = 2.0
rope_base = 10000.0
masked_score = -1e30
highest_precision = lax.Precision.HIGHEST


def unpack(flat_params):
    leading = flat_params.shape[:-1]
    block_shapes = [
        (D, 3 * RANK),
        (3, RANK, D),
        (D, RANK),
        (RANK, D),
        (D, 2 * RANK),
        (2, RANK, FF),
        (FF, RANK),
        (RANK, D),
    ]
    pieces = []
    offset = 0
    for block_shape in block_shapes:
        extent = 1
        for factor in block_shape:
            extent = extent * factor
        pieces.append(flat_params[..., offset : offset + extent].reshape(leading + block_shape))
        offset = offset + extent
    return pieces


def silu_of(values):
    return values * jax.nn.sigmoid(values)


def rms_scale(values):
    return lax.rsqrt(jnp.mean(values * values, axis=-1, keepdims=True) + epsilon)


def norm_back(values, scaling, gain_values, gradient):
    weighted = gradient * gain_values
    inner_mean = jnp.mean(values * weighted, axis=-1, keepdims=True)
    return scaling * weighted - values * (scaling * scaling * scaling) * inner_mean


def rotate(values, cosine, sinus):
    half_dim = values.shape[-1] // 2
    front_half = values[..., :half_dim]
    back_half = values[..., half_dim:]
    return jnp.concatenate(
        [front_half * cosine - back_half * sinus, back_half * cosine + front_half * sinus], axis=-1
    )


def unrotate(gradient, cosine, sinus):
    half_dim = gradient.shape[-1] // 2
    front_half = gradient[..., :half_dim]
    back_half = gradient[..., half_dim:]
    return jnp.concatenate(
        [front_half * cosine + back_half * sinus, back_half * cosine - front_half * sinus], axis=-1
    )


def angles(positions):
    half_dim = HEAD_DIM // 2
    frequency = rope_base ** (-(jnp.arange(half_dim, dtype=jnp.float32) * 2.0) / HEAD_DIM)
    turned = positions.astype(jnp.float32)[..., None] * frequency
    return (jnp.cos(turned)[..., None, :], jnp.sin(turned)[..., None, :])


def tree_layout(lengths, parent_ids):
    seg_count = lengths.shape[0]
    seg_ids = jnp.arange(seg_count, dtype=jnp.int32)
    parent_hot = (parent_ids[:, None] == seg_ids[None, :]).astype(jnp.int32)
    grand_hot = jnp.dot(parent_hot, parent_hot)
    same_seg = (seg_ids[:, None] == seg_ids[None, :]).astype(jnp.int32)
    ancestry = (same_seg + parent_hot + grand_hot > 0).astype(jnp.int32)
    starts = jnp.cumsum(lengths) - lengths
    offsets = jnp.sum((ancestry - same_seg) * lengths[None, :], axis=1)
    return (ancestry, starts, offsets)


def locate(row_ids, starts, offsets):
    segment = jnp.sum((row_ids[:, None] >= starts[None, :]).astype(jnp.int32), axis=1) - 1
    seg_hot = (segment[:, None] == jnp.arange(starts.shape[0], dtype=jnp.int32)[None, :]).astype(
        jnp.int32
    )
    positions = (
        row_ids
        - jnp.sum(seg_hot * starts[None, :], axis=1)
        + jnp.sum(seg_hot * offsets[None, :], axis=1)
    )
    return (seg_hot, positions)


SLOT_TILE = 256
TOKEN_TILE = 256


def nt_dot(left, right):
    return lax.dot_general(left, right, (((1,), (1,)), ((), ())), preferred_element_type=jnp.float32)


def tn_dot(left, right):
    return lax.dot_general(left, right, (((0,), (0,)), ((), ())), preferred_element_type=jnp.float32)


def nn_dot(left, right):
    return jnp.dot(left, right, preferred_element_type=jnp.float32)


def moe_kernel(
    spans,
    place_row,
    weight_row,
    place_col,
    weight_col,
    rows_ref,
    grads_ref,
    egu_hbm,
    edn_hbm,
    out_ref,
    back_ref,
    egu_ref,
    edn_ref,
    out_sum,
    back_sum,
    taken,
    taken_grad,
    slot_weight,
    sems,
):
    experts = egu_hbm.shape[0]
    copies = []
    for e in range(experts):
        copies.append(
            (
                pltpu.make_async_copy(egu_hbm.at[e], egu_ref.at[e], sems.at[e, 0]),
                pltpu.make_async_copy(edn_hbm.at[e], edn_ref.at[e], sems.at[e, 1]),
            )
        )
        copies[e][0].start()
        copies[e][1].start()
    out_sum[...] = jnp.zeros_like(out_sum)
    back_sum[...] = jnp.zeros_like(back_sum)
    slot_rows = lax.broadcasted_iota(jnp.int32, (SLOT_TILE, TOKEN_TILE), 0)
    slot_cols = lax.broadcasted_iota(jnp.int32, (TOKEN_TILE, SLOT_TILE), 1)
    for e in range(experts):
        copies[e][0].wait()
        copies[e][1].wait()

        def tile_step(i, carry, e=e):
            low = spans[e, 1 + 2 * i]
            high = spans[e, 2 + 2 * i]
            first = i * SLOT_TILE
            taken[...] = jnp.zeros_like(taken)
            taken_grad[...] = jnp.zeros_like(taken_grad)
            slot_weight[...] = jnp.zeros_like(slot_weight)

            def fetch(b, c):
                start = pl.multiple_of(b * TOKEN_TILE, TOKEN_TILE)
                hit = place_row[e, :, pl.ds(start, TOKEN_TILE)] == slot_rows + first
                pick = jnp.where(hit, 1.0, 0.0).astype(jnp.bfloat16)
                taken[...] += nn_dot(pick, rows_ref[pl.ds(start, TOKEN_TILE), :])
                taken_grad[...] += nn_dot(pick, grads_ref[pl.ds(start, TOKEN_TILE), :])
                slot_weight[...] += jnp.sum(
                    jnp.where(hit, weight_row[e, :, pl.ds(start, TOKEN_TILE)], 0.0),
                    axis=1,
                    keepdims=True,
                )
                return c

            lax.fori_loop(low, high, fetch, 0)
            inputs = taken[...].astype(jnp.bfloat16)
            gate_pre = nn_dot(inputs, egu_ref[e, 0])
            up_pre = nn_dot(inputs, egu_ref[e, 1])
            sigmoid_gate = jax.nn.sigmoid(gate_pre)
            silu = gate_pre * sigmoid_gate
            active = (silu * up_pre).astype(jnp.bfloat16)
            result = nn_dot(active, edn_ref[e]).astype(jnp.bfloat16)
            grad_active = nt_dot(taken_grad[...].astype(jnp.bfloat16), edn_ref[e])
            grad_active = grad_active * slot_weight[...]
            grad_gate = (
                grad_active * up_pre * sigmoid_gate * (1.0 + gate_pre * (1.0 - sigmoid_gate))
            ).astype(jnp.bfloat16)
            grad_up = (grad_active * silu).astype(jnp.bfloat16)
            grad_rows = (
                nt_dot(grad_gate, egu_ref[e, 0]) + nt_dot(grad_up, egu_ref[e, 1])
            ).astype(jnp.bfloat16)

            def give(b, c):
                start = pl.multiple_of(b * TOKEN_TILE, TOKEN_TILE)
                block = pl.ds(start, TOKEN_TILE)
                hit = place_col[block, e : e + 1] == slot_cols + first
                pick = jnp.where(hit, 1.0, 0.0).astype(jnp.bfloat16)
                out_sum[block, :] += nn_dot(pick, result) * weight_col[block, e : e + 1]
                back_sum[block, :] += nn_dot(pick, grad_rows)
                return c

            lax.fori_loop(low, high, give, 0)
            return carry

        lax.fori_loop(0, spans[e, 0], tile_step, 0)
    out_ref[...] = out_sum[...].astype(jnp.bfloat16)
    back_ref[...] = back_sum[...].astype(jnp.bfloat16)


def moe_layout(routes, weights, first_expert, experts):
    total = routes.shape[0]
    blocks = total // TOKEN_TILE
    ids = first_expert + jnp.arange(experts, dtype=jnp.int32)
    hits = routes[None] == ids[:, None, None]
    hit = jnp.any(hits, axis=-1)
    weight = jnp.sum(jnp.where(hits, weights.astype(jnp.float32)[None], 0.0), axis=-1)
    counted = hit.astype(jnp.int32)
    upto = jnp.cumsum(counted, axis=1)
    place = jnp.where(hit, upto - 1, -1)
    ends = upto.reshape(experts, blocks, TOKEN_TILE)[:, :, -1]
    begins = jnp.concatenate([jnp.zeros((experts, 1), jnp.int32), ends[:, :-1]], axis=1)
    count = ends[:, -1]
    tiles = total // SLOT_TILE
    tile_start = jnp.arange(tiles, dtype=jnp.int32) * SLOT_TILE
    low = jnp.sum((ends[:, None, :] <= tile_start[None, :, None]).astype(jnp.int32), axis=2)
    tile_end = jnp.minimum(tile_start[None] + SLOT_TILE, count[:, None])
    high = jnp.sum((begins[:, None, :] < tile_end[:, :, None]).astype(jnp.int32), axis=2)
    spans = jnp.stack([low, high], axis=2).reshape(experts, 2 * tiles)
    spans = jnp.concatenate([((count + SLOT_TILE - 1) // SLOT_TILE)[:, None], spans], axis=1)
    return spans, place, weight


def moe_call(spans, place, weight, rows, grads, egu, edn):
    total, width = rows.shape
    experts, _, _, units = egu.shape
    vmem = pl.BlockSpec(memory_space=pltpu.VMEM)
    hbm = pl.BlockSpec(memory_space=pl.ANY)
    shape = jax.ShapeDtypeStruct((total, width), jnp.bfloat16)
    return pl.pallas_call(
        moe_kernel,
        grid_spec=pltpu.PrefetchScalarGridSpec(
            num_scalar_prefetch=1,
            grid=(),
            in_specs=[vmem] * 6 + [hbm] * 2,
            out_specs=[vmem, vmem],
            scratch_shapes=[
                pltpu.VMEM(egu.shape, jnp.bfloat16),
                pltpu.VMEM(edn.shape, jnp.bfloat16),
                pltpu.VMEM((total, width), jnp.float32),
                pltpu.VMEM((total, width), jnp.float32),
                pltpu.VMEM((SLOT_TILE, width), jnp.float32),
                pltpu.VMEM((SLOT_TILE, width), jnp.float32),
                pltpu.VMEM((SLOT_TILE, 1), jnp.float32),
                pltpu.SemaphoreType.DMA((experts, 2)),
            ],
        ),
        out_shape=[shape, shape],
        name="experts",
        compiler_params=pltpu.CompilerParams(vmem_limit_bytes=60 << 20),
    )(spans, place[:, None, :], weight[:, None, :], place.T, weight.T, rows, grads, egu, edn)


MESH = pl.DeviceIdType.MESH


def place_of():
    return lax.axis_index("fsdp"), lax.axis_index("context"), lax.axis_index("tensor")


def greet(devices):
    barrier = pltpu.get_barrier_semaphore()
    for device in devices:
        pl.semaphore_signal(barrier, inc=1, device_id=device, device_id_type=MESH)
    pl.semaphore_wait(barrier, len(devices))


def send(source, target, send_sem, recv_sem, device):
    return pltpu.make_async_remote_copy(
        src_ref=source,
        dst_ref=target,
        send_sem=send_sem,
        recv_sem=recv_sem,
        device_id=device,
        device_id_type=MESH,
    )


def flip(index, bit):
    return index + (1 - 2 * lax.rem(index // (1 << bit), 2)) * (1 << bit)


def split_rows(count):
    first = (count // 2 + 15) // 16 * 16
    return ((0, first), (first, count - first))


class Gather:
    def __init__(self, bits, me, device_of, own, buf, stride, base, count, send_sems, recv_sems):
        self.stages = [[] for _ in range(bits)]
        self.arrived = [[] for _ in range(bits)]
        self.passed = [[] for _ in range(bits)]
        number = 0
        for half, (offset, size) in enumerate(split_rows(count)):
            held = [me]
            for stage in range(bits):
                bit = (stage + half) % bits
                for block in held:
                    rows = self.rows(block * stride + base + offset, size)
                    source = own.at[self.rows(base + offset, size)] if block is me else buf.at[rows]
                    self.passed[stage].append(block is not me)
                    self.stages[stage].append(
                        send(
                            source,
                            buf.at[rows],
                            send_sems.at[number],
                            recv_sems.at[number],
                            device_of(flip(me, bit)),
                        )
                    )
                    self.arrived[stage].append(
                        self.rows(flip(block, bit) * stride + base + offset, size)
                    )
                    number = number + 1
                held = held + [flip(block, bit) for block in held]

    @staticmethod
    def rows(start, size):
        return pl.ds(pl.multiple_of(start, 16), size)

    def start(self, stage):
        if stage == 0:
            for copies, passed in zip(self.stages, self.passed):
                for copy, later in zip(copies, passed):
                    if not later:
                        copy.start()
        else:
            for copy, later in zip(self.stages[stage], self.passed[stage]):
                if later:
                    copy.start()

    def wait(self, stage):
        for copy in self.stages[stage]:
            copy.wait_recv()

    def finish(self):
        for stage in self.stages:
            for copy in stage:
                copy.wait_send()


def turn(values, cosine, sinus):
    lane = lax.broadcasted_iota(jnp.int32, values.shape, 1)
    first = lax.rem(lane, HEAD_DIM) < HEAD_DIM // 2
    swapped = jnp.where(
        first,
        pltpu.roll(values, 128 - HEAD_DIM // 2, 1),
        pltpu.roll(values, HEAD_DIM // 2, 1),
    )
    return values * cosine + swapped * sinus


def two_parts(values):
    high = values.astype(jnp.bfloat16)
    low = (values - high.astype(jnp.float32)).astype(jnp.bfloat16)
    return jnp.concatenate([high, low], axis=1)


def normed(values, gain):
    scale = lax.rsqrt(jnp.mean(values * values, axis=-1, keepdims=True) + epsilon)
    return (values * scale * gain).astype(jnp.bfloat16)


def fill_bias(bias, hot_rows, reach_t, key_start, query_start):
    seen = nn_dot(hot_rows, reach_t)
    keys = key_start + lax.broadcasted_iota(jnp.int32, seen.shape, 0)
    queries = query_start + lax.broadcasted_iota(jnp.int32, seen.shape, 1)
    bias[...] = jnp.where((seen > 0.5) & (keys <= queries), 0.0, masked_score)


def head_half(shape, axis, odd):
    index = lax.broadcasted_iota(jnp.int32, shape, axis)
    return (index >= HEAD_DIM) if odd else (index < HEAD_DIM)


def forward_kernel(
    sizes,
    x_in,
    g_in,
    wq_in,
    wo_in,
    gu_in,
    dn_in,
    gains,
    cosine,
    sinus,
    hot,
    reach_t,
    a_qkv,
    b_qkv2,
    a_o,
    b_o2,
    a_gu,
    b_gu2,
    a_gu_t2,
    a_dn,
    a_dn_t2,
    b_dn2,
    n1_all,
    k_all,
    v_all,
    wq_all,
    wo_all,
    n2_all,
    g_all,
    q_t,
    q_n,
    mixed,
    o_t,
    lse,
    resid,
    shared_half,
    dn2_half,
    da_gu,
    db_gu,
    da_dn,
    db_dn,
    x_buf,
    wq,
    wo,
    gu,
    dn,
    g_own,
    n1_buf,
    k_buf,
    v_buf,
    v_t,
    peak,
    total,
    bias,
    part_out,
    part_in,
    n2_own,
    shared,
    dn2,
    shared_in,
    dn2_in,
    fs_send,
    fs_recv,
    z_send,
    z_recv,
    core_send,
    core_recv,
    local_sems,
    chunk_sems,
):
    fsdp, contexts, _ = sizes
    bits = fsdp.bit_length() - 1
    f, c, t = place_of()
    rows = x_in.shape[0]
    half = rows // 2
    heads = q_t.shape[0] // HEAD_DIM
    width = q_t.shape[0]
    units = dn_in.shape[1]
    own_n = wq_in.shape[0]
    sibling = (f, c, 1 - t)

    def peer(index):
        return (index, c, t)

    greet(
        [peer(flip(f, bit)) for bit in range(bits)]
        + [sibling, (f, lax.rem(c + 1, contexts), t), (f, lax.rem(c + contexts - 1, contexts), t)]
    )

    def half_rows(chunk, part):
        return pl.ds(pl.multiple_of(chunk * rows + part * half, 16), half)

    def up(chunk, source):
        return send(
            source,
            x_buf.at[half_rows(chunk, t)],
            z_send.at[chunk],
            z_recv.at[chunk],
            (f, c + 1, t),
        )

    def across(chunk):
        block = x_buf.at[half_rows(chunk, t)]
        return send(block, block, core_send.at[chunk], core_recv.at[chunk], sibling)

    @pl.when(c < contexts - 1)
    def _():
        up(c, x_in.at[half_rows(0, t)]).start()

    gathers = []
    for i, (own, buf) in enumerate(((wq_in, wq), (wo_in, wo), (gu_in, gu), (dn_in, dn))):
        gathers.append(
            Gather(bits, f, peer, own, buf, own_n, 0, own_n, fs_send.at[i], fs_recv.at[i])
        )
    g_gather = Gather(
        bits, f, peer, g_in, g_all, rows, t * half, half, fs_send.at[4], fs_recv.at[4]
    )
    n2_gather = Gather(
        bits, f, peer, n2_own, n2_all, rows, t * half, half, fs_send.at[5], fs_recv.at[5]
    )
    wq_gather, wo_gather, gu_gather, dn_gather = gathers
    wq_gather.start(0)
    locals_ = [pltpu.make_async_copy(x_in, x_buf.at[pl.ds(c * rows, rows)], local_sems.at[0])]
    for i, (own, buf) in enumerate(((wq_in, wq), (wo_in, wo), (gu_in, gu), (dn_in, dn))):
        locals_.append(
            pltpu.make_async_copy(own, buf.at[pl.ds(f * own_n, own_n)], local_sems.at[1 + i])
        )
    locals_.append(pltpu.make_async_copy(g_in, g_own, local_sems.at[5]))
    locals_.append(
        pltpu.make_async_copy(g_in, g_all.at[pl.ds(f * rows, rows)], local_sems.at[6])
    )
    for copy in locals_:
        copy.start()

    o_t[...] = jnp.zeros_like(o_t)
    peak[...] = jnp.full_like(peak, masked_score)
    total[...] = jnp.zeros_like(total)
    da_gu[...] = jnp.zeros_like(da_gu)
    db_gu[...] = jnp.zeros_like(db_gu)
    da_dn[...] = jnp.zeros_like(da_dn)
    db_dn[...] = jnp.zeros_like(db_dn)
    gain_one = gains[0:1, :]
    gain_two = gains[1:2, :]

    def receive(step):
        chunk = c - step

        @pl.when(step <= c)
        def _():
            up(chunk, x_buf.at[half_rows(chunk, t)]).wait_recv()

            @pl.when(c < contexts - 1)
            def _():
                up(chunk, x_buf.at[half_rows(chunk, t)]).start()

            across(chunk).start()

    def chunk_rows(chunk):
        return pl.ds(pl.multiple_of(chunk * rows, 16), rows)

    def out_copies(chunk):
        block = chunk_rows(chunk)
        return [
            pltpu.make_async_copy(n1_buf.at[block], n1_all.at[block], chunk_sems.at[0, chunk]),
            pltpu.make_async_copy(k_buf.at[block], k_all.at[block], chunk_sems.at[1, chunk]),
            pltpu.make_async_copy(v_buf.at[block], v_all.at[block], chunk_sems.at[2, chunk]),
        ]

    def project(chunk, own):
        block = chunk_rows(chunk)
        n1 = normed(x_buf[block, :].astype(jnp.float32), gain_one)
        n1_buf[block, :] = n1
        rank = two_parts(nn_dot(n1, a_qkv[...]))
        cos_rows = cosine[block, :]
        sin_rows = sinus[block, :]
        for p in range(width // 128):
            cols = slice(width + 128 * p, width + 128 * p + 128)
            key = nn_dot(n1, wq[:, cols]) + nn_dot(rank, b_qkv2[:, cols])
            k_buf[block, 128 * p : 128 * p + 128] = turn(key, cos_rows, sin_rows).astype(
                jnp.bfloat16
            )
            cols = slice(2 * width + 128 * p, 2 * width + 128 * p + 128)
            value = nn_dot(n1, wq[:, cols]) + nn_dot(rank, b_qkv2[:, cols])
            v_buf[block, 128 * p : 128 * p + 128] = value.astype(jnp.bfloat16)
            v_t[128 * p : 128 * p + 128, :] = value.T.astype(jnp.bfloat16)
            if own:
                cols = slice(128 * p, 128 * p + 128)
                query = nn_dot(n1, wq[:, cols]) + nn_dot(rank, b_qkv2[:, cols])
                query = turn(query, cos_rows, sin_rows) * 0.125
                q_n[:, cols] = query.astype(jnp.bfloat16)
                q_t[cols, :] = query.T.astype(jnp.bfloat16)
        for copy in out_copies(chunk):
            copy.start()

    def attend(chunk):
        block = chunk_rows(chunk)
        fill_bias(bias, hot[block, :], reach_t[...], chunk * rows, c * rows)

        def pair_step(p, carry):
            lanes = pl.ds(pl.multiple_of(p * 128, 128), 128)
            keys = k_buf[block, lanes]
            query = q_t[lanes, :]
            for odd in range(2):
                h = 2 * p + odd
                alone = jnp.where(
                    head_half(query.shape, 0, odd), query, jnp.zeros_like(query)
                )
                scores = nn_dot(keys, alone) + bias[...]
                before = peak[pl.ds(h, 1), :]
                now = jnp.maximum(before, jnp.max(scores, axis=0, keepdims=True))
                weights = jnp.exp(scores - now)
                shrink = jnp.exp(before - now)
                peak[pl.ds(h, 1), :] = now
                total[pl.ds(h, 1), :] = total[pl.ds(h, 1), :] * shrink + jnp.sum(
                    weights, axis=0, keepdims=True
                )
                head = pl.ds(pl.multiple_of(h * HEAD_DIM, HEAD_DIM), HEAD_DIM)
                o_t[head, :] = o_t[head, :] * shrink + nn_dot(
                    v_t[head, :], weights.astype(jnp.bfloat16)
                )
            return carry

        lax.fori_loop(0, heads // 2, pair_step, 0)

    def advance(gather, following):
        gather.wait(0)
        for stage in range(1, bits):
            gather.start(stage)
            if stage < bits - 1:
                gather.wait(stage)
        if following is not None:
            following.start(0)

    advance(wq_gather, wo_gather)
    receive(1)
    advance(wo_gather, gu_gather)
    wq_gather.wait(bits - 1)
    locals_[0].wait()
    locals_[1].wait()
    wq_out = pltpu.make_async_copy(wq, wq_all, local_sems.at[10])
    wq_out.start()
    project(c, True)
    attend(c)

    def between(step):
        if step == 1:
            advance(gu_gather, dn_gather)
        if step == 2:
            advance(dn_gather, g_gather)

    def later(step):
        chunk = c - step

        @pl.when(step <= c)
        def _():
            across(chunk).wait_recv()
            project(chunk, False)
            attend(chunk)

    for step in range(1, 3):
        receive(step + 1)
        between(step)
        later(step)

    def rest(step, carry):
        receive(step + 1)
        later(step)
        return carry

    lax.fori_loop(3, contexts, rest, 0)

    for h in range(heads):
        head = slice(h * HEAD_DIM, h * HEAD_DIM + HEAD_DIM)
        o_t[head, :] = o_t[head, :] / total[h : h + 1, :]
    lse[...] = peak[...] + jnp.log(total[...])
    for p in range(width // 128):
        mixed[:, 128 * p : 128 * p + 128] = o_t[128 * p : 128 * p + 128, :].T.astype(jnp.bfloat16)
    wo_gather.wait(bits - 1)
    locals_[2].wait()
    wo_out = pltpu.make_async_copy(wo, wo_all, local_sems.at[11])
    wo_out.start()

    def local_rows(part):
        return pl.ds(pl.multiple_of(part * half, 16), half)

    mine = local_rows(t)
    theirs = local_rows(1 - t)

    def branch(block):
        values = mixed[block, :]
        rank = two_parts(nn_dot(values, a_o[...]))
        return nt_dot(values, wo[...]) + nn_dot(rank, b_o2[...])

    part_out[...] = branch(theirs)
    number = contexts
    part_copy = send(
        part_out, part_in, core_send.at[number], core_recv.at[number], sibling
    )
    part_copy.start()
    own_part = branch(mine) + x_in_rows(x_buf, c, rows, t, half)
    part_copy.wait_recv()
    resid_half = own_part + part_in[...]
    resid[mine, :] = resid_half
    n2_own[mine, :] = normed(resid_half, gain_two)
    n2_gather.start(0)
    n2_copy = send(
        n2_own.at[mine], n2_own.at[mine], core_send.at[number + 1], core_recv.at[number + 1], sibling
    )
    n2_copy.start()
    resid_copy = send(
        resid.at[mine], resid.at[mine], core_send.at[number + 2], core_recv.at[number + 2], sibling
    )
    resid_copy.start()

    def forwards(gather, buf, first):
        copies = []
        for stage in range(bits):
            group = []
            for block in gather.arrived[stage]:
                index = first + len(copies)
                copies.append(
                    send(
                        buf.at[block],
                        buf.at[block],
                        core_send.at[index],
                        core_recv.at[index],
                        sibling,
                    )
                )
        return copies

    per_stage = [len(stage) for stage in g_gather.arrived]
    g_forward = forwards(g_gather, g_all, number + 5)
    n2_forward = forwards(n2_gather, n2_all, number + 5 + sum(per_stage))

    def pass_on(copies, stage):
        start = sum(per_stage[:stage])
        for copy in copies[start : start + per_stage[stage]]:
            copy.start()

    locals_[5].wait()
    gu_gather.wait(bits - 1)
    locals_[3].wait()
    dn_gather.wait(bits - 1)
    locals_[4].wait()

    def shared_tile(block):
        inputs = n2_own[block, :]
        grads = g_own[block, :]
        rank = nn_dot(inputs, a_gu[...])
        rank2 = two_parts(rank)
        gate = nn_dot(inputs, gu[:, :units]) + nn_dot(rank2, b_gu2[:, :units])
        up_pre = nn_dot(inputs, gu[:, units:]) + nn_dot(rank2, b_gu2[:, units:])
        sigmoid_gate = jax.nn.sigmoid(gate)
        silu = gate * sigmoid_gate
        hidden = (silu * up_pre).astype(jnp.bfloat16)
        down_rank = nn_dot(hidden, a_dn[...])
        shared[block, :] = nt_dot(hidden, dn[...]) + nn_dot(two_parts(down_rank), b_dn2[...])
        down_back = nt_dot(grads, b_dn2[0:RANK, :])
        grad_hidden = nn_dot(grads, dn[...]) + nn_dot(two_parts(down_back), a_dn_t2[...])
        grad_gate = (
            grad_hidden * up_pre * sigmoid_gate * (1.0 + gate * (1.0 - sigmoid_gate))
        ).astype(jnp.bfloat16)
        grad_up = (grad_hidden * silu).astype(jnp.bfloat16)
        rank_back = nt_dot(grad_gate, b_gu2[0 : 2 * RANK, :units]) + nt_dot(
            grad_up, b_gu2[0 : 2 * RANK, units:]
        )
        dn2[block, :] = (
            nt_dot(grad_gate, gu[:, :units])
            + nt_dot(grad_up, gu[:, units:])
            + nn_dot(two_parts(rank_back), a_gu_t2[...])
        )
        rank_low = rank.astype(jnp.bfloat16)
        da_gu[...] += tn_dot(rank_back.astype(jnp.bfloat16), inputs)
        db_gu[0:RANK, :] += 2.0 * tn_dot(rank_low, grad_gate)[0:RANK]
        db_gu[RANK:, :] += 2.0 * tn_dot(rank_low, grad_up)[RANK:]
        da_dn[...] += tn_dot(down_back.astype(jnp.bfloat16), hidden)
        db_dn[...] += 2.0 * tn_dot(down_rank.astype(jnp.bfloat16), grads)

    n2_gather.wait(0)
    for stage in range(1, bits):
        n2_gather.start(stage)
        pass_on(n2_forward, stage - 1)
        if stage < bits - 1:
            n2_gather.wait(stage)
    n2_copy.wait_recv()
    shared_tile(theirs)
    pair_copies = [
        send(
            source.at[theirs], target, core_send.at[number + 3 + i], core_recv.at[number + 3 + i], sibling
        )
        for i, (source, target) in enumerate(((dn2, dn2_in), (shared, shared_in)))
    ]
    for copy in pair_copies:
        copy.start()
    g_gather.wait(0)
    for stage in range(1, bits):
        g_gather.start(stage)
        pass_on(g_forward, stage - 1)
        if stage < bits - 1:
            g_gather.wait(stage)
    n2_out = pltpu.make_async_copy(n2_own, n2_all.at[pl.ds(f * rows, rows)], local_sems.at[12])
    n2_out.start()
    shared_tile(mine)
    for copy in pair_copies:
        copy.wait()
    dn2_half[...] = dn2[mine, :] + dn2_in[...]
    shared_half[...] = shared[mine, :] + shared_in[...]
    n2_gather.wait(bits - 1)
    pass_on(n2_forward, bits - 1)
    g_gather.wait(bits - 1)
    pass_on(g_forward, bits - 1)
    for copy in n2_forward + g_forward:
        copy.wait()
    resid_copy.wait()
    n2_copy.wait_send()
    part_copy.wait_send()
    for gather in gathers + [g_gather, n2_gather]:
        gather.finish()
    n2_out.wait()
    wq_out.wait()
    wo_out.wait()
    locals_[6].wait()

    @pl.when(c < contexts - 1)
    def _():
        up(c, x_in.at[half_rows(0, t)]).wait_send()

    def drain(step, carry):
        chunk = c - step

        @pl.when(c < contexts - 1)
        def _():
            up(chunk, x_buf.at[half_rows(chunk, t)]).wait_send()

        across(chunk).wait_send()
        return carry

    lax.fori_loop(1, c + 1, drain, 0)

    def drain_out(step, carry):
        for copy in out_copies(c - step):
            copy.wait()
        return carry

    lax.fori_loop(0, c + 1, drain_out, 0)


def x_in_rows(x_buf, chunk, rows, part, half):
    block = pl.ds(pl.multiple_of(chunk * rows + part * half, 16), half)
    return x_buf[block, :].astype(jnp.float32)


def forward_call(sizes, sharded, local):
    fsdp, contexts, _ = sizes
    x, g, wq, wo, gu, dn = sharded
    rows = x.shape[0]
    tree = rows * contexts
    width = wo.shape[1]
    units = dn.shape[1]
    bf, f32 = jnp.bfloat16, jnp.float32
    vmem = pl.BlockSpec(memory_space=pltpu.VMEM)
    hbm = pl.BlockSpec(memory_space=pl.ANY)

    def shape(kind, *dims):
        return jax.ShapeDtypeStruct(dims, kind)

    moves = 2 * (fsdp - 1)
    hops = contexts + 5 + 2 * moves
    return pl.pallas_call(
        functools.partial(forward_kernel, sizes),
        in_specs=[hbm] * 6 + [vmem] * len(local),
        out_specs=[hbm] * 7 + [vmem] * 12,
        out_shape=[
            shape(bf, tree, D),
            shape(bf, tree, width),
            shape(bf, tree, width),
            shape(bf, D, 3 * width),
            shape(bf, D, width),
            shape(bf, fsdp * rows, D),
            shape(bf, fsdp * rows, D),
            shape(bf, width, rows),
            shape(bf, rows, width),
            shape(bf, rows, width),
            shape(f32, width, rows),
            shape(f32, 8, rows),
            shape(f32, rows, D),
            shape(f32, rows // 2, D),
            shape(f32, rows // 2, D),
            shape(f32, 2 * RANK, D),
            shape(f32, 2 * RANK, units),
            shape(f32, RANK, units),
            shape(f32, RANK, D),
        ],
        scratch_shapes=[
            pltpu.VMEM((tree, D), bf),
            pltpu.VMEM((D, 3 * width), bf),
            pltpu.VMEM((D, width), bf),
            pltpu.VMEM((D, 2 * units), bf),
            pltpu.VMEM((D, units), bf),
            pltpu.VMEM((rows, D), bf),
            pltpu.VMEM((tree, D), bf),
            pltpu.VMEM((tree, width), bf),
            pltpu.VMEM((tree, width), bf),
            pltpu.VMEM((width, rows), bf),
            pltpu.VMEM((8, rows), f32),
            pltpu.VMEM((8, rows), f32),
            pltpu.VMEM((rows, rows), f32),
            pltpu.VMEM((rows // 2, D), f32),
            pltpu.VMEM((rows // 2, D), f32),
            pltpu.VMEM((rows, D), bf),
            pltpu.VMEM((rows, D), f32),
            pltpu.VMEM((rows, D), f32),
            pltpu.VMEM((rows // 2, D), f32),
            pltpu.VMEM((rows // 2, D), f32),
            pltpu.SemaphoreType.DMA((6, moves)),
            pltpu.SemaphoreType.DMA((6, moves)),
            pltpu.SemaphoreType.DMA((contexts,)),
            pltpu.SemaphoreType.DMA((contexts,)),
            pltpu.SemaphoreType.DMA((hops,)),
            pltpu.SemaphoreType.DMA((hops,)),
            pltpu.SemaphoreType.DMA((13,)),
            pltpu.SemaphoreType.DMA((3, contexts)),
        ],
        name="forward",
        compiler_params=pltpu.CompilerParams(
            collective_id=2, has_side_effects=True, vmem_limit_bytes=62 << 20
        ),
    )(*sharded, *local)


def flips(index, mask, bits):
    for bit in range(bits):
        if mask >> bit & 1:
            index = flip(index, bit)
    return index


class Scatter:
    def __init__(self, bits, me, device_of, work, inbox, count, send_sems, recv_sems):
        self.bits, self.work, self.inbox = bits, work, inbox
        self.copies = [[] for _ in range(bits)]
        self.adds = [[] for _ in range(bits)]
        number = 0
        for half, (offset, size) in enumerate(split_rows(count)):
            alive = list(range(1 << bits))
            slot = 0
            for stage in range(bits):
                bit = (stage + half) % bits
                for mask in alive:
                    if mask >> bit & 1:
                        source = Gather.rows(flips(me, mask, bits) * count + offset, size)
                        target = pl.ds(slot * count + offset, size)
                        kept = Gather.rows(flips(me, mask ^ (1 << bit), bits) * count + offset, size)
                        self.copies[stage].append(
                            send(
                                work.at[source],
                                inbox.at[target],
                                send_sems.at[number],
                                recv_sems.at[number],
                                device_of(flip(me, bit)),
                            )
                        )
                        self.adds[stage].append((kept, target, pl.ds(offset, size)))
                        number = number + 1
                        slot = slot + 1
                alive = [mask for mask in alive if not mask >> bit & 1]

    def start(self, stage):
        for copy in self.copies[stage]:
            copy.start()

    def add(self, stage):
        for copy in self.copies[stage]:
            copy.wait_recv()
        for kept, target, _ in self.adds[stage]:
            total = self.work[kept, :].astype(jnp.float32) + self.inbox[target, :].astype(
                jnp.float32
            )
            self.work[kept, :] = total.astype(jnp.bfloat16)

    def last(self, out, own):
        for copy in self.copies[self.bits - 1]:
            copy.wait_recv()
        for kept, target, rows in self.adds[self.bits - 1]:
            total = self.work[kept, :].astype(jnp.float32) + self.inbox[target, :].astype(
                jnp.float32
            )
            out[rows, :] = (total + own[rows, :]).astype(jnp.bfloat16)

    def finish(self):
        for stage in self.copies:
            for copy in stage:
                copy.wait_send()


def backward_kernel(
    sizes,
    moe_out,
    moe_back,
    n1_hbm,
    k_hbm,
    v_hbm,
    wq_hbm,
    wo_hbm,
    cos_hbm,
    sin_hbm,
    x_in,
    g_in,
    gains,
    hot,
    reach_t,
    resid,
    shared_half,
    dn2_half,
    q_t,
    q_n,
    mixed,
    o_t,
    lse,
    a_qkv,
    b_qkv2,
    a_qkv_t2,
    a_o,
    a_o_t2,
    b_o2,
    block_out,
    input_grad,
    da_qkv,
    db_qkv,
    da_o,
    db_o,
    cosine,
    sinus,
    n1_buf,
    k_buf,
    v_buf,
    wq,
    wo,
    work_back,
    pair_back,
    inbox_back,
    work_out,
    pair_out,
    inbox_out,
    total_half,
    total_full,
    ffn_half,
    ffn_full,
    dy,
    do_n,
    do_t,
    delta,
    k_t,
    dq_t,
    grad_kv,
    bias,
    part,
    part_out,
    part_in,
    z_in,
    z_out,
    dn1_full,
    fs_send,
    fs_recv,
    z_send,
    z_recv,
    core_send,
    core_recv,
    pair_send,
    pair_recv,
    local_sems,
    chunk_sems,
):
    fsdp, contexts, _ = sizes
    bits = fsdp.bit_length() - 1
    f, c, t = place_of()
    rows = x_in.shape[0]
    half = rows // 2
    width = q_t.shape[0]
    heads = width // HEAD_DIM
    sibling = (f, c, 1 - t)
    f32, bf = jnp.float32, jnp.bfloat16

    def peer(index):
        return (index, c, t)

    def local_rows(part_index):
        return pl.ds(pl.multiple_of(part_index * half, 16), half)

    mine = local_rows(t)
    theirs = local_rows(1 - t)

    def block_rows(block, part_index):
        return pl.ds(pl.multiple_of(block * rows + part_index * half, 16), half)

    def work_rows(block):
        return pl.ds(pl.multiple_of(block * half, 16), half)

    masks = list(range(fsdp - 1, -1, -1))

    def exchange(source, work, inbox, which):
        own, sent = [], []
        for mask in masks:
            block = flips(f, mask, bits)
            own.append(
                pltpu.make_async_copy(
                    source.at[block_rows(block, t)],
                    work.at[work_rows(block)],
                    local_sems.at[which, mask],
                )
            )
            sent.append(
                send(
                    source.at[block_rows(block, 1 - t)],
                    inbox.at[work_rows(block)],
                    core_send.at[which, mask],
                    core_recv.at[which, mask],
                    sibling,
                )
            )
        return own, sent

    back_own, back_sent = exchange(moe_back, work_back, pair_back, 0)
    out_own, out_sent = exchange(moe_out, work_out, pair_out, 1)
    for copy in back_own:
        copy.start()
    wo_copy = pltpu.make_async_copy(wo_hbm, wo, local_sems.at[2, 0])
    wq_copy = pltpu.make_async_copy(wq_hbm, wq, local_sems.at[2, 1])
    wo_copy.start()
    greet(
        [peer(flip(f, bit)) for bit in range(bits)]
        + [sibling, (f, lax.rem(c + 1, contexts), t), (f, lax.rem(c + contexts - 1, contexts), t)]
    )
    for copy in back_sent:
        copy.start()
    for copy in out_own:
        copy.start()
    wq_copy.start()

    def chunk_rows(chunk):
        return pl.ds(pl.multiple_of(chunk * rows, 16), rows)

    def loads(chunk):
        block = chunk_rows(chunk)
        return [
            pltpu.make_async_copy(k_hbm.at[block], k_buf.at[block], chunk_sems.at[1, chunk]),
            pltpu.make_async_copy(v_hbm.at[block], v_buf.at[block], chunk_sems.at[2, chunk]),
        ]

    def n1_load(chunk):
        return pltpu.make_async_copy(
            n1_hbm.at[chunk_rows(chunk)], n1_buf, chunk_sems.at[0, chunk]
        )

    def table_loads(chunk):
        block = chunk_rows(chunk)
        return [
            pltpu.make_async_copy(cos_hbm.at[block], cosine, chunk_sems.at[3, chunk]),
            pltpu.make_async_copy(sin_hbm.at[block], sinus, chunk_sems.at[4, chunk]),
        ]

    def start_loads(chunk, carry):
        for copy in loads(chunk):
            copy.start()
        return carry

    lax.fori_loop(0, c + 1, start_loads, 0)

    back = Scatter(
        bits, f, peer, work_back, inbox_back, half, fs_send.at[0], fs_recv.at[0]
    )
    out = Scatter(bits, f, peer, work_out, inbox_out, half, fs_send.at[1], fs_recv.at[1])

    def pair_sum(own, sent, work, inbox):
        for i, mask in enumerate(masks):
            block = work_rows(flips(f, mask, bits))
            own[i].wait()
            sent[i].wait_recv()
            work[block, :] = (
                work[block, :].astype(f32) + inbox[block, :].astype(f32)
            ).astype(bf)

    pair_sum(back_own, back_sent, work_back, pair_back)
    back.start(0)
    for copy in out_sent:
        copy.start()
    for stage in range(1, bits):
        back.add(stage - 1)
        back.start(stage)
    dq_t[...] = jnp.zeros_like(dq_t)
    da_qkv[...] = jnp.zeros_like(da_qkv)
    db_qkv[...] = jnp.zeros_like(db_qkv)
    pair_sum(out_own, out_sent, work_out, pair_out)
    back.last(total_half, dn2_half)
    out.start(0)
    total_full[mine, :] = total_half[...]
    full_copy = send(
        total_half, total_full.at[mine], core_send.at[2, 0], core_recv.at[2, 0], sibling
    )
    full_copy.start()
    gain_one = gains[0:1, :]
    gain_two = gains[1:2, :]
    wo_copy.wait()
    full_copy.wait_recv()

    def attn_tile(i, carry):
        block = local_rows(i)
        values = resid[block, :]
        gradient = g_in[block, :].astype(f32) + norm_back(
            values, rms_scale(values), gain_two, total_full[block, :].astype(f32)
        )
        dy[block, :] = gradient
        low_grad = gradient.astype(bf)
        rank_back = nt_dot(low_grad, b_o2[0:RANK, :])
        do_n[block, :] = (
            nn_dot(low_grad, wo[...]) + nn_dot(two_parts(rank_back), a_o_t2[...])
        ).astype(bf)
        values_o = mixed[block, :]
        rank = nn_dot(values_o, a_o[...])
        first = tn_dot(rank_back.astype(bf), values_o)
        second = 2.0 * tn_dot(rank.astype(bf), low_grad)

        @pl.when(i == 0)
        def _():
            da_o[...] = first
            db_o[...] = second

        @pl.when(i > 0)
        def _():
            da_o[...] += first
            db_o[...] += second

        return carry

    lax.fori_loop(0, 2, attn_tile, 0)
    for p in range(width // 128):
        lanes = slice(128 * p, 128 * p + 128)
        turned = do_n[:, lanes].astype(f32).T
        do_t[lanes, :] = turned.astype(bf)
        product = turned * o_t[lanes, :]
        for odd in range(2):
            delta[2 * p + odd : 2 * p + odd + 1, :] = jnp.sum(
                product[HEAD_DIM * odd : HEAD_DIM * odd + HEAD_DIM, :], axis=0, keepdims=True
            )
    wq_copy.wait()

    def attend_back(chunk):
        block = chunk_rows(chunk)
        n1_load(chunk).start()
        for copy in table_loads(chunk):
            copy.start()
        for copy in loads(chunk) + table_loads(chunk):
            copy.wait()
        fill_bias(bias, hot[block, :], reach_t[...], chunk * rows, c * rows)
        cos_rows = cosine[...]
        sin_rows = -sinus[...]
        for p in range(width // 128):
            lanes = slice(128 * p, 128 * p + 128)
            k_t[lanes, :] = k_buf[block, lanes].astype(f32).T.astype(bf)

        def pair_step(p, carry):
            lanes = pl.ds(pl.multiple_of(p * 128, 128), 128)
            keys = k_buf[block, lanes]
            values = v_buf[block, lanes]
            query_t = q_t[lanes, :]
            grad_t = do_t[lanes, :]
            query = q_n[:, lanes]
            grad = do_n[:, lanes]
            grad_keys = jnp.zeros((rows, 128), f32)
            grad_values = jnp.zeros((rows, 128), f32)
            for odd in range(2):
                h = 2 * p + odd
                upper = head_half(query_t.shape, 0, odd)
                side = head_half(query.shape, 1, odd)
                none_t = jnp.zeros_like(query_t)
                none = jnp.zeros_like(query)
                scores = nn_dot(keys, jnp.where(upper, query_t, none_t)) + bias[...]
                weights = jnp.exp(scores - lse[pl.ds(h, 1), :])
                grad_weights = nn_dot(values, jnp.where(upper, grad_t, none_t))
                grad_scores = (weights * (grad_weights - delta[pl.ds(h, 1), :])).astype(bf)
                grad_values += nn_dot(weights.astype(bf), jnp.where(side, grad, none))
                grad_keys += nn_dot(grad_scores, jnp.where(side, query, none))
                head = pl.ds(pl.multiple_of(h * HEAD_DIM, HEAD_DIM), HEAD_DIM)
                dq_t[head, :] += nn_dot(k_t[head, :], grad_scores)
            grad_kv[:, lanes] = turn(grad_keys, cos_rows, sin_rows).astype(bf)
            grad_kv[:, pl.ds(pl.multiple_of(width + p * 128, 128), 128)] = grad_values.astype(bf)
            return carry

        lax.fori_loop(0, heads // 2, pair_step, 0)

    def project_back(chunk, own):
        block = chunk_rows(chunk)
        grads = grad_kv[...]
        result = nt_dot(grads, wq[:, width:])
        rank_back = nt_dot(grads, b_qkv2[0 : 3 * RANK, width:])
        n1_load(chunk).wait()
        n1 = n1_buf[...]
        rank = nn_dot(n1, a_qkv[...]).astype(bf)
        both = 2.0 * tn_dot(rank, grads)
        db_qkv[RANK : 2 * RANK, :] += both[RANK : 2 * RANK, :width]
        db_qkv[2 * RANK :, :] += both[2 * RANK :, width:]
        if own:
            pieces = []
            for p in range(width // 128):
                lanes = slice(128 * p, 128 * p + 128)
                grad_query = (dq_t[lanes, :] * 0.125).T
                pieces.append(
                    turn(grad_query, cosine[...], -sinus[...]).astype(bf)
                )
            grad_query = jnp.concatenate(pieces, axis=1)
            result += nt_dot(grad_query, wq[:, :width])
            rank_back += nt_dot(grad_query, b_qkv2[0 : 3 * RANK, :width])
            db_qkv[0:RANK, :] += 2.0 * tn_dot(rank, grad_query)[0:RANK, :]
        result += nn_dot(two_parts(rank_back), a_qkv_t2[...])
        da_qkv[...] += tn_dot(rank_back.astype(bf), n1)
        part[...] = result.astype(bf)
        part_out[work_rows(chunk), :] = part[theirs, :]
        z_out[work_rows(chunk), :] = part[mine, :]

    def pair_copy(chunk):
        return send(
            part_out.at[work_rows(chunk)],
            part_in.at[work_rows(chunk)],
            pair_send.at[chunk],
            pair_recv.at[chunk],
            sibling,
        )

    def down(chunk):
        block = work_rows(chunk)
        return send(
            z_out.at[block], z_in.at[block], z_send.at[chunk], z_recv.at[chunk], (f, c - 1, t)
        )

    def chain(chunk):
        block = work_rows(chunk)
        pair_copy(chunk).wait_recv()
        summed = z_out[block, :].astype(f32) + part_in[block, :].astype(f32)
        z_out[block, :] = summed.astype(bf)

        @pl.when(c < contexts - 1)
        def _():
            down(chunk).wait_recv()
            z_out[block, :] = (summed + z_in[block, :].astype(f32)).astype(bf)

    def pass_down(chunk):
        chain(chunk)
        down(chunk).start()

    def step(chunk, carry):
        attend_back(chunk)
        project_back(chunk, False)
        pair_copy(chunk).start()

        @pl.when(c == contexts - 1)
        def _():
            pass_down(chunk)

        @pl.when((c < contexts - 1) & (chunk >= 1))
        def _():
            pass_down(chunk - 1)

        return carry

    lax.fori_loop(0, c, step, 0)
    attend_back(c)
    project_back(c, True)
    pair_copy(c).start()

    @pl.when((c < contexts - 1) & (c >= 1))
    def _():
        pass_down(c - 1)

    for stage in range(1, bits):
        out.add(stage - 1)
        out.start(stage)
    out.last(ffn_half, shared_half)
    ffn_full[mine, :] = ffn_half[...]
    ffn_copy = send(ffn_half, ffn_full.at[mine], core_send.at[2, 1], core_recv.at[2, 1], sibling)
    ffn_copy.start()
    chain(c)
    dn1_full[mine, :] = z_out[work_rows(c), :]
    dn1_copy = send(
        z_out.at[work_rows(c)],
        dn1_full.at[mine],
        core_send.at[2, 2],
        core_recv.at[2, 2],
        sibling,
    )
    dn1_copy.start()
    ffn_copy.wait_recv()
    block_out[...] = resid[...] + ffn_full[...].astype(f32)
    dn1_copy.wait_recv()

    def final_tile(i, carry):
        block = local_rows(i)
        values = x_in[block, :].astype(f32)
        input_grad[block, :] = dy[block, :] + norm_back(
            values, rms_scale(values), gain_one, dn1_full[block, :].astype(f32)
        )
        return carry

    lax.fori_loop(0, 2, final_tile, 0)
    for copy in back_sent + out_sent + [full_copy, ffn_copy, dn1_copy]:
        copy.wait_send()
    back.finish()
    out.finish()

    def drain(chunk, carry):
        pair_copy(chunk).wait_send()

        @pl.when(chunk < c)
        def _():
            down(chunk).wait_send()

        return carry

    lax.fori_loop(0, c + 1, drain, 0)


def backward_call(sizes, remote, local):
    fsdp, contexts, _ = sizes
    rows = local[0].shape[0]
    half = rows // 2
    tree = rows * contexts
    width = remote[6].shape[1]
    bf, f32 = jnp.bfloat16, jnp.float32
    vmem = pl.BlockSpec(memory_space=pltpu.VMEM)
    hbm = pl.BlockSpec(memory_space=pl.ANY)

    def shape(kind, *dims):
        return jax.ShapeDtypeStruct(dims, kind)

    moves = 2 * (fsdp - 1)
    slots = max(fsdp, 4)
    dma = pltpu.SemaphoreType.DMA
    return pl.pallas_call(
        functools.partial(backward_kernel, sizes),
        in_specs=[hbm] * len(remote) + [vmem] * len(local),
        out_specs=[vmem] * 6,
        out_shape=[
            shape(f32, rows, D),
            shape(f32, rows, D),
            shape(f32, 3 * RANK, D),
            shape(f32, 3 * RANK, width),
            shape(f32, RANK, width),
            shape(f32, RANK, D),
        ],
        scratch_shapes=[
            pltpu.VMEM((rows, 128), f32),
            pltpu.VMEM((rows, 128), f32),
            pltpu.VMEM((rows, D), bf),
            pltpu.VMEM((tree, width), bf),
            pltpu.VMEM((tree, width), bf),
            pltpu.VMEM((D, 3 * width), bf),
            pltpu.VMEM((D, width), bf),
            pltpu.VMEM((fsdp * half, D), bf),
            pltpu.VMEM((fsdp * half, D), bf),
            pltpu.VMEM(((fsdp - 1) * half, D), bf),
            pltpu.VMEM((fsdp * half, D), bf),
            pltpu.VMEM((fsdp * half, D), bf),
            pltpu.VMEM(((fsdp - 1) * half, D), bf),
            pltpu.VMEM((half, D), bf),
            pltpu.VMEM((rows, D), bf),
            pltpu.VMEM((half, D), bf),
            pltpu.VMEM((rows, D), bf),
            pltpu.VMEM((rows, D), f32),
            pltpu.VMEM((rows, width), bf),
            pltpu.VMEM((width, rows), bf),
            pltpu.VMEM((8, rows), f32),
            pltpu.VMEM((width, rows), bf),
            pltpu.VMEM((width, rows), f32),
            pltpu.VMEM((rows, 2 * width), bf),
            pltpu.VMEM((rows, rows), f32),
            pltpu.VMEM((rows, D), bf),
            pltpu.VMEM((contexts * half, D), bf),
            pltpu.VMEM((contexts * half, D), bf),
            pltpu.VMEM((contexts * half, D), bf),
            pltpu.VMEM((contexts * half, D), bf),
            pltpu.VMEM((rows, D), bf),
            dma((2, moves)),
            dma((2, moves)),
            dma((contexts,)),
            dma((contexts,)),
            dma((3, slots)),
            dma((3, slots)),
            dma((contexts,)),
            dma((contexts,)),
            dma((3, slots)),
            dma((5, contexts)),
        ],
        name="backward",
        compiler_params=pltpu.CompilerParams(
            collective_id=3, has_side_effects=True, vmem_limit_bytes=62 << 20
        ),
    )(*remote, *local)


def reduce_kernel(
    sizes, packed, table_all, out, inbox, z_out, z_in, total, f_in, send_sems, recv_sems
):
    fsdp, contexts, _ = sizes
    f, c, t = place_of()
    f32, bf = jnp.float32, jnp.bfloat16
    peers = [(lax.rem(f + k, fsdp), c, t) for k in range(1, fsdp)]
    stacked = [(f, lax.rem(c + k, contexts), t) for k in range(1, contexts)]
    sibling = (f, c, 1 - t)
    greet(peers + stacked + [sibling])
    order = [lax.rem(c + k, contexts) for k in range(1, contexts)] + [c]
    pair = []
    for k, block in enumerate(order):
        copy = send(
            packed.at[block, 1 - t], inbox.at[block], send_sems.at[0, k], recv_sems.at[0, k], sibling
        )
        copy.start()
        pair.append(copy)
    across = []
    for k, other in enumerate(stacked):
        pair[k].wait_recv()
        z_out[k] = (packed[order[k], t] + inbox[order[k]]).astype(bf)
        copy = send(z_out.at[k], z_in.at[k], send_sems.at[1, k], recv_sems.at[1, k], other)
        copy.start()
        across.append(copy)
    pair[-1].wait_recv()
    result = packed[c, t] + inbox[c]
    for k, copy in enumerate(across):
        copy.wait_recv()
        result = result + z_in[k].astype(f32)
    total[...] = result.astype(bf)
    ends = []
    for k, peer in enumerate(peers):
        copy = send(total, f_in.at[k], send_sems.at[2, k], recv_sems.at[2, k], peer)
        copy.start()
        ends.append(copy)
    own = ADAPTERS // fsdp
    wanted = [(f * own + a).astype(f32) for a in range(own)]
    sums = [jnp.where(table_all[f, 4:5, 0:1] == w, total[...].astype(f32), 0.0) for w in wanted]
    for k, copy in enumerate(ends):
        copy.wait_recv()
        tree = table_all[lax.rem(f - k - 1 + fsdp, fsdp), 4:5, 0:1]
        block = f_in[k].astype(f32)
        sums = [s + jnp.where(tree == w, block, 0.0) for s, w in zip(sums, wanted)]
    for a in range(own):
        out[a] = sums[a]
    for copy in pair + across + ends:
        copy.wait_send()


def reduce_call(sizes, packed, table_all):
    fsdp, contexts, _ = sizes
    block = packed.shape[2:]
    vmem = pl.BlockSpec(memory_space=pltpu.VMEM)
    bf, f32 = jnp.bfloat16, jnp.float32
    slots = max(fsdp, contexts)
    return pl.pallas_call(
        functools.partial(reduce_kernel, sizes),
        in_specs=[vmem, vmem],
        out_specs=vmem,
        out_shape=jax.ShapeDtypeStruct((ADAPTERS // fsdp,) + block, f32),
        scratch_shapes=[
            pltpu.VMEM((contexts,) + block, f32),
            pltpu.VMEM((contexts - 1,) + block, bf),
            pltpu.VMEM((contexts - 1,) + block, bf),
            pltpu.VMEM(block, bf),
            pltpu.VMEM((fsdp - 1,) + block, bf),
            pltpu.SemaphoreType.DMA((3, slots)),
            pltpu.SemaphoreType.DMA((3, slots)),
        ],
        name="adapter_sums",
        compiler_params=pltpu.CompilerParams(
            collective_id=4, has_side_effects=True, vmem_limit_bytes=60 << 20
        ),
    )(packed, table_all)


def small_kernel(
    sizes,
    ids_ref,
    adapters_ref,
    gains_ref,
    table_ref,
    chosen_ref,
    gains_all,
    table_all,
    adapters_all,
    send_sems,
    recv_sems,
):
    fsdp, contexts, _ = sizes
    f, c, t = place_of()
    peers = [(lax.rem(f + k, fsdp), c, t) for k in range(1, fsdp)]
    stacked = [(f, lax.rem(c + k, contexts), t) for k in range(1, contexts)]
    sibling = (f, c, 1 - t)
    greet(peers + stacked + [sibling])
    first = []
    for k, peer in enumerate(peers):
        for j, (source, target) in enumerate(
            ((adapters_ref, adapters_all), (gains_ref, gains_all), (table_ref, table_all))
        ):
            copy = send(source, target.at[f], send_sems.at[j, k], recv_sems.at[j, k], peer)
            copy.start()
            first.append(copy)
    adapters_all[f] = adapters_ref[...]
    gains_all[f] = gains_ref[...]
    table_all[f] = table_ref[...]
    for copy in first:
        copy.wait()
    wanted = ids_ref[0]
    rows = RANK
    own = ADAPTERS // fsdp
    total = jnp.zeros((rows, adapters_ref.shape[1]), jnp.float32)
    for a in range(ADAPTERS):
        block = adapters_all[a // own, pl.ds((a % own) * rows, rows), :].astype(jnp.float32)
        total = total + jnp.where(wanted == a, block, 0.0)
    chosen_ref[t, c] = total.astype(jnp.bfloat16)
    second = []
    for k, other in enumerate(stacked):
        copy = send(
            chosen_ref.at[t, c], chosen_ref.at[t, c], send_sems.at[3, k], recv_sems.at[3, k], other
        )
        copy.start()
        second.append(copy)
    for copy in second:
        copy.wait()
    last = send(chosen_ref.at[t], chosen_ref.at[t], send_sems.at[4, 0], recv_sems.at[4, 0], sibling)
    last.start()
    last.wait()


def small_call(sizes, ids, adapters, gains, table):
    fsdp, contexts, tensors = sizes
    slots = max(fsdp, contexts)
    vmem = pl.BlockSpec(memory_space=pltpu.VMEM)
    return pl.pallas_call(
        functools.partial(small_kernel, sizes),
        in_specs=[pl.BlockSpec(memory_space=pltpu.SMEM), vmem, vmem, vmem],
        out_specs=[vmem] * 3,
        out_shape=[
            jax.ShapeDtypeStruct((tensors, contexts, RANK, adapters.shape[1]), jnp.bfloat16),
            jax.ShapeDtypeStruct((fsdp,) + gains.shape, gains.dtype),
            jax.ShapeDtypeStruct((fsdp,) + table.shape, table.dtype),
        ],
        scratch_shapes=[
            pltpu.VMEM((fsdp,) + adapters.shape, adapters.dtype),
            pltpu.SemaphoreType.DMA((5, slots)),
            pltpu.SemaphoreType.DMA((5, slots)),
        ],
        name="small_gather",
        compiler_params=pltpu.CompilerParams(
            collective_id=1, has_side_effects=True, vmem_limit_bytes=60 << 20
        ),
    )(ids, adapters, gains, table)


def shards(
    tokens,
    attn_gain,
    w_qkv,
    w_out,
    ffn_gain,
    w_gu,
    w_dn,
    w_egu,
    w_edn,
    adapters,
    adapter_ids,
    parents,
    seg_lengths,
    routes,
    route_weights,
    cotangent,
):
    tree_count = tokens.shape[0]
    row_count = tokens.shape[1]
    contexts = lax.axis_size("context")
    tensors = lax.axis_size("tensor")
    fsdp_size = lax.axis_size("fsdp")
    tree_len = row_count * contexts
    token_count = tree_count * row_count
    local_heads = HEADS // tensors
    local_width = local_heads * HEAD_DIM
    local_ff = FF // tensors
    part_index = lax.axis_index("tensor")
    row_start = lax.axis_index("context") * row_count
    width_start = part_index * local_width
    ff_start = part_index * local_ff
    head_shape = (tree_count, row_count, local_heads, HEAD_DIM)
    wide_shape = (tree_count, tree_len, local_heads, HEAD_DIM)
    sizes = (fsdp_size, contexts, tensors)
    own_adapters = adapters.shape[0]
    own_width = D // fsdp_size
    gains = jnp.broadcast_to(jnp.concatenate([attn_gain, ffn_gain])[None], (16, 2 * own_width))
    route_table = jnp.concatenate(
        [
            routes[0].astype(jnp.float32).T,
            route_weights[0].astype(jnp.float32).T,
            jnp.broadcast_to(adapter_ids.astype(jnp.float32)[:, None], (1, row_count)),
            jnp.zeros((3, row_count), jnp.float32),
        ]
    )
    chosen_parts, gains_all, table_all = small_call(
        sizes, adapter_ids, adapters.reshape(own_adapters * RANK, -1), gains, route_table
    )
    chosen = chosen_parts.transpose(1, 0, 2, 3).reshape(1, PARAMS).astype(jnp.float32)
    gain_one = gains_all[:, 0, :own_width].reshape(D)
    gain_two = gains_all[:, 0, own_width:].reshape(D)
    routes_all = table_all[:, 0:2].transpose(0, 2, 1).reshape(-1, TOPK).astype(jnp.int32)
    route_weights_all = table_all[:, 2:4].transpose(0, 2, 1).reshape(-1, TOPK)
    (
        a_qkv,
        query_key_value_adapter_up,
        a_out,
        output_adapter_up,
        a_gu,
        gate_up_adapter_up,
        a_dn,
        down_adapter_up,
    ) = unpack(chosen)
    b_qkv_part = lax.dynamic_slice_in_dim(query_key_value_adapter_up, width_start, local_width, 3)
    a_out_part = lax.dynamic_slice_in_dim(a_out, width_start, local_width, 1)
    b_gu_part = lax.dynamic_slice_in_dim(gate_up_adapter_up, ff_start, local_ff, 3)
    down_adapter_slice = lax.dynamic_slice_in_dim(a_dn, ff_start, local_ff, 1)
    ancestry, starts, offsets = jax.vmap(tree_layout)(seg_lengths, parents)
    ancestry_f = ancestry.astype(jnp.float32)
    key_ids = jnp.arange(tree_len, dtype=jnp.int32)
    query_ids = row_start + jnp.arange(row_count, dtype=jnp.int32)
    key_hot, key_positions = jax.vmap(locate, in_axes=(None, 0, 0))(key_ids, starts, offsets)
    key_hot = key_hot.astype(jnp.float32)
    query_hot = lax.dynamic_slice_in_dim(key_hot, row_start, row_count, 1)
    reach = (jnp.einsum("trs,tsu->tru", query_hot, ancestry_f) > 0.5).astype(jnp.float32)
    visible = (jnp.einsum("tru,tku->trk", reach, key_hot) > 0.5) & (
        key_ids[None, None, :] <= query_ids[None, :, None]
    )
    cos_all, sin_all = angles(key_positions)
    cosine = lax.dynamic_slice_in_dim(cos_all, row_start, row_count, 1)
    sinus = lax.dynamic_slice_in_dim(sin_all, row_start, row_count, 1)
    cos_one = cos_all[0, :, 0, :]
    sin_one = sin_all[0, :, 0, :]
    cos_table = jnp.concatenate([cos_one] * 4, axis=1)
    sin_table = jnp.concatenate([-sin_one, sin_one, -sin_one, sin_one], axis=1)
    pad = 16 - key_hot.shape[2]
    hot_table = jnp.pad(key_hot[0], ((0, 0), (0, pad))).astype(jnp.bfloat16)
    reach_t = jnp.pad(reach[0], ((0, 0), (0, pad))).T.astype(jnp.bfloat16)

    def low(values):
        return values.astype(jnp.bfloat16)

    def blocks(up_rows):
        count, rank, cols = up_rows.shape
        out = jnp.zeros((count, rank, count, cols), jnp.float32)
        for j in range(count):
            out = out.at[j, :, j].set(up_rows[j])
        return out.reshape(count * rank, count * cols)

    def twice(values):
        return low(jnp.concatenate([values, values], axis=0))

    local = (
        jnp.pad(jnp.stack([gain_one, gain_two]).astype(jnp.float32), ((0, 6), (0, 0))),
        cos_table,
        sin_table,
        hot_table,
        reach_t,
        low(a_qkv[0]),
        twice(2.0 * blocks(b_qkv_part[0])),
        low(a_out_part[0]),
        twice(2.0 * output_adapter_up[0]),
        low(a_gu[0]),
        twice(2.0 * blocks(b_gu_part[0])),
        twice(a_gu[0].T),
        low(down_adapter_slice[0]),
        twice(down_adapter_slice[0].T),
        twice(2.0 * down_adapter_up[0]),
    )
    sharded = (
        tokens[0],
        cotangent[0],
        w_qkv.reshape(own_width, 3 * local_width),
        w_out.T,
        w_gu.reshape(own_width, 2 * local_ff),
        w_dn.T,
    )
    (
        n1_all,
        k_all,
        v_all,
        wq_all,
        wo_all,
        normed_all,
        cotangent_all,
        q_t,
        q_n,
        mixed_own,
        o_t,
        lse,
        resid,
        shared_half,
        dn2_half,
        da_gu_t,
        db_gu_own,
        da_dn_t,
        db_dn_own,
    ) = forward_call(sizes, sharded, local)
    own_experts = EXPERTS // fsdp_size
    spans, place, weight = moe_layout(
        routes_all, route_weights_all, lax.axis_index("fsdp") * own_experts, own_experts
    )
    moe_all, moe_back_all = moe_call(
        spans, place, weight, normed_all, cotangent_all, w_egu.transpose(0, 2, 1, 3), w_edn
    )
    remote = (moe_all, moe_back_all, n1_all, k_all, v_all, wq_all, wo_all, local[1], local[2])
    block_out, input_grad, da_qkv_t, db_qkv_own, da_o_t, db_o_own = backward_call(
        sizes,
        remote,
        (tokens[0], cotangent[0])
        + (local[0], local[3], local[4])
        + (resid, shared_half, dn2_half, q_t, q_n, mixed_own, o_t, lse)
        + (local[5], local[6], twice(a_qkv[0].T), local[7], twice(a_out_part[0].T), local[8]),
    )
    block_out = block_out[None]
    input_grad = input_grad[None]
    grad_a_qkv = da_qkv_t.T[None]
    grad_b_qkv = lax.dynamic_update_slice_in_dim(
        jnp.zeros((tree_count, 3, RANK, D), jnp.float32),
        db_qkv_own.reshape(1, 3, RANK, local_width),
        width_start,
        3,
    )
    grad_a_out = lax.dynamic_update_slice_in_dim(
        jnp.zeros((tree_count, D, RANK), jnp.float32), da_o_t.T[None], width_start, 1
    )
    output_adapter_up_gradient = db_o_own[None]
    grad_a_gu = da_gu_t.T[None]
    grad_b_gu = lax.dynamic_update_slice_in_dim(
        jnp.zeros((tree_count, 2, RANK, FF), jnp.float32),
        db_gu_own.reshape(1, 2, RANK, local_ff),
        ff_start,
        3,
    )
    grad_a_dn = lax.dynamic_update_slice_in_dim(
        jnp.zeros((tree_count, FF, RANK), jnp.float32), da_dn_t.T[None], ff_start, 1
    )
    down_adapter_up_gradient = db_dn_own[None]
    grad_pieces = [
        grad_a_qkv,
        grad_b_qkv,
        grad_a_out,
        output_adapter_up_gradient,
        grad_a_gu,
        grad_b_gu,
        grad_a_dn,
        down_adapter_up_gradient,
    ]
    packed = jnp.concatenate([piece.reshape(tree_count, -1) for piece in grad_pieces], axis=1)
    adapter_grads = reduce_call(
        sizes, packed[0].reshape(contexts, tensors, RANK, -1), table_all
    ).reshape(own_adapters, -1)
    return (block_out, input_grad, adapter_grads)


def solution(mesh):
    return jax.shard_map(
        shards,
        mesh=mesh,
        in_specs=(
            P("fsdp", "context", None),
            P("fsdp"),
            P("fsdp", None, "tensor"),
            P("tensor", "fsdp"),
            P("fsdp"),
            P("fsdp", None, "tensor"),
            P("tensor", "fsdp"),
            P("fsdp", None, None, "tensor"),
            P("fsdp", "tensor", None),
            P("fsdp", ("context", "tensor")),
            P("fsdp"),
            P("fsdp", None),
            P("fsdp", None),
            P("fsdp", "context", None),
            P("fsdp", "context", None),
            P("fsdp", "context", None),
        ),
        out_specs=(
            P("fsdp", "context", None),
            P("fsdp", "context", None),
            P("fsdp", ("context", "tensor")),
        ),
        check_vma=False,
    )
```

```python
import jax
import jax.numpy as jnp
import functools
import math

from jax import lax
from jax.experimental import pallas as pl
from jax.experimental.pallas import tpu as pltpu
from jax.sharding import PartitionSpec as P

D = 768
HEADS = 12
HEAD_DIM = 64
FF = 2048
EXPERTS = 8
TOPK = 2
RANK = 16
ADAPTERS = 8
PARAMS = 233472


epsilon = 1e-06
adapter_scale = 2.0
rope_base = 10000.0
masked_score = -1e30
highest_precision = lax.Precision.HIGHEST


def rms_scale(values):
    return lax.rsqrt(jnp.mean(values * values, axis=-1, keepdims=True) + epsilon)


def norm_back(values, scaling, gain_values, gradient):
    weighted = gradient * gain_values
    inner_mean = jnp.mean(values * weighted, axis=-1, keepdims=True)
    return scaling * weighted - values * (scaling * scaling * scaling) * inner_mean


SLOT_TILE = 256
TOKEN_TILE = 256
SLOT_WINDOW = 128


def nt_dot(left, right):
    return lax.dot_general(left, right, (((1,), (1,)), ((), ())), preferred_element_type=jnp.float32)


def tn_dot(left, right):
    return lax.dot_general(left, right, (((0,), (0,)), ((), ())), preferred_element_type=jnp.float32)


def nn_dot(left, right):
    return jnp.dot(left, right, preferred_element_type=jnp.float32)


def moe_kernel(
    starts,
    place_row,
    place_col,
    weight_col,
    rows_ref,
    grads_ref,
    egu_hbm,
    edn_hbm,
    out_ref,
    back_ref,
    egu_ref,
    edn_ref,
    taken,
    taken_grad,
    taken_weight,
    sems,
):
    f32, bf = jnp.float32, jnp.bfloat16
    experts = egu_hbm.shape[0]
    blocks = rows_ref.shape[0] // TOKEN_TILE
    copies = []
    for e in range(experts):
        copies.append(
            (
                pltpu.make_async_copy(egu_hbm.at[e], egu_ref.at[e], sems.at[e, 0]),
                pltpu.make_async_copy(edn_hbm.at[e], edn_ref.at[e], sems.at[e, 1]),
            )
        )
        copies[e][0].start()
        copies[e][1].start()
    taken[...] = jnp.zeros_like(taken)
    taken_grad[...] = jnp.zeros_like(taken_grad)
    taken_weight[...] = jnp.zeros_like(taken_weight)
    slot_rows = lax.broadcasted_iota(jnp.int32, (SLOT_WINDOW, TOKEN_TILE), 0).astype(f32)
    slot_cols = lax.broadcasted_iota(jnp.int32, (TOKEN_TILE, SLOT_WINDOW), 1).astype(f32)

    def windows(e, b):
        begin = starts[e, b] // 16 * 16
        return begin, (starts[e, b + 1] - begin + SLOT_WINDOW - 1) // SLOT_WINDOW

    def block_rows(b):
        return pl.ds(pl.multiple_of(b * TOKEN_TILE, TOKEN_TILE), TOKEN_TILE)

    def fetch(b, carry):
        block = block_rows(b)
        for e in range(experts):
            begin, count = windows(e, b)

            def window(i, c, e=e, begin=begin):
                first = pl.multiple_of(begin + i * SLOT_WINDOW, 16)
                hit = place_row[e : e + 1, block] == slot_rows + first.astype(f32)
                pick = jnp.where(hit, 1.0, 0.0).astype(bf)
                slots = pl.ds(first, SLOT_WINDOW)
                taken[e, slots, :] += nn_dot(pick, rows_ref[block, :]).astype(bf)
                taken_grad[e, slots, :] += nn_dot(pick, grads_ref[block, :]).astype(bf)
                taken_weight[e, slots, :] += nn_dot(pick, weight_col[block, :]).astype(bf)
                return c

            lax.fori_loop(0, count, window, 0)
        return carry

    lax.fori_loop(0, blocks, fetch, 0)
    for e in range(experts):
        copies[e][0].wait()
        copies[e][1].wait()

        def tile_step(i, carry, e=e):
            slots = pl.ds(pl.multiple_of(i * SLOT_TILE, SLOT_TILE), SLOT_TILE)
            inputs = taken[e, slots, :]
            gate_pre = nn_dot(inputs, egu_ref[e, 0])
            up_pre = nn_dot(inputs, egu_ref[e, 1])
            sigmoid_gate = jax.nn.sigmoid(gate_pre)
            silu = gate_pre * sigmoid_gate
            active = (silu * up_pre).astype(bf)
            taken[e, slots, :] = nn_dot(active, edn_ref[e]).astype(bf)
            grad_active = nt_dot(taken_grad[e, slots, :], edn_ref[e])
            grad_active = grad_active * taken_weight[e, slots, e : e + 1].astype(f32)
            grad_gate = (
                grad_active * up_pre * sigmoid_gate * (1.0 + gate_pre * (1.0 - sigmoid_gate))
            ).astype(bf)
            grad_up = (grad_active * silu).astype(bf)
            taken_grad[e, slots, :] = (
                nt_dot(grad_gate, egu_ref[e, 0]) + nt_dot(grad_up, egu_ref[e, 1])
            ).astype(bf)
            return carry

        lax.fori_loop(0, (starts[e, blocks] + SLOT_TILE - 1) // SLOT_TILE, tile_step, 0)

    def give(b, carry):
        block = block_rows(b)
        out_ref[block, :] = jnp.zeros((TOKEN_TILE, out_ref.shape[1]), bf)
        back_ref[block, :] = jnp.zeros((TOKEN_TILE, out_ref.shape[1]), bf)
        for e in range(experts):
            begin, count = windows(e, b)

            def window(i, c, e=e, begin=begin):
                first = pl.multiple_of(begin + i * SLOT_WINDOW, 16)
                hit = place_col[block, e : e + 1] == slot_cols + first.astype(f32)
                pick = jnp.where(hit, 1.0, 0.0).astype(bf)
                slots = pl.ds(first, SLOT_WINDOW)
                weight = weight_col[block, e : e + 1].astype(f32)
                out_ref[block, :] = (
                    out_ref[block, :].astype(f32) + nn_dot(pick, taken[e, slots, :]) * weight
                ).astype(bf)
                back_ref[block, :] = (
                    back_ref[block, :].astype(f32) + nn_dot(pick, taken_grad[e, slots, :])
                ).astype(bf)
                return c

            lax.fori_loop(0, count, window, 0)
        return carry

    lax.fori_loop(0, blocks, give, 0)


def moe_call(starts, place_row, place_col, weight_col, rows, grads, egu, edn):
    total, width = rows.shape
    experts = egu.shape[0]
    slots = total // 2 + SLOT_TILE
    vmem = pl.BlockSpec(memory_space=pltpu.VMEM)
    hbm = pl.BlockSpec(memory_space=pl.ANY)
    shape = jax.ShapeDtypeStruct((total, width), jnp.bfloat16)
    return pl.pallas_call(
        moe_kernel,
        grid_spec=pltpu.PrefetchScalarGridSpec(
            num_scalar_prefetch=1,
            grid=(),
            in_specs=[vmem] * 5 + [hbm] * 2,
            out_specs=[vmem, vmem],
            scratch_shapes=[
                pltpu.VMEM(egu.shape, jnp.bfloat16),
                pltpu.VMEM(edn.shape, jnp.bfloat16),
                pltpu.VMEM((experts, slots, width), jnp.bfloat16),
                pltpu.VMEM((experts, slots, width), jnp.bfloat16),
                pltpu.VMEM((experts, slots, 128), jnp.bfloat16),
                pltpu.SemaphoreType.DMA((experts, 2)),
            ],
        ),
        out_shape=[shape, shape],
        name="experts",
        compiler_params=pltpu.CompilerParams(vmem_limit_bytes=60 << 20),
    )(starts, place_row, place_col, weight_col, rows, grads, egu, edn)


MESH = pl.DeviceIdType.MESH


def place_of():
    return lax.axis_index("fsdp"), lax.axis_index("context"), lax.axis_index("tensor")


def greet(devices):
    barrier = pltpu.get_barrier_semaphore()
    for device in devices:
        pl.semaphore_signal(barrier, inc=1, device_id=device, device_id_type=MESH)
    pl.semaphore_wait(barrier, len(devices))


def send(source, target, send_sem, recv_sem, device):
    return pltpu.make_async_remote_copy(
        src_ref=source,
        dst_ref=target,
        send_sem=send_sem,
        recv_sem=recv_sem,
        device_id=device,
        device_id_type=MESH,
    )


def flip(index, bit):
    return index + (1 - 2 * lax.rem(index // (1 << bit), 2)) * (1 << bit)


def split_rows(count):
    first = (count // 2 + 15) // 16 * 16
    return ((0, first), (first, count - first))


class Gather:
    def __init__(self, bits, me, device_of, own, buf, stride, base, count, send_sems, recv_sems):
        self.stages = [[] for _ in range(bits)]
        self.arrived = [[] for _ in range(bits)]
        self.passed = [[] for _ in range(bits)]
        number = 0
        for half, (offset, size) in enumerate(split_rows(count)):
            held = [me]
            for stage in range(bits):
                bit = (stage + half) % bits
                for block in held:
                    rows = self.rows(block * stride + base + offset, size)
                    source = own.at[self.rows(base + offset, size)] if block is me else buf.at[rows]
                    self.passed[stage].append(block is not me)
                    self.stages[stage].append(
                        send(
                            source,
                            buf.at[rows],
                            send_sems.at[number],
                            recv_sems.at[number],
                            device_of(flip(me, bit)),
                        )
                    )
                    self.arrived[stage].append(
                        self.rows(flip(block, bit) * stride + base + offset, size)
                    )
                    number = number + 1
                held = held + [flip(block, bit) for block in held]

    @staticmethod
    def rows(start, size):
        return pl.ds(pl.multiple_of(start, 16), size)

    def start(self, stage):
        if stage == 0:
            for copies, passed in zip(self.stages, self.passed):
                for copy, later in zip(copies, passed):
                    if not later:
                        copy.start()
        else:
            for copy, later in zip(self.stages[stage], self.passed[stage]):
                if later:
                    copy.start()

    def wait(self, stage):
        for copy in self.stages[stage]:
            copy.wait_recv()

    def finish(self):
        for stage in self.stages:
            for copy in stage:
                copy.wait_send()


def turn(values, cosine, sinus):
    lane = lax.broadcasted_iota(jnp.int32, values.shape, 1)
    first = lax.rem(lane, HEAD_DIM) < HEAD_DIM // 2
    swapped = jnp.where(
        first,
        pltpu.roll(values, 128 - HEAD_DIM // 2, 1),
        pltpu.roll(values, HEAD_DIM // 2, 1),
    )
    return values * cosine + swapped * sinus


def two_parts(values):
    high = values.astype(jnp.bfloat16)
    low = (values - high.astype(jnp.float32)).astype(jnp.bfloat16)
    return jnp.concatenate([high, low], axis=1)


def normed(values, gain):
    scale = lax.rsqrt(jnp.mean(values * values, axis=-1, keepdims=True) + epsilon)
    return (values * scale * gain).astype(jnp.bfloat16)


def fill_bias(bias, hot_rows, reach_t, key_start, query_start):
    seen = nn_dot(hot_rows, reach_t)
    keys = key_start + lax.broadcasted_iota(jnp.int32, seen.shape, 0)
    queries = query_start + lax.broadcasted_iota(jnp.int32, seen.shape, 1)
    bias[...] = jnp.where((seen > 0.5) & (keys <= queries), 0.0, masked_score)


def head_half(shape, axis, odd):
    index = lax.broadcasted_iota(jnp.int32, shape, axis)
    return (index >= HEAD_DIM) if odd else (index < HEAD_DIM)


def tree_tables(parents, lengths, turns, context, rows, hot, reach_t, cosine, sinus):
    lane = lax.broadcasted_iota(jnp.int32, (1, 128), 1)
    far = jnp.full((1, 128), 1 << 30, jnp.int32)
    none = jnp.zeros((1, 128), jnp.int32)
    begins, ends, moves = far, far, none
    first, second = none - 1, none - 1
    start = jnp.int32(0)
    for s in range(parents.shape[1]):
        parent = parents[0, s]
        grand = parents[0, parent]
        here = lane == s
        above = jnp.where(parent != s, lengths[0, parent], 0) + jnp.where(
            (grand != s) & (grand != parent), lengths[0, grand], 0
        )
        begins = jnp.where(here, start, begins)
        moves = jnp.where(here, above - start, moves)
        first = jnp.where(here, parent, first)
        second = jnp.where(here, grand, second)
        start = start + lengths[0, s]
        ends = jnp.where(here, start, ends)
    over = lax.broadcasted_iota(jnp.int32, (128, 128), 0)
    under = lax.broadcasted_iota(jnp.int32, (128, 128), 1)
    ancestors = jnp.where((over == under) | (over == first) | (over == second), 1.0, 0.0).astype(
        jnp.bfloat16
    )

    def fill(chunk, carry):
        block = pl.ds(pl.multiple_of(chunk * rows, 16), rows)
        row = chunk * rows + lax.broadcasted_iota(jnp.int32, (rows, 128), 0)
        inside = (row >= begins) & (row < ends)
        hot[block, :] = jnp.where(inside, 1.0, 0.0).astype(jnp.bfloat16)
        moved = jnp.sum(jnp.where(inside, moves.astype(jnp.float32), 0.0), axis=1, keepdims=True)
        angle = (row.astype(jnp.float32) + moved) * turns[0:1, :]
        cosine[block, :] = jnp.cos(angle)
        sinus[block, :] = jnp.sin(angle) * turns[1:2, :]
        return carry

    lax.fori_loop(0, context + 1, fill, 0)
    own = pl.ds(pl.multiple_of(context * rows, 16), rows)
    reach_t[...] = nt_dot(ancestors, hot[own, :]).astype(jnp.bfloat16)


def choose(ids, adapters_all, out):
    wanted = ids[0]
    own = ADAPTERS // adapters_all.shape[0]
    count = adapters_all.shape[1] // own
    total = jnp.zeros((count, 128), jnp.float32)
    for a in range(ADAPTERS):
        block = adapters_all[a // own, pl.ds((a % own) * count, count), :].astype(jnp.float32)
        total = total + jnp.where(wanted == a, block, 0.0)
    out[...] = total.astype(jnp.bfloat16)


def route_tables(f, table_all, place_row, place_col, weight_col, marks):
    fsdp, _, rows = table_all.shape
    own = EXPERTS // fsdp
    f32 = jnp.float32
    sub = lax.broadcasted_iota(jnp.int32, (8, rows), 0)
    expert = jnp.where(sub < own, f * own + sub, -1).astype(f32)
    before = lax.broadcasted_iota(jnp.int32, (rows, rows), 0)
    after = lax.broadcasted_iota(jnp.int32, (rows, rows), 1)
    upto = jnp.where(before <= after, 1.0, 0.0).astype(jnp.bfloat16)
    lane = lax.broadcasted_iota(jnp.int32, (8, 128), 1)
    base = jnp.zeros((8, 1), f32)
    found = jnp.zeros((8, 128), f32)
    more = jnp.zeros((120, rows), f32)
    for source in range(fsdp):
        table = table_all[source]
        one = table[0:1, :] == expert
        two = table[1:2, :] == expert
        hit = one | two
        weight = jnp.where(one, table[2:3, :], 0.0) + jnp.where(two, table[3:4, :], 0.0)
        count = nn_dot(jnp.where(hit, 1.0, 0.0).astype(jnp.bfloat16), upto) + base
        place = jnp.where(hit, count - 1.0, -1.0)
        block = slice(source * rows, (source + 1) * rows)
        place_row[:, block] = place
        place_col[block, :] = jnp.concatenate([place, more], axis=0).T
        weight_col[block, :] = jnp.concatenate([weight, more], axis=0).T.astype(jnp.bfloat16)
        for token in range(TOKEN_TILE - 1, fsdp * rows, TOKEN_TILE):
            if token // rows == source:
                at = token % rows
                found = jnp.where(lane == token // TOKEN_TILE + 1, count[:, at : at + 1], found)
        base = count[:, rows - 1 : rows]
    marks[...] = found


def unpack_adapter(t, per_block, chosen, flat, wide, first, second):
    a_qkv, b_qkv2, a_qkv_t2, a_o, b_o2, a_o_t2 = first
    a_gu, b_gu2, a_gu_t2, a_dn, a_dn_t2, b_dn2 = second
    f32, bf = jnp.float32, jnp.bfloat16
    contexts = chosen.shape[1]
    width, units = a_o.shape[0], a_dn.shape[0]
    count = PARAMS // 128 // (2 * contexts)
    for context in range(contexts):
        for part in range(2):
            start = (2 * context + part) * count
            flat[start : start + count, :] = chosen[part, context, 0:count, :].astype(f32)

    def spread(start, groups, rank, out, out_t):
        total = groups * 128 // rank
        wide[...] = jnp.zeros_like(wide)
        lines = rank // math.gcd(rank, 128)
        each = lines * 128 // rank
        for i in range(each):
            row, at = divmod(i * rank, 128)
            def line(number):
                if lines == 1:
                    return flat[pl.ds(start, groups), :]
                return flat[pl.ds(start + number, groups // lines, stride=lines), :]

            piece = line(row)[:, at : min(at + rank, 128)]
            if at + rank > 128:
                piece = jnp.concatenate([piece, line(row + 1)[:, 0 : at + rank - 128]], axis=1)
            wide[pl.ds(i, groups // lines, stride=each), 0:rank] = piece
        out[...] = wide[0:total, :].astype(bf)
        if out_t is not None:
            for p in range(total // 128):
                turned = wide[128 * p : 128 * p + 128, :].T.astype(bf)
                out_t[0:128, 128 * p : 128 * p + 128] = turned
                out_t[128:256, 128 * p : 128 * p + 128] = turned

    def stack(start, lines, columns, out, row, column):
        for p, m in enumerate(columns):
            piece = (2.0 * flat[pl.ds(start + m, RANK, stride=lines), :]).astype(bf)
            lanes = slice(column + 128 * p, column + 128 * p + 128)
            out[row : row + RANK, lanes] = piece
            out[128 + row : 128 + row + RANK, lanes] = piece

    for ref in (b_qkv2, b_o2, b_gu2, b_dn2):
        ref[...] = jnp.zeros_like(ref)
    at = 0
    spread(at, 3 * RANK * D // 128, 3 * RANK, a_qkv, a_qkv_t2)
    at = at + 3 * RANK * D // 128
    lines = D // 128
    mine = [t * (width // 128) + p for p in range(width // 128)]
    for j in range(3):
        stack(at + j * RANK * lines, lines, mine, b_qkv2, j * RANK, j * width)
    at = at + 3 * RANK * lines
    spread(at + t * (width * RANK // 128), width * RANK // 128, RANK, a_o, a_o_t2)
    at = at + D * RANK // 128
    stack(at, lines, list(range(lines)), b_o2, 0, 0)
    at = at + RANK * lines
    spread(at, 2 * RANK * D // 128, 2 * RANK, a_gu, a_gu_t2)
    at = at + 2 * RANK * D // 128
    wide_lines = FF // 128
    mine = [t * (units // 128) + p for p in range(units // 128)]
    for j in range(2):
        stack(at + j * RANK * wide_lines, wide_lines, mine, b_gu2, j * RANK, j * units)
    at = at + 2 * RANK * wide_lines
    spread(at + t * (units * RANK // 128), units * RANK // 128, RANK, a_dn, a_dn_t2)
    at = at + FF * RANK // 128
    stack(at, lines, list(range(lines)), b_dn2, 0, 0)


def forward_kernel(
    sizes,
    x_in,
    g_in,
    wq_in,
    wo_in,
    gu_in,
    dn_in,
    adapters_in,
    gains_in,
    table_in,
    turns,
    ids,
    parents,
    lengths,
    n1_all,
    k_all,
    v_all,
    wq_all,
    wo_all,
    n2_all,
    g_all,
    q_t,
    q_n,
    mixed,
    o_t,
    lse,
    resid,
    shared_half,
    dn2_half,
    da_gu,
    db_gu,
    da_dn,
    db_dn,
    gains,
    cosine,
    sinus,
    hot,
    reach_t,
    a_qkv,
    b_qkv2,
    a_qkv_t2,
    a_o,
    b_o2,
    a_o_t2,
    table_all,
    place_row,
    place_col,
    weight_col,
    marks,
    x_buf,
    wq,
    wo,
    gu,
    dn,
    g_own,
    n1_buf,
    k_buf,
    v_buf,
    v_t,
    peak,
    total,
    bias,
    part_out,
    part_in,
    n2_own,
    shared,
    dn2,
    shared_in,
    dn2_in,
    adapters_all,
    gains_all,
    chosen,
    flat,
    a_wide,
    a_gu,
    b_gu2,
    a_gu_t2,
    a_dn,
    a_dn_t2,
    b_dn2,
    fs_send,
    fs_recv,
    z_send,
    z_recv,
    core_send,
    core_recv,
    local_sems,
    chunk_sems,
    small_send,
    small_recv,
):
    fsdp, contexts, _ = sizes
    bits = fsdp.bit_length() - 1
    f, c, t = place_of()
    rows = x_in.shape[0]
    half = rows // 2
    heads = q_t.shape[0] // HEAD_DIM
    width = q_t.shape[0]
    units = dn_in.shape[1]
    own_n = wq_in.shape[0]
    sibling = (f, c, 1 - t)

    def peer(index):
        return (index, c, t)

    peers = [(lax.rem(f + k, fsdp), c, t) for k in range(1, fsdp)]
    stacked = [(f, lax.rem(c + k, contexts), t) for k in range(1, contexts)]
    greet(peers + stacked + [sibling])

    def half_rows(chunk, part):
        return pl.ds(pl.multiple_of(chunk * rows + part * half, 16), half)

    def up(chunk, source):
        return send(
            source,
            x_buf.at[half_rows(chunk, t)],
            z_send.at[chunk],
            z_recv.at[chunk],
            (f, c + 1, t),
        )

    def across(chunk):
        block = x_buf.at[half_rows(chunk, t)]
        return send(block, block, core_send.at[chunk], core_recv.at[chunk], sibling)

    @pl.when(c < contexts - 1)
    def _():
        up(c, x_in.at[half_rows(0, t)]).start()

    gathers = []
    for i, (own, buf) in enumerate(((wq_in, wq), (wo_in, wo), (gu_in, gu), (dn_in, dn))):
        gathers.append(
            Gather(bits, f, peer, own, buf, own_n, 0, own_n, fs_send.at[i], fs_recv.at[i])
        )
    g_gather = Gather(
        bits, f, peer, g_in, g_all, rows, t * half, half, fs_send.at[4], fs_recv.at[4]
    )
    n2_gather = Gather(
        bits, f, peer, n2_own, n2_all, rows, t * half, half, fs_send.at[5], fs_recv.at[5]
    )
    wq_gather, wo_gather, gu_gather, dn_gather = gathers
    small = []
    for k, other in enumerate(peers):
        for j, (source, target) in enumerate(
            ((adapters_in, adapters_all), (gains_in, gains_all), (table_in, table_all))
        ):
            copy = send(source, target.at[f], small_send.at[j, k], small_recv.at[j, k], other)
            copy.start()
            small.append(copy)
    wq_gather.start(0)
    locals_ = [pltpu.make_async_copy(x_in, x_buf.at[pl.ds(c * rows, rows)], local_sems.at[0])]
    for i, (own, buf) in enumerate(((wq_in, wq), (wo_in, wo), (gu_in, gu), (dn_in, dn))):
        locals_.append(
            pltpu.make_async_copy(own, buf.at[pl.ds(f * own_n, own_n)], local_sems.at[1 + i])
        )
    locals_.append(pltpu.make_async_copy(g_in, g_own, local_sems.at[5]))
    locals_.append(
        pltpu.make_async_copy(g_in, g_all.at[pl.ds(f * rows, rows)], local_sems.at[6])
    )
    for copy in locals_:
        copy.start()

    o_t[...] = jnp.zeros_like(o_t)
    peak[...] = jnp.full_like(peak, masked_score)
    total[...] = jnp.zeros_like(total)
    da_gu[...] = jnp.zeros_like(da_gu)
    db_gu[...] = jnp.zeros_like(db_gu)
    da_dn[...] = jnp.zeros_like(da_dn)
    db_dn[...] = jnp.zeros_like(db_dn)
    adapters_all[f] = adapters_in[...]
    gains_all[f] = gains_in[...]
    table_all[f] = table_in[...]
    tree_tables(parents, lengths, turns, c, rows, hot, reach_t, cosine, sinus)

    def receive(step):
        chunk = c - step

        @pl.when(step <= c)
        def _():
            up(chunk, x_buf.at[half_rows(chunk, t)]).wait_recv()

            @pl.when(c < contexts - 1)
            def _():
                up(chunk, x_buf.at[half_rows(chunk, t)]).start()

            across(chunk).start()

    def chunk_rows(chunk):
        return pl.ds(pl.multiple_of(chunk * rows, 16), rows)

    def out_copies(chunk):
        block = chunk_rows(chunk)
        return [
            pltpu.make_async_copy(n1_buf.at[block], n1_all.at[block], chunk_sems.at[0, chunk]),
            pltpu.make_async_copy(k_buf.at[block], k_all.at[block], chunk_sems.at[1, chunk]),
            pltpu.make_async_copy(v_buf.at[block], v_all.at[block], chunk_sems.at[2, chunk]),
        ]

    def project(chunk, own):
        block = chunk_rows(chunk)
        n1 = normed(x_buf[block, :].astype(jnp.float32), gain_one)
        n1_buf[block, :] = n1
        rank = two_parts(nn_dot(n1, a_qkv[...]))
        cos_rows = cosine[block, :]
        sin_rows = sinus[block, :]
        for p in range(width // 128):
            cols = slice(width + 128 * p, width + 128 * p + 128)
            key = nn_dot(n1, wq[:, cols]) + nn_dot(rank, b_qkv2[:, cols])
            k_buf[block, 128 * p : 128 * p + 128] = turn(key, cos_rows, sin_rows).astype(
                jnp.bfloat16
            )
            cols = slice(2 * width + 128 * p, 2 * width + 128 * p + 128)
            value = nn_dot(n1, wq[:, cols]) + nn_dot(rank, b_qkv2[:, cols])
            v_buf[block, 128 * p : 128 * p + 128] = value.astype(jnp.bfloat16)
            v_t[128 * p : 128 * p + 128, :] = value.T.astype(jnp.bfloat16)
            if own:
                cols = slice(128 * p, 128 * p + 128)
                query = nn_dot(n1, wq[:, cols]) + nn_dot(rank, b_qkv2[:, cols])
                query = turn(query, cos_rows, sin_rows) * 0.125
                q_n[:, cols] = query.astype(jnp.bfloat16)
                q_t[cols, :] = query.T.astype(jnp.bfloat16)
        for copy in out_copies(chunk):
            copy.start()

    def attend(chunk):
        block = chunk_rows(chunk)
        fill_bias(bias, hot[block, :], reach_t[...], chunk * rows, c * rows)

        def pair_step(p, carry):
            lanes = pl.ds(pl.multiple_of(p * 128, 128), 128)
            keys = k_buf[block, lanes]
            query = q_t[lanes, :]
            for odd in range(2):
                h = 2 * p + odd
                alone = jnp.where(
                    head_half(query.shape, 0, odd), query, jnp.zeros_like(query)
                )
                scores = nn_dot(keys, alone) + bias[...]
                before = peak[pl.ds(h, 1), :]
                now = jnp.maximum(before, jnp.max(scores, axis=0, keepdims=True))
                weights = jnp.exp(scores - now)
                shrink = jnp.exp(before - now)
                peak[pl.ds(h, 1), :] = now
                total[pl.ds(h, 1), :] = total[pl.ds(h, 1), :] * shrink + jnp.sum(
                    weights, axis=0, keepdims=True
                )
                head = pl.ds(pl.multiple_of(h * HEAD_DIM, HEAD_DIM), HEAD_DIM)
                o_t[head, :] = o_t[head, :] * shrink + nn_dot(
                    v_t[head, :], weights.astype(jnp.bfloat16)
                )
            return carry

        lax.fori_loop(0, heads // 2, pair_step, 0)

    def advance(gather, following):
        gather.wait(0)
        for stage in range(1, bits):
            gather.start(stage)
            if stage < bits - 1:
                gather.wait(stage)
        if following is not None:
            following.start(0)

    for copy in small:
        copy.wait_recv()
    choose(ids, adapters_all, chosen.at[t, c])
    spread = []
    for k, other in enumerate(stacked):
        block = chosen.at[t, c]
        copy = send(block, block, small_send.at[3, k], small_recv.at[3, k], other)
        copy.start()
        spread.append(copy)
    gains[...] = jnp.zeros_like(gains)
    for i in range(2):
        pieces = [
            gains_all[b, 0:1, i * own_n : (i + 1) * own_n].astype(jnp.float32)
            for b in range(fsdp)
        ]
        gains[i : i + 1, :] = jnp.concatenate(pieces, axis=1)
    gain_one = gains[0:1, :]
    gain_two = gains[1:2, :]
    advance(wq_gather, wo_gather)
    for copy in spread:
        copy.wait_recv()
    shared_copy = send(
        chosen.at[t], chosen.at[t], small_send.at[4, 0], small_recv.at[4, 0], sibling
    )
    shared_copy.start()
    route_tables(f, table_all, place_row, place_col, weight_col, marks)
    shared_copy.wait_recv()
    unpack_adapter(
        t,
        adapters_in.shape[0] // (ADAPTERS // fsdp),
        chosen,
        flat,
        a_wide,
        (a_qkv, b_qkv2, a_qkv_t2, a_o, b_o2, a_o_t2),
        (a_gu, b_gu2, a_gu_t2, a_dn, a_dn_t2, b_dn2),
    )
    receive(1)
    advance(wo_gather, gu_gather)
    wq_gather.wait(bits - 1)
    locals_[0].wait()
    locals_[1].wait()
    wq_out = pltpu.make_async_copy(wq, wq_all, local_sems.at[10])
    wq_out.start()
    project(c, True)
    attend(c)

    def between(step):
        if step == 1:
            advance(gu_gather, dn_gather)
        if step == 2:
            advance(dn_gather, g_gather)

    def later(step):
        chunk = c - step

        @pl.when(step <= c)
        def _():
            across(chunk).wait_recv()
            project(chunk, False)
            attend(chunk)

    for step in range(1, 3):
        receive(step + 1)
        between(step)
        later(step)

    def rest(step, carry):
        receive(step + 1)
        later(step)
        return carry

    lax.fori_loop(3, contexts, rest, 0)

    for h in range(heads):
        head = slice(h * HEAD_DIM, h * HEAD_DIM + HEAD_DIM)
        o_t[head, :] = o_t[head, :] / total[h : h + 1, :]
    lse[...] = peak[...] + jnp.log(total[...])
    for p in range(width // 128):
        mixed[:, 128 * p : 128 * p + 128] = o_t[128 * p : 128 * p + 128, :].T.astype(jnp.bfloat16)
    wo_gather.wait(bits - 1)
    locals_[2].wait()
    wo_out = pltpu.make_async_copy(wo, wo_all, local_sems.at[11])
    wo_out.start()

    def local_rows(part):
        return pl.ds(pl.multiple_of(part * half, 16), half)

    mine = local_rows(t)
    theirs = local_rows(1 - t)

    def branch(block):
        values = mixed[block, :]
        rank = two_parts(nn_dot(values, a_o[...]))
        return nt_dot(values, wo[...]) + nn_dot(rank, b_o2[...])

    part_out[...] = branch(theirs)
    number = contexts
    part_copy = send(
        part_out, part_in, core_send.at[number], core_recv.at[number], sibling
    )
    part_copy.start()
    own_part = branch(mine) + x_in_rows(x_buf, c, rows, t, half)
    part_copy.wait_recv()
    resid_half = own_part + part_in[...]
    resid[mine, :] = resid_half
    n2_own[mine, :] = normed(resid_half, gain_two)
    n2_gather.start(0)
    n2_copy = send(
        n2_own.at[mine], n2_own.at[mine], core_send.at[number + 1], core_recv.at[number + 1], sibling
    )
    n2_copy.start()
    resid_copy = send(
        resid.at[mine], resid.at[mine], core_send.at[number + 2], core_recv.at[number + 2], sibling
    )
    resid_copy.start()

    def forwards(gather, buf, first):
        copies = []
        for stage in range(bits):
            group = []
            for block in gather.arrived[stage]:
                index = first + len(copies)
                copies.append(
                    send(
                        buf.at[block],
                        buf.at[block],
                        core_send.at[index],
                        core_recv.at[index],
                        sibling,
                    )
                )
        return copies

    per_stage = [len(stage) for stage in g_gather.arrived]
    g_forward = forwards(g_gather, g_all, number + 5)
    n2_forward = forwards(n2_gather, n2_all, number + 5 + sum(per_stage))

    def pass_on(copies, stage):
        start = sum(per_stage[:stage])
        for copy in copies[start : start + per_stage[stage]]:
            copy.start()

    locals_[5].wait()
    gu_gather.wait(bits - 1)
    locals_[3].wait()
    dn_gather.wait(bits - 1)
    locals_[4].wait()

    def shared_tile(block):
        inputs = n2_own[block, :]
        grads = g_own[block, :]
        rank = nn_dot(inputs, a_gu[...])
        rank2 = two_parts(rank)
        gate = nn_dot(inputs, gu[:, :units]) + nn_dot(rank2, b_gu2[:, :units])
        up_pre = nn_dot(inputs, gu[:, units:]) + nn_dot(rank2, b_gu2[:, units:])
        sigmoid_gate = jax.nn.sigmoid(gate)
        silu = gate * sigmoid_gate
        hidden = (silu * up_pre).astype(jnp.bfloat16)
        down_rank = nn_dot(hidden, a_dn[...])
        shared[block, :] = nt_dot(hidden, dn[...]) + nn_dot(two_parts(down_rank), b_dn2[...])
        down_back = nt_dot(grads, b_dn2[0:128, :])
        grad_hidden = nn_dot(grads, dn[...]) + nn_dot(two_parts(down_back), a_dn_t2[...])
        grad_gate = (
            grad_hidden * up_pre * sigmoid_gate * (1.0 + gate * (1.0 - sigmoid_gate))
        ).astype(jnp.bfloat16)
        grad_up = (grad_hidden * silu).astype(jnp.bfloat16)
        rank_back = nt_dot(grad_gate, b_gu2[0:128, :units]) + nt_dot(
            grad_up, b_gu2[0:128, units:]
        )
        dn2[block, :] = (
            nt_dot(grad_gate, gu[:, :units])
            + nt_dot(grad_up, gu[:, units:])
            + nn_dot(two_parts(rank_back), a_gu_t2[...])
        )
        rank_low = rank.astype(jnp.bfloat16)
        da_gu[...] += tn_dot(rank_back.astype(jnp.bfloat16), inputs)[0 : 2 * RANK]
        db_gu[0:RANK, :] += 2.0 * tn_dot(rank_low, grad_gate)[0:RANK]
        db_gu[RANK:, :] += 2.0 * tn_dot(rank_low, grad_up)[RANK : 2 * RANK]
        da_dn[...] += tn_dot(down_back.astype(jnp.bfloat16), hidden)[0:RANK]
        db_dn[...] += 2.0 * tn_dot(down_rank.astype(jnp.bfloat16), grads)[0:RANK]

    n2_gather.wait(0)
    for stage in range(1, bits):
        n2_gather.start(stage)
        pass_on(n2_forward, stage - 1)
        if stage < bits - 1:
            n2_gather.wait(stage)
    n2_copy.wait_recv()
    shared_tile(theirs)
    pair_copies = [
        send(
            source.at[theirs], target, core_send.at[number + 3 + i], core_recv.at[number + 3 + i], sibling
        )
        for i, (source, target) in enumerate(((dn2, dn2_in), (shared, shared_in)))
    ]
    for copy in pair_copies:
        copy.start()
    g_gather.wait(0)
    for stage in range(1, bits):
        g_gather.start(stage)
        pass_on(g_forward, stage - 1)
        if stage < bits - 1:
            g_gather.wait(stage)
    n2_out = pltpu.make_async_copy(n2_own, n2_all.at[pl.ds(f * rows, rows)], local_sems.at[12])
    n2_out.start()
    shared_tile(mine)
    for copy in pair_copies:
        copy.wait()
    dn2_half[...] = dn2[mine, :] + dn2_in[...]
    shared_half[...] = shared[mine, :] + shared_in[...]
    n2_gather.wait(bits - 1)
    pass_on(n2_forward, bits - 1)
    g_gather.wait(bits - 1)
    pass_on(g_forward, bits - 1)
    for copy in n2_forward + g_forward:
        copy.wait()
    for copy in small + spread + [shared_copy]:
        copy.wait_send()
    resid_copy.wait()
    n2_copy.wait_send()
    part_copy.wait_send()
    for gather in gathers + [g_gather, n2_gather]:
        gather.finish()
    n2_out.wait()
    wq_out.wait()
    wo_out.wait()
    locals_[6].wait()

    @pl.when(c < contexts - 1)
    def _():
        up(c, x_in.at[half_rows(0, t)]).wait_send()

    def drain(step, carry):
        chunk = c - step

        @pl.when(c < contexts - 1)
        def _():
            up(chunk, x_buf.at[half_rows(chunk, t)]).wait_send()

        across(chunk).wait_send()
        return carry

    lax.fori_loop(1, c + 1, drain, 0)

    def drain_out(step, carry):
        for copy in out_copies(c - step):
            copy.wait()
        return carry

    lax.fori_loop(0, c + 1, drain_out, 0)


def x_in_rows(x_buf, chunk, rows, part, half):
    block = pl.ds(pl.multiple_of(chunk * rows + part * half, 16), half)
    return x_buf[block, :].astype(jnp.float32)


def forward_call(sizes, sharded, local):
    fsdp, contexts, _ = sizes
    x, g, wq, wo, gu, dn = sharded
    adapters, gains, table = local[:3]
    rows = x.shape[0]
    tree = rows * contexts
    width = wo.shape[1]
    units = dn.shape[1]
    bf, f32 = jnp.bfloat16, jnp.float32
    vmem = pl.BlockSpec(memory_space=pltpu.VMEM)
    hbm = pl.BlockSpec(memory_space=pl.ANY)
    smem = pl.BlockSpec(memory_space=pltpu.SMEM)
    slots = max(fsdp, contexts)
    total = fsdp * rows
    per_adapter = adapters.shape[0] // (ADAPTERS // fsdp)

    def shape(kind, *dims):
        return jax.ShapeDtypeStruct(dims, kind)

    moves = 2 * (fsdp - 1)
    hops = contexts + 5 + 2 * moves
    return pl.pallas_call(
        functools.partial(forward_kernel, sizes),
        in_specs=[hbm] * 6 + [vmem] * 4 + [smem] * 3,
        out_specs=[hbm] * 7 + [vmem] * 28,
        out_shape=[
            shape(bf, tree, D),
            shape(bf, tree, width),
            shape(bf, tree, width),
            shape(bf, D, 3 * width),
            shape(bf, D, width),
            shape(bf, fsdp * rows, D),
            shape(bf, fsdp * rows, D),
            shape(bf, width, rows),
            shape(bf, rows, width),
            shape(bf, rows, width),
            shape(f32, width, rows),
            shape(f32, 8, rows),
            shape(f32, rows, D),
            shape(f32, rows // 2, D),
            shape(f32, rows // 2, D),
            shape(f32, 2 * RANK, D),
            shape(f32, 2 * RANK, units),
            shape(f32, RANK, units),
            shape(f32, RANK, D),
            shape(f32, 8, D),
            shape(f32, tree, 128),
            shape(f32, tree, 128),
            shape(bf, tree, 128),
            shape(bf, 128, rows),
            shape(bf, D, 128),
            shape(bf, 256, 3 * width),
            shape(bf, 256, D),
            shape(bf, width, 128),
            shape(bf, 256, D),
            shape(bf, 256, width),
            shape(f32, fsdp, 8, rows),
            shape(f32, 8, total),
            shape(f32, total, 128),
            shape(bf, total, 128),
            shape(f32, 8, 128),
        ],
        scratch_shapes=[
            pltpu.VMEM((tree, D), bf),
            pltpu.VMEM((D, 3 * width), bf),
            pltpu.VMEM((D, width), bf),
            pltpu.VMEM((D, 2 * units), bf),
            pltpu.VMEM((D, units), bf),
            pltpu.VMEM((rows, D), bf),
            pltpu.VMEM((tree, D), bf),
            pltpu.VMEM((tree, width), bf),
            pltpu.VMEM((tree, width), bf),
            pltpu.VMEM((width, rows), bf),
            pltpu.VMEM((8, rows), f32),
            pltpu.VMEM((8, rows), f32),
            pltpu.VMEM((rows, rows), f32),
            pltpu.VMEM((rows // 2, D), f32),
            pltpu.VMEM((rows // 2, D), f32),
            pltpu.VMEM((rows, D), bf),
            pltpu.VMEM((rows, D), f32),
            pltpu.VMEM((rows, D), f32),
            pltpu.VMEM((rows // 2, D), f32),
            pltpu.VMEM((rows // 2, D), f32),
            pltpu.VMEM((fsdp,) + adapters.shape, bf),
            pltpu.VMEM((fsdp,) + gains.shape, bf),
            pltpu.VMEM((2, contexts, per_adapter, 128), bf),
            pltpu.VMEM((PARAMS // 128, 128), f32),
            pltpu.VMEM((max(D, units), 128), f32),
            pltpu.VMEM((D, 128), bf),
            pltpu.VMEM((256, 2 * units), bf),
            pltpu.VMEM((256, D), bf),
            pltpu.VMEM((units, 128), bf),
            pltpu.VMEM((256, units), bf),
            pltpu.VMEM((256, D), bf),
            pltpu.SemaphoreType.DMA((6, moves)),
            pltpu.SemaphoreType.DMA((6, moves)),
            pltpu.SemaphoreType.DMA((contexts,)),
            pltpu.SemaphoreType.DMA((contexts,)),
            pltpu.SemaphoreType.DMA((hops,)),
            pltpu.SemaphoreType.DMA((hops,)),
            pltpu.SemaphoreType.DMA((13,)),
            pltpu.SemaphoreType.DMA((3, contexts)),
            pltpu.SemaphoreType.DMA((5, slots)),
            pltpu.SemaphoreType.DMA((5, slots)),
        ],
        name="forward",
        compiler_params=pltpu.CompilerParams(
            collective_id=2, has_side_effects=True, vmem_limit_bytes=62 << 20
        ),
    )(*sharded, *local)


def flips(index, mask, bits):
    for bit in range(bits):
        if mask >> bit & 1:
            index = flip(index, bit)
    return index


class Scatter:
    def __init__(self, bits, me, device_of, work, inbox, count, send_sems, recv_sems):
        self.bits, self.work, self.inbox = bits, work, inbox
        self.copies = [[] for _ in range(bits)]
        self.adds = [[] for _ in range(bits)]
        number = 0
        for half, (offset, size) in enumerate(split_rows(count)):
            alive = list(range(1 << bits))
            slot = 0
            for stage in range(bits):
                bit = (stage + half) % bits
                for mask in alive:
                    if mask >> bit & 1:
                        source = Gather.rows(flips(me, mask, bits) * count + offset, size)
                        target = pl.ds(slot * count + offset, size)
                        kept = Gather.rows(flips(me, mask ^ (1 << bit), bits) * count + offset, size)
                        self.copies[stage].append(
                            send(
                                work.at[source],
                                inbox.at[target],
                                send_sems.at[number],
                                recv_sems.at[number],
                                device_of(flip(me, bit)),
                            )
                        )
                        self.adds[stage].append((kept, target, pl.ds(offset, size)))
                        number = number + 1
                        slot = slot + 1
                alive = [mask for mask in alive if not mask >> bit & 1]

    def start(self, stage):
        for copy in self.copies[stage]:
            copy.start()

    def add(self, stage):
        for copy in self.copies[stage]:
            copy.wait_recv()
        for kept, target, _ in self.adds[stage]:
            total = self.work[kept, :].astype(jnp.float32) + self.inbox[target, :].astype(
                jnp.float32
            )
            self.work[kept, :] = total.astype(jnp.bfloat16)

    def last(self, out, own):
        for copy in self.copies[self.bits - 1]:
            copy.wait_recv()
        for kept, target, rows in self.adds[self.bits - 1]:
            total = self.work[kept, :].astype(jnp.float32) + self.inbox[target, :].astype(
                jnp.float32
            )
            out[rows, :] = (total + own[rows, :]).astype(jnp.bfloat16)

    def finish(self):
        for stage in self.copies:
            for copy in stage:
                copy.wait_send()


def backward_kernel(
    sizes,
    moe_out,
    moe_back,
    n1_hbm,
    k_hbm,
    v_hbm,
    wq_hbm,
    wo_hbm,
    cos_hbm,
    sin_hbm,
    x_in,
    g_in,
    gains,
    hot,
    reach_t,
    resid,
    shared_half,
    dn2_half,
    q_t,
    q_n,
    mixed,
    o_t,
    lse,
    a_qkv,
    b_qkv2,
    a_qkv_t2,
    a_o,
    a_o_t2,
    b_o2,
    block_out,
    input_grad,
    da_qkv,
    db_qkv,
    da_o,
    db_o,
    cosine,
    sinus,
    n1_buf,
    k_buf,
    v_buf,
    wq,
    wo,
    work_back,
    pair_back,
    inbox_back,
    work_out,
    pair_out,
    inbox_out,
    total_half,
    total_full,
    ffn_half,
    ffn_full,
    dy,
    do_n,
    do_t,
    delta,
    k_t,
    dq_t,
    grad_kv,
    bias,
    part,
    part_out,
    part_in,
    z_in,
    z_out,
    dn1_full,
    fs_send,
    fs_recv,
    z_send,
    z_recv,
    core_send,
    core_recv,
    pair_send,
    pair_recv,
    local_sems,
    chunk_sems,
):
    fsdp, contexts, _ = sizes
    bits = fsdp.bit_length() - 1
    f, c, t = place_of()
    rows = x_in.shape[0]
    half = rows // 2
    width = q_t.shape[0]
    heads = width // HEAD_DIM
    sibling = (f, c, 1 - t)
    f32, bf = jnp.float32, jnp.bfloat16

    def peer(index):
        return (index, c, t)

    def local_rows(part_index):
        return pl.ds(pl.multiple_of(part_index * half, 16), half)

    mine = local_rows(t)
    theirs = local_rows(1 - t)

    def block_rows(block, part_index):
        return pl.ds(pl.multiple_of(block * rows + part_index * half, 16), half)

    def work_rows(block):
        return pl.ds(pl.multiple_of(block * half, 16), half)

    masks = list(range(fsdp - 1, -1, -1))

    def exchange(source, work, inbox, which):
        own, sent = [], []
        for mask in masks:
            block = flips(f, mask, bits)
            own.append(
                pltpu.make_async_copy(
                    source.at[block_rows(block, t)],
                    work.at[work_rows(block)],
                    local_sems.at[which, mask],
                )
            )
            sent.append(
                send(
                    source.at[block_rows(block, 1 - t)],
                    inbox.at[work_rows(block)],
                    core_send.at[which, mask],
                    core_recv.at[which, mask],
                    sibling,
                )
            )
        return own, sent

    back_own, back_sent = exchange(moe_back, work_back, pair_back, 0)
    out_own, out_sent = exchange(moe_out, work_out, pair_out, 1)
    for copy in back_own:
        copy.start()
    wo_copy = pltpu.make_async_copy(wo_hbm, wo, local_sems.at[2, 0])
    wq_copy = pltpu.make_async_copy(wq_hbm, wq, local_sems.at[2, 1])
    wo_copy.start()
    greet(
        [peer(flip(f, bit)) for bit in range(bits)]
        + [sibling, (f, lax.rem(c + 1, contexts), t), (f, lax.rem(c + contexts - 1, contexts), t)]
    )
    for copy in back_sent:
        copy.start()
    for copy in out_own:
        copy.start()
    wq_copy.start()

    def chunk_rows(chunk):
        return pl.ds(pl.multiple_of(chunk * rows, 16), rows)

    def loads(chunk):
        block = chunk_rows(chunk)
        return [
            pltpu.make_async_copy(k_hbm.at[block], k_buf.at[block], chunk_sems.at[1, chunk]),
            pltpu.make_async_copy(v_hbm.at[block], v_buf.at[block], chunk_sems.at[2, chunk]),
        ]

    def n1_load(chunk):
        return pltpu.make_async_copy(
            n1_hbm.at[chunk_rows(chunk)], n1_buf, chunk_sems.at[0, chunk]
        )

    def table_loads(chunk):
        block = chunk_rows(chunk)
        return [
            pltpu.make_async_copy(cos_hbm.at[block], cosine, chunk_sems.at[3, chunk]),
            pltpu.make_async_copy(sin_hbm.at[block], sinus, chunk_sems.at[4, chunk]),
        ]

    def start_loads(chunk, carry):
        for copy in loads(chunk):
            copy.start()
        return carry

    lax.fori_loop(0, c + 1, start_loads, 0)

    back = Scatter(
        bits, f, peer, work_back, inbox_back, half, fs_send.at[0], fs_recv.at[0]
    )
    out = Scatter(bits, f, peer, work_out, inbox_out, half, fs_send.at[1], fs_recv.at[1])

    def pair_sum(own, sent, work, inbox):
        for i, mask in enumerate(masks):
            block = work_rows(flips(f, mask, bits))
            own[i].wait()
            sent[i].wait_recv()
            work[block, :] = (
                work[block, :].astype(f32) + inbox[block, :].astype(f32)
            ).astype(bf)

    pair_sum(back_own, back_sent, work_back, pair_back)
    back.start(0)
    for copy in out_sent:
        copy.start()
    for stage in range(1, bits):
        back.add(stage - 1)
        back.start(stage)
    dq_t[...] = jnp.zeros_like(dq_t)
    da_qkv[...] = jnp.zeros_like(da_qkv)
    db_qkv[...] = jnp.zeros_like(db_qkv)
    pair_sum(out_own, out_sent, work_out, pair_out)
    back.last(total_half, dn2_half)
    out.start(0)
    total_full[mine, :] = total_half[...]
    full_copy = send(
        total_half, total_full.at[mine], core_send.at[2, 0], core_recv.at[2, 0], sibling
    )
    full_copy.start()
    gain_one = gains[0:1, :]
    gain_two = gains[1:2, :]
    wo_copy.wait()
    full_copy.wait_recv()

    def attn_tile(i, carry):
        block = local_rows(i)
        values = resid[block, :]
        gradient = g_in[block, :].astype(f32) + norm_back(
            values, rms_scale(values), gain_two, total_full[block, :].astype(f32)
        )
        dy[block, :] = gradient
        low_grad = gradient.astype(bf)
        rank_back = nt_dot(low_grad, b_o2[0:128, :])
        do_n[block, :] = (
            nn_dot(low_grad, wo[...]) + nn_dot(two_parts(rank_back), a_o_t2[...])
        ).astype(bf)
        values_o = mixed[block, :]
        rank = nn_dot(values_o, a_o[...])
        first = tn_dot(rank_back.astype(bf), values_o)[0:RANK]
        second = 2.0 * tn_dot(rank.astype(bf), low_grad)[0:RANK]

        @pl.when(i == 0)
        def _():
            da_o[...] = first
            db_o[...] = second

        @pl.when(i > 0)
        def _():
            da_o[...] += first
            db_o[...] += second

        return carry

    lax.fori_loop(0, 2, attn_tile, 0)
    for p in range(width // 128):
        lanes = slice(128 * p, 128 * p + 128)
        turned = do_n[:, lanes].astype(f32).T
        do_t[lanes, :] = turned.astype(bf)
        product = turned * o_t[lanes, :]
        for odd in range(2):
            delta[2 * p + odd : 2 * p + odd + 1, :] = jnp.sum(
                product[HEAD_DIM * odd : HEAD_DIM * odd + HEAD_DIM, :], axis=0, keepdims=True
            )
    wq_copy.wait()

    def attend_back(chunk):
        block = chunk_rows(chunk)
        n1_load(chunk).start()
        for copy in table_loads(chunk):
            copy.start()
        for copy in loads(chunk) + table_loads(chunk):
            copy.wait()
        fill_bias(bias, hot[block, :], reach_t[...], chunk * rows, c * rows)
        cos_rows = cosine[...]
        sin_rows = -sinus[...]
        for p in range(width // 128):
            lanes = slice(128 * p, 128 * p + 128)
            k_t[lanes, :] = k_buf[block, lanes].astype(f32).T.astype(bf)

        def pair_step(p, carry):
            lanes = pl.ds(pl.multiple_of(p * 128, 128), 128)
            keys = k_buf[block, lanes]
            values = v_buf[block, lanes]
            query_t = q_t[lanes, :]
            grad_t = do_t[lanes, :]
            query = q_n[:, lanes]
            grad = do_n[:, lanes]
            grad_keys = jnp.zeros((rows, 128), f32)
            grad_values = jnp.zeros((rows, 128), f32)
            for odd in range(2):
                h = 2 * p + odd
                upper = head_half(query_t.shape, 0, odd)
                side = head_half(query.shape, 1, odd)
                none_t = jnp.zeros_like(query_t)
                none = jnp.zeros_like(query)
                scores = nn_dot(keys, jnp.where(upper, query_t, none_t)) + bias[...]
                weights = jnp.exp(scores - lse[pl.ds(h, 1), :])
                grad_weights = nn_dot(values, jnp.where(upper, grad_t, none_t))
                grad_scores = (weights * (grad_weights - delta[pl.ds(h, 1), :])).astype(bf)
                grad_values += nn_dot(weights.astype(bf), jnp.where(side, grad, none))
                grad_keys += nn_dot(grad_scores, jnp.where(side, query, none))
                head = pl.ds(pl.multiple_of(h * HEAD_DIM, HEAD_DIM), HEAD_DIM)
                dq_t[head, :] += nn_dot(k_t[head, :], grad_scores)
            grad_kv[:, lanes] = turn(grad_keys, cos_rows, sin_rows).astype(bf)
            grad_kv[:, pl.ds(pl.multiple_of(width + p * 128, 128), 128)] = grad_values.astype(bf)
            return carry

        lax.fori_loop(0, heads // 2, pair_step, 0)

    def project_back(chunk, own):
        block = chunk_rows(chunk)
        grads = grad_kv[...]
        result = nt_dot(grads, wq[:, width:])
        rank_back = nt_dot(grads, b_qkv2[0:128, width:])
        n1_load(chunk).wait()
        n1 = n1_buf[...]
        rank = nn_dot(n1, a_qkv[...]).astype(bf)
        both = 2.0 * tn_dot(rank, grads)
        db_qkv[RANK : 2 * RANK, :] += both[RANK : 2 * RANK, :width]
        db_qkv[2 * RANK :, :] += both[2 * RANK : 3 * RANK, width:]
        if own:
            pieces = []
            for p in range(width // 128):
                lanes = slice(128 * p, 128 * p + 128)
                grad_query = (dq_t[lanes, :] * 0.125).T
                pieces.append(
                    turn(grad_query, cosine[...], -sinus[...]).astype(bf)
                )
            grad_query = jnp.concatenate(pieces, axis=1)
            result += nt_dot(grad_query, wq[:, :width])
            rank_back += nt_dot(grad_query, b_qkv2[0:128, :width])
            db_qkv[0:RANK, :] += 2.0 * tn_dot(rank, grad_query)[0:RANK, :]
        result += nn_dot(two_parts(rank_back), a_qkv_t2[...])
        da_qkv[...] += tn_dot(rank_back.astype(bf), n1)[0 : 3 * RANK]
        part[...] = result.astype(bf)
        part_out[work_rows(chunk), :] = part[theirs, :]
        z_out[work_rows(chunk), :] = part[mine, :]

    def pair_copy(chunk):
        return send(
            part_out.at[work_rows(chunk)],
            part_in.at[work_rows(chunk)],
            pair_send.at[chunk],
            pair_recv.at[chunk],
            sibling,
        )

    def down(chunk):
        block = work_rows(chunk)
        return send(
            z_out.at[block], z_in.at[block], z_send.at[chunk], z_recv.at[chunk], (f, c - 1, t)
        )

    def chain(chunk):
        block = work_rows(chunk)
        pair_copy(chunk).wait_recv()
        summed = z_out[block, :].astype(f32) + part_in[block, :].astype(f32)
        z_out[block, :] = summed.astype(bf)

        @pl.when(c < contexts - 1)
        def _():
            down(chunk).wait_recv()
            z_out[block, :] = (summed + z_in[block, :].astype(f32)).astype(bf)

    def pass_down(chunk):
        chain(chunk)
        down(chunk).start()

    def step(chunk, carry):
        attend_back(chunk)
        project_back(chunk, False)
        pair_copy(chunk).start()

        @pl.when(c == contexts - 1)
        def _():
            pass_down(chunk)

        @pl.when((c < contexts - 1) & (chunk >= 1))
        def _():
            pass_down(chunk - 1)

        return carry

    lax.fori_loop(0, c, step, 0)
    attend_back(c)
    project_back(c, True)
    pair_copy(c).start()

    @pl.when((c < contexts - 1) & (c >= 1))
    def _():
        pass_down(c - 1)

    for stage in range(1, bits):
        out.add(stage - 1)
        out.start(stage)
    out.last(ffn_half, shared_half)
    ffn_full[mine, :] = ffn_half[...]
    ffn_copy = send(ffn_half, ffn_full.at[mine], core_send.at[2, 1], core_recv.at[2, 1], sibling)
    ffn_copy.start()
    chain(c)
    dn1_full[mine, :] = z_out[work_rows(c), :]
    dn1_copy = send(
        z_out.at[work_rows(c)],
        dn1_full.at[mine],
        core_send.at[2, 2],
        core_recv.at[2, 2],
        sibling,
    )
    dn1_copy.start()
    ffn_copy.wait_recv()
    block_out[...] = resid[...] + ffn_full[...].astype(f32)
    dn1_copy.wait_recv()

    def final_tile(i, carry):
        block = local_rows(i)
        values = x_in[block, :].astype(f32)
        input_grad[block, :] = dy[block, :] + norm_back(
            values, rms_scale(values), gain_one, dn1_full[block, :].astype(f32)
        )
        return carry

    lax.fori_loop(0, 2, final_tile, 0)
    for copy in back_sent + out_sent + [full_copy, ffn_copy, dn1_copy]:
        copy.wait_send()
    back.finish()
    out.finish()

    def drain(chunk, carry):
        pair_copy(chunk).wait_send()

        @pl.when(chunk < c)
        def _():
            down(chunk).wait_send()

        return carry

    lax.fori_loop(0, c + 1, drain, 0)


def backward_call(sizes, remote, local):
    fsdp, contexts, _ = sizes
    rows = local[0].shape[0]
    half = rows // 2
    tree = rows * contexts
    width = remote[6].shape[1]
    bf, f32 = jnp.bfloat16, jnp.float32
    vmem = pl.BlockSpec(memory_space=pltpu.VMEM)
    hbm = pl.BlockSpec(memory_space=pl.ANY)

    def shape(kind, *dims):
        return jax.ShapeDtypeStruct(dims, kind)

    moves = 2 * (fsdp - 1)
    slots = max(fsdp, 4)
    dma = pltpu.SemaphoreType.DMA
    return pl.pallas_call(
        functools.partial(backward_kernel, sizes),
        in_specs=[hbm] * len(remote) + [vmem] * len(local),
        out_specs=[vmem] * 6,
        out_shape=[
            shape(f32, rows, D),
            shape(f32, rows, D),
            shape(f32, 3 * RANK, D),
            shape(f32, 3 * RANK, width),
            shape(f32, RANK, width),
            shape(f32, RANK, D),
        ],
        scratch_shapes=[
            pltpu.VMEM((rows, 128), f32),
            pltpu.VMEM((rows, 128), f32),
            pltpu.VMEM((rows, D), bf),
            pltpu.VMEM((tree, width), bf),
            pltpu.VMEM((tree, width), bf),
            pltpu.VMEM((D, 3 * width), bf),
            pltpu.VMEM((D, width), bf),
            pltpu.VMEM((fsdp * half, D), bf),
            pltpu.VMEM((fsdp * half, D), bf),
            pltpu.VMEM(((fsdp - 1) * half, D), bf),
            pltpu.VMEM((fsdp * half, D), bf),
            pltpu.VMEM((fsdp * half, D), bf),
            pltpu.VMEM(((fsdp - 1) * half, D), bf),
            pltpu.VMEM((half, D), bf),
            pltpu.VMEM((rows, D), bf),
            pltpu.VMEM((half, D), bf),
            pltpu.VMEM((rows, D), bf),
            pltpu.VMEM((rows, D), f32),
            pltpu.VMEM((rows, width), bf),
            pltpu.VMEM((width, rows), bf),
            pltpu.VMEM((8, rows), f32),
            pltpu.VMEM((width, rows), bf),
            pltpu.VMEM((width, rows), f32),
            pltpu.VMEM((rows, 2 * width), bf),
            pltpu.VMEM((rows, rows), f32),
            pltpu.VMEM((rows, D), bf),
            pltpu.VMEM((contexts * half, D), bf),
            pltpu.VMEM((contexts * half, D), bf),
            pltpu.VMEM((contexts * half, D), bf),
            pltpu.VMEM((contexts * half, D), bf),
            pltpu.VMEM((rows, D), bf),
            dma((2, moves)),
            dma((2, moves)),
            dma((contexts,)),
            dma((contexts,)),
            dma((3, slots)),
            dma((3, slots)),
            dma((contexts,)),
            dma((contexts,)),
            dma((3, slots)),
            dma((5, contexts)),
        ],
        name="backward",
        compiler_params=pltpu.CompilerParams(
            collective_id=3, has_side_effects=True, vmem_limit_bytes=62 << 20
        ),
    )(*remote, *local)


def reduce_kernel(
    sizes, packed, table_all, out, inbox, z_out, z_in, total, f_in, send_sems, recv_sems
):
    fsdp, contexts, _ = sizes
    f, c, t = place_of()
    f32, bf = jnp.float32, jnp.bfloat16
    peers = [(lax.rem(f + k, fsdp), c, t) for k in range(1, fsdp)]
    stacked = [(f, lax.rem(c + k, contexts), t) for k in range(1, contexts)]
    sibling = (f, c, 1 - t)
    greet(peers + stacked + [sibling])
    order = [lax.rem(c + k, contexts) for k in range(1, contexts)] + [c]
    pair = []
    for k, block in enumerate(order):
        copy = send(
            packed.at[block, 1 - t], inbox.at[block], send_sems.at[0, k], recv_sems.at[0, k], sibling
        )
        copy.start()
        pair.append(copy)
    across = []
    for k, other in enumerate(stacked):
        pair[k].wait_recv()
        z_out[k] = (packed[order[k], t] + inbox[order[k]]).astype(bf)
        copy = send(z_out.at[k], z_in.at[k], send_sems.at[1, k], recv_sems.at[1, k], other)
        copy.start()
        across.append(copy)
    pair[-1].wait_recv()
    result = packed[c, t] + inbox[c]
    for k, copy in enumerate(across):
        copy.wait_recv()
        result = result + z_in[k].astype(f32)
    total[...] = result.astype(bf)
    ends = []
    for k, peer in enumerate(peers):
        copy = send(total, f_in.at[k], send_sems.at[2, k], recv_sems.at[2, k], peer)
        copy.start()
        ends.append(copy)
    own = ADAPTERS // fsdp
    wanted = [(f * own + a).astype(f32) for a in range(own)]
    sums = [jnp.where(table_all[f, 4:5, 0:1] == w, total[...].astype(f32), 0.0) for w in wanted]
    for k, copy in enumerate(ends):
        copy.wait_recv()
        tree = table_all[lax.rem(f - k - 1 + fsdp, fsdp), 4:5, 0:1]
        block = f_in[k].astype(f32)
        sums = [s + jnp.where(tree == w, block, 0.0) for s, w in zip(sums, wanted)]
    for a in range(own):
        out[a] = sums[a]
    for copy in pair + across + ends:
        copy.wait_send()


def reduce_call(sizes, packed, table_all):
    fsdp, contexts, _ = sizes
    block = packed.shape[2:]
    vmem = pl.BlockSpec(memory_space=pltpu.VMEM)
    bf, f32 = jnp.bfloat16, jnp.float32
    slots = max(fsdp, contexts)
    return pl.pallas_call(
        functools.partial(reduce_kernel, sizes),
        in_specs=[vmem, vmem],
        out_specs=vmem,
        out_shape=jax.ShapeDtypeStruct((ADAPTERS // fsdp,) + block, f32),
        scratch_shapes=[
            pltpu.VMEM((contexts,) + block, f32),
            pltpu.VMEM((contexts - 1,) + block, bf),
            pltpu.VMEM((contexts - 1,) + block, bf),
            pltpu.VMEM(block, bf),
            pltpu.VMEM((fsdp - 1,) + block, bf),
            pltpu.SemaphoreType.DMA((3, slots)),
            pltpu.SemaphoreType.DMA((3, slots)),
        ],
        name="adapter_sums",
        compiler_params=pltpu.CompilerParams(
            collective_id=4, has_side_effects=True, vmem_limit_bytes=60 << 20
        ),
    )(packed, table_all)


def shards(
    tokens,
    attn_gain,
    w_qkv,
    w_out,
    ffn_gain,
    w_gu,
    w_dn,
    w_egu,
    w_edn,
    adapters,
    adapter_ids,
    parents,
    seg_lengths,
    routes,
    route_weights,
    cotangent,
):
    tree_count, row_count = tokens.shape[:2]
    contexts = lax.axis_size("context")
    tensors = lax.axis_size("tensor")
    fsdp_size = lax.axis_size("fsdp")
    sizes = (fsdp_size, contexts, tensors)
    local_width = w_qkv.shape[2]
    local_ff = w_dn.shape[0]
    part_index = lax.axis_index("tensor")
    width_start = part_index * local_width
    ff_start = part_index * local_ff
    own_adapters = adapters.shape[0]
    own_width = D // fsdp_size
    gains = jnp.broadcast_to(jnp.concatenate([attn_gain, ffn_gain])[None], (16, 2 * own_width))
    route_table = jnp.concatenate(
        [
            routes[0].astype(jnp.float32).T,
            route_weights[0].astype(jnp.float32).T,
            jnp.broadcast_to(adapter_ids.astype(jnp.float32)[:, None], (1, row_count)),
            jnp.zeros((3, row_count), jnp.float32),
        ]
    )
    lines = adapters.shape[1] // 128
    padded = (lines + 15) // 16 * 16
    adapter_rows = jnp.pad(
        adapters.reshape(own_adapters, lines, 128), ((0, 0), (0, padded - lines), (0, 0))
    ).reshape(own_adapters * padded, 128)
    half_dim = HEAD_DIM // 2
    frequency = rope_base ** (-(jnp.arange(half_dim, dtype=jnp.float32) * 2.0) / HEAD_DIM)
    signs = jnp.concatenate([-jnp.ones((half_dim,)), jnp.ones((half_dim,))])
    turns = jnp.concatenate(
        [jnp.tile(frequency, 4)[None], jnp.tile(signs, 2)[None], jnp.zeros((6, 128))]
    ).astype(jnp.float32)
    sharded = (
        tokens[0],
        cotangent[0],
        w_qkv.reshape(own_width, 3 * local_width),
        w_out.T,
        w_gu.reshape(own_width, 2 * local_ff),
        w_dn.T,
    )
    (
        n1_all,
        k_all,
        v_all,
        wq_all,
        wo_all,
        normed_all,
        cotangent_all,
        q_t,
        q_n,
        mixed_own,
        o_t,
        lse,
        resid,
        shared_half,
        dn2_half,
        da_gu_t,
        db_gu_own,
        da_dn_t,
        db_dn_own,
        gains_full,
        cosine,
        sinus,
        hot,
        reach_t,
        a_qkv,
        b_qkv2,
        a_qkv_t2,
        a_o,
        b_o2,
        a_o_t2,
        table_all,
        place_row,
        place_col,
        weight_col,
        marks,
    ) = forward_call(
        sizes,
        sharded,
        (adapter_rows, gains, route_table, turns, adapter_ids, parents, seg_lengths),
    )
    own_experts = EXPERTS // fsdp_size
    starts = marks[:own_experts].astype(jnp.int32)
    moe_all, moe_back_all = moe_call(
        starts,
        place_row,
        place_col,
        weight_col,
        normed_all,
        cotangent_all,
        w_egu.transpose(0, 2, 1, 3),
        w_edn,
    )
    remote = (moe_all, moe_back_all, n1_all, k_all, v_all, wq_all, wo_all, cosine, sinus)
    block_out, input_grad, da_qkv_t, db_qkv_own, da_o_t, db_o_own = backward_call(
        sizes,
        remote,
        (tokens[0], cotangent[0], gains_full, hot, reach_t)
        + (resid, shared_half, dn2_half, q_t, q_n, mixed_own, o_t, lse)
        + (a_qkv, b_qkv2, a_qkv_t2, a_o, a_o_t2, b_o2),
    )
    block_out = block_out[None]
    input_grad = input_grad[None]
    grad_a_qkv = da_qkv_t.T[None]
    grad_b_qkv = lax.dynamic_update_slice_in_dim(
        jnp.zeros((tree_count, 3, RANK, D), jnp.float32),
        db_qkv_own.reshape(1, 3, RANK, local_width),
        width_start,
        3,
    )
    grad_a_out = lax.dynamic_update_slice_in_dim(
        jnp.zeros((tree_count, D, RANK), jnp.float32), da_o_t.T[None], width_start, 1
    )
    output_adapter_up_gradient = db_o_own[None]
    grad_a_gu = da_gu_t.T[None]
    grad_b_gu = lax.dynamic_update_slice_in_dim(
        jnp.zeros((tree_count, 2, RANK, FF), jnp.float32),
        db_gu_own.reshape(1, 2, RANK, local_ff),
        ff_start,
        3,
    )
    grad_a_dn = lax.dynamic_update_slice_in_dim(
        jnp.zeros((tree_count, FF, RANK), jnp.float32), da_dn_t.T[None], ff_start, 1
    )
    down_adapter_up_gradient = db_dn_own[None]
    grad_pieces = [
        grad_a_qkv,
        grad_b_qkv,
        grad_a_out,
        output_adapter_up_gradient,
        grad_a_gu,
        grad_b_gu,
        grad_a_dn,
        down_adapter_up_gradient,
    ]
    packed = jnp.concatenate([piece.reshape(tree_count, -1) for piece in grad_pieces], axis=1)
    adapter_grads = reduce_call(
        sizes, packed[0].reshape(contexts, tensors, RANK, -1), table_all
    ).reshape(own_adapters, -1)
    return (block_out, input_grad, adapter_grads)


def solution(mesh):
    return jax.shard_map(
        shards,
        mesh=mesh,
        in_specs=(
            P("fsdp", "context", None),
            P("fsdp"),
            P("fsdp", None, "tensor"),
            P("tensor", "fsdp"),
            P("fsdp"),
            P("fsdp", None, "tensor"),
            P("tensor", "fsdp"),
            P("fsdp", None, None, "tensor"),
            P("fsdp", "tensor", None),
            P("fsdp", ("context", "tensor")),
            P("fsdp"),
            P("fsdp", None),
            P("fsdp", None),
            P("fsdp", "context", None),
            P("fsdp", "context", None),
            P("fsdp", "context", None),
        ),
        out_specs=(
            P("fsdp", "context", None),
            P("fsdp", "context", None),
            P("fsdp", ("context", "tensor")),
        ),
        check_vma=False,
    )
```

```python
import jax
import jax.numpy as jnp
import functools
import math

from jax import lax
from jax.experimental import pallas as pl
from jax.experimental.pallas import tpu as pltpu
from jax.sharding import PartitionSpec as P

D = 768
HEADS = 12
HEAD_DIM = 64
FF = 2048
EXPERTS = 8
TOPK = 2
RANK = 16
ADAPTERS = 8
PARAMS = 233472


epsilon = 1e-06
adapter_scale = 2.0
rope_base = 10000.0
masked_score = -1e30
highest_precision = lax.Precision.HIGHEST


def rms_scale(values):
    return lax.rsqrt(jnp.mean(values * values, axis=-1, keepdims=True) + epsilon)


def norm_back(values, scaling, gain_values, gradient):
    weighted = gradient * gain_values
    inner_mean = jnp.mean(values * weighted, axis=-1, keepdims=True)
    return scaling * weighted - values * (scaling * scaling * scaling) * inner_mean


SLOT_TILE = 512
TOKEN_TILE = 256
SLOT_WINDOW = 128


def nt_dot(left, right):
    return lax.dot_general(left, right, (((1,), (1,)), ((), ())), preferred_element_type=jnp.float32)


def tn_dot(left, right):
    return lax.dot_general(left, right, (((0,), (0,)), ((), ())), preferred_element_type=jnp.float32)


def nn_dot(left, right):
    return jnp.dot(left, right, preferred_element_type=jnp.float32)


def moe_kernel(
    starts,
    place_row,
    place_hbm,
    weight_hbm,
    rows_hbm,
    grads_hbm,
    egu_hbm,
    edn_hbm,
    out_hbm,
    back_hbm,
    place_col,
    weight_col,
    rows_ref,
    grads_ref,
    egu_ref,
    edn_ref,
    out_ref,
    back_ref,
    taken,
    taken_grad,
    taken_weight,
    sems,
    block_sems,
):
    f32, bf = jnp.float32, jnp.bfloat16
    experts = egu_hbm.shape[0]
    blocks = rows_ref.shape[0] // TOKEN_TILE

    def block_rows(b):
        return pl.ds(pl.multiple_of(b * TOKEN_TILE, TOKEN_TILE), TOKEN_TILE)

    def loads(b):
        block = block_rows(b)
        return [
            pltpu.make_async_copy(source.at[block], target.at[block], block_sems.at[i, b])
            for i, (source, target) in enumerate(
                ((rows_hbm, rows_ref), (grads_hbm, grads_ref), (weight_hbm, weight_col))
            )
        ]

    def stores(b):
        block = block_rows(b)
        return [
            pltpu.make_async_copy(source.at[block], target.at[block], block_sems.at[3 + i, b])
            for i, (source, target) in enumerate(((out_ref, out_hbm), (back_ref, back_hbm)))
        ]

    def weights(e):
        return [
            pltpu.make_async_copy(egu_hbm.at[e], egu_ref.at[e], sems.at[0, e]),
            pltpu.make_async_copy(edn_hbm.at[e], edn_ref.at[e], sems.at[1, e]),
        ]

    def each(count, copies, action):
        def step(i, carry):
            for copy in copies(i):
                getattr(copy, action)()
            return carry

        lax.fori_loop(0, count, step, 0)

    each(blocks, loads, "start")
    each(experts, weights, "start")
    place_copy = pltpu.make_async_copy(place_hbm, place_col, sems.at[2, 0])
    place_copy.start()
    taken[...] = jnp.zeros_like(taken)
    taken_grad[...] = jnp.zeros_like(taken_grad)
    taken_weight[...] = jnp.zeros_like(taken_weight)
    slot_rows = lax.broadcasted_iota(jnp.int32, (SLOT_WINDOW, TOKEN_TILE), 0).astype(f32)
    slot_cols = lax.broadcasted_iota(jnp.int32, (TOKEN_TILE, SLOT_WINDOW), 1).astype(f32)

    def windows(e, b):
        begin = starts[e, b] // 16 * 16
        return begin, (starts[e, b + 1] - begin + SLOT_WINDOW - 1) // SLOT_WINDOW

    def window_rows(begin, i):
        return pl.ds(pl.multiple_of(begin + i * SLOT_WINDOW, 16), SLOT_WINDOW)

    def fetch(b, carry):
        block = block_rows(b)
        for copy in loads(b):
            copy.wait()

        def take(which):
            picks = []
            for e, first in which:
                hit = place_row[e : e + 1, block] == slot_rows + first.astype(f32)
                picks.append(jnp.where(hit, 1.0, 0.0).astype(bf))
            pick = picks[0] if len(picks) == 1 else jnp.concatenate(picks, axis=0)
            for source, target in (
                (rows_ref, taken),
                (grads_ref, taken_grad),
                (weight_col, taken_weight),
            ):
                got = nn_dot(pick, source[block, :]).astype(bf)
                for i, (e, first) in enumerate(which):
                    slots = window_rows(first, 0)
                    target[e, slots, :] += got[i * SLOT_WINDOW : (i + 1) * SLOT_WINDOW, :]

        spans = [windows(e, b) for e in range(experts)]
        take([(e, spans[e][0]) for e in range(experts)])
        for e in range(experts):

            def more(i, c, e=e):
                take([(e, spans[e][0] + i * SLOT_WINDOW)])
                return c

            lax.fori_loop(1, spans[e][1], more, 0)
        return carry

    lax.fori_loop(0, blocks, fetch, 0)

    def tile(e, start, size):
        slots = pl.ds(pl.multiple_of(start, 128), size)
        inputs = taken[e, slots, :]
        gate_pre = nn_dot(inputs, egu_ref[e, 0])
        up_pre = nn_dot(inputs, egu_ref[e, 1])
        sigmoid_gate = jax.nn.sigmoid(gate_pre)
        silu = gate_pre * sigmoid_gate
        active = (silu * up_pre).astype(bf)
        taken[e, slots, :] = nn_dot(active, edn_ref[e]).astype(bf)
        grad_active = nt_dot(taken_grad[e, slots, :], edn_ref[e])
        lane = lax.broadcasted_iota(jnp.int32, (size, 128), 1)
        scale = jnp.sum(
            jnp.where(lane == e, taken_weight[e, slots, :].astype(f32), 0.0), axis=1, keepdims=True
        )
        grad_active = grad_active * scale
        grad_gate = (
            grad_active * up_pre * sigmoid_gate * (1.0 + gate_pre * (1.0 - sigmoid_gate))
        ).astype(bf)
        grad_up = (grad_active * silu).astype(bf)
        taken_grad[e, slots, :] = (
            nt_dot(grad_gate, egu_ref[e, 0]) + nt_dot(grad_up, egu_ref[e, 1])
        ).astype(bf)

    def expert_step(e, carry):
        for copy in weights(e):
            copy.wait()
        count = starts[e, blocks]
        whole = count // SLOT_TILE
        rest = count - whole * SLOT_TILE

        def step(i, c):
            tile(e, i * SLOT_TILE, SLOT_TILE)
            return c

        lax.fori_loop(0, whole + jnp.where(rest > SLOT_TILE - 128, 1, 0), step, 0)
        for size in range(128, SLOT_TILE, 128):

            @pl.when((rest > size - 128) & (rest <= size))
            def _(size=size):
                tile(e, whole * SLOT_TILE, size)

        return carry

    lax.fori_loop(0, experts, expert_step, 0)
    place_copy.wait()

    def give(b, carry):
        block = block_rows(b)

        def hand(which):
            plain, scaled, values, values_grad = [], [], [], []
            for e, first in which:
                hit = place_col[block, e : e + 1] == slot_cols + first.astype(f32)
                plain.append(jnp.where(hit, 1.0, 0.0).astype(bf))
                weight = weight_col[block, e : e + 1].astype(f32)
                scaled.append(jnp.where(hit, weight, 0.0).astype(bf))
                values.append(taken[e, window_rows(first, 0), :])
                values_grad.append(taken_grad[e, window_rows(first, 0), :])

            def join(pieces, axis):
                return pieces[0] if len(pieces) == 1 else jnp.concatenate(pieces, axis=axis)

            return (
                nn_dot(join(scaled, 1), join(values, 0)),
                nn_dot(join(plain, 1), join(values_grad, 0)),
            )

        spans = [windows(e, b) for e in range(experts)]
        first, second = hand([(e, spans[e][0]) for e in range(experts)])
        out_ref[block, :] = first.astype(bf)
        back_ref[block, :] = second.astype(bf)
        for e in range(experts):

            def more(i, c, e=e):
                first, second = hand([(e, spans[e][0] + i * SLOT_WINDOW)])
                out_ref[block, :] = (out_ref[block, :].astype(f32) + first).astype(bf)
                back_ref[block, :] = (back_ref[block, :].astype(f32) + second).astype(bf)
                return c

            lax.fori_loop(1, spans[e][1], more, 0)
        for copy in stores(b):
            copy.start()
        return carry

    lax.fori_loop(0, blocks, give, 0)
    each(blocks, stores, "wait")


def moe_call(starts, place_row, place_col, weight_col, rows, grads, egu, edn):
    total, width = rows.shape
    experts = egu.shape[0]
    slots = total // 2 + SLOT_TILE
    blocks = total // TOKEN_TILE
    bf, f32 = jnp.bfloat16, jnp.float32
    vmem = pl.BlockSpec(memory_space=pltpu.VMEM)
    hbm = pl.BlockSpec(memory_space=pl.ANY)
    shape = jax.ShapeDtypeStruct((total, width), bf)
    return pl.pallas_call(
        moe_kernel,
        grid_spec=pltpu.PrefetchScalarGridSpec(
            num_scalar_prefetch=1,
            grid=(),
            in_specs=[vmem] + [hbm] * 6,
            out_specs=[hbm, hbm],
            scratch_shapes=[
                pltpu.VMEM((total, 128), f32),
                pltpu.VMEM((total, 128), bf),
                pltpu.VMEM((total, width), bf),
                pltpu.VMEM((total, width), bf),
                pltpu.VMEM(egu.shape, bf),
                pltpu.VMEM(edn.shape, bf),
                pltpu.VMEM((total, width), bf),
                pltpu.VMEM((total, width), bf),
                pltpu.VMEM((experts, slots, width), bf),
                pltpu.VMEM((experts, slots, width), bf),
                pltpu.VMEM((experts, slots, 128), bf),
                pltpu.SemaphoreType.DMA((3, experts)),
                pltpu.SemaphoreType.DMA((5, blocks)),
            ],
        ),
        out_shape=[shape, shape],
        name="experts",
        compiler_params=pltpu.CompilerParams(vmem_limit_bytes=62 << 20),
    )(starts, place_row, place_col, weight_col, rows, grads, egu, edn)


MESH = pl.DeviceIdType.MESH


def place_of():
    return lax.axis_index("fsdp"), lax.axis_index("context"), lax.axis_index("tensor")


def greet(devices):
    barrier = pltpu.get_barrier_semaphore()
    for device in devices:
        pl.semaphore_signal(barrier, inc=1, device_id=device, device_id_type=MESH)
    pl.semaphore_wait(barrier, len(devices))


def send(source, target, send_sem, recv_sem, device):
    return pltpu.make_async_remote_copy(
        src_ref=source,
        dst_ref=target,
        send_sem=send_sem,
        recv_sem=recv_sem,
        device_id=device,
        device_id_type=MESH,
    )


def flip(index, bit):
    return index + (1 - 2 * lax.rem(index // (1 << bit), 2)) * (1 << bit)


def split_rows(count):
    first = (count // 2 + 15) // 16 * 16
    return ((0, first), (first, count - first))


class Gather:
    def __init__(self, bits, me, device_of, own, buf, stride, base, count, send_sems, recv_sems):
        self.stages = [[] for _ in range(bits)]
        self.arrived = [[] for _ in range(bits)]
        self.passed = [[] for _ in range(bits)]
        number = 0
        for half, (offset, size) in enumerate(split_rows(count)):
            held = [me]
            for stage in range(bits):
                bit = (stage + half) % bits
                for block in held:
                    rows = self.rows(block * stride + base + offset, size)
                    source = own.at[self.rows(base + offset, size)] if block is me else buf.at[rows]
                    self.passed[stage].append(block is not me)
                    self.stages[stage].append(
                        send(
                            source,
                            buf.at[rows],
                            send_sems.at[number],
                            recv_sems.at[number],
                            device_of(flip(me, bit)),
                        )
                    )
                    self.arrived[stage].append(
                        self.rows(flip(block, bit) * stride + base + offset, size)
                    )
                    number = number + 1
                held = held + [flip(block, bit) for block in held]

    @staticmethod
    def rows(start, size):
        return pl.ds(pl.multiple_of(start, 16), size)

    def start(self, stage):
        if stage == 0:
            for copies, passed in zip(self.stages, self.passed):
                for copy, later in zip(copies, passed):
                    if not later:
                        copy.start()
        else:
            for copy, later in zip(self.stages[stage], self.passed[stage]):
                if later:
                    copy.start()

    def wait(self, stage):
        for copy in self.stages[stage]:
            copy.wait_recv()

    def finish(self):
        for stage in self.stages:
            for copy in stage:
                copy.wait_send()


def turn(values, cosine, sinus):
    lane = lax.broadcasted_iota(jnp.int32, values.shape, 1)
    first = lax.rem(lane, HEAD_DIM) < HEAD_DIM // 2
    swapped = jnp.where(
        first,
        pltpu.roll(values, 128 - HEAD_DIM // 2, 1),
        pltpu.roll(values, HEAD_DIM // 2, 1),
    )
    return values * cosine + swapped * sinus


def two_parts(values):
    high = values.astype(jnp.bfloat16)
    low = (values - high.astype(jnp.float32)).astype(jnp.bfloat16)
    return jnp.concatenate([high, low], axis=1)


def normed(values, gain):
    scale = lax.rsqrt(jnp.mean(values * values, axis=-1, keepdims=True) + epsilon)
    return (values * scale * gain).astype(jnp.bfloat16)


def fill_bias(bias, hot_rows, reach_t, key_start, query_start):
    seen = nn_dot(hot_rows, reach_t)
    keys = key_start + lax.broadcasted_iota(jnp.int32, seen.shape, 0)
    queries = query_start + lax.broadcasted_iota(jnp.int32, seen.shape, 1)
    bias[...] = jnp.where((seen > 0.5) & (keys <= queries), 0.0, masked_score)


def head_half(shape, axis, odd):
    index = lax.broadcasted_iota(jnp.int32, shape, axis)
    return (index >= HEAD_DIM) if odd else (index < HEAD_DIM)


def tree_tables(parents, lengths, turns, context, rows, hot, reach_t, cosine, sinus):
    lane = lax.broadcasted_iota(jnp.int32, (1, 128), 1)
    far = jnp.full((1, 128), 1 << 30, jnp.int32)
    none = jnp.zeros((1, 128), jnp.int32)
    begins, ends, moves = far, far, none
    first, second = none - 1, none - 1
    start = jnp.int32(0)
    for s in range(parents.shape[1]):
        parent = parents[0, s]
        grand = parents[0, parent]
        here = lane == s
        above = jnp.where(parent != s, lengths[0, parent], 0) + jnp.where(
            (grand != s) & (grand != parent), lengths[0, grand], 0
        )
        begins = jnp.where(here, start, begins)
        moves = jnp.where(here, above - start, moves)
        first = jnp.where(here, parent, first)
        second = jnp.where(here, grand, second)
        start = start + lengths[0, s]
        ends = jnp.where(here, start, ends)
    over = lax.broadcasted_iota(jnp.int32, (128, 128), 0)
    under = lax.broadcasted_iota(jnp.int32, (128, 128), 1)
    ancestors = jnp.where((over == under) | (over == first) | (over == second), 1.0, 0.0).astype(
        jnp.bfloat16
    )

    def fill(chunk, carry):
        block = pl.ds(pl.multiple_of(chunk * rows, 16), rows)
        row = chunk * rows + lax.broadcasted_iota(jnp.int32, (rows, 128), 0)
        inside = (row >= begins) & (row < ends)
        hot[block, :] = jnp.where(inside, 1.0, 0.0).astype(jnp.bfloat16)
        moved = jnp.sum(jnp.where(inside, moves.astype(jnp.float32), 0.0), axis=1, keepdims=True)
        angle = (row.astype(jnp.float32) + moved) * turns[0:1, :]
        cosine[block, :] = jnp.cos(angle)
        sinus[block, :] = jnp.sin(angle) * turns[1:2, :]
        return carry

    lax.fori_loop(0, context + 1, fill, 0)
    own = pl.ds(pl.multiple_of(context * rows, 16), rows)
    reach_t[...] = nt_dot(ancestors, hot[own, :]).astype(jnp.bfloat16)


def choose(ids, adapters_all, out):
    wanted = ids[0]
    own = ADAPTERS // adapters_all.shape[0]
    count = adapters_all.shape[1] // own
    total = jnp.zeros((count, 128), jnp.float32)
    for a in range(ADAPTERS):
        block = adapters_all[a // own, pl.ds((a % own) * count, count), :].astype(jnp.float32)
        total = total + jnp.where(wanted == a, block, 0.0)
    out[...] = total.astype(jnp.bfloat16)


def route_tables(f, table_all, place_row, place_col, weight_col, marks):
    fsdp, _, rows = table_all.shape
    own = EXPERTS // fsdp
    f32 = jnp.float32
    sub = lax.broadcasted_iota(jnp.int32, (8, rows), 0)
    expert = jnp.where(sub < own, f * own + sub, -1).astype(f32)
    before = lax.broadcasted_iota(jnp.int32, (rows, rows), 0)
    after = lax.broadcasted_iota(jnp.int32, (rows, rows), 1)
    upto = jnp.where(before <= after, 1.0, 0.0).astype(jnp.bfloat16)
    lane = lax.broadcasted_iota(jnp.int32, (8, 128), 1)
    base = jnp.zeros((8, 1), f32)
    found = jnp.zeros((8, 128), f32)
    more = jnp.zeros((120, rows), f32)
    for source in range(fsdp):
        table = table_all[source]
        one = table[0:1, :] == expert
        two = table[1:2, :] == expert
        hit = one | two
        weight = jnp.where(one, table[2:3, :], 0.0) + jnp.where(two, table[3:4, :], 0.0)
        count = nn_dot(jnp.where(hit, 1.0, 0.0).astype(jnp.bfloat16), upto) + base
        place = jnp.where(hit, count - 1.0, -1.0)
        block = slice(source * rows, (source + 1) * rows)
        place_row[:, block] = place
        place_col[block, :] = jnp.concatenate([place, more], axis=0).T
        weight_col[block, :] = jnp.concatenate([weight, more], axis=0).T.astype(jnp.bfloat16)
        for token in range(TOKEN_TILE - 1, fsdp * rows, TOKEN_TILE):
            if token // rows == source:
                at = token % rows
                found = jnp.where(lane == token // TOKEN_TILE + 1, count[:, at : at + 1], found)
        base = count[:, rows - 1 : rows]
    marks[...] = found


def unpack_adapter(t, per_block, chosen, flat, wide, first, second):
    a_qkv, b_qkv2, a_qkv_t2, a_o, b_o2, a_o_t2 = first
    a_gu, b_gu2, a_gu_t2, a_dn, a_dn_t2, b_dn2 = second
    f32, bf = jnp.float32, jnp.bfloat16
    contexts = chosen.shape[1]
    width, units = a_o.shape[0], a_dn.shape[0]
    count = PARAMS // 128 // (2 * contexts)
    for context in range(contexts):
        for part in range(2):
            start = (2 * context + part) * count
            flat[start : start + count, :] = chosen[part, context, 0:count, :].astype(f32)

    def spread(start, groups, rank, out, out_t):
        total = groups * 128 // rank
        wide[...] = jnp.zeros_like(wide)
        lines = rank // math.gcd(rank, 128)
        each = lines * 128 // rank
        for i in range(each):
            row, at = divmod(i * rank, 128)
            def line(number):
                if lines == 1:
                    return flat[pl.ds(start, groups), :]
                return flat[pl.ds(start + number, groups // lines, stride=lines), :]

            piece = line(row)[:, at : min(at + rank, 128)]
            if at + rank > 128:
                piece = jnp.concatenate([piece, line(row + 1)[:, 0 : at + rank - 128]], axis=1)
            wide[pl.ds(i, groups // lines, stride=each), 0:rank] = piece
        out[...] = wide[0:total, :].astype(bf)
        if out_t is not None:
            for p in range(total // 128):
                turned = wide[128 * p : 128 * p + 128, :].T.astype(bf)
                out_t[0:128, 128 * p : 128 * p + 128] = turned
                out_t[128:256, 128 * p : 128 * p + 128] = turned

    def stack(start, lines, columns, out, row, column):
        for p, m in enumerate(columns):
            piece = (2.0 * flat[pl.ds(start + m, RANK, stride=lines), :]).astype(bf)
            lanes = slice(column + 128 * p, column + 128 * p + 128)
            out[row : row + RANK, lanes] = piece
            out[128 + row : 128 + row + RANK, lanes] = piece

    for ref in (b_qkv2, b_o2, b_gu2, b_dn2):
        ref[...] = jnp.zeros_like(ref)
    at = 0
    spread(at, 3 * RANK * D // 128, 3 * RANK, a_qkv, a_qkv_t2)
    at = at + 3 * RANK * D // 128
    lines = D // 128
    mine = [t * (width // 128) + p for p in range(width // 128)]
    for j in range(3):
        stack(at + j * RANK * lines, lines, mine, b_qkv2, j * RANK, j * width)
    at = at + 3 * RANK * lines
    spread(at + t * (width * RANK // 128), width * RANK // 128, RANK, a_o, a_o_t2)
    at = at + D * RANK // 128
    stack(at, lines, list(range(lines)), b_o2, 0, 0)
    at = at + RANK * lines
    spread(at, 2 * RANK * D // 128, 2 * RANK, a_gu, a_gu_t2)
    at = at + 2 * RANK * D // 128
    wide_lines = FF // 128
    mine = [t * (units // 128) + p for p in range(units // 128)]
    for j in range(2):
        stack(at + j * RANK * wide_lines, wide_lines, mine, b_gu2, j * RANK, j * units)
    at = at + 2 * RANK * wide_lines
    spread(at + t * (units * RANK // 128), units * RANK // 128, RANK, a_dn, a_dn_t2)
    at = at + FF * RANK // 128
    stack(at, lines, list(range(lines)), b_dn2, 0, 0)


def forward_kernel(
    sizes,
    x_in,
    g_in,
    wq_in,
    wo_in,
    gu_in,
    dn_in,
    adapters_in,
    gains_in,
    table_in,
    turns,
    ids,
    parents,
    lengths,
    n1_all,
    k_all,
    v_all,
    wq_all,
    wo_all,
    n2_all,
    g_all,
    q_t_out,
    q_n_out,
    mixed_out,
    o_t_out,
    lse_out,
    resid_out,
    shared_half,
    dn2_half,
    da_gu,
    db_gu,
    da_dn,
    db_dn,
    gains_out,
    cosine_out,
    sinus_out,
    hot_out,
    reach_t_out,
    a_qkv_out,
    b_qkv2_out,
    a_qkv_t2_out,
    a_o_out,
    b_o2_out,
    a_o_t2_out,
    table_all_out,
    place_row_out,
    place_col_out,
    weight_col_out,
    marks,
    x_buf,
    wq,
    wo,
    gu,
    dn,
    g_own,
    n1_buf,
    k_buf,
    v_buf,
    v_t,
    peak,
    total,
    bias,
    part_out,
    part_in,
    n2_own,
    shared,
    dn2,
    shared_in,
    dn2_in,
    adapters_all,
    gains_all,
    chosen,
    flat,
    a_wide,
    a_gu,
    b_gu2,
    a_gu_t2,
    a_dn,
    a_dn_t2,
    b_dn2,
    fs_send,
    fs_recv,
    z_send,
    z_recv,
    core_send,
    core_recv,
    local_sems,
    chunk_sems,
    small_send,
    small_recv,
    lend_send,
    lend_recv,
    q_t,
    q_n,
    mixed,
    o_t,
    lse,
    resid,
    gains,
    cosine,
    sinus,
    hot,
    reach_t,
    a_qkv,
    b_qkv2,
    a_qkv_t2,
    a_o,
    b_o2,
    a_o_t2,
    table_all,
    place_row,
    place_col,
    weight_col,
    out_sems,
):
    fsdp, contexts, _ = sizes
    bits = fsdp.bit_length() - 1
    f, c, t = place_of()
    rows = x_in.shape[0]
    half = rows // 2
    heads = q_t.shape[0] // HEAD_DIM
    width = q_t.shape[0]
    units = dn_in.shape[1]
    own_n = wq_in.shape[0]
    sibling = (f, c, 1 - t)

    def peer(index):
        return (index, c, t)

    peers = [(lax.rem(f + k, fsdp), c, t) for k in range(1, fsdp)]
    stacked = [(f, lax.rem(c + k, contexts), t) for k in range(1, contexts)]
    greet(peers + stacked + [sibling])

    targets = (
        (q_t, q_t_out),
        (q_n, q_n_out),
        (mixed, mixed_out),
        (o_t, o_t_out),
        (lse, lse_out),
        (resid, resid_out),
        (gains, gains_out),
        (cosine, cosine_out),
        (sinus, sinus_out),
        (hot, hot_out),
        (reach_t, reach_t_out),
        (a_qkv, a_qkv_out),
        (b_qkv2, b_qkv2_out),
        (a_qkv_t2, a_qkv_t2_out),
        (a_o, a_o_out),
        (b_o2, b_o2_out),
        (a_o_t2, a_o_t2_out),
        (table_all, table_all_out),
        (place_row, place_row_out),
        (place_col, place_col_out),
        (weight_col, weight_col_out),
    )
    given = []

    def give_out(refs):
        for i, (ref, target) in enumerate(targets):
            if any(ref is other for other in refs):
                copy = pltpu.make_async_copy(ref, target, out_sems.at[i])
                copy.start()
                given.append(copy)

    def half_rows(chunk, part):
        return pl.ds(pl.multiple_of(chunk * rows + part * half, 16), half)

    def up(chunk, source):
        return send(
            source,
            x_buf.at[half_rows(chunk, t)],
            z_send.at[chunk],
            z_recv.at[chunk],
            (f, c + 1, t),
        )

    def across(chunk):
        block = x_buf.at[half_rows(chunk, t)]
        return send(block, block, core_send.at[chunk], core_recv.at[chunk], sibling)

    @pl.when(c < contexts - 1)
    def _():
        up(c, x_in.at[half_rows(0, t)]).start()

    gathers = []
    halved = (False, False, True, False)
    neighbour = (f, c + 1 - 2 * lax.rem(c, 2), t)
    own_half = own_n // 2
    for i, (own, buf) in enumerate(((wq_in, wq), (wo_in, wo), (gu_in, gu), (dn_in, dn))):
        base, count = (lax.rem(c, 2) * own_half, own_half) if halved[i] else (0, own_n)
        gathers.append(
            Gather(bits, f, peer, own, buf, own_n, base, count, fs_send.at[i], fs_recv.at[i])
        )

    def lent(gather, buf, which):
        copies, number = [], 0
        for stage in range(bits):
            group = []
            for block in gather.arrived[stage]:
                group.append(
                    send(
                        buf.at[block],
                        buf.at[block],
                        lend_send.at[which, number],
                        lend_recv.at[which, number],
                        neighbour,
                    )
                )
                number = number + 1
            copies.append(group)
        return copies

    gu_lent = lent(gathers[2], gu, 0)
    dn_lent = lent(gathers[3], dn, 1)

    def lend(copies, stage):
        for copy in copies[stage]:
            copy.start()
    g_gather = Gather(
        bits, f, peer, g_in, g_all, rows, t * half, half, fs_send.at[4], fs_recv.at[4]
    )
    n2_gather = Gather(
        bits, f, peer, n2_own, n2_all, rows, t * half, half, fs_send.at[5], fs_recv.at[5]
    )
    wq_gather, wo_gather, gu_gather, dn_gather = gathers
    small = []
    for k, other in enumerate(peers):
        for j, (source, target) in enumerate(
            ((adapters_in, adapters_all), (gains_in, gains_all), (table_in, table_all))
        ):
            copy = send(source, target.at[f], small_send.at[j, k], small_recv.at[j, k], other)
            copy.start()
            small.append(copy)
    wq_gather.start(0)
    locals_ = [pltpu.make_async_copy(x_in, x_buf.at[pl.ds(c * rows, rows)], local_sems.at[0])]
    for i, (own, buf) in enumerate(((wq_in, wq), (wo_in, wo), (gu_in, gu), (dn_in, dn))):
        locals_.append(
            pltpu.make_async_copy(own, buf.at[pl.ds(f * own_n, own_n)], local_sems.at[1 + i])
        )
    locals_.append(pltpu.make_async_copy(g_in, g_own, local_sems.at[5]))
    locals_.append(
        pltpu.make_async_copy(g_in, g_all.at[pl.ds(f * rows, rows)], local_sems.at[6])
    )
    for copy in locals_:
        copy.start()

    o_t[...] = jnp.zeros_like(o_t)
    peak[...] = jnp.full_like(peak, masked_score)
    total[...] = jnp.zeros_like(total)
    da_gu[...] = jnp.zeros_like(da_gu)
    db_gu[...] = jnp.zeros_like(db_gu)
    da_dn[...] = jnp.zeros_like(da_dn)
    db_dn[...] = jnp.zeros_like(db_dn)
    adapters_all[f] = adapters_in[...]
    gains_all[f] = gains_in[...]
    table_all[f] = table_in[...]
    tree_tables(parents, lengths, turns, c, rows, hot, reach_t, cosine, sinus)

    def receive(step):
        chunk = c - step

        @pl.when(step <= c)
        def _():
            up(chunk, x_buf.at[half_rows(chunk, t)]).wait_recv()

            @pl.when(c < contexts - 1)
            def _():
                up(chunk, x_buf.at[half_rows(chunk, t)]).start()

            across(chunk).start()

    def chunk_rows(chunk):
        return pl.ds(pl.multiple_of(chunk * rows, 16), rows)

    def out_copies(chunk):
        block = chunk_rows(chunk)
        return [
            pltpu.make_async_copy(n1_buf.at[block], n1_all.at[block], chunk_sems.at[0, chunk]),
            pltpu.make_async_copy(k_buf.at[block], k_all.at[block], chunk_sems.at[1, chunk]),
            pltpu.make_async_copy(v_buf.at[block], v_all.at[block], chunk_sems.at[2, chunk]),
        ]

    def project(chunk, own):
        block = chunk_rows(chunk)
        n1 = normed(x_buf[block, :].astype(jnp.float32), gain_one)
        n1_buf[block, :] = n1
        rank = two_parts(nn_dot(n1, a_qkv[...]))
        cos_rows = cosine[block, :]
        sin_rows = sinus[block, :]
        for p in range(width // 128):
            cols = slice(width + 128 * p, width + 128 * p + 128)
            key = nn_dot(n1, wq[:, cols]) + nn_dot(rank, b_qkv2[:, cols])
            k_buf[block, 128 * p : 128 * p + 128] = turn(key, cos_rows, sin_rows).astype(
                jnp.bfloat16
            )
            cols = slice(2 * width + 128 * p, 2 * width + 128 * p + 128)
            value = nn_dot(n1, wq[:, cols]) + nn_dot(rank, b_qkv2[:, cols])
            v_buf[block, 128 * p : 128 * p + 128] = value.astype(jnp.bfloat16)
            v_t[128 * p : 128 * p + 128, :] = value.T.astype(jnp.bfloat16)
            if own:
                cols = slice(128 * p, 128 * p + 128)
                query = nn_dot(n1, wq[:, cols]) + nn_dot(rank, b_qkv2[:, cols])
                query = turn(query, cos_rows, sin_rows) * 0.125
                q_n[:, cols] = query.astype(jnp.bfloat16)
                q_t[cols, :] = query.T.astype(jnp.bfloat16)
        for copy in out_copies(chunk):
            copy.start()

    def attend(chunk):
        block = chunk_rows(chunk)
        fill_bias(bias, hot[block, :], reach_t[...], chunk * rows, c * rows)

        def pair_step(p, carry):
            lanes = pl.ds(pl.multiple_of(p * 128, 128), 128)
            keys = k_buf[block, lanes]
            query = q_t[lanes, :]
            for odd in range(2):
                h = 2 * p + odd
                alone = jnp.where(
                    head_half(query.shape, 0, odd), query, jnp.zeros_like(query)
                )
                scores = nn_dot(keys, alone) + bias[...]
                before = peak[pl.ds(h, 1), :]
                now = jnp.maximum(before, jnp.max(scores, axis=0, keepdims=True))
                weights = jnp.exp(scores - now)
                shrink = jnp.exp(before - now)
                peak[pl.ds(h, 1), :] = now
                total[pl.ds(h, 1), :] = total[pl.ds(h, 1), :] * shrink + jnp.sum(
                    weights, axis=0, keepdims=True
                )
                head = pl.ds(pl.multiple_of(h * HEAD_DIM, HEAD_DIM), HEAD_DIM)
                o_t[head, :] = o_t[head, :] * shrink + nn_dot(
                    v_t[head, :], weights.astype(jnp.bfloat16)
                )
            return carry

        lax.fori_loop(0, heads // 2, pair_step, 0)

    def advance(gather, following, copies=None):
        gather.wait(0)
        for stage in range(1, bits):
            gather.start(stage)
            if copies is not None:
                lend(copies, stage - 1)
            if stage < bits - 1:
                gather.wait(stage)
        following.start(0)

    for copy in small:
        copy.wait_recv()
    choose(ids, adapters_all, chosen.at[t, c])
    spread = []
    for k, other in enumerate(stacked):
        block = chosen.at[t, c]
        copy = send(block, block, small_send.at[3, k], small_recv.at[3, k], other)
        copy.start()
        spread.append(copy)
    gains[...] = jnp.zeros_like(gains)
    for i in range(2):
        pieces = [
            gains_all[b, 0:1, i * own_n : (i + 1) * own_n].astype(jnp.float32)
            for b in range(fsdp)
        ]
        gains[i : i + 1, :] = jnp.concatenate(pieces, axis=1)
    gain_one = gains[0:1, :]
    gain_two = gains[1:2, :]
    advance(wq_gather, wo_gather)
    for copy in spread:
        copy.wait_recv()
    shared_copy = send(
        chosen.at[t], chosen.at[t], small_send.at[4, 0], small_recv.at[4, 0], sibling
    )
    shared_copy.start()
    route_tables(f, table_all, place_row, place_col, weight_col, marks)
    give_out(
        (table_all, place_row, place_col, weight_col, gains, cosine, sinus, hot, reach_t)
    )
    advance(wo_gather, gu_gather)
    shared_copy.wait_recv()
    unpack_adapter(
        t,
        adapters_in.shape[0] // (ADAPTERS // fsdp),
        chosen,
        flat,
        a_wide,
        (a_qkv, b_qkv2, a_qkv_t2, a_o, b_o2, a_o_t2),
        (a_gu, b_gu2, a_gu_t2, a_dn, a_dn_t2, b_dn2),
    )
    give_out((a_qkv, b_qkv2, a_qkv_t2, a_o, b_o2, a_o_t2))
    receive(1)
    wq_gather.wait(bits - 1)
    locals_[0].wait()
    locals_[1].wait()
    wq_out = pltpu.make_async_copy(wq, wq_all, local_sems.at[10])
    wq_out.start()
    project(c, True)
    attend(c)

    def between(step):
        if step == 1:
            advance(gu_gather, dn_gather, gu_lent)
        if step == 2:
            gu_gather.wait(bits - 1)
            lend(gu_lent, bits - 1)
            advance(dn_gather, g_gather)

    def later(step):
        chunk = c - step

        @pl.when(step <= c)
        def _():
            across(chunk).wait_recv()
            project(chunk, False)
            attend(chunk)

    for step in range(1, 3):
        receive(step + 1)
        between(step)
        later(step)

    def rest(step, carry):
        receive(step + 1)
        later(step)
        return carry

    lax.fori_loop(3, contexts, rest, 0)

    for h in range(heads):
        head = slice(h * HEAD_DIM, h * HEAD_DIM + HEAD_DIM)
        o_t[head, :] = o_t[head, :] / total[h : h + 1, :]
    lse[...] = peak[...] + jnp.log(total[...])
    for p in range(width // 128):
        mixed[:, 128 * p : 128 * p + 128] = o_t[128 * p : 128 * p + 128, :].T.astype(jnp.bfloat16)
    give_out((q_t, q_n, mixed, o_t, lse))
    wo_gather.wait(bits - 1)
    locals_[2].wait()
    wo_out = pltpu.make_async_copy(wo, wo_all, local_sems.at[11])
    wo_out.start()

    def local_rows(part):
        return pl.ds(pl.multiple_of(part * half, 16), half)

    mine = local_rows(t)
    theirs = local_rows(1 - t)

    def branch(block):
        values = mixed[block, :]
        rank = two_parts(nn_dot(values, a_o[...]))
        return nt_dot(values, wo[...]) + nn_dot(rank, b_o2[...])

    part_out[...] = branch(theirs)
    number = contexts
    part_copy = send(
        part_out, part_in, core_send.at[number], core_recv.at[number], sibling
    )
    part_copy.start()
    own_part = branch(mine) + x_in_rows(x_buf, c, rows, t, half)
    part_copy.wait_recv()
    resid_half = own_part + part_in[...]
    resid[mine, :] = resid_half
    n2_own[mine, :] = normed(resid_half, gain_two)
    n2_gather.start(0)
    n2_copy = send(
        n2_own.at[mine], n2_own.at[mine], core_send.at[number + 1], core_recv.at[number + 1], sibling
    )
    n2_copy.start()
    resid_copy = send(
        resid.at[mine], resid.at[mine], core_send.at[number + 2], core_recv.at[number + 2], sibling
    )
    resid_copy.start()

    def forwards(gather, buf, first):
        copies = []
        for stage in range(bits):
            group = []
            for block in gather.arrived[stage]:
                index = first + len(copies)
                copies.append(
                    send(
                        buf.at[block],
                        buf.at[block],
                        core_send.at[index],
                        core_recv.at[index],
                        sibling,
                    )
                )
        return copies

    per_stage = [len(stage) for stage in g_gather.arrived]
    g_forward = forwards(g_gather, g_all, number + 5)
    n2_forward = forwards(n2_gather, n2_all, number + 5 + sum(per_stage))

    def pass_on(copies, stage):
        start = sum(per_stage[:stage])
        for copy in copies[start : start + per_stage[stage]]:
            copy.start()

    locals_[5].wait()
    for group in gu_lent:
        for copy in group:
            copy.wait_recv()
    locals_[3].wait()
    dn_gather.wait(bits - 1)
    locals_[4].wait()

    def shared_tile(block):
        inputs = n2_own[block, :]
        grads = g_own[block, :]
        rank = nn_dot(inputs, a_gu[...])
        rank2 = two_parts(rank)
        gate = nn_dot(inputs, gu[:, :units]) + nn_dot(rank2, b_gu2[:, :units])
        up_pre = nn_dot(inputs, gu[:, units:]) + nn_dot(rank2, b_gu2[:, units:])
        sigmoid_gate = jax.nn.sigmoid(gate)
        silu = gate * sigmoid_gate
        hidden = (silu * up_pre).astype(jnp.bfloat16)
        down_rank = nn_dot(hidden, a_dn[...])
        shared[block, :] = nt_dot(hidden, dn[...]) + nn_dot(two_parts(down_rank), b_dn2[...])
        down_back = nt_dot(grads, b_dn2[0:128, :])
        grad_hidden = nn_dot(grads, dn[...]) + nn_dot(two_parts(down_back), a_dn_t2[...])
        grad_gate = (
            grad_hidden * up_pre * sigmoid_gate * (1.0 + gate * (1.0 - sigmoid_gate))
        ).astype(jnp.bfloat16)
        grad_up = (grad_hidden * silu).astype(jnp.bfloat16)
        rank_back = nt_dot(grad_gate, b_gu2[0:128, :units]) + nt_dot(
            grad_up, b_gu2[0:128, units:]
        )
        dn2[block, :] = (
            nt_dot(grad_gate, gu[:, :units])
            + nt_dot(grad_up, gu[:, units:])
            + nn_dot(two_parts(rank_back), a_gu_t2[...])
        )
        rank_low = rank.astype(jnp.bfloat16)
        da_gu[...] += tn_dot(rank_back.astype(jnp.bfloat16), inputs)[0 : 2 * RANK]
        db_gu[0:RANK, :] += 2.0 * tn_dot(rank_low, grad_gate)[0:RANK]
        db_gu[RANK:, :] += 2.0 * tn_dot(rank_low, grad_up)[RANK : 2 * RANK]
        da_dn[...] += tn_dot(down_back.astype(jnp.bfloat16), hidden)[0:RANK]
        db_dn[...] += 2.0 * tn_dot(down_rank.astype(jnp.bfloat16), grads)[0:RANK]

    n2_gather.wait(0)
    for stage in range(1, bits):
        n2_gather.start(stage)
        pass_on(n2_forward, stage - 1)
        if stage < bits - 1:
            n2_gather.wait(stage)
    n2_copy.wait_recv()
    shared_tile(theirs)
    pair_copies = [
        send(
            source.at[theirs], target, core_send.at[number + 3 + i], core_recv.at[number + 3 + i], sibling
        )
        for i, (source, target) in enumerate(((dn2, dn2_in), (shared, shared_in)))
    ]
    for copy in pair_copies:
        copy.start()
    g_gather.wait(0)
    for stage in range(1, bits):
        g_gather.start(stage)
        pass_on(g_forward, stage - 1)
        if stage < bits - 1:
            g_gather.wait(stage)
    n2_out = pltpu.make_async_copy(n2_own, n2_all.at[pl.ds(f * rows, rows)], local_sems.at[12])
    n2_out.start()
    shared_tile(mine)
    resid_copy.wait_recv()
    give_out((resid,))
    for copy in pair_copies:
        copy.wait()
    dn2_half[...] = dn2[mine, :] + dn2_in[...]
    shared_half[...] = shared[mine, :] + shared_in[...]
    n2_gather.wait(bits - 1)
    pass_on(n2_forward, bits - 1)
    g_gather.wait(bits - 1)
    pass_on(g_forward, bits - 1)
    for copy in n2_forward + g_forward:
        copy.wait()
    for copy in small + spread + [shared_copy]:
        copy.wait_send()
    for group in gu_lent:
        for copy in group:
            copy.wait_send()
    resid_copy.wait_send()
    for copy in given:
        copy.wait()
    n2_copy.wait_send()
    part_copy.wait_send()
    for gather in gathers + [g_gather, n2_gather]:
        gather.finish()
    n2_out.wait()
    wq_out.wait()
    wo_out.wait()
    locals_[6].wait()

    @pl.when(c < contexts - 1)
    def _():
        up(c, x_in.at[half_rows(0, t)]).wait_send()

    def drain(step, carry):
        chunk = c - step

        @pl.when(c < contexts - 1)
        def _():
            up(chunk, x_buf.at[half_rows(chunk, t)]).wait_send()

        across(chunk).wait_send()
        return carry

    lax.fori_loop(1, c + 1, drain, 0)

    def drain_out(step, carry):
        for copy in out_copies(c - step):
            copy.wait()
        return carry

    lax.fori_loop(0, c + 1, drain_out, 0)


def x_in_rows(x_buf, chunk, rows, part, half):
    block = pl.ds(pl.multiple_of(chunk * rows + part * half, 16), half)
    return x_buf[block, :].astype(jnp.float32)


def forward_call(sizes, sharded, local):
    fsdp, contexts, _ = sizes
    x, g, wq, wo, gu, dn = sharded
    adapters, gains, table = local[:3]
    rows = x.shape[0]
    tree = rows * contexts
    width = wo.shape[1]
    units = dn.shape[1]
    bf, f32 = jnp.bfloat16, jnp.float32
    vmem = pl.BlockSpec(memory_space=pltpu.VMEM)
    hbm = pl.BlockSpec(memory_space=pl.ANY)
    smem = pl.BlockSpec(memory_space=pltpu.SMEM)
    slots = max(fsdp, contexts)
    total = fsdp * rows
    per_adapter = adapters.shape[0] // (ADAPTERS // fsdp)

    def shape(kind, *dims):
        return jax.ShapeDtypeStruct(dims, kind)

    moves = 2 * (fsdp - 1)
    hops = contexts + 5 + 2 * moves
    return pl.pallas_call(
        functools.partial(forward_kernel, sizes),
        in_specs=[hbm] * 6 + [vmem] * 4 + [smem] * 3,
        out_specs=[hbm] * 7 + [hbm, hbm, hbm, hbm, hbm, hbm, vmem, vmem, vmem, vmem, vmem, vmem, hbm, hbm, hbm, hbm, hbm, hbm, hbm, hbm, hbm, hbm, hbm, hbm, hbm, hbm, hbm, vmem],
        out_shape=[
            shape(bf, tree, D),
            shape(bf, tree, width),
            shape(bf, tree, width),
            shape(bf, D, 3 * width),
            shape(bf, D, width),
            shape(bf, fsdp * rows, D),
            shape(bf, fsdp * rows, D),
            shape(bf, width, rows),
            shape(bf, rows, width),
            shape(bf, rows, width),
            shape(f32, width, rows),
            shape(f32, 8, rows),
            shape(f32, rows, D),
            shape(f32, rows // 2, D),
            shape(f32, rows // 2, D),
            shape(f32, 2 * RANK, D),
            shape(f32, 2 * RANK, units),
            shape(f32, RANK, units),
            shape(f32, RANK, D),
            shape(f32, 8, D),
            shape(f32, tree, 128),
            shape(f32, tree, 128),
            shape(bf, tree, 128),
            shape(bf, 128, rows),
            shape(bf, D, 128),
            shape(bf, 256, 3 * width),
            shape(bf, 256, D),
            shape(bf, width, 128),
            shape(bf, 256, D),
            shape(bf, 256, width),
            shape(f32, fsdp, 8, rows),
            shape(f32, 8, total),
            shape(f32, total, 128),
            shape(bf, total, 128),
            shape(f32, 8, 128),
        ],
        scratch_shapes=[
            pltpu.VMEM((tree, D), bf),
            pltpu.VMEM((D, 3 * width), bf),
            pltpu.VMEM((D, width), bf),
            pltpu.VMEM((D, 2 * units), bf),
            pltpu.VMEM((D, units), bf),
            pltpu.VMEM((rows, D), bf),
            pltpu.VMEM((tree, D), bf),
            pltpu.VMEM((tree, width), bf),
            pltpu.VMEM((tree, width), bf),
            pltpu.VMEM((width, rows), bf),
            pltpu.VMEM((8, rows), f32),
            pltpu.VMEM((8, rows), f32),
            pltpu.VMEM((rows, rows), f32),
            pltpu.VMEM((rows // 2, D), f32),
            pltpu.VMEM((rows // 2, D), f32),
            pltpu.VMEM((rows, D), bf),
            pltpu.VMEM((rows, D), f32),
            pltpu.VMEM((rows, D), f32),
            pltpu.VMEM((rows // 2, D), f32),
            pltpu.VMEM((rows // 2, D), f32),
            pltpu.VMEM((fsdp,) + adapters.shape, bf),
            pltpu.VMEM((fsdp,) + gains.shape, bf),
            pltpu.VMEM((2, contexts, per_adapter, 128), bf),
            pltpu.VMEM((PARAMS // 128, 128), f32),
            pltpu.VMEM((max(D, units), 128), f32),
            pltpu.VMEM((D, 128), bf),
            pltpu.VMEM((256, 2 * units), bf),
            pltpu.VMEM((256, D), bf),
            pltpu.VMEM((units, 128), bf),
            pltpu.VMEM((256, units), bf),
            pltpu.VMEM((256, D), bf),
            pltpu.SemaphoreType.DMA((6, moves)),
            pltpu.SemaphoreType.DMA((6, moves)),
            pltpu.SemaphoreType.DMA((contexts,)),
            pltpu.SemaphoreType.DMA((contexts,)),
            pltpu.SemaphoreType.DMA((hops,)),
            pltpu.SemaphoreType.DMA((hops,)),
            pltpu.SemaphoreType.DMA((13,)),
            pltpu.SemaphoreType.DMA((3, contexts)),
            pltpu.SemaphoreType.DMA((5, slots)),
            pltpu.SemaphoreType.DMA((5, slots)),
            pltpu.SemaphoreType.DMA((2, moves)),
            pltpu.SemaphoreType.DMA((2, moves)),
            pltpu.VMEM((width, rows), bf),
            pltpu.VMEM((rows, width), bf),
            pltpu.VMEM((rows, width), bf),
            pltpu.VMEM((width, rows), f32),
            pltpu.VMEM((8, rows), f32),
            pltpu.VMEM((rows, D), f32),
            pltpu.VMEM((8, D), f32),
            pltpu.VMEM((tree, 128), f32),
            pltpu.VMEM((tree, 128), f32),
            pltpu.VMEM((tree, 128), bf),
            pltpu.VMEM((128, rows), bf),
            pltpu.VMEM((D, 128), bf),
            pltpu.VMEM((256, 3 * width), bf),
            pltpu.VMEM((256, D), bf),
            pltpu.VMEM((width, 128), bf),
            pltpu.VMEM((256, D), bf),
            pltpu.VMEM((256, width), bf),
            pltpu.VMEM((fsdp, 8, rows), f32),
            pltpu.VMEM((8, total), f32),
            pltpu.VMEM((total, 128), f32),
            pltpu.VMEM((total, 128), bf),
            pltpu.SemaphoreType.DMA((21,)),
        ],
        name="forward",
        compiler_params=pltpu.CompilerParams(
            collective_id=2, has_side_effects=True, vmem_limit_bytes=62 << 20
        ),
    )(*sharded, *local)


def flips(index, mask, bits):
    for bit in range(bits):
        if mask >> bit & 1:
            index = flip(index, bit)
    return index


class Scatter:
    def __init__(self, bits, me, device_of, work, inbox, count, send_sems, recv_sems):
        self.bits, self.work, self.inbox = bits, work, inbox
        self.copies = [[] for _ in range(bits)]
        self.adds = [[] for _ in range(bits)]
        number = 0
        for half, (offset, size) in enumerate(split_rows(count)):
            alive = list(range(1 << bits))
            slot = 0
            for stage in range(bits):
                bit = (stage + half) % bits
                for mask in alive:
                    if mask >> bit & 1:
                        source = Gather.rows(flips(me, mask, bits) * count + offset, size)
                        target = pl.ds(slot * count + offset, size)
                        kept = Gather.rows(flips(me, mask ^ (1 << bit), bits) * count + offset, size)
                        self.copies[stage].append(
                            send(
                                work.at[source],
                                inbox.at[target],
                                send_sems.at[number],
                                recv_sems.at[number],
                                device_of(flip(me, bit)),
                            )
                        )
                        self.adds[stage].append((kept, target, pl.ds(offset, size)))
                        number = number + 1
                        slot = slot + 1
                alive = [mask for mask in alive if not mask >> bit & 1]

    def start(self, stage):
        for copy in self.copies[stage]:
            copy.start()

    def add(self, stage):
        for copy in self.copies[stage]:
            copy.wait_recv()
        for kept, target, _ in self.adds[stage]:
            total = self.work[kept, :].astype(jnp.float32) + self.inbox[target, :].astype(
                jnp.float32
            )
            self.work[kept, :] = total.astype(jnp.bfloat16)

    def last(self, out, own):
        for copy in self.copies[self.bits - 1]:
            copy.wait_recv()
        for kept, target, rows in self.adds[self.bits - 1]:
            total = self.work[kept, :].astype(jnp.float32) + self.inbox[target, :].astype(
                jnp.float32
            )
            out[rows, :] = (total + own[rows, :]).astype(jnp.bfloat16)

    def finish(self):
        for stage in self.copies:
            for copy in stage:
                copy.wait_send()


def backward_kernel(
    sizes,
    moe_out,
    moe_back,
    n1_hbm,
    k_hbm,
    v_hbm,
    wq_hbm,
    wo_hbm,
    cos_hbm,
    sin_hbm,
    x_in,
    g_in,
    gains,
    hot,
    reach_t,
    resid,
    shared_half,
    dn2_half,
    q_t,
    q_n,
    mixed,
    o_t,
    lse,
    a_qkv,
    b_qkv2,
    a_qkv_t2,
    a_o,
    a_o_t2,
    b_o2,
    block_out,
    input_grad,
    da_qkv,
    db_qkv,
    da_o,
    db_o,
    cosine,
    sinus,
    n1_buf,
    k_buf,
    v_buf,
    wq,
    wo,
    work_back,
    pair_back,
    inbox_back,
    work_out,
    pair_out,
    inbox_out,
    total_half,
    total_full,
    ffn_half,
    ffn_full,
    dy,
    do_n,
    do_t,
    delta,
    k_t,
    dq_t,
    grad_kv,
    bias,
    part,
    part_out,
    part_in,
    z_in,
    z_out,
    dn1_full,
    fs_send,
    fs_recv,
    z_send,
    z_recv,
    core_send,
    core_recv,
    pair_send,
    pair_recv,
    local_sems,
    chunk_sems,
):
    fsdp, contexts, _ = sizes
    bits = fsdp.bit_length() - 1
    f, c, t = place_of()
    rows = x_in.shape[0]
    half = rows // 2
    width = q_t.shape[0]
    heads = width // HEAD_DIM
    sibling = (f, c, 1 - t)
    f32, bf = jnp.float32, jnp.bfloat16

    def peer(index):
        return (index, c, t)

    def local_rows(part_index):
        return pl.ds(pl.multiple_of(part_index * half, 16), half)

    mine = local_rows(t)
    theirs = local_rows(1 - t)

    def block_rows(block, part_index):
        return pl.ds(pl.multiple_of(block * rows + part_index * half, 16), half)

    def work_rows(block):
        return pl.ds(pl.multiple_of(block * half, 16), half)

    masks = list(range(fsdp - 1, -1, -1))

    def exchange(source, work, inbox, which):
        own, sent = [], []
        for mask in masks:
            block = flips(f, mask, bits)
            own.append(
                pltpu.make_async_copy(
                    source.at[block_rows(block, t)],
                    work.at[work_rows(block)],
                    local_sems.at[which, mask],
                )
            )
            sent.append(
                send(
                    source.at[block_rows(block, 1 - t)],
                    inbox.at[work_rows(block)],
                    core_send.at[which, mask],
                    core_recv.at[which, mask],
                    sibling,
                )
            )
        return own, sent

    back_own, back_sent = exchange(moe_back, work_back, pair_back, 0)
    out_own, out_sent = exchange(moe_out, work_out, pair_out, 1)
    for copy in back_own:
        copy.start()
    wo_copy = pltpu.make_async_copy(wo_hbm, wo, local_sems.at[2, 0])
    wq_copy = pltpu.make_async_copy(wq_hbm, wq, local_sems.at[2, 1])
    wo_copy.start()
    greet(
        [peer(flip(f, bit)) for bit in range(bits)]
        + [sibling, (f, lax.rem(c + 1, contexts), t), (f, lax.rem(c + contexts - 1, contexts), t)]
    )
    for copy in back_sent:
        copy.start()
    for copy in out_own:
        copy.start()
    wq_copy.start()

    def chunk_rows(chunk):
        return pl.ds(pl.multiple_of(chunk * rows, 16), rows)

    def loads(chunk):
        block = chunk_rows(chunk)
        return [
            pltpu.make_async_copy(k_hbm.at[block], k_buf.at[block], chunk_sems.at[1, chunk]),
            pltpu.make_async_copy(v_hbm.at[block], v_buf.at[block], chunk_sems.at[2, chunk]),
        ]

    def n1_load(chunk):
        return pltpu.make_async_copy(
            n1_hbm.at[chunk_rows(chunk)], n1_buf, chunk_sems.at[0, chunk]
        )

    def table_loads(chunk):
        block = chunk_rows(chunk)
        return [
            pltpu.make_async_copy(cos_hbm.at[block], cosine, chunk_sems.at[3, chunk]),
            pltpu.make_async_copy(sin_hbm.at[block], sinus, chunk_sems.at[4, chunk]),
        ]

    def start_loads(chunk, carry):
        for copy in loads(chunk):
            copy.start()
        return carry

    lax.fori_loop(0, c + 1, start_loads, 0)

    back = Scatter(
        bits, f, peer, work_back, inbox_back, half, fs_send.at[0], fs_recv.at[0]
    )
    out = Scatter(bits, f, peer, work_out, inbox_out, half, fs_send.at[1], fs_recv.at[1])

    def pair_sum(own, sent, work, inbox):
        for i, mask in enumerate(masks):
            block = work_rows(flips(f, mask, bits))
            own[i].wait()
            sent[i].wait_recv()
            work[block, :] = (
                work[block, :].astype(f32) + inbox[block, :].astype(f32)
            ).astype(bf)

    pair_sum(back_own, back_sent, work_back, pair_back)
    back.start(0)
    for copy in out_sent:
        copy.start()
    for stage in range(1, bits):
        back.add(stage - 1)
        back.start(stage)
    dq_t[...] = jnp.zeros_like(dq_t)
    da_qkv[...] = jnp.zeros_like(da_qkv)
    db_qkv[...] = jnp.zeros_like(db_qkv)
    pair_sum(out_own, out_sent, work_out, pair_out)
    back.last(total_half, dn2_half)
    out.start(0)
    total_full[mine, :] = total_half[...]
    full_copy = send(
        total_half, total_full.at[mine], core_send.at[2, 0], core_recv.at[2, 0], sibling
    )
    full_copy.start()
    gain_one = gains[0:1, :]
    gain_two = gains[1:2, :]
    wo_copy.wait()
    full_copy.wait_recv()

    def attn_tile(i, carry):
        block = local_rows(i)
        values = resid[block, :]
        gradient = g_in[block, :].astype(f32) + norm_back(
            values, rms_scale(values), gain_two, total_full[block, :].astype(f32)
        )
        dy[block, :] = gradient
        low_grad = gradient.astype(bf)
        rank_back = nt_dot(low_grad, b_o2[0:128, :])
        do_n[block, :] = (
            nn_dot(low_grad, wo[...]) + nn_dot(two_parts(rank_back), a_o_t2[...])
        ).astype(bf)
        values_o = mixed[block, :]
        rank = nn_dot(values_o, a_o[...])
        first = tn_dot(rank_back.astype(bf), values_o)[0:RANK]
        second = 2.0 * tn_dot(rank.astype(bf), low_grad)[0:RANK]

        @pl.when(i == 0)
        def _():
            da_o[...] = first
            db_o[...] = second

        @pl.when(i > 0)
        def _():
            da_o[...] += first
            db_o[...] += second

        return carry

    lax.fori_loop(0, 2, attn_tile, 0)
    for p in range(width // 128):
        lanes = slice(128 * p, 128 * p + 128)
        turned = do_n[:, lanes].astype(f32).T
        do_t[lanes, :] = turned.astype(bf)
        product = turned * o_t[lanes, :]
        for odd in range(2):
            delta[2 * p + odd : 2 * p + odd + 1, :] = jnp.sum(
                product[HEAD_DIM * odd : HEAD_DIM * odd + HEAD_DIM, :], axis=0, keepdims=True
            )
    wq_copy.wait()

    def attend_back(chunk):
        block = chunk_rows(chunk)
        n1_load(chunk).start()
        for copy in table_loads(chunk):
            copy.start()
        for copy in loads(chunk) + table_loads(chunk):
            copy.wait()
        fill_bias(bias, hot[block, :], reach_t[...], chunk * rows, c * rows)
        cos_rows = cosine[...]
        sin_rows = -sinus[...]
        for p in range(width // 128):
            lanes = slice(128 * p, 128 * p + 128)
            k_t[lanes, :] = k_buf[block, lanes].astype(f32).T.astype(bf)

        def pair_step(p, carry):
            lanes = pl.ds(pl.multiple_of(p * 128, 128), 128)
            keys = k_buf[block, lanes]
            values = v_buf[block, lanes]
            query_t = q_t[lanes, :]
            grad_t = do_t[lanes, :]
            query = q_n[:, lanes]
            grad = do_n[:, lanes]
            grad_keys = jnp.zeros((rows, 128), f32)
            grad_values = jnp.zeros((rows, 128), f32)
            for odd in range(2):
                h = 2 * p + odd
                upper = head_half(query_t.shape, 0, odd)
                side = head_half(query.shape, 1, odd)
                none_t = jnp.zeros_like(query_t)
                none = jnp.zeros_like(query)
                scores = nn_dot(keys, jnp.where(upper, query_t, none_t)) + bias[...]
                weights = jnp.exp(scores - lse[pl.ds(h, 1), :])
                grad_weights = nn_dot(values, jnp.where(upper, grad_t, none_t))
                grad_scores = (weights * (grad_weights - delta[pl.ds(h, 1), :])).astype(bf)
                grad_values += nn_dot(weights.astype(bf), jnp.where(side, grad, none))
                grad_keys += nn_dot(grad_scores, jnp.where(side, query, none))
                head = pl.ds(pl.multiple_of(h * HEAD_DIM, HEAD_DIM), HEAD_DIM)
                dq_t[head, :] += nn_dot(k_t[head, :], grad_scores)
            grad_kv[:, lanes] = turn(grad_keys, cos_rows, sin_rows).astype(bf)
            grad_kv[:, pl.ds(pl.multiple_of(width + p * 128, 128), 128)] = grad_values.astype(bf)
            return carry

        lax.fori_loop(0, heads // 2, pair_step, 0)

    def project_back(chunk, own):
        block = chunk_rows(chunk)
        grads = grad_kv[...]
        result = nt_dot(grads, wq[:, width:])
        rank_back = nt_dot(grads, b_qkv2[0:128, width:])
        n1_load(chunk).wait()
        n1 = n1_buf[...]
        rank = nn_dot(n1, a_qkv[...]).astype(bf)
        both = 2.0 * tn_dot(rank, grads)
        db_qkv[RANK : 2 * RANK, :] += both[RANK : 2 * RANK, :width]
        db_qkv[2 * RANK :, :] += both[2 * RANK : 3 * RANK, width:]
        if own:
            pieces = []
            for p in range(width // 128):
                lanes = slice(128 * p, 128 * p + 128)
                grad_query = (dq_t[lanes, :] * 0.125).T
                pieces.append(
                    turn(grad_query, cosine[...], -sinus[...]).astype(bf)
                )
            grad_query = jnp.concatenate(pieces, axis=1)
            result += nt_dot(grad_query, wq[:, :width])
            rank_back += nt_dot(grad_query, b_qkv2[0:128, :width])
            db_qkv[0:RANK, :] += 2.0 * tn_dot(rank, grad_query)[0:RANK, :]
        result += nn_dot(two_parts(rank_back), a_qkv_t2[...])
        da_qkv[...] += tn_dot(rank_back.astype(bf), n1)[0 : 3 * RANK]
        part[...] = result.astype(bf)
        part_out[work_rows(chunk), :] = part[theirs, :]
        z_out[work_rows(chunk), :] = part[mine, :]

    def pair_copy(chunk):
        return send(
            part_out.at[work_rows(chunk)],
            part_in.at[work_rows(chunk)],
            pair_send.at[chunk],
            pair_recv.at[chunk],
            sibling,
        )

    def down(chunk):
        block = work_rows(chunk)
        return send(
            z_out.at[block], z_in.at[block], z_send.at[chunk], z_recv.at[chunk], (f, c - 1, t)
        )

    def chain(chunk):
        block = work_rows(chunk)
        pair_copy(chunk).wait_recv()
        summed = z_out[block, :].astype(f32) + part_in[block, :].astype(f32)
        z_out[block, :] = summed.astype(bf)

        @pl.when(c < contexts - 1)
        def _():
            down(chunk).wait_recv()
            z_out[block, :] = (summed + z_in[block, :].astype(f32)).astype(bf)

    def pass_down(chunk):
        chain(chunk)
        down(chunk).start()

    def step(chunk, carry):
        attend_back(chunk)
        project_back(chunk, False)
        pair_copy(chunk).start()

        @pl.when(c == contexts - 1)
        def _():
            pass_down(chunk)

        @pl.when((c < contexts - 1) & (chunk >= 1))
        def _():
            pass_down(chunk - 1)

        return carry

    lax.fori_loop(0, c, step, 0)
    attend_back(c)
    project_back(c, True)
    pair_copy(c).start()

    @pl.when((c < contexts - 1) & (c >= 1))
    def _():
        pass_down(c - 1)

    for stage in range(1, bits):
        out.add(stage - 1)
        out.start(stage)
    out.last(ffn_half, shared_half)
    ffn_full[mine, :] = ffn_half[...]
    ffn_copy = send(ffn_half, ffn_full.at[mine], core_send.at[2, 1], core_recv.at[2, 1], sibling)
    ffn_copy.start()
    chain(c)
    dn1_full[mine, :] = z_out[work_rows(c), :]
    dn1_copy = send(
        z_out.at[work_rows(c)],
        dn1_full.at[mine],
        core_send.at[2, 2],
        core_recv.at[2, 2],
        sibling,
    )
    dn1_copy.start()
    ffn_copy.wait_recv()
    block_out[...] = resid[...] + ffn_full[...].astype(f32)
    dn1_copy.wait_recv()

    def final_tile(i, carry):
        block = local_rows(i)
        values = x_in[block, :].astype(f32)
        input_grad[block, :] = dy[block, :] + norm_back(
            values, rms_scale(values), gain_one, dn1_full[block, :].astype(f32)
        )
        return carry

    lax.fori_loop(0, 2, final_tile, 0)
    for copy in back_sent + out_sent + [full_copy, ffn_copy, dn1_copy]:
        copy.wait_send()
    back.finish()
    out.finish()

    def drain(chunk, carry):
        pair_copy(chunk).wait_send()

        @pl.when(chunk < c)
        def _():
            down(chunk).wait_send()

        return carry

    lax.fori_loop(0, c + 1, drain, 0)


def backward_call(sizes, remote, local):
    fsdp, contexts, _ = sizes
    rows = local[0].shape[0]
    half = rows // 2
    tree = rows * contexts
    width = remote[6].shape[1]
    bf, f32 = jnp.bfloat16, jnp.float32
    vmem = pl.BlockSpec(memory_space=pltpu.VMEM)
    hbm = pl.BlockSpec(memory_space=pl.ANY)

    def shape(kind, *dims):
        return jax.ShapeDtypeStruct(dims, kind)

    moves = 2 * (fsdp - 1)
    slots = max(fsdp, 4)
    dma = pltpu.SemaphoreType.DMA
    return pl.pallas_call(
        functools.partial(backward_kernel, sizes),
        in_specs=[hbm] * len(remote) + [vmem] * len(local),
        out_specs=[vmem] * 6,
        out_shape=[
            shape(f32, rows, D),
            shape(f32, rows, D),
            shape(f32, 3 * RANK, D),
            shape(f32, 3 * RANK, width),
            shape(f32, RANK, width),
            shape(f32, RANK, D),
        ],
        scratch_shapes=[
            pltpu.VMEM((rows, 128), f32),
            pltpu.VMEM((rows, 128), f32),
            pltpu.VMEM((rows, D), bf),
            pltpu.VMEM((tree, width), bf),
            pltpu.VMEM((tree, width), bf),
            pltpu.VMEM((D, 3 * width), bf),
            pltpu.VMEM((D, width), bf),
            pltpu.VMEM((fsdp * half, D), bf),
            pltpu.VMEM((fsdp * half, D), bf),
            pltpu.VMEM(((fsdp - 1) * half, D), bf),
            pltpu.VMEM((fsdp * half, D), bf),
            pltpu.VMEM((fsdp * half, D), bf),
            pltpu.VMEM(((fsdp - 1) * half, D), bf),
            pltpu.VMEM((half, D), bf),
            pltpu.VMEM((rows, D), bf),
            pltpu.VMEM((half, D), bf),
            pltpu.VMEM((rows, D), bf),
            pltpu.VMEM((rows, D), f32),
            pltpu.VMEM((rows, width), bf),
            pltpu.VMEM((width, rows), bf),
            pltpu.VMEM((8, rows), f32),
            pltpu.VMEM((width, rows), bf),
            pltpu.VMEM((width, rows), f32),
            pltpu.VMEM((rows, 2 * width), bf),
            pltpu.VMEM((rows, rows), f32),
            pltpu.VMEM((rows, D), bf),
            pltpu.VMEM((contexts * half, D), bf),
            pltpu.VMEM((contexts * half, D), bf),
            pltpu.VMEM((contexts * half, D), bf),
            pltpu.VMEM((contexts * half, D), bf),
            pltpu.VMEM((rows, D), bf),
            dma((2, moves)),
            dma((2, moves)),
            dma((contexts,)),
            dma((contexts,)),
            dma((3, slots)),
            dma((3, slots)),
            dma((contexts,)),
            dma((contexts,)),
            dma((3, slots)),
            dma((5, contexts)),
        ],
        name="backward",
        compiler_params=pltpu.CompilerParams(
            collective_id=3, has_side_effects=True, vmem_limit_bytes=62 << 20
        ),
    )(*remote, *local)


def reduce_kernel(
    sizes, packed, table_all, out, inbox, z_out, z_in, total, f_in, send_sems, recv_sems
):
    fsdp, contexts, _ = sizes
    f, c, t = place_of()
    f32, bf = jnp.float32, jnp.bfloat16
    peers = [(lax.rem(f + k, fsdp), c, t) for k in range(1, fsdp)]
    stacked = [(f, lax.rem(c + k, contexts), t) for k in range(1, contexts)]
    sibling = (f, c, 1 - t)
    greet(peers + stacked + [sibling])
    order = [lax.rem(c + k, contexts) for k in range(1, contexts)] + [c]
    pair = []
    for k, block in enumerate(order):
        copy = send(
            packed.at[block, 1 - t], inbox.at[block], send_sems.at[0, k], recv_sems.at[0, k], sibling
        )
        copy.start()
        pair.append(copy)
    across = []
    for k, other in enumerate(stacked):
        pair[k].wait_recv()
        z_out[k] = (packed[order[k], t] + inbox[order[k]]).astype(bf)
        copy = send(z_out.at[k], z_in.at[k], send_sems.at[1, k], recv_sems.at[1, k], other)
        copy.start()
        across.append(copy)
    pair[-1].wait_recv()
    result = packed[c, t] + inbox[c]
    for k, copy in enumerate(across):
        copy.wait_recv()
        result = result + z_in[k].astype(f32)
    total[...] = result.astype(bf)
    ends = []
    for k, peer in enumerate(peers):
        copy = send(total, f_in.at[k], send_sems.at[2, k], recv_sems.at[2, k], peer)
        copy.start()
        ends.append(copy)
    own = ADAPTERS // fsdp
    wanted = [(f * own + a).astype(f32) for a in range(own)]
    sums = [jnp.where(table_all[f, 4:5, 0:1] == w, total[...].astype(f32), 0.0) for w in wanted]
    for k, copy in enumerate(ends):
        copy.wait_recv()
        tree = table_all[lax.rem(f - k - 1 + fsdp, fsdp), 4:5, 0:1]
        block = f_in[k].astype(f32)
        sums = [s + jnp.where(tree == w, block, 0.0) for s, w in zip(sums, wanted)]
    for a in range(own):
        out[a] = sums[a]
    for copy in pair + across + ends:
        copy.wait_send()


def reduce_call(sizes, packed, table_all):
    fsdp, contexts, _ = sizes
    block = packed.shape[2:]
    vmem = pl.BlockSpec(memory_space=pltpu.VMEM)
    bf, f32 = jnp.bfloat16, jnp.float32
    slots = max(fsdp, contexts)
    return pl.pallas_call(
        functools.partial(reduce_kernel, sizes),
        in_specs=[vmem, vmem],
        out_specs=vmem,
        out_shape=jax.ShapeDtypeStruct((ADAPTERS // fsdp,) + block, f32),
        scratch_shapes=[
            pltpu.VMEM((contexts,) + block, f32),
            pltpu.VMEM((contexts - 1,) + block, bf),
            pltpu.VMEM((contexts - 1,) + block, bf),
            pltpu.VMEM(block, bf),
            pltpu.VMEM((fsdp - 1,) + block, bf),
            pltpu.SemaphoreType.DMA((3, slots)),
            pltpu.SemaphoreType.DMA((3, slots)),
        ],
        name="adapter_sums",
        compiler_params=pltpu.CompilerParams(
            collective_id=4, has_side_effects=True, vmem_limit_bytes=60 << 20
        ),
    )(packed, table_all)


def shards(
    tokens,
    attn_gain,
    w_qkv,
    w_out,
    ffn_gain,
    w_gu,
    w_dn,
    w_egu,
    w_edn,
    adapters,
    adapter_ids,
    parents,
    seg_lengths,
    routes,
    route_weights,
    cotangent,
):
    tree_count, row_count = tokens.shape[:2]
    contexts = lax.axis_size("context")
    tensors = lax.axis_size("tensor")
    fsdp_size = lax.axis_size("fsdp")
    sizes = (fsdp_size, contexts, tensors)
    local_width = w_qkv.shape[2]
    local_ff = w_dn.shape[0]
    part_index = lax.axis_index("tensor")
    width_start = part_index * local_width
    ff_start = part_index * local_ff
    own_adapters = adapters.shape[0]
    own_width = D // fsdp_size
    gains = jnp.broadcast_to(jnp.concatenate([attn_gain, ffn_gain])[None], (16, 2 * own_width))
    route_table = jnp.concatenate(
        [
            routes[0].astype(jnp.float32).T,
            route_weights[0].astype(jnp.float32).T,
            jnp.broadcast_to(adapter_ids.astype(jnp.float32)[:, None], (1, row_count)),
            jnp.zeros((3, row_count), jnp.float32),
        ]
    )
    lines = adapters.shape[1] // 128
    padded = (lines + 15) // 16 * 16
    adapter_rows = jnp.pad(
        adapters.reshape(own_adapters, lines, 128), ((0, 0), (0, padded - lines), (0, 0))
    ).reshape(own_adapters * padded, 128)
    half_dim = HEAD_DIM // 2
    frequency = rope_base ** (-(jnp.arange(half_dim, dtype=jnp.float32) * 2.0) / HEAD_DIM)
    signs = jnp.concatenate([-jnp.ones((half_dim,)), jnp.ones((half_dim,))])
    turns = jnp.concatenate(
        [jnp.tile(frequency, 4)[None], jnp.tile(signs, 2)[None], jnp.zeros((6, 128))]
    ).astype(jnp.float32)
    sharded = (
        tokens[0],
        cotangent[0],
        w_qkv.reshape(own_width, 3 * local_width),
        w_out.T,
        w_gu.reshape(own_width, 2 * local_ff),
        w_dn.T,
    )
    (
        n1_all,
        k_all,
        v_all,
        wq_all,
        wo_all,
        normed_all,
        cotangent_all,
        q_t,
        q_n,
        mixed_own,
        o_t,
        lse,
        resid,
        shared_half,
        dn2_half,
        da_gu_t,
        db_gu_own,
        da_dn_t,
        db_dn_own,
        gains_full,
        cosine,
        sinus,
        hot,
        reach_t,
        a_qkv,
        b_qkv2,
        a_qkv_t2,
        a_o,
        b_o2,
        a_o_t2,
        table_all,
        place_row,
        place_col,
        weight_col,
        marks,
    ) = forward_call(
        sizes,
        sharded,
        (adapter_rows, gains, route_table, turns, adapter_ids, parents, seg_lengths),
    )
    own_experts = EXPERTS // fsdp_size
    starts = marks[:own_experts].astype(jnp.int32)
    moe_all, moe_back_all = moe_call(
        starts,
        place_row,
        place_col,
        weight_col,
        normed_all,
        cotangent_all,
        w_egu.transpose(0, 2, 1, 3),
        w_edn,
    )
    remote = (moe_all, moe_back_all, n1_all, k_all, v_all, wq_all, wo_all, cosine, sinus)
    block_out, input_grad, da_qkv_t, db_qkv_own, da_o_t, db_o_own = backward_call(
        sizes,
        remote,
        (tokens[0], cotangent[0], gains_full, hot, reach_t)
        + (resid, shared_half, dn2_half, q_t, q_n, mixed_own, o_t, lse)
        + (a_qkv, b_qkv2, a_qkv_t2, a_o, a_o_t2, b_o2),
    )
    block_out = block_out[None]
    input_grad = input_grad[None]
    grad_a_qkv = da_qkv_t.T[None]
    grad_b_qkv = lax.dynamic_update_slice_in_dim(
        jnp.zeros((tree_count, 3, RANK, D), jnp.float32),
        db_qkv_own.reshape(1, 3, RANK, local_width),
        width_start,
        3,
    )
    grad_a_out = lax.dynamic_update_slice_in_dim(
        jnp.zeros((tree_count, D, RANK), jnp.float32), da_o_t.T[None], width_start, 1
    )
    output_adapter_up_gradient = db_o_own[None]
    grad_a_gu = da_gu_t.T[None]
    grad_b_gu = lax.dynamic_update_slice_in_dim(
        jnp.zeros((tree_count, 2, RANK, FF), jnp.float32),
        db_gu_own.reshape(1, 2, RANK, local_ff),
        ff_start,
        3,
    )
    grad_a_dn = lax.dynamic_update_slice_in_dim(
        jnp.zeros((tree_count, FF, RANK), jnp.float32), da_dn_t.T[None], ff_start, 1
    )
    down_adapter_up_gradient = db_dn_own[None]
    grad_pieces = [
        grad_a_qkv,
        grad_b_qkv,
        grad_a_out,
        output_adapter_up_gradient,
        grad_a_gu,
        grad_b_gu,
        grad_a_dn,
        down_adapter_up_gradient,
    ]
    packed = jnp.concatenate([piece.reshape(tree_count, -1) for piece in grad_pieces], axis=1)
    adapter_grads = reduce_call(
        sizes, packed[0].reshape(contexts, tensors, RANK, -1), table_all
    ).reshape(own_adapters, -1)
    return (block_out, input_grad, adapter_grads)


def solution(mesh):
    return jax.shard_map(
        shards,
        mesh=mesh,
        in_specs=(
            P("fsdp", "context", None),
            P("fsdp"),
            P("fsdp", None, "tensor"),
            P("tensor", "fsdp"),
            P("fsdp"),
            P("fsdp", None, "tensor"),
            P("tensor", "fsdp"),
            P("fsdp", None, None, "tensor"),
            P("fsdp", "tensor", None),
            P("fsdp", ("context", "tensor")),
            P("fsdp"),
            P("fsdp", None),
            P("fsdp", None),
            P("fsdp", "context", None),
            P("fsdp", "context", None),
            P("fsdp", "context", None),
        ),
        out_specs=(
            P("fsdp", "context", None),
            P("fsdp", "context", None),
            P("fsdp", ("context", "tensor")),
        ),
        check_vma=False,
    )
```

```python
import jax
import jax.numpy as jnp
import functools
import math

from jax import lax
from jax.experimental import pallas as pl
from jax.experimental.pallas import tpu as pltpu
from jax.sharding import PartitionSpec as P

D = 768
HEADS = 12
HEAD_DIM = 64
FF = 2048
EXPERTS = 8
TOPK = 2
RANK = 16
ADAPTERS = 8
PARAMS = 233472


epsilon = 1e-06
adapter_scale = 2.0
rope_base = 10000.0
masked_score = -1e30
highest_precision = lax.Precision.HIGHEST


def rms_scale(values):
    return lax.rsqrt(jnp.mean(values * values, axis=-1, keepdims=True) + epsilon)


def norm_back(values, scaling, gain_values, gradient):
    weighted = gradient * gain_values
    inner_mean = jnp.mean(values * weighted, axis=-1, keepdims=True)
    return scaling * weighted - values * (scaling * scaling * scaling) * inner_mean


SLOT_TILE = 512
TOKEN_TILE = 256
SLOT_WINDOW = 128
AHEAD = 1


def nt_dot(left, right):
    return lax.dot_general(left, right, (((1,), (1,)), ((), ())), preferred_element_type=jnp.float32)


def tn_dot(left, right):
    return lax.dot_general(left, right, (((0,), (0,)), ((), ())), preferred_element_type=jnp.float32)


def nn_dot(left, right):
    return jnp.dot(left, right, preferred_element_type=jnp.float32)


def moe_kernel(
    starts,
    place_row,
    place_hbm,
    weight_hbm,
    rows_hbm,
    grads_hbm,
    egu_hbm,
    edn_hbm,
    out_hbm,
    back_hbm,
    place_col,
    weight_col,
    rows_ref,
    grads_ref,
    egu_ref,
    edn_ref,
    out_ref,
    back_ref,
    taken,
    taken_grad,
    taken_weight,
    sems,
    block_sems,
):
    f32, bf = jnp.float32, jnp.bfloat16
    experts = egu_hbm.shape[0]
    blocks = rows_ref.shape[0] // TOKEN_TILE

    def block_rows(b):
        return pl.ds(pl.multiple_of(b * TOKEN_TILE, TOKEN_TILE), TOKEN_TILE)

    def loads(b):
        block = block_rows(b)
        return [
            pltpu.make_async_copy(source.at[block], target.at[block], block_sems.at[i, b])
            for i, (source, target) in enumerate(
                ((rows_hbm, rows_ref), (grads_hbm, grads_ref), (weight_hbm, weight_col))
            )
        ]

    def stores(b):
        block = block_rows(b)
        return [
            pltpu.make_async_copy(source.at[block], target.at[block], block_sems.at[3 + i, b])
            for i, (source, target) in enumerate(((out_ref, out_hbm), (back_ref, back_hbm)))
        ]

    def weights(e):
        return [
            pltpu.make_async_copy(egu_hbm.at[e], egu_ref.at[e], sems.at[0, e]),
            pltpu.make_async_copy(edn_hbm.at[e], edn_ref.at[e], sems.at[1, e]),
        ]

    def each(count, copies, action):
        def step(i, carry):
            for copy in copies(i):
                getattr(copy, action)()
            return carry

        lax.fori_loop(0, count, step, 0)

    each(blocks, loads, "start")
    each(experts, weights, "start")
    place_copy = pltpu.make_async_copy(place_hbm, place_col, sems.at[2, 0])
    place_copy.start()
    taken[...] = jnp.zeros_like(taken)
    taken_grad[...] = jnp.zeros_like(taken_grad)
    taken_weight[...] = jnp.zeros_like(taken_weight)
    slot_rows = lax.broadcasted_iota(jnp.int32, (SLOT_WINDOW, TOKEN_TILE), 0).astype(f32)
    slot_cols = lax.broadcasted_iota(jnp.int32, (TOKEN_TILE, SLOT_WINDOW), 1).astype(f32)

    def windows(e, b):
        begin = starts[e, b] // 16 * 16
        return begin, (starts[e, b + 1] - begin + SLOT_WINDOW - 1) // SLOT_WINDOW

    def window_rows(begin, i):
        return pl.ds(pl.multiple_of(begin + i * SLOT_WINDOW, 16), SLOT_WINDOW)

    def fetch(b, carry):
        block = block_rows(b)
        for copy in loads(b):
            copy.wait()

        def take(which):
            picks = []
            for e, first in which:
                hit = place_row[e : e + 1, block] == slot_rows + first.astype(f32)
                picks.append(jnp.where(hit, 1.0, 0.0).astype(bf))
            pick = picks[0] if len(picks) == 1 else jnp.concatenate(picks, axis=0)
            for source, target in (
                (rows_ref, taken),
                (grads_ref, taken_grad),
                (weight_col, taken_weight),
            ):
                got = nn_dot(pick, source[block, :]).astype(bf)
                for i, (e, first) in enumerate(which):
                    slots = window_rows(first, 0)
                    target[e, slots, :] += got[i * SLOT_WINDOW : (i + 1) * SLOT_WINDOW, :]

        spans = [windows(e, b) for e in range(experts)]
        take([(e, spans[e][0]) for e in range(experts)])
        for e in range(experts):

            def more(i, c, e=e):
                take([(e, spans[e][0] + i * SLOT_WINDOW)])
                return c

            lax.fori_loop(1, spans[e][1], more, 0)
        return carry

    lax.fori_loop(0, blocks, fetch, 0)

    def tile(e, start, size):
        slots = pl.ds(pl.multiple_of(start, 128), size)
        inputs = taken[e, slots, :]
        gate_pre = nn_dot(inputs, egu_ref[e, 0])
        up_pre = nn_dot(inputs, egu_ref[e, 1])
        sigmoid_gate = jax.nn.sigmoid(gate_pre)
        silu = gate_pre * sigmoid_gate
        active = (silu * up_pre).astype(bf)
        taken[e, slots, :] = nn_dot(active, edn_ref[e]).astype(bf)
        grad_active = nt_dot(taken_grad[e, slots, :], edn_ref[e])
        lane = lax.broadcasted_iota(jnp.int32, (size, 128), 1)
        scale = jnp.sum(
            jnp.where(lane == e, taken_weight[e, slots, :].astype(f32), 0.0), axis=1, keepdims=True
        )
        grad_active = grad_active * scale
        grad_gate = (
            grad_active * up_pre * sigmoid_gate * (1.0 + gate_pre * (1.0 - sigmoid_gate))
        ).astype(bf)
        grad_up = (grad_active * silu).astype(bf)
        taken_grad[e, slots, :] = (
            nt_dot(grad_gate, egu_ref[e, 0]) + nt_dot(grad_up, egu_ref[e, 1])
        ).astype(bf)

    def expert_step(e, carry):
        for copy in weights(e):
            copy.wait()
        count = starts[e, blocks]
        whole = count // SLOT_TILE
        rest = count - whole * SLOT_TILE

        def step(i, c):
            tile(e, i * SLOT_TILE, SLOT_TILE)
            return c

        lax.fori_loop(0, whole + jnp.where(rest > SLOT_TILE - 128, 1, 0), step, 0)
        for size in range(128, SLOT_TILE, 128):

            @pl.when((rest > size - 128) & (rest <= size))
            def _(size=size):
                tile(e, whole * SLOT_TILE, size)

        return carry

    lax.fori_loop(0, experts, expert_step, 0)
    place_copy.wait()

    def give(b, carry):
        block = block_rows(b)

        def hand(which):
            plain, scaled, values, values_grad = [], [], [], []
            for e, first in which:
                hit = place_col[block, e : e + 1] == slot_cols + first.astype(f32)
                plain.append(jnp.where(hit, 1.0, 0.0).astype(bf))
                weight = weight_col[block, e : e + 1].astype(f32)
                scaled.append(jnp.where(hit, weight, 0.0).astype(bf))
                values.append(taken[e, window_rows(first, 0), :])
                values_grad.append(taken_grad[e, window_rows(first, 0), :])

            def join(pieces, axis):
                return pieces[0] if len(pieces) == 1 else jnp.concatenate(pieces, axis=axis)

            return (
                nn_dot(join(scaled, 1), join(values, 0)),
                nn_dot(join(plain, 1), join(values_grad, 0)),
            )

        spans = [windows(e, b) for e in range(experts)]
        first, second = hand([(e, spans[e][0]) for e in range(experts)])
        out_ref[block, :] = first.astype(bf)
        back_ref[block, :] = second.astype(bf)
        for e in range(experts):

            def more(i, c, e=e):
                first, second = hand([(e, spans[e][0] + i * SLOT_WINDOW)])
                out_ref[block, :] = (out_ref[block, :].astype(f32) + first).astype(bf)
                back_ref[block, :] = (back_ref[block, :].astype(f32) + second).astype(bf)
                return c

            lax.fori_loop(1, spans[e][1], more, 0)
        for copy in stores(b):
            copy.start()
        return carry

    lax.fori_loop(0, blocks, give, 0)
    each(blocks, stores, "wait")


def moe_call(starts, place_row, place_col, weight_col, rows, grads, egu, edn):
    total, width = rows.shape
    experts = egu.shape[0]
    slots = total // 2 + SLOT_TILE
    blocks = total // TOKEN_TILE
    bf, f32 = jnp.bfloat16, jnp.float32
    vmem = pl.BlockSpec(memory_space=pltpu.VMEM)
    hbm = pl.BlockSpec(memory_space=pl.ANY)
    shape = jax.ShapeDtypeStruct((total, width), bf)
    return pl.pallas_call(
        moe_kernel,
        grid_spec=pltpu.PrefetchScalarGridSpec(
            num_scalar_prefetch=1,
            grid=(),
            in_specs=[vmem] + [hbm] * 6,
            out_specs=[hbm, hbm],
            scratch_shapes=[
                pltpu.VMEM((total, 128), f32),
                pltpu.VMEM((total, 128), bf),
                pltpu.VMEM((total, width), bf),
                pltpu.VMEM((total, width), bf),
                pltpu.VMEM(egu.shape, bf),
                pltpu.VMEM(edn.shape, bf),
                pltpu.VMEM((total, width), bf),
                pltpu.VMEM((total, width), bf),
                pltpu.VMEM((experts, slots, width), bf),
                pltpu.VMEM((experts, slots, width), bf),
                pltpu.VMEM((experts, slots, 128), bf),
                pltpu.SemaphoreType.DMA((3, experts)),
                pltpu.SemaphoreType.DMA((5, blocks)),
            ],
        ),
        out_shape=[shape, shape],
        name="experts",
        compiler_params=pltpu.CompilerParams(vmem_limit_bytes=62 << 20),
    )(starts, place_row, place_col, weight_col, rows, grads, egu, edn)


MESH = pl.DeviceIdType.MESH


def place_of():
    return lax.axis_index("fsdp"), lax.axis_index("context"), lax.axis_index("tensor")


def greet(devices):
    barrier = pltpu.get_barrier_semaphore()
    for device in devices:
        pl.semaphore_signal(barrier, inc=1, device_id=device, device_id_type=MESH)
    pl.semaphore_wait(barrier, len(devices))


def send(source, target, send_sem, recv_sem, device):
    return pltpu.make_async_remote_copy(
        src_ref=source,
        dst_ref=target,
        send_sem=send_sem,
        recv_sem=recv_sem,
        device_id=device,
        device_id_type=MESH,
    )


def flip(index, bit):
    return index + (1 - 2 * lax.rem(index // (1 << bit), 2)) * (1 << bit)


def split_rows(count):
    first = (count // 2 + 15) // 16 * 16
    return ((0, first), (first, count - first))


class Gather:
    def __init__(self, bits, me, device_of, own, buf, stride, base, count, send_sems, recv_sems):
        self.stages = [[] for _ in range(bits)]
        self.arrived = [[] for _ in range(bits)]
        self.passed = [[] for _ in range(bits)]
        number = 0
        for half, (offset, size) in enumerate(split_rows(count)):
            held = [me]
            for stage in range(bits):
                bit = (stage + half) % bits
                for block in held:
                    rows = self.rows(block * stride + base + offset, size)
                    source = own.at[self.rows(base + offset, size)] if block is me else buf.at[rows]
                    self.passed[stage].append(block is not me)
                    self.stages[stage].append(
                        send(
                            source,
                            buf.at[rows],
                            send_sems.at[number],
                            recv_sems.at[number],
                            device_of(flip(me, bit)),
                        )
                    )
                    self.arrived[stage].append(
                        self.rows(flip(block, bit) * stride + base + offset, size)
                    )
                    number = number + 1
                held = held + [flip(block, bit) for block in held]

    @staticmethod
    def rows(start, size):
        return pl.ds(pl.multiple_of(start, 16), size)

    def start(self, stage):
        if stage == 0:
            for copies, passed in zip(self.stages, self.passed):
                for copy, later in zip(copies, passed):
                    if not later:
                        copy.start()
        else:
            for copy, later in zip(self.stages[stage], self.passed[stage]):
                if later:
                    copy.start()

    def wait(self, stage):
        for copy in self.stages[stage]:
            copy.wait_recv()

    def finish(self):
        for stage in self.stages:
            for copy in stage:
                copy.wait_send()


def turn(values, cosine, sinus):
    lane = lax.broadcasted_iota(jnp.int32, values.shape, 1)
    first = lax.rem(lane, HEAD_DIM) < HEAD_DIM // 2
    swapped = jnp.where(
        first,
        pltpu.roll(values, 128 - HEAD_DIM // 2, 1),
        pltpu.roll(values, HEAD_DIM // 2, 1),
    )
    return values * cosine + swapped * sinus


def two_parts(values):
    high = values.astype(jnp.bfloat16)
    low = (values - high.astype(jnp.float32)).astype(jnp.bfloat16)
    return jnp.concatenate([high, low], axis=1)


def normed(values, gain):
    scale = lax.rsqrt(jnp.mean(values * values, axis=-1, keepdims=True) + epsilon)
    return (values * scale * gain).astype(jnp.bfloat16)


def fill_bias(bias, hot_rows, reach_t, key_start, query_start):
    seen = nn_dot(hot_rows, reach_t)
    keys = key_start + lax.broadcasted_iota(jnp.int32, seen.shape, 0)
    queries = query_start + lax.broadcasted_iota(jnp.int32, seen.shape, 1)
    bias[...] = jnp.where((seen > 0.5) & (keys <= queries), 0.0, masked_score)


def head_half(shape, axis, odd):
    index = lax.broadcasted_iota(jnp.int32, shape, axis)
    return (index >= HEAD_DIM) if odd else (index < HEAD_DIM)


def tree_tables(parents, lengths, turns, context, rows, hot, reach_t, cosine, sinus):
    lane = lax.broadcasted_iota(jnp.int32, (1, 128), 1)
    far = jnp.full((1, 128), 1 << 30, jnp.int32)
    none = jnp.zeros((1, 128), jnp.int32)
    begins, ends, moves = far, far, none
    first, second = none - 1, none - 1
    start = jnp.int32(0)
    for s in range(parents.shape[1]):
        parent = parents[0, s]
        grand = parents[0, parent]
        here = lane == s
        above = jnp.where(parent != s, lengths[0, parent], 0) + jnp.where(
            (grand != s) & (grand != parent), lengths[0, grand], 0
        )
        begins = jnp.where(here, start, begins)
        moves = jnp.where(here, above - start, moves)
        first = jnp.where(here, parent, first)
        second = jnp.where(here, grand, second)
        start = start + lengths[0, s]
        ends = jnp.where(here, start, ends)
    over = lax.broadcasted_iota(jnp.int32, (128, 128), 0)
    under = lax.broadcasted_iota(jnp.int32, (128, 128), 1)
    ancestors = jnp.where((over == under) | (over == first) | (over == second), 1.0, 0.0).astype(
        jnp.bfloat16
    )

    def fill(chunk, carry):
        block = pl.ds(pl.multiple_of(chunk * rows, 16), rows)
        row = chunk * rows + lax.broadcasted_iota(jnp.int32, (rows, 128), 0)
        inside = (row >= begins) & (row < ends)
        hot[block, :] = jnp.where(inside, 1.0, 0.0).astype(jnp.bfloat16)
        moved = jnp.sum(jnp.where(inside, moves.astype(jnp.float32), 0.0), axis=1, keepdims=True)
        angle = (row.astype(jnp.float32) + moved) * turns[0:1, :]
        cosine[block, :] = jnp.cos(angle)
        sinus[block, :] = jnp.sin(angle) * turns[1:2, :]
        return carry

    lax.fori_loop(0, context + 1, fill, 0)
    own = pl.ds(pl.multiple_of(context * rows, 16), rows)
    reach_t[...] = nt_dot(ancestors, hot[own, :]).astype(jnp.bfloat16)


def choose(ids, adapters_all, out):
    wanted = ids[0]
    own = ADAPTERS // adapters_all.shape[0]
    count = adapters_all.shape[1] // own
    total = jnp.zeros((count, 128), jnp.float32)
    for a in range(ADAPTERS):
        block = adapters_all[a // own, pl.ds((a % own) * count, count), :].astype(jnp.float32)
        total = total + jnp.where(wanted == a, block, 0.0)
    out[...] = total.astype(jnp.bfloat16)


def route_tables(f, table_all, place_row, place_col, weight_col, marks):
    fsdp, _, rows = table_all.shape
    own = EXPERTS // fsdp
    f32 = jnp.float32
    sub = lax.broadcasted_iota(jnp.int32, (8, rows), 0)
    expert = jnp.where(sub < own, f * own + sub, -1).astype(f32)
    before = lax.broadcasted_iota(jnp.int32, (rows, rows), 0)
    after = lax.broadcasted_iota(jnp.int32, (rows, rows), 1)
    upto = jnp.where(before <= after, 1.0, 0.0).astype(jnp.bfloat16)
    lane = lax.broadcasted_iota(jnp.int32, (8, 128), 1)
    base = jnp.zeros((8, 1), f32)
    found = jnp.zeros((8, 128), f32)
    more = jnp.zeros((120, rows), f32)
    for source in range(fsdp):
        table = table_all[source]
        one = table[0:1, :] == expert
        two = table[1:2, :] == expert
        hit = one | two
        weight = jnp.where(one, table[2:3, :], 0.0) + jnp.where(two, table[3:4, :], 0.0)
        count = nn_dot(jnp.where(hit, 1.0, 0.0).astype(jnp.bfloat16), upto) + base
        place = jnp.where(hit, count - 1.0, -1.0)
        block = slice(source * rows, (source + 1) * rows)
        place_row[:, block] = place
        place_col[block, :] = jnp.concatenate([place, more], axis=0).T
        weight_col[block, :] = jnp.concatenate([weight, more], axis=0).T.astype(jnp.bfloat16)
        for token in range(TOKEN_TILE - 1, fsdp * rows, TOKEN_TILE):
            if token // rows == source:
                at = token % rows
                found = jnp.where(lane == token // TOKEN_TILE + 1, count[:, at : at + 1], found)
        base = count[:, rows - 1 : rows]
    marks[...] = found


def unpack_adapter(t, per_block, chosen, flat, wide, first, second):
    a_qkv, b_qkv2, a_qkv_t2, a_o, b_o2, a_o_t2 = first
    a_gu, b_gu2, a_gu_t2, a_dn, a_dn_t2, b_dn2 = second
    f32, bf = jnp.float32, jnp.bfloat16
    contexts = chosen.shape[1]
    width, units = a_o.shape[0], a_dn.shape[0]
    count = PARAMS // 128 // (2 * contexts)
    for context in range(contexts):
        for part in range(2):
            start = (2 * context + part) * count
            flat[start : start + count, :] = chosen[part, context, 0:count, :].astype(f32)

    def spread(start, groups, rank, out, out_t):
        total = groups * 128 // rank
        wide[...] = jnp.zeros_like(wide)
        lines = rank // math.gcd(rank, 128)
        each = lines * 128 // rank
        for i in range(each):
            row, at = divmod(i * rank, 128)
            def line(number):
                if lines == 1:
                    return flat[pl.ds(start, groups), :]
                return flat[pl.ds(start + number, groups // lines, stride=lines), :]

            piece = line(row)[:, at : min(at + rank, 128)]
            if at + rank > 128:
                piece = jnp.concatenate([piece, line(row + 1)[:, 0 : at + rank - 128]], axis=1)
            wide[pl.ds(i, groups // lines, stride=each), 0:rank] = piece
        out[...] = wide[0:total, :].astype(bf)
        if out_t is not None:
            for p in range(total // 128):
                turned = wide[128 * p : 128 * p + 128, :].T.astype(bf)
                out_t[0:128, 128 * p : 128 * p + 128] = turned
                out_t[128:256, 128 * p : 128 * p + 128] = turned

    def stack(start, lines, columns, out, row, column):
        for p, m in enumerate(columns):
            piece = (2.0 * flat[pl.ds(start + m, RANK, stride=lines), :]).astype(bf)
            lanes = slice(column + 128 * p, column + 128 * p + 128)
            out[row : row + RANK, lanes] = piece
            out[128 + row : 128 + row + RANK, lanes] = piece

    for ref in (b_qkv2, b_o2, b_gu2, b_dn2):
        ref[...] = jnp.zeros_like(ref)
    at = 0
    spread(at, 3 * RANK * D // 128, 3 * RANK, a_qkv, a_qkv_t2)
    at = at + 3 * RANK * D // 128
    lines = D // 128
    mine = [t * (width // 128) + p for p in range(width // 128)]
    for j in range(3):
        stack(at + j * RANK * lines, lines, mine, b_qkv2, j * RANK, j * width)
    at = at + 3 * RANK * lines
    spread(at + t * (width * RANK // 128), width * RANK // 128, RANK, a_o, a_o_t2)
    at = at + D * RANK // 128
    stack(at, lines, list(range(lines)), b_o2, 0, 0)
    at = at + RANK * lines
    spread(at, 2 * RANK * D // 128, 2 * RANK, a_gu, a_gu_t2)
    at = at + 2 * RANK * D // 128
    wide_lines = FF // 128
    mine = [t * (units // 128) + p for p in range(units // 128)]
    for j in range(2):
        stack(at + j * RANK * wide_lines, wide_lines, mine, b_gu2, j * RANK, j * units)
    at = at + 2 * RANK * wide_lines
    spread(at + t * (units * RANK // 128), units * RANK // 128, RANK, a_dn, a_dn_t2)
    at = at + FF * RANK // 128
    stack(at, lines, list(range(lines)), b_dn2, 0, 0)


def forward_kernel(
    sizes,
    x_in,
    g_in,
    wq_in,
    wo_in,
    gu_in,
    dn_in,
    adapters_in,
    gains_in,
    table_in,
    turns,
    ids,
    parents,
    lengths,
    n1_all,
    k_all,
    v_all,
    wq_all,
    wo_all,
    n2_all,
    g_all,
    q_t_out,
    q_n_out,
    mixed_out,
    o_t_out,
    lse_out,
    resid_out,
    shared_out,
    dn2_out,
    da_gu,
    db_gu,
    da_dn,
    db_dn,
    gains_out,
    cosine_out,
    sinus_out,
    hot_out,
    reach_t_out,
    a_qkv_out,
    b_qkv2_out,
    a_qkv_t2_out,
    a_o_out,
    b_o2_out,
    a_o_t2_out,
    table_all_out,
    place_row_out,
    place_col_out,
    weight_col_out,
    marks,
    x_buf,
    wq,
    wo,
    gu,
    dn,
    g_own,
    n1_buf,
    k_buf,
    v_buf,
    v_t,
    peak,
    total,
    bias,
    part_out,
    part_in,
    n2_own,
    shared,
    dn2,
    adapters_all,
    gains_all,
    chosen,
    flat,
    a_wide,
    a_gu,
    b_gu2,
    a_gu_t2,
    a_dn,
    a_dn_t2,
    b_dn2,
    fs_send,
    fs_recv,
    z_send,
    z_recv,
    core_send,
    core_recv,
    local_sems,
    chunk_sems,
    small_send,
    small_recv,
    lend_send,
    lend_recv,
    q_t,
    q_n,
    mixed,
    o_t,
    lse,
    resid,
    gains,
    cosine,
    sinus,
    hot,
    reach_t,
    a_qkv,
    b_qkv2,
    a_qkv_t2,
    a_o,
    b_o2,
    a_o_t2,
    table_all,
    place_row,
    place_col,
    weight_col,
    out_sems,
):
    fsdp, contexts, _ = sizes
    bits = fsdp.bit_length() - 1
    f, c, t = place_of()
    rows = x_in.shape[0]
    half = rows // 2
    heads = q_t.shape[0] // HEAD_DIM
    width = q_t.shape[0]
    units = dn_in.shape[1]
    own_n = wq_in.shape[0]
    sibling = (f, c, 1 - t)

    def peer(index):
        return (index, c, t)

    peers = [(lax.rem(f + k, fsdp), c, t) for k in range(1, fsdp)]
    stacked = [(f, lax.rem(c + k, contexts), t) for k in range(1, contexts)]
    greet(peers + stacked + [sibling])

    targets = (
        (q_t, q_t_out),
        (q_n, q_n_out),
        (mixed, mixed_out),
        (o_t, o_t_out),
        (lse, lse_out),
        (resid, resid_out),
        (shared, shared_out),
        (dn2, dn2_out),
        (gains, gains_out),
        (cosine, cosine_out),
        (sinus, sinus_out),
        (hot, hot_out),
        (reach_t, reach_t_out),
        (a_qkv, a_qkv_out),
        (b_qkv2, b_qkv2_out),
        (a_qkv_t2, a_qkv_t2_out),
        (a_o, a_o_out),
        (b_o2, b_o2_out),
        (a_o_t2, a_o_t2_out),
        (table_all, table_all_out),
        (place_row, place_row_out),
        (place_col, place_col_out),
        (weight_col, weight_col_out),
    )
    given = []

    def give_out(refs):
        for i, (ref, target) in enumerate(targets):
            if any(ref is other for other in refs):
                copy = pltpu.make_async_copy(ref, target, out_sems.at[i])
                copy.start()
                given.append(copy)

    def half_rows(chunk, part):
        return pl.ds(pl.multiple_of(chunk * rows + part * half, 16), half)

    def up(chunk, source):
        return send(
            source,
            x_buf.at[half_rows(chunk, t)],
            z_send.at[chunk],
            z_recv.at[chunk],
            (f, c + 1, t),
        )

    def across(chunk):
        block = x_buf.at[half_rows(chunk, t)]
        return send(block, block, core_send.at[chunk], core_recv.at[chunk], sibling)

    @pl.when(c < contexts - 1)
    def _():
        up(c, x_in.at[half_rows(0, t)]).start()

    gathers = []
    halved = (False, False, True, False)
    neighbour = (f, c + 1 - 2 * lax.rem(c, 2), t)
    own_half = own_n // 2
    for i, (own, buf) in enumerate(((wq_in, wq), (wo_in, wo), (gu_in, gu), (dn_in, dn))):
        base, count = (lax.rem(c, 2) * own_half, own_half) if halved[i] else (0, own_n)
        gathers.append(
            Gather(bits, f, peer, own, buf, own_n, base, count, fs_send.at[i], fs_recv.at[i])
        )

    def lent(gather, buf, which):
        copies, number = [], 0
        for stage in range(bits):
            group = []
            for block in gather.arrived[stage]:
                group.append(
                    send(
                        buf.at[block],
                        buf.at[block],
                        lend_send.at[which, number],
                        lend_recv.at[which, number],
                        neighbour,
                    )
                )
                number = number + 1
            copies.append(group)
        return copies

    gu_lent = lent(gathers[2], gu, 0)

    z_busy = (lax.rem(c, 2) == 0) & (c > 0)

    def lend(copies, stage):
        for copy in copies[stage]:
            copy.start()
    g_gather = Gather(
        bits, f, peer, g_in, g_all, rows, t * half, half, fs_send.at[4], fs_recv.at[4]
    )
    n2_gather = Gather(
        bits, f, peer, n2_own, n2_all, rows, t * half, half, fs_send.at[5], fs_recv.at[5]
    )
    wq_gather, wo_gather, gu_gather, dn_gather = gathers
    small = []
    for k, other in enumerate(peers):
        for j, (source, target) in enumerate(
            ((adapters_in, adapters_all), (gains_in, gains_all), (table_in, table_all))
        ):
            copy = send(source, target.at[f], small_send.at[j, k], small_recv.at[j, k], other)
            copy.start()
            small.append(copy)
    wq_gather.start(0)
    locals_ = [pltpu.make_async_copy(x_in, x_buf.at[pl.ds(c * rows, rows)], local_sems.at[0])]
    for i, (own, buf) in enumerate(((wq_in, wq), (wo_in, wo), (gu_in, gu), (dn_in, dn))):
        locals_.append(
            pltpu.make_async_copy(own, buf.at[pl.ds(f * own_n, own_n)], local_sems.at[1 + i])
        )
    locals_.append(pltpu.make_async_copy(g_in, g_own, local_sems.at[5]))
    locals_.append(
        pltpu.make_async_copy(g_in, g_all.at[pl.ds(f * rows, rows)], local_sems.at[6])
    )
    for copy in locals_:
        copy.start()

    o_t[...] = jnp.zeros_like(o_t)
    peak[...] = jnp.full_like(peak, masked_score)
    total[...] = jnp.zeros_like(total)
    da_gu[...] = jnp.zeros_like(da_gu)
    db_gu[...] = jnp.zeros_like(db_gu)
    da_dn[...] = jnp.zeros_like(da_dn)
    db_dn[...] = jnp.zeros_like(db_dn)
    adapters_all[f] = adapters_in[...]
    gains_all[f] = gains_in[...]
    table_all[f] = table_in[...]
    tree_tables(parents, lengths, turns, c, rows, hot, reach_t, cosine, sinus)

    def receive(step):
        chunk = c - step

        @pl.when(step <= c)
        def _():
            up(chunk, x_buf.at[half_rows(chunk, t)]).wait_recv()

            @pl.when(c < contexts - 1)
            def _():
                up(chunk, x_buf.at[half_rows(chunk, t)]).start()

            across(chunk).start()

    def chunk_rows(chunk):
        return pl.ds(pl.multiple_of(chunk * rows, 16), rows)

    def out_copies(chunk):
        block = chunk_rows(chunk)
        return [
            pltpu.make_async_copy(n1_buf.at[block], n1_all.at[block], chunk_sems.at[0, chunk]),
            pltpu.make_async_copy(k_buf.at[block], k_all.at[block], chunk_sems.at[1, chunk]),
            pltpu.make_async_copy(v_buf.at[block], v_all.at[block], chunk_sems.at[2, chunk]),
        ]

    def project(chunk, own):
        block = chunk_rows(chunk)
        n1 = normed(x_buf[block, :].astype(jnp.float32), gain_one)
        n1_buf[block, :] = n1
        rank = two_parts(nn_dot(n1, a_qkv[...]))
        cos_rows = cosine[block, :]
        sin_rows = sinus[block, :]
        for p in range(width // 128):
            cols = slice(width + 128 * p, width + 128 * p + 128)
            key = nn_dot(n1, wq[:, cols]) + nn_dot(rank, b_qkv2[:, cols])
            k_buf[block, 128 * p : 128 * p + 128] = turn(key, cos_rows, sin_rows).astype(
                jnp.bfloat16
            )
            cols = slice(2 * width + 128 * p, 2 * width + 128 * p + 128)
            value = nn_dot(n1, wq[:, cols]) + nn_dot(rank, b_qkv2[:, cols])
            v_buf[block, 128 * p : 128 * p + 128] = value.astype(jnp.bfloat16)
            v_t[128 * p : 128 * p + 128, :] = value.T.astype(jnp.bfloat16)
            if own:
                cols = slice(128 * p, 128 * p + 128)
                query = nn_dot(n1, wq[:, cols]) + nn_dot(rank, b_qkv2[:, cols])
                query = turn(query, cos_rows, sin_rows) * 0.125
                q_n[:, cols] = query.astype(jnp.bfloat16)
                q_t[cols, :] = query.T.astype(jnp.bfloat16)
        for copy in out_copies(chunk):
            copy.start()

    def attend(chunk):
        block = chunk_rows(chunk)
        fill_bias(bias, hot[block, :], reach_t[...], chunk * rows, c * rows)

        def pair_step(p, carry):
            lanes = pl.ds(pl.multiple_of(p * 128, 128), 128)
            keys = k_buf[block, lanes]
            query = q_t[lanes, :]
            for odd in range(2):
                h = 2 * p + odd
                alone = jnp.where(
                    head_half(query.shape, 0, odd), query, jnp.zeros_like(query)
                )
                scores = nn_dot(keys, alone) + bias[...]
                before = peak[pl.ds(h, 1), :]
                now = jnp.maximum(before, jnp.max(scores, axis=0, keepdims=True))
                weights = jnp.exp(scores - now)
                shrink = jnp.exp(before - now)
                peak[pl.ds(h, 1), :] = now
                total[pl.ds(h, 1), :] = total[pl.ds(h, 1), :] * shrink + jnp.sum(
                    weights, axis=0, keepdims=True
                )
                head = pl.ds(pl.multiple_of(h * HEAD_DIM, HEAD_DIM), HEAD_DIM)
                o_t[head, :] = o_t[head, :] * shrink + nn_dot(
                    v_t[head, :], weights.astype(jnp.bfloat16)
                )
            return carry

        lax.fori_loop(0, heads // 2, pair_step, 0)

    def advance(gather, following, copies=None):
        gather.wait(0)
        for stage in range(1, bits):
            gather.start(stage)
            if copies is not None:
                lend(copies, stage - 1)
            if stage < bits - 1:
                gather.wait(stage)
        following.start(0)

    for copy in small:
        copy.wait_recv()
    choose(ids, adapters_all, chosen.at[t, c])
    spread = []
    for k, other in enumerate(stacked):
        block = chosen.at[t, c]
        copy = send(block, block, small_send.at[3, k], small_recv.at[3, k], other)
        copy.start()
        spread.append(copy)
    gains[...] = jnp.zeros_like(gains)
    for i in range(2):
        pieces = [
            gains_all[b, 0:1, i * own_n : (i + 1) * own_n].astype(jnp.float32)
            for b in range(fsdp)
        ]
        gains[i : i + 1, :] = jnp.concatenate(pieces, axis=1)
    gain_one = gains[0:1, :]
    gain_two = gains[1:2, :]
    advance(wq_gather, wo_gather)
    receive(1)
    for copy in spread:
        copy.wait_recv()
    shared_copy = send(
        chosen.at[t], chosen.at[t], small_send.at[4, 0], small_recv.at[4, 0], sibling
    )
    shared_copy.start()
    route_tables(f, table_all, place_row, place_col, weight_col, marks)
    give_out(
        (table_all, place_row, place_col, weight_col, gains, cosine, sinus, hot, reach_t)
    )
    advance(wo_gather, gu_gather)
    shared_copy.wait_recv()
    unpack_adapter(
        t,
        adapters_in.shape[0] // (ADAPTERS // fsdp),
        chosen,
        flat,
        a_wide,
        (a_qkv, b_qkv2, a_qkv_t2, a_o, b_o2, a_o_t2),
        (a_gu, b_gu2, a_gu_t2, a_dn, a_dn_t2, b_dn2),
    )
    give_out((a_qkv, b_qkv2, a_qkv_t2, a_o, b_o2, a_o_t2))
    wq_gather.wait(bits - 1)
    locals_[0].wait()
    locals_[1].wait()
    wq_out = pltpu.make_async_copy(wq, wq_all, local_sems.at[10])
    wq_out.start()
    project(c, True)
    receive(2)
    attend(c)

    number = contexts

    def forwards(gather, buf, first):
        copies = []
        for stage in range(bits):
            group = []
            for block in gather.arrived[stage]:
                index = first + len(copies)
                copies.append(
                    send(
                        buf.at[block],
                        buf.at[block],
                        core_send.at[index],
                        core_recv.at[index],
                        sibling,
                    )
                )
        return copies

    per_stage = [len(stage) for stage in g_gather.arrived]
    g_forward = forwards(g_gather, g_all, number + 5)
    n2_forward = forwards(n2_gather, n2_all, number + 5 + sum(per_stage))

    def pass_on(copies, stage):
        start = sum(per_stage[:stage])
        for copy in copies[start : start + per_stage[stage]]:
            copy.start()

    def between(step):
        if step == 1:
            advance(gu_gather, dn_gather)

            @pl.when(jnp.logical_not(z_busy))
            def _():
                lend(gu_lent, 0)

        if step == 2:
            advance(dn_gather, g_gather)
            gu_gather.wait(bits - 1)

            @pl.when(z_busy)
            def _():
                lend(gu_lent, 0)

            for stage in range(1, bits):
                lend(gu_lent, stage)
        if step == 3:
            g_gather.wait(0)
            for stage in range(1, bits):
                g_gather.start(stage)
                pass_on(g_forward, stage - 1)
                if stage < bits - 1:
                    g_gather.wait(stage)

    def later(step):
        chunk = c - step

        @pl.when(step <= c)
        def _():
            across(chunk).wait_recv()
            project(chunk, False)
            receive(step + 2)
            attend(chunk)

    for step in range(1, 3):
        between(step)
        later(step)

    @pl.when(c >= 3)
    def _():
        between(3)
        later(3)

    def rest(step, carry):
        later(step)
        return carry

    lax.fori_loop(4, contexts, rest, 0)

    for h in range(heads):
        head = slice(h * HEAD_DIM, h * HEAD_DIM + HEAD_DIM)
        o_t[head, :] = o_t[head, :] / total[h : h + 1, :]
    lse[...] = peak[...] + jnp.log(total[...])
    for p in range(width // 128):
        mixed[:, 128 * p : 128 * p + 128] = o_t[128 * p : 128 * p + 128, :].T.astype(jnp.bfloat16)
    give_out((q_t, q_n, mixed, o_t, lse))
    wo_gather.wait(bits - 1)
    locals_[2].wait()
    wo_out = pltpu.make_async_copy(wo, wo_all, local_sems.at[11])
    wo_out.start()

    def local_rows(part):
        return pl.ds(pl.multiple_of(part * half, 16), half)

    mine = local_rows(t)
    theirs = local_rows(1 - t)

    def branch(block):
        values = mixed[block, :]
        rank = two_parts(nn_dot(values, a_o[...]))
        return nt_dot(values, wo[...]) + nn_dot(rank, b_o2[...])

    part_copies = []
    for i, block in enumerate((theirs, mine)):
        part_out[block, :] = branch(block).astype(jnp.bfloat16)
        copy = send(
            part_out.at[block],
            part_in.at[block],
            core_send.at[number + i],
            core_recv.at[number + i],
            sibling,
        )
        copy.start()
        part_copies.append(copy)

    def attended(block, copy):
        copy.wait_recv()
        resid[block, :] = x_rows(x_buf, c, rows, block) + (
            part_out[block, :].astype(jnp.float32) + part_in[block, :].astype(jnp.float32)
        )
        n2_own[block, :] = normed(resid[block, :], gain_two)

    attended(mine, part_copies[0])
    n2_gather.start(0)
    attended(theirs, part_copies[1])
    give_out((resid,))
    n2_out = pltpu.make_async_copy(n2_own, n2_all.at[pl.ds(f * rows, rows)], local_sems.at[12])
    n2_out.start()

    @pl.when(c < 3)
    def _():
        between(3)


    locals_[5].wait()
    for group in gu_lent:
        for copy in group:
            copy.wait_recv()
    locals_[3].wait()
    dn_gather.wait(bits - 1)
    locals_[4].wait()

    def shared_tile(block):
        inputs = n2_own[block, :]
        grads = g_own[block, :]
        rank = nn_dot(inputs, a_gu[...])
        rank2 = two_parts(rank)
        gate = nn_dot(inputs, gu[:, :units]) + nn_dot(rank2, b_gu2[:, :units])
        up_pre = nn_dot(inputs, gu[:, units:]) + nn_dot(rank2, b_gu2[:, units:])
        sigmoid_gate = jax.nn.sigmoid(gate)
        silu = gate * sigmoid_gate
        hidden = (silu * up_pre).astype(jnp.bfloat16)
        down_rank = nn_dot(hidden, a_dn[...])
        shared[block, :] = (
            nt_dot(hidden, dn[...]) + nn_dot(two_parts(down_rank), b_dn2[...])
        ).astype(jnp.bfloat16)
        down_back = nt_dot(grads, b_dn2[0:128, :])
        grad_hidden = nn_dot(grads, dn[...]) + nn_dot(two_parts(down_back), a_dn_t2[...])
        grad_gate = (
            grad_hidden * up_pre * sigmoid_gate * (1.0 + gate * (1.0 - sigmoid_gate))
        ).astype(jnp.bfloat16)
        grad_up = (grad_hidden * silu).astype(jnp.bfloat16)
        rank_back = nt_dot(grad_gate, b_gu2[0:128, :units]) + nt_dot(
            grad_up, b_gu2[0:128, units:]
        )
        dn2[block, :] = (
            nt_dot(grad_gate, gu[:, :units])
            + nt_dot(grad_up, gu[:, units:])
            + nn_dot(two_parts(rank_back), a_gu_t2[...])
        ).astype(jnp.bfloat16)
        rank_low = rank.astype(jnp.bfloat16)
        da_gu[...] += tn_dot(rank_back.astype(jnp.bfloat16), inputs)[0 : 2 * RANK]
        db_gu[0:RANK, :] += 2.0 * tn_dot(rank_low, grad_gate)[0:RANK]
        db_gu[RANK:, :] += 2.0 * tn_dot(rank_low, grad_up)[RANK : 2 * RANK]
        da_dn[...] += tn_dot(down_back.astype(jnp.bfloat16), hidden)[0:RANK]
        db_dn[...] += 2.0 * tn_dot(down_rank.astype(jnp.bfloat16), grads)[0:RANK]

    def pass_pieces(gather, copies, stage):
        start = sum(per_stage[:stage])
        for i, copy in enumerate(gather.stages[stage]):
            copy.wait_recv()
            copies[start + i].start()

    shared_tile(mine)
    n2_gather.wait(0)
    for stage in range(1, bits):
        n2_gather.start(stage)
        pass_on(n2_forward, stage - 1)
        if stage < bits - 1:
            n2_gather.wait(stage)
    shared_tile(theirs)
    give_out((shared, dn2))
    pass_pieces(g_gather, g_forward, bits - 1)
    pass_pieces(n2_gather, n2_forward, bits - 1)
    for copy in n2_forward + g_forward:
        copy.wait()
    for copy in small + spread + [shared_copy]:
        copy.wait_send()
    for group in gu_lent:
        for copy in group:
            copy.wait_send()
    for copy in given:
        copy.wait()
    for copy in part_copies:
        copy.wait_send()
    for gather in gathers + [g_gather, n2_gather]:
        gather.finish()
    n2_out.wait()
    wq_out.wait()
    wo_out.wait()
    locals_[6].wait()

    @pl.when(c < contexts - 1)
    def _():
        up(c, x_in.at[half_rows(0, t)]).wait_send()

    def drain(step, carry):
        chunk = c - step

        @pl.when(c < contexts - 1)
        def _():
            up(chunk, x_buf.at[half_rows(chunk, t)]).wait_send()

        across(chunk).wait_send()
        return carry

    lax.fori_loop(1, c + 1, drain, 0)

    def drain_out(step, carry):
        for copy in out_copies(c - step):
            copy.wait()
        return carry

    lax.fori_loop(0, c + 1, drain_out, 0)


def x_rows(x_buf, chunk, rows, block):
    return x_buf[pl.ds(pl.multiple_of(chunk * rows, 16) + block.start, block.size), :].astype(
        jnp.float32
    )


def forward_call(sizes, sharded, local):
    fsdp, contexts, _ = sizes
    x, g, wq, wo, gu, dn = sharded
    adapters, gains, table = local[:3]
    rows = x.shape[0]
    tree = rows * contexts
    width = wo.shape[1]
    units = dn.shape[1]
    bf, f32 = jnp.bfloat16, jnp.float32
    vmem = pl.BlockSpec(memory_space=pltpu.VMEM)
    hbm = pl.BlockSpec(memory_space=pl.ANY)
    smem = pl.BlockSpec(memory_space=pltpu.SMEM)
    slots = max(fsdp, contexts)
    total = fsdp * rows
    per_adapter = adapters.shape[0] // (ADAPTERS // fsdp)

    def shape(kind, *dims):
        return jax.ShapeDtypeStruct(dims, kind)

    moves = 2 * (fsdp - 1)
    hops = contexts + 5 + 2 * moves
    return pl.pallas_call(
        functools.partial(forward_kernel, sizes),
        in_specs=[hbm] * 6 + [vmem] * 4 + [smem] * 3,
        out_specs=[hbm] * 7 + [hbm, hbm, hbm, hbm, hbm, hbm, hbm, hbm, vmem, vmem, vmem, vmem, hbm, hbm, hbm, hbm, hbm, hbm, hbm, hbm, hbm, hbm, hbm, hbm, hbm, hbm, hbm, vmem],
        out_shape=[
            shape(bf, tree, D),
            shape(bf, tree, width),
            shape(bf, tree, width),
            shape(bf, D, 3 * width),
            shape(bf, D, width),
            shape(bf, fsdp * rows, D),
            shape(bf, fsdp * rows, D),
            shape(bf, width, rows),
            shape(bf, rows, width),
            shape(bf, rows, width),
            shape(f32, width, rows),
            shape(f32, 8, rows),
            shape(f32, rows, D),
            shape(bf, rows, D),
            shape(bf, rows, D),
            shape(f32, 2 * RANK, D),
            shape(f32, 2 * RANK, units),
            shape(f32, RANK, units),
            shape(f32, RANK, D),
            shape(f32, 8, D),
            shape(f32, tree, 128),
            shape(f32, tree, 128),
            shape(bf, tree, 128),
            shape(bf, 128, rows),
            shape(bf, D, 128),
            shape(bf, 256, 3 * width),
            shape(bf, 256, D),
            shape(bf, width, 128),
            shape(bf, 256, D),
            shape(bf, 256, width),
            shape(f32, fsdp, 8, rows),
            shape(f32, 8, total),
            shape(f32, total, 128),
            shape(bf, total, 128),
            shape(f32, 8, 128),
        ],
        scratch_shapes=[
            pltpu.VMEM((tree, D), bf),
            pltpu.VMEM((D, 3 * width), bf),
            pltpu.VMEM((D, width), bf),
            pltpu.VMEM((D, 2 * units), bf),
            pltpu.VMEM((D, units), bf),
            pltpu.VMEM((rows, D), bf),
            pltpu.VMEM((tree, D), bf),
            pltpu.VMEM((tree, width), bf),
            pltpu.VMEM((tree, width), bf),
            pltpu.VMEM((width, rows), bf),
            pltpu.VMEM((8, rows), f32),
            pltpu.VMEM((8, rows), f32),
            pltpu.VMEM((rows, rows), f32),
            pltpu.VMEM((rows, D), bf),
            pltpu.VMEM((rows, D), bf),
            pltpu.VMEM((rows, D), bf),
            pltpu.VMEM((rows, D), bf),
            pltpu.VMEM((rows, D), bf),
            pltpu.VMEM((fsdp,) + adapters.shape, bf),
            pltpu.VMEM((fsdp,) + gains.shape, bf),
            pltpu.VMEM((2, contexts, per_adapter, 128), bf),
            pltpu.VMEM((PARAMS // 128, 128), f32),
            pltpu.VMEM((max(D, units), 128), f32),
            pltpu.VMEM((D, 128), bf),
            pltpu.VMEM((256, 2 * units), bf),
            pltpu.VMEM((256, D), bf),
            pltpu.VMEM((units, 128), bf),
            pltpu.VMEM((256, units), bf),
            pltpu.VMEM((256, D), bf),
            pltpu.SemaphoreType.DMA((6, moves)),
            pltpu.SemaphoreType.DMA((6, moves)),
            pltpu.SemaphoreType.DMA((contexts,)),
            pltpu.SemaphoreType.DMA((contexts,)),
            pltpu.SemaphoreType.DMA((hops,)),
            pltpu.SemaphoreType.DMA((hops,)),
            pltpu.SemaphoreType.DMA((13,)),
            pltpu.SemaphoreType.DMA((3, contexts)),
            pltpu.SemaphoreType.DMA((5, slots)),
            pltpu.SemaphoreType.DMA((5, slots)),
            pltpu.SemaphoreType.DMA((2, moves)),
            pltpu.SemaphoreType.DMA((2, moves)),
            pltpu.VMEM((width, rows), bf),
            pltpu.VMEM((rows, width), bf),
            pltpu.VMEM((rows, width), bf),
            pltpu.VMEM((width, rows), f32),
            pltpu.VMEM((8, rows), f32),
            pltpu.VMEM((rows, D), f32),
            pltpu.VMEM((8, D), f32),
            pltpu.VMEM((tree, 128), f32),
            pltpu.VMEM((tree, 128), f32),
            pltpu.VMEM((tree, 128), bf),
            pltpu.VMEM((128, rows), bf),
            pltpu.VMEM((D, 128), bf),
            pltpu.VMEM((256, 3 * width), bf),
            pltpu.VMEM((256, D), bf),
            pltpu.VMEM((width, 128), bf),
            pltpu.VMEM((256, D), bf),
            pltpu.VMEM((256, width), bf),
            pltpu.VMEM((fsdp, 8, rows), f32),
            pltpu.VMEM((8, total), f32),
            pltpu.VMEM((total, 128), f32),
            pltpu.VMEM((total, 128), bf),
            pltpu.SemaphoreType.DMA((23,)),
        ],
        name="forward",
        compiler_params=pltpu.CompilerParams(
            collective_id=2, has_side_effects=True, vmem_limit_bytes=62 << 20
        ),
    )(*sharded, *local)


def flips(index, mask, bits):
    for bit in range(bits):
        if mask >> bit & 1:
            index = flip(index, bit)
    return index


class Scatter:
    def __init__(self, bits, me, device_of, work, inbox, count, send_sems, recv_sems):
        self.bits, self.work, self.inbox = bits, work, inbox
        self.copies = [[] for _ in range(bits)]
        self.masks = [[] for _ in range(bits)]
        self.adds = [[] for _ in range(bits)]
        number = 0
        for half, (offset, size) in enumerate(split_rows(count)):
            alive = list(range(1 << bits))
            slot = 0
            for stage in range(bits):
                bit = (stage + half) % bits
                for mask in alive:
                    if mask >> bit & 1:
                        source = Gather.rows(flips(me, mask, bits) * count + offset, size)
                        target = pl.ds(slot * count + offset, size)
                        kept = Gather.rows(flips(me, mask ^ (1 << bit), bits) * count + offset, size)
                        self.copies[stage].append(
                            send(
                                work.at[source],
                                inbox.at[target],
                                send_sems.at[number],
                                recv_sems.at[number],
                                device_of(flip(me, bit)),
                            )
                        )
                        self.adds[stage].append((kept, target, pl.ds(offset, size)))
                        self.masks[stage].append(mask)
                        number = number + 1
                        slot = slot + 1
                alive = [mask for mask in alive if not mask >> bit & 1]

    def start(self, stage):
        for copy in self.copies[stage]:
            copy.start()

    def start_mask(self, mask):
        for copy, number in zip(self.copies[0], self.masks[0]):
            if number == mask:
                copy.start()

    def add(self, stage):
        for copy in self.copies[stage]:
            copy.wait_recv()
        for kept, target, _ in self.adds[stage]:
            total = self.work[kept, :].astype(jnp.float32) + self.inbox[target, :].astype(
                jnp.float32
            )
            self.work[kept, :] = total.astype(jnp.bfloat16)

    def last(self, out):
        for copy in self.copies[self.bits - 1]:
            copy.wait_recv()
        for kept, target, rows in self.adds[self.bits - 1]:
            total = self.work[kept, :].astype(jnp.float32) + self.inbox[target, :].astype(
                jnp.float32
            )
            out[rows, :] = total.astype(jnp.bfloat16)

    def finish(self):
        for stage in self.copies:
            for copy in stage:
                copy.wait_send()


def pack_rows(grad_t, start, rank, flat, wide):
    total = grad_t.shape[1]
    more = jnp.zeros((128 - rank, 128), jnp.float32)
    for p in range(total // 128):
        piece = grad_t[:, 128 * p : 128 * p + 128]
        wide[128 * p : 128 * p + 128, :] = jnp.concatenate([piece, more], axis=0).T
    lines = rank // math.gcd(rank, 128)
    each = lines * 128 // rank
    count = total // each
    joined = jnp.concatenate(
        [wide[pl.ds(i, count, stride=each), :][:, 0:rank] for i in range(each)], axis=1
    )
    if lines == 1:
        flat[pl.ds(start, count), :] = joined
    else:
        for i in range(lines):
            flat[pl.ds(start + i, count, stride=lines), :] = joined[:, 128 * i : 128 * i + 128]


def pack_lines(grad, start, lines, columns, flat):
    for p, m in enumerate(columns):
        flat[pl.ds(start + m, grad.shape[0], stride=lines), :] = grad[:, 128 * p : 128 * p + 128]


def pack_first(t, flat, wide, da_qkv, db_qkv, da_o, db_o):
    width = da_o.shape[1]
    lines = D // 128
    mine = [t * (width // 128) + p for p in range(width // 128)]
    pack_rows(da_qkv[...], 0, 3 * RANK, flat, wide)
    at = 3 * RANK * D // 128
    for j in range(3):
        rows = slice(j * RANK, (j + 1) * RANK)
        pack_lines(db_qkv[rows, :], at + j * RANK * lines, lines, mine, flat)
    at = at + 3 * RANK * lines
    pack_rows(da_o[...], at + t * (width * RANK // 128), RANK, flat, wide)
    at = at + D * RANK // 128
    pack_lines(db_o[...], at, lines, list(range(lines)), flat)


def pack_second(t, flat, wide, da_gu, db_gu, da_dn, db_dn):
    units = da_dn.shape[1]
    lines = D // 128
    at = 8 * RANK * D // 128
    pack_rows(da_gu[...], at, 2 * RANK, flat, wide)
    at = at + 2 * RANK * D // 128
    wide_lines = FF // 128
    mine = [t * (units // 128) + p for p in range(units // 128)]
    for j in range(2):
        rows = slice(j * RANK, (j + 1) * RANK)
        pack_lines(db_gu[rows, :], at + j * RANK * wide_lines, wide_lines, mine, flat)
    at = at + 2 * RANK * wide_lines
    pack_rows(da_dn[...], at + t * (units * RANK // 128), RANK, flat, wide)
    at = at + FF * RANK // 128
    pack_lines(db_dn[...], at, lines, list(range(lines)), flat)


def backward_kernel(
    sizes,
    moe_out,
    moe_back,
    n1_hbm,
    k_hbm,
    v_hbm,
    wq_hbm,
    wo_hbm,
    cos_hbm,
    sin_hbm,
    x_in_hbm,
    g_in_hbm,
    gains,
    hot_hbm,
    reach_t,
    resid_hbm,
    shared_hbm,
    dn2_hbm,
    q_t_hbm,
    q_n_hbm,
    mixed_hbm,
    o_t_hbm,
    lse,
    a_qkv_hbm,
    b_qkv2_hbm,
    a_qkv_t2_hbm,
    a_o_hbm,
    a_o_t2_hbm,
    b_o2_hbm,
    da_gu,
    db_gu,
    da_dn,
    db_dn,
    table_all,
    block_out,
    input_grad,
    adapter_out,
    cosine,
    sinus,
    k_buf,
    v_buf,
    wq,
    wo,
    work_back,
    pair_back,
    inbox_back,
    work_out,
    pair_out,
    inbox_out,
    total_half,
    total_full,
    ffn_half,
    ffn_full,
    dy,
    do_n,
    do_t,
    delta,
    k_t,
    dq_t,
    bias,
    part_in,
    z_in,
    dn1_full,
    fs_send,
    fs_recv,
    z_send,
    z_recv,
    core_send,
    core_recv,
    pair_send,
    pair_recv,
    local_sems,
    chunk_sems,
    x_in,
    g_in,
    hot,
    resid,
    shared,
    dn2,
    q_t,
    q_n,
    mixed,
    o_t,
    a_qkv,
    b_qkv2,
    a_qkv_t2,
    a_o,
    a_o_t2,
    b_o2,
    da_qkv,
    db_qkv,
    da_o,
    db_o,
    flat,
    wide,
    packed,
    packed_in,
    up_out,
    up_in,
    own_sum,
    tree_sums,
    in_sems,
    sum_send,
    sum_recv,
    ahead,
    whole_back,
    whole_out,
):
    fsdp, contexts, _ = sizes
    bits = fsdp.bit_length() - 1
    f, c, t = place_of()
    rows = x_in.shape[0]
    half = rows // 2
    width = q_t.shape[0]
    inputs = []
    for i, (source, target) in enumerate(
        (
            (x_in_hbm, x_in),
            (g_in_hbm, g_in),
            (hot_hbm, hot),
            (resid_hbm, resid),
            (shared_hbm, shared),
            (dn2_hbm, dn2),
            (q_t_hbm, q_t),
            (q_n_hbm, q_n),
            (mixed_hbm, mixed),
            (o_t_hbm, o_t),
            (a_qkv_hbm, a_qkv),
            (b_qkv2_hbm, b_qkv2),
            (a_qkv_t2_hbm, a_qkv_t2),
            (a_o_hbm, a_o),
            (a_o_t2_hbm, a_o_t2),
            (b_o2_hbm, b_o2),
        )
    ):
        inputs.append(pltpu.make_async_copy(source, target, in_sems.at[i]))
    heads = width // HEAD_DIM
    part_out, z_out, grad_kv = pair_back, work_back, inbox_back
    part, n1_buf = whole_back, whole_out
    kv_rows = pl.ds(0, rows)
    sibling = (f, c, 1 - t)
    f32, bf = jnp.float32, jnp.bfloat16

    def peer(index):
        return (index, c, t)

    def local_rows(part_index):
        return pl.ds(pl.multiple_of(part_index * half, 16), half)

    mine = local_rows(t)
    theirs = local_rows(1 - t)

    def block_rows(block, part_index):
        return pl.ds(pl.multiple_of(block * rows + part_index * half, 16), half)

    def work_rows(block):
        return pl.ds(pl.multiple_of(block * half, 16), half)

    masks = list(range(fsdp - 1, -1, -1))

    def exchange(source, work, inbox, which, whole):
        own, sent = [], []
        for mask in masks:
            block = flips(f, mask, bits)
            if mask == 0:
                own.append(
                    pltpu.make_async_copy(
                        source.at[pl.ds(pl.multiple_of(f * rows, 16), rows)],
                        whole,
                        local_sems.at[which, mask],
                    )
                )
                sent.append(
                    send(
                        whole.at[theirs],
                        inbox.at[work_rows(block)],
                        core_send.at[which, mask],
                        core_recv.at[which, mask],
                        sibling,
                    )
                )
                continue
            own.append(
                pltpu.make_async_copy(
                    source.at[block_rows(block, t)],
                    work.at[work_rows(block)],
                    local_sems.at[which, mask],
                )
            )
            sent.append(
                send(
                    source.at[block_rows(block, 1 - t)],
                    inbox.at[work_rows(block)],
                    core_send.at[which, mask],
                    core_recv.at[which, mask],
                    sibling,
                )
            )
        return own, sent

    back_own, back_sent = exchange(moe_back, work_back, pair_back, 0, whole_back)
    out_own, out_sent = exchange(moe_out, work_out, pair_out, 1, whole_out)
    for copy in back_own:
        copy.start()
    wo_copy = pltpu.make_async_copy(wo_hbm, wo, local_sems.at[2, 0])
    wq_copy = pltpu.make_async_copy(wq_hbm, wq, local_sems.at[2, 1])
    wo_copy.start()
    for copy in inputs:
        copy.start()
    peers = [(lax.rem(f + k, fsdp), c, t) for k in range(1, fsdp)]
    stacked = [(f, lax.rem(c + k, contexts), t) for k in range(1, contexts)]
    greet(peers + stacked + [sibling])
    for copy in back_sent[:-1]:
        copy.start()
    for copy in out_own:
        copy.start()
    wq_copy.start()

    lines = PARAMS // 128 // (2 * contexts)
    early = -(-(8 * RANK * D // 128) // (2 * lines))

    def fill_blocks(first, last):
        for context in range(first, last):
            for part_index in range(2):
                start = (2 * context + part_index) * lines
                packed[context, part_index, 0:lines, :] = flat[start : start + lines, :]

    def pair_block(block):
        return send(
            packed.at[block, 1 - t],
            packed_in.at[block],
            sum_send.at[0, block],
            sum_recv.at[0, block],
            sibling,
        )

    def to_owner(k):
        return send(
            up_out.at[k], up_in.at[k], sum_send.at[1, k], sum_recv.at[1, k], stacked[k]
        )

    def push_blocks(soon):
        for k in range(contexts - 1):
            owner = lax.rem(c + k + 1, contexts)

            @pl.when((owner >= early) if soon else (owner < early))
            def _(k=k, owner=owner):
                up_out[k] = (packed[owner, t] + packed_in[owner]).astype(bf)
                to_owner(k).start()

    def to_peer(k):
        return send(
            own_sum, tree_sums.at[k], sum_send.at[2, k], sum_recv.at[2, k], peers[k]
        )

    def sum_own():
        result = packed[c, t] + packed_in[c]
        for k in range(contexts - 1):
            to_owner(k).wait_recv()
            result = result + up_in[k].astype(f32)
        own_sum[...] = result.astype(bf)
        for k in range(fsdp - 1):
            to_peer(k).start()

    def chunk_rows(chunk):
        return pl.ds(pl.multiple_of(chunk * rows, 16), rows)

    def loads(chunk):
        block = chunk_rows(chunk)
        return [
            pltpu.make_async_copy(k_hbm.at[block], k_buf.at[block], chunk_sems.at[1, chunk]),
            pltpu.make_async_copy(v_hbm.at[block], v_buf.at[block], chunk_sems.at[2, chunk]),
        ]

    def n1_load(chunk):
        return pltpu.make_async_copy(
            n1_hbm.at[chunk_rows(chunk)], n1_buf, chunk_sems.at[0, chunk]
        )

    def table_loads(chunk):
        block = chunk_rows(chunk)
        return [
            pltpu.make_async_copy(cos_hbm.at[block], cosine, chunk_sems.at[3, chunk]),
            pltpu.make_async_copy(sin_hbm.at[block], sinus, chunk_sems.at[4, chunk]),
        ]

    def start_loads(chunk, carry):
        for copy in loads(chunk):
            copy.start()
        return carry

    lax.fori_loop(0, c + 1, start_loads, 0)

    back = Scatter(
        bits, f, peer, work_back, inbox_back, half, fs_send.at[0], fs_recv.at[0]
    )
    out = Scatter(bits, f, peer, work_out, inbox_out, half, fs_send.at[1], fs_recv.at[1])

    def join(own, sent, whole, extra, work):
        own[-1].wait()
        whole[...] = (whole[...].astype(f32) + extra[...].astype(f32)).astype(bf)
        sent[-1].start()
        work[work_rows(f), :] = whole[mine, :]

    def pair_sum(own, sent, work, inbox, scatter):
        for i, mask in enumerate(masks):
            block = work_rows(flips(f, mask, bits))
            if mask != 0:
                own[i].wait()
            sent[i].wait_recv()
            work[block, :] = (
                work[block, :].astype(f32) + inbox[block, :].astype(f32)
            ).astype(bf)
            scatter.start_mask(mask)

    for copy in inputs:
        copy.wait()
    join(back_own, back_sent, whole_back, dn2, work_back)
    pair_sum(back_own, back_sent, work_back, pair_back, back)
    for copy in out_sent[:-1]:
        copy.start()
    join(out_own, out_sent, whole_out, shared, work_out)
    flat[...] = jnp.zeros_like(flat)
    pack_second(t, flat, wide, da_gu, db_gu, da_dn, db_dn)
    fill_blocks(early, contexts)
    for block in range(early, contexts):
        pair_block(block).start()
    def look_ahead(chunk):
        block = chunk_rows(chunk)
        for copy in loads(chunk):
            copy.wait()
        fill_bias(bias, hot[block, :], reach_t[...], chunk * rows, c * rows)

        def pair_step(p, carry):
            lanes = pl.ds(pl.multiple_of(p * 128, 128), 128)
            keys = k_buf[block, lanes]
            query_t = q_t[lanes, :]
            for odd in range(2):
                h = 2 * p + odd
                alone = jnp.where(
                    head_half(query_t.shape, 0, odd), query_t, jnp.zeros_like(query_t)
                )
                scores = nn_dot(keys, alone) + bias[...]
                ahead[chunk * heads + h] = jnp.exp(scores - lse[pl.ds(h, 1), :]).astype(bf)
            return carry

        lax.fori_loop(0, heads // 2, pair_step, 0)

    def look_step(chunk, carry):
        look_ahead(chunk)
        return carry

    lax.fori_loop(0, jnp.minimum(c, 1), look_step, 0)
    for stage in range(1, bits):
        back.add(stage - 1)
        back.start(stage)
    lax.fori_loop(1, jnp.minimum(c, AHEAD), look_step, 0)
    dq_t[...] = jnp.zeros_like(dq_t)
    da_qkv[...] = jnp.zeros_like(da_qkv)
    db_qkv[...] = jnp.zeros_like(db_qkv)
    for block in range(early, contexts):
        pair_block(block).wait_recv()
    push_blocks(True)
    back.last(total_half)
    pair_sum(out_own, out_sent, work_out, pair_out, out)
    for copy in out_sent:
        copy.wait_send()
    total_full[mine, :] = total_half[...]
    full_copy = send(
        total_half, total_full.at[mine], core_send.at[2, 0], core_recv.at[2, 0], sibling
    )
    full_copy.start()
    back.finish()
    for copy in back_sent:
        copy.wait_send()
    gain_one = gains[0:1, :]
    gain_two = gains[1:2, :]
    wo_copy.wait()
    full_copy.wait_recv()

    def attn_tile(i, carry):
        block = local_rows(i)
        values = resid[block, :]
        gradient = g_in[block, :].astype(f32) + norm_back(
            values, rms_scale(values), gain_two, total_full[block, :].astype(f32)
        )
        dy[block, :] = gradient
        low_grad = gradient.astype(bf)
        rank_back = nt_dot(low_grad, b_o2[0:128, :])
        do_n[block, :] = (
            nn_dot(low_grad, wo[...]) + nn_dot(two_parts(rank_back), a_o_t2[...])
        ).astype(bf)
        values_o = mixed[block, :]
        rank = nn_dot(values_o, a_o[...])
        first = tn_dot(rank_back.astype(bf), values_o)[0:RANK]
        second = 2.0 * tn_dot(rank.astype(bf), low_grad)[0:RANK]

        @pl.when(i == 0)
        def _():
            da_o[...] = first
            db_o[...] = second

        @pl.when(i > 0)
        def _():
            da_o[...] += first
            db_o[...] += second

        return carry

    lax.fori_loop(0, 2, attn_tile, 0)
    for p in range(width // 128):
        lanes = slice(128 * p, 128 * p + 128)
        turned = do_n[:, lanes].astype(f32).T
        do_t[lanes, :] = turned.astype(bf)
        product = turned * o_t[lanes, :]
        for odd in range(2):
            delta[2 * p + odd : 2 * p + odd + 1, :] = jnp.sum(
                product[HEAD_DIM * odd : HEAD_DIM * odd + HEAD_DIM, :], axis=0, keepdims=True
            )
    wq_copy.wait()

    def attend_back(chunk, known=False):
        block = chunk_rows(chunk)
        n1_load(chunk).start()
        for copy in table_loads(chunk):
            copy.start()
        for copy in table_loads(chunk) + ([] if known else loads(chunk)):
            copy.wait()
        if not known:
            fill_bias(bias, hot[block, :], reach_t[...], chunk * rows, c * rows)
        cos_rows = cosine[...]
        sin_rows = -sinus[...]
        for p in range(width // 128):
            lanes = slice(128 * p, 128 * p + 128)
            k_t[lanes, :] = k_buf[block, lanes].astype(f32).T.astype(bf)

        def pair_step(p, carry):
            lanes = pl.ds(pl.multiple_of(p * 128, 128), 128)
            keys = k_buf[block, lanes]
            values = v_buf[block, lanes]
            query_t = q_t[lanes, :]
            grad_t = do_t[lanes, :]
            query = q_n[:, lanes]
            grad = do_n[:, lanes]
            grad_keys = jnp.zeros((rows, 128), f32)
            grad_values = jnp.zeros((rows, 128), f32)
            for odd in range(2):
                h = 2 * p + odd
                upper = head_half(query_t.shape, 0, odd)
                side = head_half(query.shape, 1, odd)
                none_t = jnp.zeros_like(query_t)
                none = jnp.zeros_like(query)
                if known:
                    low_weights = ahead[chunk * heads + h]
                    weights = low_weights.astype(f32)
                else:
                    scores = nn_dot(keys, jnp.where(upper, query_t, none_t)) + bias[...]
                    weights = jnp.exp(scores - lse[pl.ds(h, 1), :])
                    low_weights = weights.astype(bf)
                grad_weights = nn_dot(values, jnp.where(upper, grad_t, none_t))
                grad_scores = (weights * (grad_weights - delta[pl.ds(h, 1), :])).astype(bf)
                grad_values += nn_dot(low_weights, jnp.where(side, grad, none))
                grad_keys += nn_dot(grad_scores, jnp.where(side, query, none))
                head = pl.ds(pl.multiple_of(h * HEAD_DIM, HEAD_DIM), HEAD_DIM)
                dq_t[head, :] += nn_dot(k_t[head, :], grad_scores)
            grad_kv[kv_rows, lanes] = turn(grad_keys, cos_rows, sin_rows).astype(bf)
            grad_kv[kv_rows, pl.ds(pl.multiple_of(width + p * 128, 128), 128)] = grad_values.astype(bf)
            return carry

        lax.fori_loop(0, heads // 2, pair_step, 0)

    def project_back(chunk, own):
        block = chunk_rows(chunk)
        grads = grad_kv[kv_rows, :]
        result = nt_dot(grads, wq[:, width:])
        rank_back = nt_dot(grads, b_qkv2[0:128, width:])
        n1_load(chunk).wait()
        n1 = n1_buf[...]
        rank = nn_dot(n1, a_qkv[...]).astype(bf)
        both = 2.0 * tn_dot(rank, grads)
        db_qkv[RANK : 2 * RANK, :] += both[RANK : 2 * RANK, :width]
        db_qkv[2 * RANK :, :] += both[2 * RANK : 3 * RANK, width:]
        if own:
            pieces = []
            for p in range(width // 128):
                lanes = slice(128 * p, 128 * p + 128)
                grad_query = (dq_t[lanes, :] * 0.125).T
                pieces.append(
                    turn(grad_query, cosine[...], -sinus[...]).astype(bf)
                )
            grad_query = jnp.concatenate(pieces, axis=1)
            result += nt_dot(grad_query, wq[:, :width])
            rank_back += nt_dot(grad_query, b_qkv2[0:128, :width])
            db_qkv[0:RANK, :] += 2.0 * tn_dot(rank, grad_query)[0:RANK, :]
        result += nn_dot(two_parts(rank_back), a_qkv_t2[...])
        da_qkv[...] += tn_dot(rank_back.astype(bf), n1)[0 : 3 * RANK]
        part[...] = result.astype(bf)
        part_out[work_rows(chunk), :] = part[theirs, :]
        z_out[work_rows(chunk), :] = part[mine, :]

    def pair_copy(chunk):
        return send(
            part_out.at[work_rows(chunk)],
            part_in.at[work_rows(chunk)],
            pair_send.at[chunk],
            pair_recv.at[chunk],
            sibling,
        )

    def down(chunk):
        block = work_rows(chunk)
        return send(
            z_out.at[block], z_in.at[block], z_send.at[chunk], z_recv.at[chunk], (f, c - 1, t)
        )

    def chain(chunk):
        block = work_rows(chunk)
        pair_copy(chunk).wait_recv()
        summed = z_out[block, :].astype(f32) + part_in[block, :].astype(f32)
        z_out[block, :] = summed.astype(bf)

        @pl.when(c < contexts - 1)
        def _():
            down(chunk).wait_recv()
            z_out[block, :] = (summed + z_in[block, :].astype(f32)).astype(bf)

    def pass_down(chunk):
        chain(chunk)
        down(chunk).start()

    def sum_moe():
        for stage in range(1, bits):
            out.add(stage - 1)
            out.start(stage)

    ffn_copy = send(ffn_half, ffn_full.at[mine], core_send.at[2, 1], core_recv.at[2, 1], sibling)

    def share_moe():
        out.last(ffn_half)
        ffn_full[mine, :] = ffn_half[...]
        ffn_copy.start()

    def step(chunk, carry, known=False):
        attend_back(chunk, known)
        project_back(chunk, False)
        pair_copy(chunk).start()

        @pl.when(c == contexts - 1)
        def _():
            pass_down(chunk)

        @pl.when((c < contexts - 1) & (chunk >= 1))
        def _():
            pass_down(chunk - 1)

        @pl.when(chunk == 0)
        def _():
            sum_moe()

        @pl.when(chunk == 1)
        def _():
            share_moe()

            @pl.when(c >= early)
            def _():
                sum_own()

        return carry

    lax.fori_loop(0, jnp.minimum(c, AHEAD), functools.partial(step, known=True), 0)
    lax.fori_loop(AHEAD, c, step, 0)
    attend_back(c)
    project_back(c, True)
    pair_copy(c).start()
    pack_first(t, flat, wide, da_qkv, db_qkv, da_o, db_o)
    fill_blocks(0, early)
    for block in range(early):
        pair_block(block).start()

    @pl.when((c < 2) & (c >= early))
    def _():
        sum_own()

    @pl.when(c == 0)
    def _():
        sum_moe()

    @pl.when((c < contexts - 1) & (c >= 1))
    def _():
        pass_down(c - 1)

    for block in range(early):
        pair_block(block).wait_recv()
    push_blocks(False)

    @pl.when(c < 2)
    def _():
        share_moe()

    chain(c)
    dn1_full[mine, :] = z_out[work_rows(c), :]
    dn1_copy = send(
        z_out.at[work_rows(c)],
        dn1_full.at[mine],
        core_send.at[2, 2],
        core_recv.at[2, 2],
        sibling,
    )
    dn1_copy.start()
    ffn_copy.wait_recv()
    resid[...] = resid[...] + ffn_full[...].astype(f32)
    block_copy = pltpu.make_async_copy(resid, block_out, in_sems.at[len(inputs)])
    block_copy.start()
    dn1_copy.wait_recv()

    def final_tile(i, carry):
        block = local_rows(i)
        values = x_in[block, :].astype(f32)
        dy[block, :] = dy[block, :] + norm_back(
            values, rms_scale(values), gain_one, dn1_full[block, :].astype(f32)
        )
        return carry

    lax.fori_loop(0, 2, final_tile, 0)
    grad_copy = pltpu.make_async_copy(dy, input_grad, in_sems.at[len(inputs) + 1])
    grad_copy.start()
    @pl.when(c < early)
    def _():
        sum_own()

    own = ADAPTERS // fsdp
    wanted = [(f * own + a).astype(f32) for a in range(own)]
    mine_sum = own_sum[...].astype(f32)
    sums = [jnp.where(table_all[f, 4:5, 0:1] == w, mine_sum, 0.0) for w in wanted]
    for k in range(fsdp - 1):
        to_peer(k).wait_recv()
        tree = table_all[lax.rem(f - k - 1 + fsdp, fsdp), 4:5, 0:1]
        block = tree_sums[k].astype(f32)
        sums = [total + jnp.where(tree == w, block, 0.0) for total, w in zip(sums, wanted)]
    for a in range(own):
        adapter_out[a] = sums[a]
    for copy in [full_copy, ffn_copy, dn1_copy]:
        copy.wait_send()
    block_copy.wait()
    grad_copy.wait()
    for block in range(contexts):
        pair_block(block).wait_send()
    for k in range(contexts - 1):
        to_owner(k).wait_send()
    for k in range(fsdp - 1):
        to_peer(k).wait_send()
    out.finish()

    def drain(chunk, carry):
        pair_copy(chunk).wait_send()

        @pl.when(chunk < c)
        def _():
            down(chunk).wait_send()

        return carry

    lax.fori_loop(0, c + 1, drain, 0)


def backward_call(sizes, remote, local):
    fsdp, contexts, _ = sizes
    rows = local[0].shape[0]
    padded = (PARAMS // 128 // (2 * contexts) + 15) // 16 * 16
    half = rows // 2
    tree = rows * contexts
    width = remote[6].shape[1]
    units = local[20].shape[1]
    bf, f32 = jnp.bfloat16, jnp.float32
    vmem = pl.BlockSpec(memory_space=pltpu.VMEM)
    hbm = pl.BlockSpec(memory_space=pl.ANY)

    def shape(kind, *dims):
        return jax.ShapeDtypeStruct(dims, kind)

    moves = 2 * (fsdp - 1)
    slots = max(fsdp, 4)
    dma = pltpu.SemaphoreType.DMA
    return pl.pallas_call(
        functools.partial(backward_kernel, sizes),
        in_specs=[hbm] * len(remote) + [hbm, hbm, vmem, hbm, vmem, hbm, hbm, hbm, hbm, hbm, hbm, hbm, vmem, hbm, hbm, hbm, hbm, hbm, hbm, vmem, vmem, vmem, vmem, vmem],
        out_specs=[hbm, hbm, vmem],
        out_shape=[
            shape(f32, rows, D),
            shape(f32, rows, D),
            shape(f32, ADAPTERS // fsdp, padded, 128),
        ],
        scratch_shapes=[
            pltpu.VMEM((rows, 128), f32),
            pltpu.VMEM((rows, 128), f32),
            pltpu.VMEM((tree, width), bf),
            pltpu.VMEM((tree, width), bf),
            pltpu.VMEM((D, 3 * width), bf),
            pltpu.VMEM((D, width), bf),
            pltpu.VMEM((max(fsdp, contexts) * half, D), bf),
            pltpu.VMEM((max(fsdp, contexts) * half, D), bf),
            pltpu.VMEM((max(fsdp - 1, 2) * half, D), bf),
            pltpu.VMEM((fsdp * half, D), bf),
            pltpu.VMEM((fsdp * half, D), bf),
            pltpu.VMEM(((fsdp - 1) * half, D), bf),
            pltpu.VMEM((half, D), bf),
            pltpu.VMEM((rows, D), bf),
            pltpu.VMEM((half, D), bf),
            pltpu.VMEM((rows, D), bf),
            pltpu.VMEM((rows, D), f32),
            pltpu.VMEM((rows, width), bf),
            pltpu.VMEM((width, rows), bf),
            pltpu.VMEM((8, rows), f32),
            pltpu.VMEM((width, rows), bf),
            pltpu.VMEM((width, rows), f32),
            pltpu.VMEM((rows, rows), f32),
            pltpu.VMEM((contexts * half, D), bf),
            pltpu.VMEM((contexts * half, D), bf),
            pltpu.VMEM((rows, D), bf),
            dma((2, moves)),
            dma((2, moves)),
            dma((contexts,)),
            dma((contexts,)),
            dma((3, slots)),
            dma((3, slots)),
            dma((contexts,)),
            dma((contexts,)),
            dma((3, slots)),
            dma((5, contexts)),
            pltpu.VMEM((rows, D), bf),
            pltpu.VMEM((rows, D), bf),
            pltpu.VMEM((tree, 128), bf),
            pltpu.VMEM((rows, D), f32),
            pltpu.VMEM((rows, D), bf),
            pltpu.VMEM((rows, D), bf),
            pltpu.VMEM((width, rows), bf),
            pltpu.VMEM((rows, width), bf),
            pltpu.VMEM((rows, width), bf),
            pltpu.VMEM((width, rows), f32),
            pltpu.VMEM((D, 128), bf),
            pltpu.VMEM((256, 3 * width), bf),
            pltpu.VMEM((256, D), bf),
            pltpu.VMEM((width, 128), bf),
            pltpu.VMEM((256, width), bf),
            pltpu.VMEM((256, D), bf),
            pltpu.VMEM((3 * RANK, D), f32),
            pltpu.VMEM((3 * RANK, width), f32),
            pltpu.VMEM((RANK, width), f32),
            pltpu.VMEM((RANK, D), f32),
            pltpu.VMEM((PARAMS // 128, 128), f32),
            pltpu.VMEM((max(D, units), 128), f32),
            pltpu.VMEM((contexts, 2, padded, 128), f32),
            pltpu.VMEM((contexts, padded, 128), f32),
            pltpu.VMEM((contexts - 1, padded, 128), bf),
            pltpu.VMEM((contexts - 1, padded, 128), bf),
            pltpu.VMEM((padded, 128), bf),
            pltpu.VMEM((fsdp - 1, padded, 128), bf),
            dma((18,)),
            dma((3, max(fsdp, contexts))),
            dma((3, max(fsdp, contexts))),
            pltpu.VMEM((AHEAD * (width // HEAD_DIM), rows, rows), bf),
            pltpu.VMEM((rows, D), bf),
            pltpu.VMEM((rows, D), bf),
        ],
        name="backward",
        compiler_params=pltpu.CompilerParams(
            collective_id=3, has_side_effects=True, vmem_limit_bytes=63 << 20
        ),
    )(*remote, *local)


def shards(
    tokens,
    attn_gain,
    w_qkv,
    w_out,
    ffn_gain,
    w_gu,
    w_dn,
    w_egu,
    w_edn,
    adapters,
    adapter_ids,
    parents,
    seg_lengths,
    routes,
    route_weights,
    cotangent,
):
    row_count = tokens.shape[1]
    contexts = lax.axis_size("context")
    tensors = lax.axis_size("tensor")
    fsdp_size = lax.axis_size("fsdp")
    sizes = (fsdp_size, contexts, tensors)
    local_width = w_qkv.shape[2]
    local_ff = w_dn.shape[0]
    own_adapters = adapters.shape[0]
    own_width = D // fsdp_size
    gains = jnp.broadcast_to(jnp.concatenate([attn_gain, ffn_gain])[None], (16, 2 * own_width))
    route_table = jnp.concatenate(
        [
            routes[0].astype(jnp.float32).T,
            route_weights[0].astype(jnp.float32).T,
            jnp.broadcast_to(adapter_ids.astype(jnp.float32)[:, None], (1, row_count)),
            jnp.zeros((3, row_count), jnp.float32),
        ]
    )
    lines = adapters.shape[1] // 128
    padded = (lines + 15) // 16 * 16
    adapter_rows = jnp.pad(
        adapters.reshape(own_adapters, lines, 128), ((0, 0), (0, padded - lines), (0, 0))
    ).reshape(own_adapters * padded, 128)
    half_dim = HEAD_DIM // 2
    frequency = rope_base ** (-(jnp.arange(half_dim, dtype=jnp.float32) * 2.0) / HEAD_DIM)
    signs = jnp.concatenate([-jnp.ones((half_dim,)), jnp.ones((half_dim,))])
    turns = jnp.concatenate(
        [jnp.tile(frequency, 4)[None], jnp.tile(signs, 2)[None], jnp.zeros((6, 128))]
    ).astype(jnp.float32)
    sharded = (
        tokens[0],
        cotangent[0],
        w_qkv.reshape(own_width, 3 * local_width),
        w_out.T,
        w_gu.reshape(own_width, 2 * local_ff),
        w_dn.T,
    )
    (
        n1_all,
        k_all,
        v_all,
        wq_all,
        wo_all,
        normed_all,
        cotangent_all,
        q_t,
        q_n,
        mixed_own,
        o_t,
        lse,
        resid,
        shared,
        dn2,
        da_gu_t,
        db_gu_own,
        da_dn_t,
        db_dn_own,
        gains_full,
        cosine,
        sinus,
        hot,
        reach_t,
        a_qkv,
        b_qkv2,
        a_qkv_t2,
        a_o,
        b_o2,
        a_o_t2,
        table_all,
        place_row,
        place_col,
        weight_col,
        marks,
    ) = forward_call(
        sizes,
        sharded,
        (adapter_rows, gains, route_table, turns, adapter_ids, parents, seg_lengths),
    )
    own_experts = EXPERTS // fsdp_size
    starts = marks[:own_experts].astype(jnp.int32)
    moe_all, moe_back_all = moe_call(
        starts,
        place_row,
        place_col,
        weight_col,
        normed_all,
        cotangent_all,
        w_egu.transpose(0, 2, 1, 3),
        w_edn,
    )
    remote = (moe_all, moe_back_all, n1_all, k_all, v_all, wq_all, wo_all, cosine, sinus)
    block_out, input_grad, sums = backward_call(
        sizes,
        remote,
        (tokens[0], cotangent[0], gains_full, hot, reach_t)
        + (resid, shared, dn2, q_t, q_n, mixed_own, o_t, lse)
        + (a_qkv, b_qkv2, a_qkv_t2, a_o, a_o_t2, b_o2)
        + (da_gu_t, db_gu_own, da_dn_t, db_dn_own, table_all),
    )
    adapter_grads = sums[:, :lines].reshape(own_adapters, -1)
    return (block_out[None], input_grad[None], adapter_grads)


def solution(mesh):
    return jax.shard_map(
        shards,
        mesh=mesh,
        in_specs=(
            P("fsdp", "context", None),
            P("fsdp"),
            P("fsdp", None, "tensor"),
            P("tensor", "fsdp"),
            P("fsdp"),
            P("fsdp", None, "tensor"),
            P("tensor", "fsdp"),
            P("fsdp", None, None, "tensor"),
            P("fsdp", "tensor", None),
            P("fsdp", ("context", "tensor")),
            P("fsdp"),
            P("fsdp", None),
            P("fsdp", None),
            P("fsdp", "context", None),
            P("fsdp", "context", None),
            P("fsdp", "context", None),
        ),
        out_specs=(
            P("fsdp", "context", None),
            P("fsdp", "context", None),
            P("fsdp", ("context", "tensor")),
        ),
        check_vma=False,
    )
```

```python
import jax
import jax.numpy as jnp
import functools
import math

from jax import lax
from jax.experimental import pallas as pl
from jax.experimental.pallas import tpu as pltpu
from jax.sharding import PartitionSpec as P

D = 768
HEADS = 12
HEAD_DIM = 64
FF = 2048
EXPERTS = 8
TOPK = 2
RANK = 16
ADAPTERS = 8
PARAMS = 233472


epsilon = 1e-06
adapter_scale = 2.0
rope_base = 10000.0
masked_score = -1e30
highest_precision = lax.Precision.HIGHEST


def rms_scale(values):
    return lax.rsqrt(jnp.mean(values * values, axis=-1, keepdims=True) + epsilon)


def norm_back(values, scaling, gain_values, gradient):
    weighted = gradient * gain_values
    inner_mean = jnp.mean(values * weighted, axis=-1, keepdims=True)
    return scaling * weighted - values * (scaling * scaling * scaling) * inner_mean


SLOT_TILE = 512
TOKEN_TILE = 256
SLOT_WINDOW = 128


def nt_dot(left, right):
    return lax.dot_general(left, right, (((1,), (1,)), ((), ())), preferred_element_type=jnp.float32)


def tn_dot(left, right):
    return lax.dot_general(left, right, (((0,), (0,)), ((), ())), preferred_element_type=jnp.float32)


def nn_dot(left, right):
    return jnp.dot(left, right, preferred_element_type=jnp.float32)


def moe_kernel(
    starts,
    place_row,
    place_hbm,
    weight_hbm,
    rows_hbm,
    grads_hbm,
    egu_hbm,
    edn_hbm,
    out_hbm,
    back_hbm,
    place_col,
    weight_col,
    rows_ref,
    grads_ref,
    egu_ref,
    edn_ref,
    out_ref,
    back_ref,
    taken,
    taken_grad,
    taken_weight,
    sems,
    block_sems,
):
    f32, bf = jnp.float32, jnp.bfloat16
    experts = egu_hbm.shape[0]
    blocks = rows_ref.shape[0] // TOKEN_TILE

    def block_rows(b):
        return pl.ds(pl.multiple_of(b * TOKEN_TILE, TOKEN_TILE), TOKEN_TILE)

    def loads(b):
        block = block_rows(b)
        return [
            pltpu.make_async_copy(source.at[block], target.at[block], block_sems.at[i, b])
            for i, (source, target) in enumerate(
                ((rows_hbm, rows_ref), (grads_hbm, grads_ref), (weight_hbm, weight_col))
            )
        ]

    def stores(b):
        block = block_rows(b)
        return [
            pltpu.make_async_copy(source.at[block], target.at[block], block_sems.at[3 + i, b])
            for i, (source, target) in enumerate(((out_ref, out_hbm), (back_ref, back_hbm)))
        ]

    def weights(e):
        return [
            pltpu.make_async_copy(egu_hbm.at[e], egu_ref.at[e], sems.at[0, e]),
            pltpu.make_async_copy(edn_hbm.at[e], edn_ref.at[e], sems.at[1, e]),
        ]

    def each(count, copies, action):
        def step(i, carry):
            for copy in copies(i):
                getattr(copy, action)()
            return carry

        lax.fori_loop(0, count, step, 0)

    each(blocks, loads, "start")
    each(experts, weights, "start")
    place_copy = pltpu.make_async_copy(place_hbm, place_col, sems.at[2, 0])
    place_copy.start()
    taken[...] = jnp.zeros_like(taken)
    taken_grad[...] = jnp.zeros_like(taken_grad)
    taken_weight[...] = jnp.zeros_like(taken_weight)
    slot_rows = lax.broadcasted_iota(jnp.int32, (SLOT_WINDOW, TOKEN_TILE), 0).astype(f32)
    slot_cols = lax.broadcasted_iota(jnp.int32, (TOKEN_TILE, SLOT_WINDOW), 1).astype(f32)

    def windows(e, b):
        begin = starts[e, b] // 16 * 16
        return begin, (starts[e, b + 1] - begin + SLOT_WINDOW - 1) // SLOT_WINDOW

    def window_rows(begin, i):
        return pl.ds(pl.multiple_of(begin + i * SLOT_WINDOW, 16), SLOT_WINDOW)

    def fetch(b, carry):
        block = block_rows(b)
        for copy in loads(b):
            copy.wait()

        def take(which):
            picks = []
            for e, first in which:
                hit = place_row[e : e + 1, block] == slot_rows + first.astype(f32)
                picks.append(jnp.where(hit, 1.0, 0.0).astype(bf))
            pick = picks[0] if len(picks) == 1 else jnp.concatenate(picks, axis=0)
            for source, target in (
                (rows_ref, taken),
                (grads_ref, taken_grad),
                (weight_col, taken_weight),
            ):
                got = nn_dot(pick, source[block, :]).astype(bf)
                for i, (e, first) in enumerate(which):
                    slots = window_rows(first, 0)
                    target[e, slots, :] += got[i * SLOT_WINDOW : (i + 1) * SLOT_WINDOW, :]

        spans = [windows(e, b) for e in range(experts)]
        take([(e, spans[e][0]) for e in range(experts)])
        for e in range(experts):

            def more(i, c, e=e):
                take([(e, spans[e][0] + i * SLOT_WINDOW)])
                return c

            lax.fori_loop(1, spans[e][1], more, 0)
        return carry

    lax.fori_loop(0, blocks, fetch, 0)

    def tile(e, start, size):
        slots = pl.ds(pl.multiple_of(start, 128), size)
        inputs = taken[e, slots, :]
        gate_pre = nn_dot(inputs, egu_ref[e, 0])
        up_pre = nn_dot(inputs, egu_ref[e, 1])
        sigmoid_gate = jax.nn.sigmoid(gate_pre)
        silu = gate_pre * sigmoid_gate
        active = (silu * up_pre).astype(bf)
        taken[e, slots, :] = nn_dot(active, edn_ref[e]).astype(bf)
        grad_active = nt_dot(taken_grad[e, slots, :], edn_ref[e])
        lane = lax.broadcasted_iota(jnp.int32, (size, 128), 1)
        scale = jnp.sum(
            jnp.where(lane == e, taken_weight[e, slots, :].astype(f32), 0.0), axis=1, keepdims=True
        )
        grad_active = grad_active * scale
        grad_gate = (
            grad_active * up_pre * sigmoid_gate * (1.0 + gate_pre * (1.0 - sigmoid_gate))
        ).astype(bf)
        grad_up = (grad_active * silu).astype(bf)
        taken_grad[e, slots, :] = (
            nt_dot(grad_gate, egu_ref[e, 0]) + nt_dot(grad_up, egu_ref[e, 1])
        ).astype(bf)

    def expert_step(e, carry):
        for copy in weights(e):
            copy.wait()
        count = starts[e, blocks]
        whole = count // SLOT_TILE
        rest = count - whole * SLOT_TILE

        def step(i, c):
            tile(e, i * SLOT_TILE, SLOT_TILE)
            return c

        lax.fori_loop(0, whole + jnp.where(rest > SLOT_TILE - 128, 1, 0), step, 0)
        for size in range(128, SLOT_TILE, 128):

            @pl.when((rest > size - 128) & (rest <= size))
            def _(size=size):
                tile(e, whole * SLOT_TILE, size)

        return carry

    lax.fori_loop(0, experts, expert_step, 0)
    place_copy.wait()

    def give(b, carry):
        block = block_rows(b)

        def hand(which):
            plain, scaled, values, values_grad = [], [], [], []
            for e, first in which:
                hit = place_col[block, e : e + 1] == slot_cols + first.astype(f32)
                plain.append(jnp.where(hit, 1.0, 0.0).astype(bf))
                weight = weight_col[block, e : e + 1].astype(f32)
                scaled.append(jnp.where(hit, weight, 0.0).astype(bf))
                values.append(taken[e, window_rows(first, 0), :])
                values_grad.append(taken_grad[e, window_rows(first, 0), :])

            def join(pieces, axis):
                return pieces[0] if len(pieces) == 1 else jnp.concatenate(pieces, axis=axis)

            return (
                nn_dot(join(scaled, 1), join(values, 0)),
                nn_dot(join(plain, 1), join(values_grad, 0)),
            )

        spans = [windows(e, b) for e in range(experts)]
        first, second = hand([(e, spans[e][0]) for e in range(experts)])
        out_ref[block, :] = first.astype(bf)
        back_ref[block, :] = second.astype(bf)
        for e in range(experts):

            def more(i, c, e=e):
                first, second = hand([(e, spans[e][0] + i * SLOT_WINDOW)])
                out_ref[block, :] = (out_ref[block, :].astype(f32) + first).astype(bf)
                back_ref[block, :] = (back_ref[block, :].astype(f32) + second).astype(bf)
                return c

            lax.fori_loop(1, spans[e][1], more, 0)
        for copy in stores(b):
            copy.start()
        return carry

    lax.fori_loop(0, blocks, give, 0)
    each(blocks, stores, "wait")


def moe_call(starts, place_row, place_col, weight_col, rows, grads, egu, edn):
    total, width = rows.shape
    experts = egu.shape[0]
    slots = total // 2 + SLOT_TILE
    blocks = total // TOKEN_TILE
    bf, f32 = jnp.bfloat16, jnp.float32
    vmem = pl.BlockSpec(memory_space=pltpu.VMEM)
    hbm = pl.BlockSpec(memory_space=pl.ANY)
    shape = jax.ShapeDtypeStruct((total, width), bf)
    return pl.pallas_call(
        moe_kernel,
        grid_spec=pltpu.PrefetchScalarGridSpec(
            num_scalar_prefetch=1,
            grid=(),
            in_specs=[vmem] + [hbm] * 6,
            out_specs=[hbm, hbm],
            scratch_shapes=[
                pltpu.VMEM((total, 128), f32),
                pltpu.VMEM((total, 128), bf),
                pltpu.VMEM((total, width), bf),
                pltpu.VMEM((total, width), bf),
                pltpu.VMEM(egu.shape, bf),
                pltpu.VMEM(edn.shape, bf),
                pltpu.VMEM((total, width), bf),
                pltpu.VMEM((total, width), bf),
                pltpu.VMEM((experts, slots, width), bf),
                pltpu.VMEM((experts, slots, width), bf),
                pltpu.VMEM((experts, slots, 128), bf),
                pltpu.SemaphoreType.DMA((3, experts)),
                pltpu.SemaphoreType.DMA((5, blocks)),
            ],
        ),
        out_shape=[shape, shape],
        name="experts",
        compiler_params=pltpu.CompilerParams(vmem_limit_bytes=62 << 20),
    )(starts, place_row, place_col, weight_col, rows, grads, egu, edn)


MESH = pl.DeviceIdType.MESH


def place_of():
    return lax.axis_index("fsdp"), lax.axis_index("context"), lax.axis_index("tensor")


def greet(devices):
    barrier = pltpu.get_barrier_semaphore()
    for device in devices:
        pl.semaphore_signal(barrier, inc=1, device_id=device, device_id_type=MESH)
    pl.semaphore_wait(barrier, len(devices))


def send(source, target, send_sem, recv_sem, device):
    return pltpu.make_async_remote_copy(
        src_ref=source,
        dst_ref=target,
        send_sem=send_sem,
        recv_sem=recv_sem,
        device_id=device,
        device_id_type=MESH,
    )


def flip(index, bit):
    return index + (1 - 2 * lax.rem(index // (1 << bit), 2)) * (1 << bit)


def split_rows(count):
    first = (count // 2 + 15) // 16 * 16
    return ((0, first), (first, count - first))


class Gather:
    def __init__(self, bits, me, device_of, own, buf, stride, base, count, send_sems, recv_sems):
        self.stages = [[] for _ in range(bits)]
        self.arrived = [[] for _ in range(bits)]
        self.passed = [[] for _ in range(bits)]
        number = 0
        for half, (offset, size) in enumerate(split_rows(count)):
            held = [me]
            for stage in range(bits):
                bit = (stage + half) % bits
                for block in held:
                    rows = self.rows(block * stride + base + offset, size)
                    source = own.at[self.rows(base + offset, size)] if block is me else buf.at[rows]
                    self.passed[stage].append(block is not me)
                    self.stages[stage].append(
                        send(
                            source,
                            buf.at[rows],
                            send_sems.at[number],
                            recv_sems.at[number],
                            device_of(flip(me, bit)),
                        )
                    )
                    self.arrived[stage].append(
                        self.rows(flip(block, bit) * stride + base + offset, size)
                    )
                    number = number + 1
                held = held + [flip(block, bit) for block in held]

    @staticmethod
    def rows(start, size):
        return pl.ds(pl.multiple_of(start, 16), size)

    def start(self, stage):
        if stage == 0:
            for copies, passed in zip(self.stages, self.passed):
                for copy, later in zip(copies, passed):
                    if not later:
                        copy.start()
        else:
            for copy, later in zip(self.stages[stage], self.passed[stage]):
                if later:
                    copy.start()

    def wait(self, stage):
        for copy in self.stages[stage]:
            copy.wait_recv()

    def finish(self):
        for stage in self.stages:
            for copy in stage:
                copy.wait_send()


def turn(values, cosine, sinus):
    lane = lax.broadcasted_iota(jnp.int32, values.shape, 1)
    first = lax.rem(lane, HEAD_DIM) < HEAD_DIM // 2
    swapped = jnp.where(
        first,
        pltpu.roll(values, 128 - HEAD_DIM // 2, 1),
        pltpu.roll(values, HEAD_DIM // 2, 1),
    )
    return values * cosine + swapped * sinus


def two_parts(values):
    high = values.astype(jnp.bfloat16)
    low = (values - high.astype(jnp.float32)).astype(jnp.bfloat16)
    return jnp.concatenate([high, low], axis=1)


def normed(values, gain):
    scale = lax.rsqrt(jnp.mean(values * values, axis=-1, keepdims=True) + epsilon)
    return (values * scale * gain).astype(jnp.bfloat16)


def fill_bias(bias, hot_rows, reach_t, key_start, query_start):
    seen = nn_dot(hot_rows, reach_t)
    keys = key_start + lax.broadcasted_iota(jnp.int32, seen.shape, 0)
    queries = query_start + lax.broadcasted_iota(jnp.int32, seen.shape, 1)
    bias[...] = jnp.where((seen > 0.5) & (keys <= queries), 0.0, masked_score)


def head_half(shape, axis, odd):
    index = lax.broadcasted_iota(jnp.int32, shape, axis)
    return (index >= HEAD_DIM) if odd else (index < HEAD_DIM)


def tree_tables(parents, lengths, turns, context, rows, hot, reach_t, cosine, sinus):
    lane = lax.broadcasted_iota(jnp.int32, (1, 128), 1)
    far = jnp.full((1, 128), 1 << 30, jnp.int32)
    none = jnp.zeros((1, 128), jnp.int32)
    begins, ends, moves = far, far, none
    first, second = none - 1, none - 1
    start = jnp.int32(0)
    for s in range(parents.shape[1]):
        parent = parents[0, s]
        grand = parents[0, parent]
        here = lane == s
        above = jnp.where(parent != s, lengths[0, parent], 0) + jnp.where(
            (grand != s) & (grand != parent), lengths[0, grand], 0
        )
        begins = jnp.where(here, start, begins)
        moves = jnp.where(here, above - start, moves)
        first = jnp.where(here, parent, first)
        second = jnp.where(here, grand, second)
        start = start + lengths[0, s]
        ends = jnp.where(here, start, ends)
    over = lax.broadcasted_iota(jnp.int32, (128, 128), 0)
    under = lax.broadcasted_iota(jnp.int32, (128, 128), 1)
    ancestors = jnp.where((over == under) | (over == first) | (over == second), 1.0, 0.0).astype(
        jnp.bfloat16
    )

    def fill(chunk, carry):
        block = pl.ds(pl.multiple_of(chunk * rows, 16), rows)
        row = chunk * rows + lax.broadcasted_iota(jnp.int32, (rows, 128), 0)
        inside = (row >= begins) & (row < ends)
        hot[block, :] = jnp.where(inside, 1.0, 0.0).astype(jnp.bfloat16)
        moved = jnp.sum(jnp.where(inside, moves.astype(jnp.float32), 0.0), axis=1, keepdims=True)
        angle = (row.astype(jnp.float32) + moved) * turns[0:1, :]
        cosine[block, :] = jnp.cos(angle)
        sinus[block, :] = jnp.sin(angle) * turns[1:2, :]
        return carry

    lax.fori_loop(0, context + 1, fill, 0)
    own = pl.ds(pl.multiple_of(context * rows, 16), rows)
    reach_t[...] = nt_dot(ancestors, hot[own, :]).astype(jnp.bfloat16)


def choose(ids, adapters_all, out):
    wanted = ids[0]
    own = ADAPTERS // adapters_all.shape[0]
    count = adapters_all.shape[1] // own
    total = jnp.zeros((count, 128), jnp.float32)
    for a in range(ADAPTERS):
        block = adapters_all[a // own, pl.ds((a % own) * count, count), :].astype(jnp.float32)
        total = total + jnp.where(wanted == a, block, 0.0)
    out[...] = total.astype(jnp.bfloat16)


def route_tables(f, table_all, place_row, place_col, weight_col, marks):
    fsdp, _, rows = table_all.shape
    own = EXPERTS // fsdp
    f32 = jnp.float32
    sub = lax.broadcasted_iota(jnp.int32, (8, rows), 0)
    expert = jnp.where(sub < own, f * own + sub, -1).astype(f32)
    before = lax.broadcasted_iota(jnp.int32, (rows, rows), 0)
    after = lax.broadcasted_iota(jnp.int32, (rows, rows), 1)
    upto = jnp.where(before <= after, 1.0, 0.0).astype(jnp.bfloat16)
    lane = lax.broadcasted_iota(jnp.int32, (8, 128), 1)
    base = jnp.zeros((8, 1), f32)
    found = jnp.zeros((8, 128), f32)
    more = jnp.zeros((120, rows), f32)
    for source in range(fsdp):
        table = table_all[source]
        one = table[0:1, :] == expert
        two = table[1:2, :] == expert
        hit = one | two
        weight = jnp.where(one, table[2:3, :], 0.0) + jnp.where(two, table[3:4, :], 0.0)
        count = nn_dot(jnp.where(hit, 1.0, 0.0).astype(jnp.bfloat16), upto) + base
        place = jnp.where(hit, count - 1.0, -1.0)
        block = slice(source * rows, (source + 1) * rows)
        place_row[:, block] = place
        place_col[block, :] = jnp.concatenate([place, more], axis=0).T
        weight_col[block, :] = jnp.concatenate([weight, more], axis=0).T.astype(jnp.bfloat16)
        for token in range(TOKEN_TILE - 1, fsdp * rows, TOKEN_TILE):
            if token // rows == source:
                at = token % rows
                found = jnp.where(lane == token // TOKEN_TILE + 1, count[:, at : at + 1], found)
        base = count[:, rows - 1 : rows]
    marks[...] = found


def unpack_adapter(t, per_block, chosen, flat, wide, first, second):
    a_qkv, b_qkv2, a_qkv_t2, a_o, b_o2, a_o_t2 = first
    a_gu, b_gu2, a_gu_t2, a_dn, a_dn_t2, b_dn2 = second
    f32, bf = jnp.float32, jnp.bfloat16
    contexts = chosen.shape[1]
    width, units = a_o.shape[0], a_dn.shape[0]
    count = PARAMS // 128 // (2 * contexts)
    for context in range(contexts):
        for part in range(2):
            start = (2 * context + part) * count
            flat[start : start + count, :] = chosen[part, context, 0:count, :].astype(f32)

    def spread(start, groups, rank, out, out_t):
        total = groups * 128 // rank
        wide[...] = jnp.zeros_like(wide)
        lines = rank // math.gcd(rank, 128)
        each = lines * 128 // rank
        for i in range(each):
            row, at = divmod(i * rank, 128)
            def line(number):
                if lines == 1:
                    return flat[pl.ds(start, groups), :]
                return flat[pl.ds(start + number, groups // lines, stride=lines), :]

            piece = line(row)[:, at : min(at + rank, 128)]
            if at + rank > 128:
                piece = jnp.concatenate([piece, line(row + 1)[:, 0 : at + rank - 128]], axis=1)
            wide[pl.ds(i, groups // lines, stride=each), 0:rank] = piece
        out[...] = wide[0:total, :].astype(bf)
        if out_t is not None:
            for p in range(total // 128):
                turned = wide[128 * p : 128 * p + 128, :].T.astype(bf)
                out_t[0:128, 128 * p : 128 * p + 128] = turned
                out_t[128:256, 128 * p : 128 * p + 128] = turned

    def stack(start, lines, columns, out, row, column):
        for p, m in enumerate(columns):
            piece = (2.0 * flat[pl.ds(start + m, RANK, stride=lines), :]).astype(bf)
            lanes = slice(column + 128 * p, column + 128 * p + 128)
            out[row : row + RANK, lanes] = piece
            out[128 + row : 128 + row + RANK, lanes] = piece

    for ref in (b_qkv2, b_o2, b_gu2, b_dn2):
        ref[...] = jnp.zeros_like(ref)
    at = 0
    spread(at, 3 * RANK * D // 128, 3 * RANK, a_qkv, a_qkv_t2)
    at = at + 3 * RANK * D // 128
    lines = D // 128
    mine = [t * (width // 128) + p for p in range(width // 128)]
    for j in range(3):
        stack(at + j * RANK * lines, lines, mine, b_qkv2, j * RANK, j * width)
    at = at + 3 * RANK * lines
    spread(at + t * (width * RANK // 128), width * RANK // 128, RANK, a_o, a_o_t2)
    at = at + D * RANK // 128
    stack(at, lines, list(range(lines)), b_o2, 0, 0)
    at = at + RANK * lines
    spread(at, 2 * RANK * D // 128, 2 * RANK, a_gu, a_gu_t2)
    at = at + 2 * RANK * D // 128
    wide_lines = FF // 128
    mine = [t * (units // 128) + p for p in range(units // 128)]
    for j in range(2):
        stack(at + j * RANK * wide_lines, wide_lines, mine, b_gu2, j * RANK, j * units)
    at = at + 2 * RANK * wide_lines
    spread(at + t * (units * RANK // 128), units * RANK // 128, RANK, a_dn, a_dn_t2)
    at = at + FF * RANK // 128
    stack(at, lines, list(range(lines)), b_dn2, 0, 0)


def forward_kernel(
    sizes,
    x_in,
    g_in,
    wq_in,
    wo_in,
    gu_in,
    dn_in,
    adapters_in,
    gains_in,
    table_in,
    turns,
    ids,
    parents,
    lengths,
    n1_all,
    k_all,
    v_all,
    wq_all,
    wo_all,
    n2_all,
    g_all,
    p_all,
    q_t_out,
    q_n_out,
    mixed_out,
    o_t_out,
    lse_out,
    resid_out,
    shared_out,
    dn2_out,
    da_gu,
    db_gu,
    da_dn,
    db_dn,
    gains_out,
    cosine_out,
    sinus_out,
    hot_out,
    reach_t_out,
    a_qkv_out,
    b_qkv2_out,
    a_qkv_t2_out,
    a_o_out,
    b_o2_out,
    a_o_t2_out,
    table_all_out,
    place_row_out,
    place_col_out,
    weight_col_out,
    marks,
    peaks,
    x_buf,
    wq,
    wo,
    gu,
    dn,
    g_own,
    n1_buf,
    k_buf,
    v_buf,
    v_t,
    peak,
    total,
    bias,
    part_out,
    part_in,
    n2_own,
    shared,
    dn2,
    adapters_all,
    gains_all,
    chosen,
    flat,
    a_wide,
    a_gu,
    b_gu2,
    a_gu_t2,
    a_dn,
    a_dn_t2,
    b_dn2,
    fs_send,
    fs_recv,
    z_send,
    z_recv,
    core_send,
    core_recv,
    local_sems,
    chunk_sems,
    small_send,
    small_recv,
    lend_send,
    lend_recv,
    q_t,
    q_n,
    mixed,
    o_t,
    lse,
    resid,
    gains,
    cosine,
    sinus,
    hot,
    reach_t,
    a_qkv,
    b_qkv2,
    a_qkv_t2,
    a_o,
    b_o2,
    a_o_t2,
    table_all,
    place_row,
    place_col,
    weight_col,
    out_sems,
    p_buf,
    p_sems,
):
    fsdp, contexts, _ = sizes
    bits = fsdp.bit_length() - 1
    f, c, t = place_of()
    rows = x_in.shape[0]
    half = rows // 2
    heads = q_t.shape[0] // HEAD_DIM
    width = q_t.shape[0]
    units = dn_in.shape[1]
    own_n = wq_in.shape[0]
    sibling = (f, c, 1 - t)

    def peer(index):
        return (index, c, t)

    peers = [(lax.rem(f + k, fsdp), c, t) for k in range(1, fsdp)]
    stacked = [(f, lax.rem(c + k, contexts), t) for k in range(1, contexts)]
    greet(peers + stacked + [sibling])

    targets = (
        (q_t, q_t_out),
        (q_n, q_n_out),
        (mixed, mixed_out),
        (o_t, o_t_out),
        (lse, lse_out),
        (resid, resid_out),
        (shared, shared_out),
        (dn2, dn2_out),
        (gains, gains_out),
        (cosine, cosine_out),
        (sinus, sinus_out),
        (hot, hot_out),
        (reach_t, reach_t_out),
        (a_qkv, a_qkv_out),
        (b_qkv2, b_qkv2_out),
        (a_qkv_t2, a_qkv_t2_out),
        (a_o, a_o_out),
        (b_o2, b_o2_out),
        (a_o_t2, a_o_t2_out),
        (table_all, table_all_out),
        (place_row, place_row_out),
        (place_col, place_col_out),
        (weight_col, weight_col_out),
    )
    given = []

    def give_out(refs):
        for i, (ref, target) in enumerate(targets):
            if any(ref is other for other in refs):
                copy = pltpu.make_async_copy(ref, target, out_sems.at[i])
                copy.start()
                given.append(copy)

    def half_rows(chunk, part):
        return pl.ds(pl.multiple_of(chunk * rows + part * half, 16), half)

    def up(chunk, source):
        return send(
            source,
            x_buf.at[half_rows(chunk, t)],
            z_send.at[chunk],
            z_recv.at[chunk],
            (f, c + 1, t),
        )

    def across(chunk):
        block = x_buf.at[half_rows(chunk, t)]
        return send(block, block, core_send.at[chunk], core_recv.at[chunk], sibling)

    @pl.when(c < contexts - 1)
    def _():
        up(c, x_in.at[half_rows(0, t)]).start()

    gathers = []
    halved = (False, False, True, False)
    neighbour = (f, c + 1 - 2 * lax.rem(c, 2), t)
    own_half = own_n // 2
    for i, (own, buf) in enumerate(((wq_in, wq), (wo_in, wo), (gu_in, gu), (dn_in, dn))):
        base, count = (lax.rem(c, 2) * own_half, own_half) if halved[i] else (0, own_n)
        gathers.append(
            Gather(bits, f, peer, own, buf, own_n, base, count, fs_send.at[i], fs_recv.at[i])
        )

    def lent(gather, buf, which):
        copies, number = [], 0
        for stage in range(bits):
            group = []
            for block in gather.arrived[stage]:
                group.append(
                    send(
                        buf.at[block],
                        buf.at[block],
                        lend_send.at[which, number],
                        lend_recv.at[which, number],
                        neighbour,
                    )
                )
                number = number + 1
            copies.append(group)
        return copies

    gu_lent = lent(gathers[2], gu, 0)

    z_busy = (lax.rem(c, 2) == 0) & (c > 0)

    def lend(copies, stage):
        for copy in copies[stage]:
            copy.start()
    g_gather = Gather(
        bits, f, peer, g_in, g_all, rows, t * half, half, fs_send.at[4], fs_recv.at[4]
    )
    n2_gather = Gather(
        bits, f, peer, n2_own, n2_all, rows, t * half, half, fs_send.at[5], fs_recv.at[5]
    )
    wq_gather, wo_gather, gu_gather, dn_gather = gathers
    small = []
    for k, other in enumerate(peers):
        for j, (source, target) in enumerate(
            ((adapters_in, adapters_all), (gains_in, gains_all), (table_in, table_all))
        ):
            copy = send(source, target.at[f], small_send.at[j, k], small_recv.at[j, k], other)
            copy.start()
            small.append(copy)
    wq_gather.start(0)
    locals_ = [pltpu.make_async_copy(x_in, x_buf.at[pl.ds(c * rows, rows)], local_sems.at[0])]
    for i, (own, buf) in enumerate(((wq_in, wq), (wo_in, wo), (gu_in, gu), (dn_in, dn))):
        locals_.append(
            pltpu.make_async_copy(own, buf.at[pl.ds(f * own_n, own_n)], local_sems.at[1 + i])
        )
    locals_.append(pltpu.make_async_copy(g_in, g_own, local_sems.at[5]))
    locals_.append(
        pltpu.make_async_copy(g_in, g_all.at[pl.ds(f * rows, rows)], local_sems.at[6])
    )
    for copy in locals_:
        copy.start()

    o_t[...] = jnp.zeros_like(o_t)
    peak[...] = jnp.full_like(peak, masked_score)
    total[...] = jnp.zeros_like(total)
    da_gu[...] = jnp.zeros_like(da_gu)
    db_gu[...] = jnp.zeros_like(db_gu)
    da_dn[...] = jnp.zeros_like(da_dn)
    db_dn[...] = jnp.zeros_like(db_dn)
    adapters_all[f] = adapters_in[...]
    gains_all[f] = gains_in[...]
    table_all[f] = table_in[...]
    tree_tables(parents, lengths, turns, c, rows, hot, reach_t, cosine, sinus)

    def receive(step):
        chunk = c - step

        @pl.when(step <= c)
        def _():
            up(chunk, x_buf.at[half_rows(chunk, t)]).wait_recv()

            @pl.when(c < contexts - 1)
            def _():
                up(chunk, x_buf.at[half_rows(chunk, t)]).start()

            across(chunk).start()

    def chunk_rows(chunk):
        return pl.ds(pl.multiple_of(chunk * rows, 16), rows)

    def out_copies(chunk):
        block = chunk_rows(chunk)
        return [
            pltpu.make_async_copy(n1_buf.at[block], n1_all.at[block], chunk_sems.at[0, chunk]),
            pltpu.make_async_copy(k_buf.at[block], k_all.at[block], chunk_sems.at[1, chunk]),
            pltpu.make_async_copy(v_buf.at[block], v_all.at[block], chunk_sems.at[2, chunk]),
        ]

    def project(chunk, own):
        block = chunk_rows(chunk)
        n1 = normed(x_buf[block, :].astype(jnp.float32), gain_one)
        n1_buf[block, :] = n1
        rank = two_parts(nn_dot(n1, a_qkv[...]))
        cos_rows = cosine[block, :]
        sin_rows = sinus[block, :]
        start = 0 if own else width
        result = nn_dot(n1, wq[:, start:]) + nn_dot(rank, b_qkv2[:, start:])
        for p in range(width // 128):
            lanes = slice(128 * p, 128 * p + 128)
            cols = slice(width - start + 128 * p, width - start + 128 * p + 128)
            k_buf[block, lanes] = turn(result[:, cols], cos_rows, sin_rows).astype(jnp.bfloat16)
            cols = slice(2 * width - start + 128 * p, 2 * width - start + 128 * p + 128)
            value = result[:, cols]
            v_buf[block, lanes] = value.astype(jnp.bfloat16)
            v_t[lanes, :] = value.T.astype(jnp.bfloat16)
            if own:
                query = turn(result[:, lanes], cos_rows, sin_rows) * 0.125
                q_n[:, lanes] = query.astype(jnp.bfloat16)
                q_t[lanes, :] = query.T.astype(jnp.bfloat16)
        for copy in out_copies(chunk):
            copy.start()

    def weights_out(chunk, p):
        target = p_all.at[pl.ds(chunk * heads + 2 * p, 2)]
        return pltpu.make_async_copy(p_buf.at[pl.ds(2 * p, 2)], target, p_sems.at[p])

    def attend(chunk, first):
        block = chunk_rows(chunk)
        fill_bias(bias, hot[block, :], reach_t[...], chunk * rows, c * rows)

        def pair_step(p, carry):
            lanes = pl.ds(pl.multiple_of(p * 128, 128), 128)
            keys = k_buf[block, lanes]
            query = q_t[lanes, :]
            if not first:
                weights_out(chunk, p).wait()
            for odd in range(2):
                h = 2 * p + odd
                alone = jnp.where(
                    head_half(query.shape, 0, odd), query, jnp.zeros_like(query)
                )
                scores = nn_dot(keys, alone) + bias[...]
                before = peak[pl.ds(h, 1), :]
                now = jnp.maximum(before, jnp.max(scores, axis=0, keepdims=True))
                weights = jnp.exp(scores - now)
                shrink = jnp.exp(before - now)
                peak[pl.ds(h, 1), :] = now
                peaks[pl.ds(chunk * 8 + h, 1), :] = now
                low_weights = weights.astype(jnp.bfloat16)
                p_buf[h] = low_weights
                total[pl.ds(h, 1), :] = total[pl.ds(h, 1), :] * shrink + jnp.sum(
                    weights, axis=0, keepdims=True
                )
                head = pl.ds(pl.multiple_of(h * HEAD_DIM, HEAD_DIM), HEAD_DIM)
                o_t[head, :] = o_t[head, :] * shrink + nn_dot(
                    v_t[head, :], low_weights
                )
            weights_out(chunk, p).start()
            return carry

        lax.fori_loop(0, heads // 2, pair_step, 0)

    def advance(gather, following, copies=None):
        gather.wait(0)
        for stage in range(1, bits):
            gather.start(stage)
            if copies is not None:
                lend(copies, stage - 1)
            if stage < bits - 1:
                gather.wait(stage)
        following.start(0)

    for copy in small:
        copy.wait_recv()
    choose(ids, adapters_all, chosen.at[t, c])
    spread = []
    for k, other in enumerate(stacked):
        block = chosen.at[t, c]
        copy = send(block, block, small_send.at[3, k], small_recv.at[3, k], other)
        copy.start()
        spread.append(copy)
    gains[...] = jnp.zeros_like(gains)
    for i in range(2):
        pieces = [
            gains_all[b, 0:1, i * own_n : (i + 1) * own_n].astype(jnp.float32)
            for b in range(fsdp)
        ]
        gains[i : i + 1, :] = jnp.concatenate(pieces, axis=1)
    gain_one = gains[0:1, :]
    gain_two = gains[1:2, :]
    advance(wq_gather, wo_gather)
    receive(1)
    for copy in spread:
        copy.wait_recv()
    shared_copy = send(
        chosen.at[t], chosen.at[t], small_send.at[4, 0], small_recv.at[4, 0], sibling
    )
    shared_copy.start()
    route_tables(f, table_all, place_row, place_col, weight_col, marks)
    give_out(
        (table_all, place_row, place_col, weight_col, gains, cosine, sinus, hot, reach_t)
    )
    advance(wo_gather, gu_gather)
    shared_copy.wait_recv()
    unpack_adapter(
        t,
        adapters_in.shape[0] // (ADAPTERS // fsdp),
        chosen,
        flat,
        a_wide,
        (a_qkv, b_qkv2, a_qkv_t2, a_o, b_o2, a_o_t2),
        (a_gu, b_gu2, a_gu_t2, a_dn, a_dn_t2, b_dn2),
    )
    give_out((a_qkv, b_qkv2, a_qkv_t2, a_o, b_o2, a_o_t2))
    wq_gather.wait(bits - 1)
    locals_[0].wait()
    locals_[1].wait()
    wq_out = pltpu.make_async_copy(wq, wq_all, local_sems.at[10])
    wq_out.start()
    project(c, True)
    receive(2)
    attend(c, True)

    number = contexts

    def forwards(gather, buf, first):
        copies = []
        for stage in range(bits):
            group = []
            for block in gather.arrived[stage]:
                index = first + len(copies)
                copies.append(
                    send(
                        buf.at[block],
                        buf.at[block],
                        core_send.at[index],
                        core_recv.at[index],
                        sibling,
                    )
                )
        return copies

    per_stage = [len(stage) for stage in g_gather.arrived]
    g_forward = forwards(g_gather, g_all, number + 5)
    n2_forward = forwards(n2_gather, n2_all, number + 5 + sum(per_stage))

    def pass_on(copies, stage):
        start = sum(per_stage[:stage])
        for copy in copies[start : start + per_stage[stage]]:
            copy.start()

    def between(step):
        if step == 1:
            advance(gu_gather, dn_gather)

            @pl.when(jnp.logical_not(z_busy))
            def _():
                lend(gu_lent, 0)

        if step == 2:
            advance(dn_gather, g_gather)
            gu_gather.wait(bits - 1)

            @pl.when(z_busy)
            def _():
                lend(gu_lent, 0)

            for stage in range(1, bits):
                lend(gu_lent, stage)
        if step == 3:
            g_gather.wait(0)
            for stage in range(1, bits):
                g_gather.start(stage)
                pass_on(g_forward, stage - 1)
                if stage < bits - 1:
                    g_gather.wait(stage)

    def later(step):
        chunk = c - step

        @pl.when(step <= c)
        def _():
            across(chunk).wait_recv()
            project(chunk, False)
            receive(step + 2)
            attend(chunk, False)

    for step in range(1, 3):
        between(step)
        later(step)

    @pl.when(c >= 3)
    def _():
        between(3)
        later(3)

    def rest(step, carry):
        later(step)
        return carry

    lax.fori_loop(4, contexts, rest, 0)

    for h in range(heads):
        head = slice(h * HEAD_DIM, h * HEAD_DIM + HEAD_DIM)
        o_t[head, :] = o_t[head, :] / total[h : h + 1, :]
    lse[...] = peak[...] + jnp.log(total[...])
    for p in range(width // 128):
        mixed[:, 128 * p : 128 * p + 128] = o_t[128 * p : 128 * p + 128, :].T.astype(jnp.bfloat16)
    give_out((q_t, q_n, mixed, o_t, lse))
    wo_gather.wait(bits - 1)
    locals_[2].wait()
    wo_out = pltpu.make_async_copy(wo, wo_all, local_sems.at[11])
    wo_out.start()

    def local_rows(part):
        return pl.ds(pl.multiple_of(part * half, 16), half)

    mine = local_rows(t)
    theirs = local_rows(1 - t)

    def branch(block):
        values = mixed[block, :]
        rank = two_parts(nn_dot(values, a_o[...]))
        return nt_dot(values, wo[...]) + nn_dot(rank, b_o2[...])

    part_copies = []
    for i, block in enumerate((theirs, mine)):
        part_out[block, :] = branch(block).astype(jnp.bfloat16)
        copy = send(
            part_out.at[block],
            part_in.at[block],
            core_send.at[number + i],
            core_recv.at[number + i],
            sibling,
        )
        copy.start()
        part_copies.append(copy)

    def attended(block, copy):
        copy.wait_recv()
        resid[block, :] = x_rows(x_buf, c, rows, block) + (
            part_out[block, :].astype(jnp.float32) + part_in[block, :].astype(jnp.float32)
        )
        n2_own[block, :] = normed(resid[block, :], gain_two)

    attended(mine, part_copies[0])
    n2_gather.start(0)
    attended(theirs, part_copies[1])
    give_out((resid,))
    n2_out = pltpu.make_async_copy(n2_own, n2_all.at[pl.ds(f * rows, rows)], local_sems.at[12])
    n2_out.start()

    @pl.when(c < 3)
    def _():
        between(3)


    locals_[5].wait()
    for group in gu_lent:
        for copy in group:
            copy.wait_recv()
    locals_[3].wait()
    dn_gather.wait(bits - 1)
    locals_[4].wait()

    def shared_tile(block):
        inputs = n2_own[block, :]
        grads = g_own[block, :]
        rank = nn_dot(inputs, a_gu[...])
        rank2 = two_parts(rank)
        gate = nn_dot(inputs, gu[:, :units]) + nn_dot(rank2, b_gu2[:, :units])
        up_pre = nn_dot(inputs, gu[:, units:]) + nn_dot(rank2, b_gu2[:, units:])
        sigmoid_gate = jax.nn.sigmoid(gate)
        silu = gate * sigmoid_gate
        hidden = (silu * up_pre).astype(jnp.bfloat16)
        down_rank = nn_dot(hidden, a_dn[...])
        shared[block, :] = (
            nt_dot(hidden, dn[...]) + nn_dot(two_parts(down_rank), b_dn2[...])
        ).astype(jnp.bfloat16)
        down_back = nt_dot(grads, b_dn2[0:128, :])
        grad_hidden = nn_dot(grads, dn[...]) + nn_dot(two_parts(down_back), a_dn_t2[...])
        grad_gate = (
            grad_hidden * up_pre * sigmoid_gate * (1.0 + gate * (1.0 - sigmoid_gate))
        ).astype(jnp.bfloat16)
        grad_up = (grad_hidden * silu).astype(jnp.bfloat16)
        rank_back = nt_dot(grad_gate, b_gu2[0:128, :units]) + nt_dot(
            grad_up, b_gu2[0:128, units:]
        )
        dn2[block, :] = (
            nt_dot(grad_gate, gu[:, :units])
            + nt_dot(grad_up, gu[:, units:])
            + nn_dot(two_parts(rank_back), a_gu_t2[...])
        ).astype(jnp.bfloat16)
        rank_low = rank.astype(jnp.bfloat16)
        da_gu[...] += tn_dot(rank_back.astype(jnp.bfloat16), inputs)[0 : 2 * RANK]
        db_gu[0:RANK, :] += 2.0 * tn_dot(rank_low, grad_gate)[0:RANK]
        db_gu[RANK:, :] += 2.0 * tn_dot(rank_low, grad_up)[RANK : 2 * RANK]
        da_dn[...] += tn_dot(down_back.astype(jnp.bfloat16), hidden)[0:RANK]
        db_dn[...] += 2.0 * tn_dot(down_rank.astype(jnp.bfloat16), grads)[0:RANK]

    def pass_pieces(gather, copies, stage):
        start = sum(per_stage[:stage])
        for i, copy in enumerate(gather.stages[stage]):
            copy.wait_recv()
            copies[start + i].start()

    shared_tile(mine)
    n2_gather.wait(0)
    for stage in range(1, bits):
        n2_gather.start(stage)
        pass_on(n2_forward, stage - 1)
        if stage < bits - 1:
            n2_gather.wait(stage)
    shared_tile(theirs)
    give_out((shared, dn2))
    pass_pieces(g_gather, g_forward, bits - 1)
    pass_pieces(n2_gather, n2_forward, bits - 1)
    for copy in n2_forward + g_forward:
        copy.wait()
    for copy in small + spread + [shared_copy]:
        copy.wait_send()
    for group in gu_lent:
        for copy in group:
            copy.wait_send()
    for copy in given:
        copy.wait()
    for copy in part_copies:
        copy.wait_send()
    for gather in gathers + [g_gather, n2_gather]:
        gather.finish()
    n2_out.wait()
    wq_out.wait()
    wo_out.wait()
    locals_[6].wait()

    @pl.when(c < contexts - 1)
    def _():
        up(c, x_in.at[half_rows(0, t)]).wait_send()

    def drain(step, carry):
        chunk = c - step

        @pl.when(c < contexts - 1)
        def _():
            up(chunk, x_buf.at[half_rows(chunk, t)]).wait_send()

        across(chunk).wait_send()
        return carry

    lax.fori_loop(1, c + 1, drain, 0)

    def drain_out(step, carry):
        for copy in out_copies(c - step):
            copy.wait()
        return carry

    lax.fori_loop(0, c + 1, drain_out, 0)
    for p in range(heads // 2):
        weights_out(0, p).wait()


def x_rows(x_buf, chunk, rows, block):
    return x_buf[pl.ds(pl.multiple_of(chunk * rows, 16) + block.start, block.size), :].astype(
        jnp.float32
    )


def forward_call(sizes, sharded, local):
    fsdp, contexts, _ = sizes
    x, g, wq, wo, gu, dn = sharded
    adapters, gains, table = local[:3]
    rows = x.shape[0]
    tree = rows * contexts
    width = wo.shape[1]
    units = dn.shape[1]
    bf, f32 = jnp.bfloat16, jnp.float32
    vmem = pl.BlockSpec(memory_space=pltpu.VMEM)
    hbm = pl.BlockSpec(memory_space=pl.ANY)
    smem = pl.BlockSpec(memory_space=pltpu.SMEM)
    slots = max(fsdp, contexts)
    total = fsdp * rows
    per_adapter = adapters.shape[0] // (ADAPTERS // fsdp)

    def shape(kind, *dims):
        return jax.ShapeDtypeStruct(dims, kind)

    moves = 2 * (fsdp - 1)
    hops = contexts + 5 + 2 * moves
    return pl.pallas_call(
        functools.partial(forward_kernel, sizes),
        in_specs=[hbm] * 6 + [vmem] * 4 + [smem] * 3,
        out_specs=[hbm] * 8 + [hbm, hbm, hbm, hbm, hbm, hbm, hbm, hbm, vmem, vmem, vmem, vmem, hbm, hbm, hbm, hbm, hbm, hbm, hbm, hbm, hbm, hbm, hbm, hbm, hbm, hbm, hbm, vmem, vmem],
        out_shape=[
            shape(bf, tree, D),
            shape(bf, tree, width),
            shape(bf, tree, width),
            shape(bf, D, 3 * width),
            shape(bf, D, width),
            shape(bf, fsdp * rows, D),
            shape(bf, fsdp * rows, D),
            shape(bf, contexts * (width // HEAD_DIM), rows, rows),
            shape(bf, width, rows),
            shape(bf, rows, width),
            shape(bf, rows, width),
            shape(f32, width, rows),
            shape(f32, 8, rows),
            shape(f32, rows, D),
            shape(bf, rows, D),
            shape(bf, rows, D),
            shape(f32, 2 * RANK, D),
            shape(f32, 2 * RANK, units),
            shape(f32, RANK, units),
            shape(f32, RANK, D),
            shape(f32, 8, D),
            shape(f32, tree, 128),
            shape(f32, tree, 128),
            shape(bf, tree, 128),
            shape(bf, 128, rows),
            shape(bf, D, 128),
            shape(bf, 256, 3 * width),
            shape(bf, 256, D),
            shape(bf, width, 128),
            shape(bf, 256, D),
            shape(bf, 256, width),
            shape(f32, fsdp, 8, rows),
            shape(f32, 8, total),
            shape(f32, total, 128),
            shape(bf, total, 128),
            shape(f32, 8, 128),
            shape(f32, contexts * 8, rows),
        ],
        scratch_shapes=[
            pltpu.VMEM((tree, D), bf),
            pltpu.VMEM((D, 3 * width), bf),
            pltpu.VMEM((D, width), bf),
            pltpu.VMEM((D, 2 * units), bf),
            pltpu.VMEM((D, units), bf),
            pltpu.VMEM((rows, D), bf),
            pltpu.VMEM((tree, D), bf),
            pltpu.VMEM((tree, width), bf),
            pltpu.VMEM((tree, width), bf),
            pltpu.VMEM((width, rows), bf),
            pltpu.VMEM((8, rows), f32),
            pltpu.VMEM((8, rows), f32),
            pltpu.VMEM((rows, rows), f32),
            pltpu.VMEM((rows, D), bf),
            pltpu.VMEM((rows, D), bf),
            pltpu.VMEM((rows, D), bf),
            pltpu.VMEM((rows, D), bf),
            pltpu.VMEM((rows, D), bf),
            pltpu.VMEM((fsdp,) + adapters.shape, bf),
            pltpu.VMEM((fsdp,) + gains.shape, bf),
            pltpu.VMEM((2, contexts, per_adapter, 128), bf),
            pltpu.VMEM((PARAMS // 128, 128), f32),
            pltpu.VMEM((max(D, units), 128), f32),
            pltpu.VMEM((D, 128), bf),
            pltpu.VMEM((256, 2 * units), bf),
            pltpu.VMEM((256, D), bf),
            pltpu.VMEM((units, 128), bf),
            pltpu.VMEM((256, units), bf),
            pltpu.VMEM((256, D), bf),
            pltpu.SemaphoreType.DMA((6, moves)),
            pltpu.SemaphoreType.DMA((6, moves)),
            pltpu.SemaphoreType.DMA((contexts,)),
            pltpu.SemaphoreType.DMA((contexts,)),
            pltpu.SemaphoreType.DMA((hops,)),
            pltpu.SemaphoreType.DMA((hops,)),
            pltpu.SemaphoreType.DMA((13,)),
            pltpu.SemaphoreType.DMA((3, contexts)),
            pltpu.SemaphoreType.DMA((5, slots)),
            pltpu.SemaphoreType.DMA((5, slots)),
            pltpu.SemaphoreType.DMA((2, moves)),
            pltpu.SemaphoreType.DMA((2, moves)),
            pltpu.VMEM((width, rows), bf),
            pltpu.VMEM((rows, width), bf),
            pltpu.VMEM((rows, width), bf),
            pltpu.VMEM((width, rows), f32),
            pltpu.VMEM((8, rows), f32),
            pltpu.VMEM((rows, D), f32),
            pltpu.VMEM((8, D), f32),
            pltpu.VMEM((tree, 128), f32),
            pltpu.VMEM((tree, 128), f32),
            pltpu.VMEM((tree, 128), bf),
            pltpu.VMEM((128, rows), bf),
            pltpu.VMEM((D, 128), bf),
            pltpu.VMEM((256, 3 * width), bf),
            pltpu.VMEM((256, D), bf),
            pltpu.VMEM((width, 128), bf),
            pltpu.VMEM((256, D), bf),
            pltpu.VMEM((256, width), bf),
            pltpu.VMEM((fsdp, 8, rows), f32),
            pltpu.VMEM((8, total), f32),
            pltpu.VMEM((total, 128), f32),
            pltpu.VMEM((total, 128), bf),
            pltpu.SemaphoreType.DMA((23,)),
            pltpu.VMEM((width // HEAD_DIM, rows, rows), bf),
            pltpu.SemaphoreType.DMA((width // HEAD_DIM // 2,)),
        ],
        name="forward",
        compiler_params=pltpu.CompilerParams(
            collective_id=2, has_side_effects=True, vmem_limit_bytes=62 << 20
        ),
    )(*sharded, *local)


def flips(index, mask, bits):
    for bit in range(bits):
        if mask >> bit & 1:
            index = flip(index, bit)
    return index


class Scatter:
    def __init__(self, bits, me, device_of, work, inbox, count, send_sems, recv_sems):
        self.bits, self.work, self.inbox = bits, work, inbox
        self.copies = [[] for _ in range(bits)]
        self.masks = [[] for _ in range(bits)]
        self.adds = [[] for _ in range(bits)]
        number = 0
        for half, (offset, size) in enumerate(split_rows(count)):
            alive = list(range(1 << bits))
            slot = 0
            for stage in range(bits):
                bit = (stage + half) % bits
                for mask in alive:
                    if mask >> bit & 1:
                        source = Gather.rows(flips(me, mask, bits) * count + offset, size)
                        target = pl.ds(slot * count + offset, size)
                        kept = Gather.rows(flips(me, mask ^ (1 << bit), bits) * count + offset, size)
                        self.copies[stage].append(
                            send(
                                work.at[source],
                                inbox.at[target],
                                send_sems.at[number],
                                recv_sems.at[number],
                                device_of(flip(me, bit)),
                            )
                        )
                        self.adds[stage].append((kept, target, pl.ds(offset, size)))
                        self.masks[stage].append(mask)
                        number = number + 1
                        slot = slot + 1
                alive = [mask for mask in alive if not mask >> bit & 1]

    def start(self, stage):
        for copy in self.copies[stage]:
            copy.start()

    def start_mask(self, mask):
        for copy, number in zip(self.copies[0], self.masks[0]):
            if number == mask:
                copy.start()

    def add(self, stage):
        for copy in self.copies[stage]:
            copy.wait_recv()
        for kept, target, _ in self.adds[stage]:
            total = self.work[kept, :].astype(jnp.float32) + self.inbox[target, :].astype(
                jnp.float32
            )
            self.work[kept, :] = total.astype(jnp.bfloat16)

    def last(self, out):
        for copy in self.copies[self.bits - 1]:
            copy.wait_recv()
        for kept, target, rows in self.adds[self.bits - 1]:
            total = self.work[kept, :].astype(jnp.float32) + self.inbox[target, :].astype(
                jnp.float32
            )
            out[rows, :] = total.astype(jnp.bfloat16)

    def finish(self):
        for stage in self.copies:
            for copy in stage:
                copy.wait_send()


def pack_rows(grad_t, start, rank, flat, wide):
    total = grad_t.shape[1]
    more = jnp.zeros((128 - rank, 128), jnp.float32)
    for p in range(total // 128):
        piece = grad_t[:, 128 * p : 128 * p + 128]
        wide[128 * p : 128 * p + 128, :] = jnp.concatenate([piece, more], axis=0).T
    lines = rank // math.gcd(rank, 128)
    each = lines * 128 // rank
    count = total // each
    joined = jnp.concatenate(
        [wide[pl.ds(i, count, stride=each), :][:, 0:rank] for i in range(each)], axis=1
    )
    if lines == 1:
        flat[pl.ds(start, count), :] = joined
    else:
        for i in range(lines):
            flat[pl.ds(start + i, count, stride=lines), :] = joined[:, 128 * i : 128 * i + 128]


def pack_lines(grad, start, lines, columns, flat):
    for p, m in enumerate(columns):
        flat[pl.ds(start + m, grad.shape[0], stride=lines), :] = grad[:, 128 * p : 128 * p + 128]


def pack_first(t, flat, wide, da_qkv, db_qkv, da_o, db_o):
    width = da_o.shape[1]
    lines = D // 128
    mine = [t * (width // 128) + p for p in range(width // 128)]
    pack_rows(da_qkv[...], 0, 3 * RANK, flat, wide)
    at = 3 * RANK * D // 128
    for j in range(3):
        rows = slice(j * RANK, (j + 1) * RANK)
        pack_lines(db_qkv[rows, :], at + j * RANK * lines, lines, mine, flat)
    at = at + 3 * RANK * lines
    pack_rows(da_o[...], at + t * (width * RANK // 128), RANK, flat, wide)
    at = at + D * RANK // 128
    pack_lines(db_o[...], at, lines, list(range(lines)), flat)


def pack_second(t, flat, wide, da_gu, db_gu, da_dn, db_dn):
    units = da_dn.shape[1]
    lines = D // 128
    at = 8 * RANK * D // 128
    pack_rows(da_gu[...], at, 2 * RANK, flat, wide)
    at = at + 2 * RANK * D // 128
    wide_lines = FF // 128
    mine = [t * (units // 128) + p for p in range(units // 128)]
    for j in range(2):
        rows = slice(j * RANK, (j + 1) * RANK)
        pack_lines(db_gu[rows, :], at + j * RANK * wide_lines, wide_lines, mine, flat)
    at = at + 2 * RANK * wide_lines
    pack_rows(da_dn[...], at + t * (units * RANK // 128), RANK, flat, wide)
    at = at + FF * RANK // 128
    pack_lines(db_dn[...], at, lines, list(range(lines)), flat)


def backward_kernel(
    sizes,
    moe_out,
    moe_back,
    n1_hbm,
    k_hbm,
    v_hbm,
    wq_hbm,
    wo_hbm,
    cos_hbm,
    sin_hbm,
    p_hbm,
    x_in_hbm,
    g_in_hbm,
    gains,
    peaks,
    resid_hbm,
    shared_hbm,
    dn2_hbm,
    q_t_hbm,
    q_n_hbm,
    mixed_hbm,
    o_t_hbm,
    lse,
    a_qkv_hbm,
    b_qkv2_hbm,
    a_qkv_t2_hbm,
    a_o_hbm,
    a_o_t2_hbm,
    b_o2_hbm,
    da_gu,
    db_gu,
    da_dn,
    db_dn,
    table_all,
    block_out,
    input_grad,
    adapter_out,
    cosine,
    sinus,
    k_buf,
    v_buf,
    wq,
    wo,
    work_back,
    pair_back,
    inbox_back,
    work_out,
    pair_out,
    inbox_out,
    total_half,
    total_full,
    ffn_half,
    ffn_full,
    dy,
    do_n,
    do_t,
    delta,
    factor,
    k_t,
    dq_t,
    part_in,
    z_in,
    dn1_full,
    fs_send,
    fs_recv,
    z_send,
    z_recv,
    core_send,
    core_recv,
    pair_send,
    pair_recv,
    local_sems,
    chunk_sems,
    x_in,
    g_in,
    resid,
    shared,
    dn2,
    q_t,
    q_n,
    mixed,
    o_t,
    a_qkv,
    b_qkv2,
    a_qkv_t2,
    a_o,
    a_o_t2,
    b_o2,
    da_qkv,
    db_qkv,
    da_o,
    db_o,
    flat,
    wide,
    packed,
    packed_in,
    up_out,
    up_in,
    own_sum,
    tree_sums,
    in_sems,
    sum_send,
    sum_recv,
    p_buf,
    p_sems,
    whole_back,
    whole_out,
):
    fsdp, contexts, _ = sizes
    bits = fsdp.bit_length() - 1
    f, c, t = place_of()
    rows = x_in.shape[0]
    half = rows // 2
    width = q_t.shape[0]
    inputs = []
    for i, (source, target) in enumerate(
        (
            (x_in_hbm, x_in),
            (g_in_hbm, g_in),
            (resid_hbm, resid),
            (shared_hbm, shared),
            (dn2_hbm, dn2),
            (q_t_hbm, q_t),
            (q_n_hbm, q_n),
            (mixed_hbm, mixed),
            (o_t_hbm, o_t),
            (a_qkv_hbm, a_qkv),
            (b_qkv2_hbm, b_qkv2),
            (a_qkv_t2_hbm, a_qkv_t2),
            (a_o_hbm, a_o),
            (a_o_t2_hbm, a_o_t2),
            (b_o2_hbm, b_o2),
        )
    ):
        inputs.append(pltpu.make_async_copy(source, target, in_sems.at[i]))
    heads = width // HEAD_DIM
    part_out, z_out, grad_kv = pair_back, work_back, inbox_back
    part, n1_buf = whole_back, whole_out
    kv_rows = pl.ds(0, rows)
    sibling = (f, c, 1 - t)
    f32, bf = jnp.float32, jnp.bfloat16

    def peer(index):
        return (index, c, t)

    def local_rows(part_index):
        return pl.ds(pl.multiple_of(part_index * half, 16), half)

    mine = local_rows(t)
    theirs = local_rows(1 - t)

    def block_rows(block, part_index):
        return pl.ds(pl.multiple_of(block * rows + part_index * half, 16), half)

    def work_rows(block):
        return pl.ds(pl.multiple_of(block * half, 16), half)

    masks = list(range(fsdp - 1, -1, -1))

    def exchange(source, work, inbox, which, whole):
        own, sent = [], []
        for mask in masks:
            block = flips(f, mask, bits)
            if mask == 0:
                own.append(
                    pltpu.make_async_copy(
                        source.at[pl.ds(pl.multiple_of(f * rows, 16), rows)],
                        whole,
                        local_sems.at[which, mask],
                    )
                )
                sent.append(
                    send(
                        whole.at[theirs],
                        inbox.at[work_rows(block)],
                        core_send.at[which, mask],
                        core_recv.at[which, mask],
                        sibling,
                    )
                )
                continue
            own.append(
                pltpu.make_async_copy(
                    source.at[block_rows(block, t)],
                    work.at[work_rows(block)],
                    local_sems.at[which, mask],
                )
            )
            sent.append(
                send(
                    source.at[block_rows(block, 1 - t)],
                    inbox.at[work_rows(block)],
                    core_send.at[which, mask],
                    core_recv.at[which, mask],
                    sibling,
                )
            )
        return own, sent

    back_own, back_sent = exchange(moe_back, work_back, pair_back, 0, whole_back)
    out_own, out_sent = exchange(moe_out, work_out, pair_out, 1, whole_out)
    for copy in back_own:
        copy.start()
    wo_copy = pltpu.make_async_copy(wo_hbm, wo, local_sems.at[2, 0])
    wq_copy = pltpu.make_async_copy(wq_hbm, wq, local_sems.at[2, 1])
    wo_copy.start()
    for copy in inputs:
        copy.start()
    peers = [(lax.rem(f + k, fsdp), c, t) for k in range(1, fsdp)]
    stacked = [(f, lax.rem(c + k, contexts), t) for k in range(1, contexts)]
    greet(peers + stacked + [sibling])
    for copy in back_sent[:-1]:
        copy.start()
    for copy in out_own:
        copy.start()
    wq_copy.start()

    lines = PARAMS // 128 // (2 * contexts)
    early = -(-(8 * RANK * D // 128) // (2 * lines))

    def fill_blocks(first, last):
        for context in range(first, last):
            for part_index in range(2):
                start = (2 * context + part_index) * lines
                packed[context, part_index, 0:lines, :] = flat[start : start + lines, :]

    def pair_block(block):
        return send(
            packed.at[block, 1 - t],
            packed_in.at[block],
            sum_send.at[0, block],
            sum_recv.at[0, block],
            sibling,
        )

    def to_owner(k):
        return send(
            up_out.at[k], up_in.at[k], sum_send.at[1, k], sum_recv.at[1, k], stacked[k]
        )

    def push_blocks(soon):
        for k in range(contexts - 1):
            owner = lax.rem(c + k + 1, contexts)

            @pl.when((owner >= early) if soon else (owner < early))
            def _(k=k, owner=owner):
                up_out[k] = (packed[owner, t] + packed_in[owner]).astype(bf)
                to_owner(k).start()

    def to_peer(k):
        return send(
            own_sum, tree_sums.at[k], sum_send.at[2, k], sum_recv.at[2, k], peers[k]
        )

    def sum_own():
        result = packed[c, t] + packed_in[c]
        for k in range(contexts - 1):
            to_owner(k).wait_recv()
            result = result + up_in[k].astype(f32)
        own_sum[...] = result.astype(bf)
        for k in range(fsdp - 1):
            to_peer(k).start()

    def chunk_rows(chunk):
        return pl.ds(pl.multiple_of(chunk * rows, 16), rows)

    def loads(chunk):
        block = chunk_rows(chunk)
        return [
            pltpu.make_async_copy(k_hbm.at[block], k_buf.at[block], chunk_sems.at[1, chunk]),
            pltpu.make_async_copy(v_hbm.at[block], v_buf.at[block], chunk_sems.at[2, chunk]),
        ]

    def n1_load(chunk):
        return pltpu.make_async_copy(
            n1_hbm.at[chunk_rows(chunk)], n1_buf, chunk_sems.at[0, chunk]
        )

    def table_loads(chunk):
        block = chunk_rows(chunk)
        return [
            pltpu.make_async_copy(cos_hbm.at[block], cosine, chunk_sems.at[3, chunk]),
            pltpu.make_async_copy(sin_hbm.at[block], sinus, chunk_sems.at[4, chunk]),
        ]

    def start_loads(chunk, carry):
        for copy in loads(chunk):
            copy.start()
        return carry

    lax.fori_loop(0, c + 1, start_loads, 0)

    def weights_in(chunk, p):
        source = p_hbm.at[pl.ds(chunk * heads + 2 * p, 2)]
        return pltpu.make_async_copy(source, p_buf.at[pl.ds(2 * p, 2)], p_sems.at[p])

    for p in range(heads // 2):
        weights_in(0, p).start()

    back = Scatter(
        bits, f, peer, work_back, inbox_back, half, fs_send.at[0], fs_recv.at[0]
    )
    out = Scatter(bits, f, peer, work_out, inbox_out, half, fs_send.at[1], fs_recv.at[1])

    def join(own, sent, whole, extra, work):
        own[-1].wait()
        whole[...] = (whole[...].astype(f32) + extra[...].astype(f32)).astype(bf)
        sent[-1].start()
        work[work_rows(f), :] = whole[mine, :]

    def pair_sum(own, sent, work, inbox, scatter):
        for i, mask in enumerate(masks):
            block = work_rows(flips(f, mask, bits))
            if mask != 0:
                own[i].wait()
            sent[i].wait_recv()
            work[block, :] = (
                work[block, :].astype(f32) + inbox[block, :].astype(f32)
            ).astype(bf)
            scatter.start_mask(mask)

    for copy in inputs:
        copy.wait()
    join(back_own, back_sent, whole_back, dn2, work_back)
    pair_sum(back_own, back_sent, work_back, pair_back, back)
    for copy in out_sent[:-1]:
        copy.start()
    join(out_own, out_sent, whole_out, shared, work_out)
    flat[...] = jnp.zeros_like(flat)
    pack_second(t, flat, wide, da_gu, db_gu, da_dn, db_dn)
    fill_blocks(early, contexts)
    for block in range(early, contexts):
        pair_block(block).start()
    for stage in range(1, bits):
        back.add(stage - 1)
        back.start(stage)
    dq_t[...] = jnp.zeros_like(dq_t)
    da_qkv[...] = jnp.zeros_like(da_qkv)
    db_qkv[...] = jnp.zeros_like(db_qkv)
    for block in range(early, contexts):
        pair_block(block).wait_recv()
    push_blocks(True)
    back.last(total_half)
    pair_sum(out_own, out_sent, work_out, pair_out, out)
    for copy in out_sent:
        copy.wait_send()
    total_full[mine, :] = total_half[...]
    full_copy = send(
        total_half, total_full.at[mine], core_send.at[2, 0], core_recv.at[2, 0], sibling
    )
    full_copy.start()
    back.finish()
    for copy in back_sent:
        copy.wait_send()
    gain_one = gains[0:1, :]
    gain_two = gains[1:2, :]
    wo_copy.wait()
    full_copy.wait_recv()

    def attn_tile(i, carry):
        block = local_rows(i)
        values = resid[block, :]
        gradient = g_in[block, :].astype(f32) + norm_back(
            values, rms_scale(values), gain_two, total_full[block, :].astype(f32)
        )
        dy[block, :] = gradient
        low_grad = gradient.astype(bf)
        rank_back = nt_dot(low_grad, b_o2[0:128, :])
        do_n[block, :] = (
            nn_dot(low_grad, wo[...]) + nn_dot(two_parts(rank_back), a_o_t2[...])
        ).astype(bf)
        values_o = mixed[block, :]
        rank = nn_dot(values_o, a_o[...])
        first = tn_dot(rank_back.astype(bf), values_o)[0:RANK]
        second = 2.0 * tn_dot(rank.astype(bf), low_grad)[0:RANK]

        @pl.when(i == 0)
        def _():
            da_o[...] = first
            db_o[...] = second

        @pl.when(i > 0)
        def _():
            da_o[...] += first
            db_o[...] += second

        return carry

    lax.fori_loop(0, 2, attn_tile, 0)
    for p in range(width // 128):
        lanes = slice(128 * p, 128 * p + 128)
        turned = do_n[:, lanes].astype(f32).T
        do_t[lanes, :] = turned.astype(bf)
        product = turned * o_t[lanes, :]
        for odd in range(2):
            delta[2 * p + odd : 2 * p + odd + 1, :] = jnp.sum(
                product[HEAD_DIM * odd : HEAD_DIM * odd + HEAD_DIM, :], axis=0, keepdims=True
            )
    wq_copy.wait()

    def attend_back(chunk):
        block = chunk_rows(chunk)
        n1_load(chunk).start()
        for copy in table_loads(chunk):
            copy.start()
        for copy in table_loads(chunk) + loads(chunk):
            copy.wait()
        scale = jnp.exp(peaks[pl.ds(pl.multiple_of(chunk * 8, 8), 8), :] - lse[...])
        factor[...] = scale
        cos_rows = cosine[...]
        sin_rows = -sinus[...]
        for p in range(width // 128):
            lanes = slice(128 * p, 128 * p + 128)
            k_t[lanes, :] = k_buf[block, lanes].astype(f32).T.astype(bf)

        def pair_step(p, carry):
            lanes = pl.ds(pl.multiple_of(p * 128, 128), 128)
            weights_in(chunk, p).wait()
            values = v_buf[block, lanes]
            grad_t = do_t[lanes, :]
            query = q_n[:, lanes]
            grad = do_n[:, lanes]
            grad_keys = jnp.zeros((rows, 128), f32)
            grad_values = jnp.zeros((rows, 128), f32)
            for odd in range(2):
                h = 2 * p + odd
                upper = head_half(grad_t.shape, 0, odd)
                side = head_half(query.shape, 1, odd)
                none_t = jnp.zeros_like(grad_t)
                none = jnp.zeros_like(query)
                weights = p_buf[h].astype(f32) * factor[pl.ds(h, 1), :]
                low_weights = weights.astype(bf)
                grad_weights = nn_dot(values, jnp.where(upper, grad_t, none_t))
                grad_scores = (weights * (grad_weights - delta[pl.ds(h, 1), :])).astype(bf)
                grad_values += nn_dot(low_weights, jnp.where(side, grad, none))
                grad_keys += nn_dot(grad_scores, jnp.where(side, query, none))
                head = pl.ds(pl.multiple_of(h * HEAD_DIM, HEAD_DIM), HEAD_DIM)
                dq_t[head, :] += nn_dot(k_t[head, :], grad_scores)
            grad_kv[kv_rows, lanes] = turn(grad_keys, cos_rows, sin_rows).astype(bf)
            grad_kv[kv_rows, pl.ds(pl.multiple_of(width + p * 128, 128), 128)] = grad_values.astype(bf)

            @pl.when(chunk < c)
            def _():
                weights_in(chunk + 1, p).start()

            return carry

        lax.fori_loop(0, heads // 2, pair_step, 0)

    def project_back(chunk, own):
        block = chunk_rows(chunk)
        grads = grad_kv[kv_rows, :]
        result = nt_dot(grads, wq[:, width:])
        rank_back = nt_dot(grads, b_qkv2[0:128, width:])
        n1_load(chunk).wait()
        n1 = n1_buf[...]
        rank = nn_dot(n1, a_qkv[...]).astype(bf)
        both = 2.0 * tn_dot(rank, grads)
        db_qkv[RANK : 2 * RANK, :] += both[RANK : 2 * RANK, :width]
        db_qkv[2 * RANK :, :] += both[2 * RANK : 3 * RANK, width:]
        if own:
            pieces = []
            for p in range(width // 128):
                lanes = slice(128 * p, 128 * p + 128)
                grad_query = (dq_t[lanes, :] * 0.125).T
                pieces.append(
                    turn(grad_query, cosine[...], -sinus[...]).astype(bf)
                )
            grad_query = jnp.concatenate(pieces, axis=1)
            result += nt_dot(grad_query, wq[:, :width])
            rank_back += nt_dot(grad_query, b_qkv2[0:128, :width])
            db_qkv[0:RANK, :] += 2.0 * tn_dot(rank, grad_query)[0:RANK, :]
        result += nn_dot(two_parts(rank_back), a_qkv_t2[...])
        da_qkv[...] += tn_dot(rank_back.astype(bf), n1)[0 : 3 * RANK]
        part[...] = result.astype(bf)
        part_out[work_rows(chunk), :] = part[theirs, :]
        z_out[work_rows(chunk), :] = part[mine, :]

    def pair_copy(chunk):
        return send(
            part_out.at[work_rows(chunk)],
            part_in.at[work_rows(chunk)],
            pair_send.at[chunk],
            pair_recv.at[chunk],
            sibling,
        )

    def down(chunk):
        block = work_rows(chunk)
        return send(
            z_out.at[block], z_in.at[block], z_send.at[chunk], z_recv.at[chunk], (f, c - 1, t)
        )

    def chain(chunk):
        block = work_rows(chunk)
        pair_copy(chunk).wait_recv()
        summed = z_out[block, :].astype(f32) + part_in[block, :].astype(f32)
        z_out[block, :] = summed.astype(bf)

        @pl.when(c < contexts - 1)
        def _():
            down(chunk).wait_recv()
            z_out[block, :] = (summed + z_in[block, :].astype(f32)).astype(bf)

    def pass_down(chunk):
        chain(chunk)
        down(chunk).start()

    def sum_moe():
        for stage in range(1, bits):
            out.add(stage - 1)
            out.start(stage)

    ffn_copy = send(ffn_half, ffn_full.at[mine], core_send.at[2, 1], core_recv.at[2, 1], sibling)

    def share_moe():
        out.last(ffn_half)
        ffn_full[mine, :] = ffn_half[...]
        ffn_copy.start()

    def step(chunk, carry):
        attend_back(chunk)
        project_back(chunk, False)
        pair_copy(chunk).start()

        @pl.when(c == contexts - 1)
        def _():
            pass_down(chunk)

        @pl.when((c < contexts - 1) & (chunk >= 1))
        def _():
            pass_down(chunk - 1)

        @pl.when(chunk == 0)
        def _():
            sum_moe()

        @pl.when(chunk == 1)
        def _():
            share_moe()

            @pl.when(c >= early)
            def _():
                sum_own()

        return carry

    lax.fori_loop(0, c, step, 0)
    attend_back(c)
    project_back(c, True)
    pair_copy(c).start()
    pack_first(t, flat, wide, da_qkv, db_qkv, da_o, db_o)
    fill_blocks(0, early)
    for block in range(early):
        pair_block(block).start()

    @pl.when((c < 2) & (c >= early))
    def _():
        sum_own()

    @pl.when(c == 0)
    def _():
        sum_moe()

    @pl.when((c < contexts - 1) & (c >= 1))
    def _():
        pass_down(c - 1)

    for block in range(early):
        pair_block(block).wait_recv()
    push_blocks(False)

    @pl.when(c < 2)
    def _():
        share_moe()

    chain(c)
    dn1_full[mine, :] = z_out[work_rows(c), :]
    dn1_copy = send(
        z_out.at[work_rows(c)],
        dn1_full.at[mine],
        core_send.at[2, 2],
        core_recv.at[2, 2],
        sibling,
    )
    dn1_copy.start()
    ffn_copy.wait_recv()
    resid[...] = resid[...] + ffn_full[...].astype(f32)
    block_copy = pltpu.make_async_copy(resid, block_out, in_sems.at[len(inputs)])
    block_copy.start()
    dn1_copy.wait_recv()

    def final_tile(i, carry):
        block = local_rows(i)
        values = x_in[block, :].astype(f32)
        dy[block, :] = dy[block, :] + norm_back(
            values, rms_scale(values), gain_one, dn1_full[block, :].astype(f32)
        )
        return carry

    lax.fori_loop(0, 2, final_tile, 0)
    grad_copy = pltpu.make_async_copy(dy, input_grad, in_sems.at[len(inputs) + 1])
    grad_copy.start()
    @pl.when(c < early)
    def _():
        sum_own()

    own = ADAPTERS // fsdp
    wanted = [(f * own + a).astype(f32) for a in range(own)]
    mine_sum = own_sum[...].astype(f32)
    sums = [jnp.where(table_all[f, 4:5, 0:1] == w, mine_sum, 0.0) for w in wanted]
    for k in range(fsdp - 1):
        to_peer(k).wait_recv()
        tree = table_all[lax.rem(f - k - 1 + fsdp, fsdp), 4:5, 0:1]
        block = tree_sums[k].astype(f32)
        sums = [total + jnp.where(tree == w, block, 0.0) for total, w in zip(sums, wanted)]
    for a in range(own):
        adapter_out[a] = sums[a]
    for copy in [full_copy, ffn_copy, dn1_copy]:
        copy.wait_send()
    block_copy.wait()
    grad_copy.wait()
    for block in range(contexts):
        pair_block(block).wait_send()
    for k in range(contexts - 1):
        to_owner(k).wait_send()
    for k in range(fsdp - 1):
        to_peer(k).wait_send()
    out.finish()

    def drain(chunk, carry):
        pair_copy(chunk).wait_send()

        @pl.when(chunk < c)
        def _():
            down(chunk).wait_send()

        return carry

    lax.fori_loop(0, c + 1, drain, 0)


def backward_call(sizes, remote, local):
    fsdp, contexts, _ = sizes
    rows = local[0].shape[0]
    padded = (PARAMS // 128 // (2 * contexts) + 15) // 16 * 16
    half = rows // 2
    tree = rows * contexts
    width = remote[6].shape[1]
    units = local[19].shape[1]
    bf, f32 = jnp.bfloat16, jnp.float32
    vmem = pl.BlockSpec(memory_space=pltpu.VMEM)
    hbm = pl.BlockSpec(memory_space=pl.ANY)

    def shape(kind, *dims):
        return jax.ShapeDtypeStruct(dims, kind)

    moves = 2 * (fsdp - 1)
    slots = max(fsdp, 4)
    dma = pltpu.SemaphoreType.DMA
    return pl.pallas_call(
        functools.partial(backward_kernel, sizes),
        in_specs=[hbm] * len(remote) + [hbm, hbm, vmem, vmem, hbm, hbm, hbm, hbm, hbm, hbm, hbm, vmem, hbm, hbm, hbm, hbm, hbm, hbm, vmem, vmem, vmem, vmem, vmem],
        out_specs=[hbm, hbm, vmem],
        out_shape=[
            shape(f32, rows, D),
            shape(f32, rows, D),
            shape(f32, ADAPTERS // fsdp, padded, 128),
        ],
        scratch_shapes=[
            pltpu.VMEM((rows, 128), f32),
            pltpu.VMEM((rows, 128), f32),
            pltpu.VMEM((tree, width), bf),
            pltpu.VMEM((tree, width), bf),
            pltpu.VMEM((D, 3 * width), bf),
            pltpu.VMEM((D, width), bf),
            pltpu.VMEM((max(fsdp, contexts) * half, D), bf),
            pltpu.VMEM((max(fsdp, contexts) * half, D), bf),
            pltpu.VMEM((max(fsdp - 1, 2) * half, D), bf),
            pltpu.VMEM((fsdp * half, D), bf),
            pltpu.VMEM((fsdp * half, D), bf),
            pltpu.VMEM(((fsdp - 1) * half, D), bf),
            pltpu.VMEM((half, D), bf),
            pltpu.VMEM((rows, D), bf),
            pltpu.VMEM((half, D), bf),
            pltpu.VMEM((rows, D), bf),
            pltpu.VMEM((rows, D), f32),
            pltpu.VMEM((rows, width), bf),
            pltpu.VMEM((width, rows), bf),
            pltpu.VMEM((8, rows), f32),
            pltpu.VMEM((8, rows), f32),
            pltpu.VMEM((width, rows), bf),
            pltpu.VMEM((width, rows), f32),
            pltpu.VMEM((contexts * half, D), bf),
            pltpu.VMEM((contexts * half, D), bf),
            pltpu.VMEM((rows, D), bf),
            dma((2, moves)),
            dma((2, moves)),
            dma((contexts,)),
            dma((contexts,)),
            dma((3, slots)),
            dma((3, slots)),
            dma((contexts,)),
            dma((contexts,)),
            dma((3, slots)),
            dma((5, contexts)),
            pltpu.VMEM((rows, D), bf),
            pltpu.VMEM((rows, D), bf),
            pltpu.VMEM((rows, D), f32),
            pltpu.VMEM((rows, D), bf),
            pltpu.VMEM((rows, D), bf),
            pltpu.VMEM((width, rows), bf),
            pltpu.VMEM((rows, width), bf),
            pltpu.VMEM((rows, width), bf),
            pltpu.VMEM((width, rows), f32),
            pltpu.VMEM((D, 128), bf),
            pltpu.VMEM((256, 3 * width), bf),
            pltpu.VMEM((256, D), bf),
            pltpu.VMEM((width, 128), bf),
            pltpu.VMEM((256, width), bf),
            pltpu.VMEM((256, D), bf),
            pltpu.VMEM((3 * RANK, D), f32),
            pltpu.VMEM((3 * RANK, width), f32),
            pltpu.VMEM((RANK, width), f32),
            pltpu.VMEM((RANK, D), f32),
            pltpu.VMEM((PARAMS // 128, 128), f32),
            pltpu.VMEM((max(D, units), 128), f32),
            pltpu.VMEM((contexts, 2, padded, 128), f32),
            pltpu.VMEM((contexts, padded, 128), f32),
            pltpu.VMEM((contexts - 1, padded, 128), bf),
            pltpu.VMEM((contexts - 1, padded, 128), bf),
            pltpu.VMEM((padded, 128), bf),
            pltpu.VMEM((fsdp - 1, padded, 128), bf),
            dma((17,)),
            dma((3, max(fsdp, contexts))),
            dma((3, max(fsdp, contexts))),
            pltpu.VMEM((width // HEAD_DIM, rows, rows), bf),
            dma((width // HEAD_DIM // 2,)),
            pltpu.VMEM((rows, D), bf),
            pltpu.VMEM((rows, D), bf),
        ],
        name="backward",
        compiler_params=pltpu.CompilerParams(
            collective_id=3, has_side_effects=True, vmem_limit_bytes=63 << 20
        ),
    )(*remote, *local)


def shards(
    tokens,
    attn_gain,
    w_qkv,
    w_out,
    ffn_gain,
    w_gu,
    w_dn,
    w_egu,
    w_edn,
    adapters,
    adapter_ids,
    parents,
    seg_lengths,
    routes,
    route_weights,
    cotangent,
):
    row_count = tokens.shape[1]
    contexts = lax.axis_size("context")
    tensors = lax.axis_size("tensor")
    fsdp_size = lax.axis_size("fsdp")
    sizes = (fsdp_size, contexts, tensors)
    local_width = w_qkv.shape[2]
    local_ff = w_dn.shape[0]
    own_adapters = adapters.shape[0]
    own_width = D // fsdp_size
    gains = jnp.broadcast_to(jnp.concatenate([attn_gain, ffn_gain])[None], (16, 2 * own_width))
    route_table = jnp.concatenate(
        [
            routes[0].astype(jnp.float32).T,
            route_weights[0].astype(jnp.float32).T,
            jnp.broadcast_to(adapter_ids.astype(jnp.float32)[:, None], (1, row_count)),
            jnp.zeros((3, row_count), jnp.float32),
        ]
    )
    lines = adapters.shape[1] // 128
    padded = (lines + 15) // 16 * 16
    adapter_rows = jnp.pad(
        adapters.reshape(own_adapters, lines, 128), ((0, 0), (0, padded - lines), (0, 0))
    ).reshape(own_adapters * padded, 128)
    half_dim = HEAD_DIM // 2
    frequency = rope_base ** (-(jnp.arange(half_dim, dtype=jnp.float32) * 2.0) / HEAD_DIM)
    signs = jnp.concatenate([-jnp.ones((half_dim,)), jnp.ones((half_dim,))])
    turns = jnp.concatenate(
        [jnp.tile(frequency, 4)[None], jnp.tile(signs, 2)[None], jnp.zeros((6, 128))]
    ).astype(jnp.float32)
    sharded = (
        tokens[0],
        cotangent[0],
        w_qkv.reshape(own_width, 3 * local_width),
        w_out.T,
        w_gu.reshape(own_width, 2 * local_ff),
        w_dn.T,
    )
    (
        n1_all,
        k_all,
        v_all,
        wq_all,
        wo_all,
        normed_all,
        cotangent_all,
        p_all,
        q_t,
        q_n,
        mixed_own,
        o_t,
        lse,
        resid,
        shared,
        dn2,
        da_gu_t,
        db_gu_own,
        da_dn_t,
        db_dn_own,
        gains_full,
        cosine,
        sinus,
        hot,
        reach_t,
        a_qkv,
        b_qkv2,
        a_qkv_t2,
        a_o,
        b_o2,
        a_o_t2,
        table_all,
        place_row,
        place_col,
        weight_col,
        marks,
        peaks,
    ) = forward_call(
        sizes,
        sharded,
        (adapter_rows, gains, route_table, turns, adapter_ids, parents, seg_lengths),
    )
    own_experts = EXPERTS // fsdp_size
    starts = marks[:own_experts].astype(jnp.int32)
    moe_all, moe_back_all = moe_call(
        starts,
        place_row,
        place_col,
        weight_col,
        normed_all,
        cotangent_all,
        w_egu.transpose(0, 2, 1, 3),
        w_edn,
    )
    remote = (moe_all, moe_back_all, n1_all, k_all, v_all, wq_all, wo_all, cosine, sinus, p_all)
    block_out, input_grad, sums = backward_call(
        sizes,
        remote,
        (tokens[0], cotangent[0], gains_full, peaks)
        + (resid, shared, dn2, q_t, q_n, mixed_own, o_t, lse)
        + (a_qkv, b_qkv2, a_qkv_t2, a_o, a_o_t2, b_o2)
        + (da_gu_t, db_gu_own, da_dn_t, db_dn_own, table_all),
    )
    adapter_grads = sums[:, :lines].reshape(own_adapters, -1)
    return (block_out[None], input_grad[None], adapter_grads)


def solution(mesh):
    return jax.shard_map(
        shards,
        mesh=mesh,
        in_specs=(
            P("fsdp", "context", None),
            P("fsdp"),
            P("fsdp", None, "tensor"),
            P("tensor", "fsdp"),
            P("fsdp"),
            P("fsdp", None, "tensor"),
            P("tensor", "fsdp"),
            P("fsdp", None, None, "tensor"),
            P("fsdp", "tensor", None),
            P("fsdp", ("context", "tensor")),
            P("fsdp"),
            P("fsdp", None),
            P("fsdp", None),
            P("fsdp", "context", None),
            P("fsdp", "context", None),
            P("fsdp", "context", None),
        ),
        out_specs=(
            P("fsdp", "context", None),
            P("fsdp", "context", None),
            P("fsdp", ("context", "tensor")),
        ),
        check_vma=False,
    )
```

```python
import jax
import jax.numpy as jnp
import numpy as np
import functools
import math

from jax import lax
from jax.experimental import pallas as pl
from jax.experimental.pallas import tpu as pltpu
from jax.sharding import PartitionSpec as P

D = 768
HEADS = 12
HEAD_DIM = 64
FF = 2048
EXPERTS = 8
TOPK = 2
RANK = 16
ADAPTERS = 8
PARAMS = 233472


epsilon = 1e-06
adapter_scale = 2.0
rope_base = 10000.0
masked_score = -1e30
highest_precision = lax.Precision.HIGHEST


def rms_scale(values):
    return lax.rsqrt(jnp.mean(values * values, axis=-1, keepdims=True) + epsilon)


def norm_back(values, scaling, gain_values, gradient):
    weighted = gradient * gain_values
    inner_mean = jnp.mean(values * weighted, axis=-1, keepdims=True)
    return scaling * weighted - values * (scaling * scaling * scaling) * inner_mean


SLOT_TILE = 512
TOKEN_TILE = 256
SLOT_WINDOW = 128


def nt_dot(left, right):
    return lax.dot_general(left, right, (((1,), (1,)), ((), ())), preferred_element_type=jnp.float32)


def tn_dot(left, right):
    return lax.dot_general(left, right, (((0,), (0,)), ((), ())), preferred_element_type=jnp.float32)


def nn_dot(left, right):
    return jnp.dot(left, right, preferred_element_type=jnp.float32)


def moe_kernel(
    starts,
    place_row,
    place_hbm,
    weight_hbm,
    rows_hbm,
    grads_hbm,
    egu_hbm,
    edn_hbm,
    out_hbm,
    back_hbm,
    place_col,
    weight_col,
    rows_ref,
    grads_ref,
    egu_ref,
    edn_ref,
    out_ref,
    back_ref,
    taken,
    taken_grad,
    taken_weight,
    sems,
    block_sems,
):
    f32, bf = jnp.float32, jnp.bfloat16
    experts = egu_hbm.shape[0]
    blocks = rows_ref.shape[0] // TOKEN_TILE

    def block_rows(b):
        return pl.ds(pl.multiple_of(b * TOKEN_TILE, TOKEN_TILE), TOKEN_TILE)

    def loads(b):
        block = block_rows(b)
        return [
            pltpu.make_async_copy(source.at[block], target.at[block], block_sems.at[i, b])
            for i, (source, target) in enumerate(
                ((rows_hbm, rows_ref), (grads_hbm, grads_ref), (weight_hbm, weight_col))
            )
        ]

    def stores(b):
        block = block_rows(b)
        return [
            pltpu.make_async_copy(source.at[block], target.at[block], block_sems.at[3 + i, b])
            for i, (source, target) in enumerate(((out_ref, out_hbm), (back_ref, back_hbm)))
        ]

    def weights(e):
        return [
            pltpu.make_async_copy(egu_hbm.at[e], egu_ref.at[e], sems.at[0, e]),
            pltpu.make_async_copy(edn_hbm.at[e], edn_ref.at[e], sems.at[1, e]),
        ]

    def each(count, copies, action):
        def step(i, carry):
            for copy in copies(i):
                getattr(copy, action)()
            return carry

        lax.fori_loop(0, count, step, 0)

    each(blocks, loads, "start")
    each(experts, weights, "start")
    place_copy = pltpu.make_async_copy(place_hbm, place_col, sems.at[2, 0])
    place_copy.start()
    taken[...] = jnp.zeros_like(taken)
    taken_grad[...] = jnp.zeros_like(taken_grad)
    taken_weight[...] = jnp.zeros_like(taken_weight)
    slot_rows = lax.broadcasted_iota(jnp.int32, (SLOT_WINDOW, TOKEN_TILE), 0).astype(f32)
    slot_cols = lax.broadcasted_iota(jnp.int32, (TOKEN_TILE, SLOT_WINDOW), 1).astype(f32)

    def windows(e, b):
        begin = starts[e, b] // 16 * 16
        return begin, (starts[e, b + 1] - begin + SLOT_WINDOW - 1) // SLOT_WINDOW

    def window_rows(begin, i):
        return pl.ds(pl.multiple_of(begin + i * SLOT_WINDOW, 16), SLOT_WINDOW)

    def fetch(b, carry):
        block = block_rows(b)
        for copy in loads(b):
            copy.wait()

        def take(which):
            picks = []
            for e, first in which:
                hit = place_row[e : e + 1, block] == slot_rows + first.astype(f32)
                picks.append(jnp.where(hit, 1.0, 0.0).astype(bf))
            pick = picks[0] if len(picks) == 1 else jnp.concatenate(picks, axis=0)
            for source, target in (
                (rows_ref, taken),
                (grads_ref, taken_grad),
                (weight_col, taken_weight),
            ):
                got = nn_dot(pick, source[block, :]).astype(bf)
                for i, (e, first) in enumerate(which):
                    slots = window_rows(first, 0)
                    target[e, slots, :] += got[i * SLOT_WINDOW : (i + 1) * SLOT_WINDOW, :]

        spans = [windows(e, b) for e in range(experts)]
        take([(e, spans[e][0]) for e in range(experts)])
        for e in range(experts):

            def more(i, c, e=e):
                take([(e, spans[e][0] + i * SLOT_WINDOW)])
                return c

            lax.fori_loop(1, spans[e][1], more, 0)
        return carry

    lax.fori_loop(0, blocks, fetch, 0)

    def tile(e, start, size):
        slots = pl.ds(pl.multiple_of(start, 128), size)
        inputs = taken[e, slots, :]
        gate_pre = nn_dot(inputs, egu_ref[e, 0])
        up_pre = nn_dot(inputs, egu_ref[e, 1])
        sigmoid_gate = jax.nn.sigmoid(gate_pre)
        silu = gate_pre * sigmoid_gate
        active = (silu * up_pre).astype(bf)
        taken[e, slots, :] = nn_dot(active, edn_ref[e]).astype(bf)
        grad_active = nt_dot(taken_grad[e, slots, :], edn_ref[e])
        lane = lax.broadcasted_iota(jnp.int32, (size, 128), 1)
        scale = jnp.sum(
            jnp.where(lane == e, taken_weight[e, slots, :].astype(f32), 0.0), axis=1, keepdims=True
        )
        grad_active = grad_active * scale
        grad_gate = (
            grad_active * up_pre * sigmoid_gate * (1.0 + gate_pre * (1.0 - sigmoid_gate))
        ).astype(bf)
        grad_up = (grad_active * silu).astype(bf)
        taken_grad[e, slots, :] = (
            nt_dot(grad_gate, egu_ref[e, 0]) + nt_dot(grad_up, egu_ref[e, 1])
        ).astype(bf)

    def expert_step(e, carry):
        for copy in weights(e):
            copy.wait()
        count = starts[e, blocks]
        whole = count // SLOT_TILE
        rest = count - whole * SLOT_TILE

        def step(i, c):
            tile(e, i * SLOT_TILE, SLOT_TILE)
            return c

        lax.fori_loop(0, whole + jnp.where(rest > SLOT_TILE - 128, 1, 0), step, 0)
        for size in range(128, SLOT_TILE, 128):

            @pl.when((rest > size - 128) & (rest <= size))
            def _(size=size):
                tile(e, whole * SLOT_TILE, size)

        return carry

    lax.fori_loop(0, experts, expert_step, 0)
    place_copy.wait()

    def give(b, carry):
        block = block_rows(b)

        def hand(which):
            plain, scaled, values, values_grad = [], [], [], []
            for e, first in which:
                hit = place_col[block, e : e + 1] == slot_cols + first.astype(f32)
                plain.append(jnp.where(hit, 1.0, 0.0).astype(bf))
                weight = weight_col[block, e : e + 1].astype(f32)
                scaled.append(jnp.where(hit, weight, 0.0).astype(bf))
                values.append(taken[e, window_rows(first, 0), :])
                values_grad.append(taken_grad[e, window_rows(first, 0), :])

            def join(pieces, axis):
                return pieces[0] if len(pieces) == 1 else jnp.concatenate(pieces, axis=axis)

            return (
                nn_dot(join(scaled, 1), join(values, 0)),
                nn_dot(join(plain, 1), join(values_grad, 0)),
            )

        spans = [windows(e, b) for e in range(experts)]
        first, second = hand([(e, spans[e][0]) for e in range(experts)])
        out_ref[block, :] = first.astype(bf)
        back_ref[block, :] = second.astype(bf)
        for e in range(experts):

            def more(i, c, e=e):
                first, second = hand([(e, spans[e][0] + i * SLOT_WINDOW)])
                out_ref[block, :] = (out_ref[block, :].astype(f32) + first).astype(bf)
                back_ref[block, :] = (back_ref[block, :].astype(f32) + second).astype(bf)
                return c

            lax.fori_loop(1, spans[e][1], more, 0)
        for copy in stores(b):
            copy.start()
        return carry

    lax.fori_loop(0, blocks, give, 0)
    each(blocks, stores, "wait")


def moe_call(starts, place_row, place_col, weight_col, rows, grads, egu, edn):
    total, width = rows.shape
    experts = egu.shape[0]
    slots = total // 2 + SLOT_TILE
    blocks = total // TOKEN_TILE
    bf, f32 = jnp.bfloat16, jnp.float32
    vmem = pl.BlockSpec(memory_space=pltpu.VMEM)
    hbm = pl.BlockSpec(memory_space=pl.ANY)
    shape = jax.ShapeDtypeStruct((total, width), bf)
    return pl.pallas_call(
        moe_kernel,
        grid_spec=pltpu.PrefetchScalarGridSpec(
            num_scalar_prefetch=1,
            grid=(),
            in_specs=[vmem] + [hbm] * 6,
            out_specs=[hbm, hbm],
            scratch_shapes=[
                pltpu.VMEM((total, 128), f32),
                pltpu.VMEM((total, 128), bf),
                pltpu.VMEM((total, width), bf),
                pltpu.VMEM((total, width), bf),
                pltpu.VMEM(egu.shape, bf),
                pltpu.VMEM(edn.shape, bf),
                pltpu.VMEM((total, width), bf),
                pltpu.VMEM((total, width), bf),
                pltpu.VMEM((experts, slots, width), bf),
                pltpu.VMEM((experts, slots, width), bf),
                pltpu.VMEM((experts, slots, 128), bf),
                pltpu.SemaphoreType.DMA((3, experts)),
                pltpu.SemaphoreType.DMA((5, blocks)),
            ],
        ),
        out_shape=[shape, shape],
        name="experts",
        compiler_params=pltpu.CompilerParams(vmem_limit_bytes=62 << 20),
    )(starts, place_row, place_col, weight_col, rows, grads, egu, edn)


MESH = pl.DeviceIdType.MESH


def place_of():
    return lax.axis_index("fsdp"), lax.axis_index("context"), lax.axis_index("tensor")


def greet(devices):
    barrier = pltpu.get_barrier_semaphore()
    for device in devices:
        pl.semaphore_signal(barrier, inc=1, device_id=device, device_id_type=MESH)
    pl.semaphore_wait(barrier, len(devices))


def send(source, target, send_sem, recv_sem, device):
    return pltpu.make_async_remote_copy(
        src_ref=source,
        dst_ref=target,
        send_sem=send_sem,
        recv_sem=recv_sem,
        device_id=device,
        device_id_type=MESH,
    )


def flip(index, bit):
    return index + (1 - 2 * lax.rem(index // (1 << bit), 2)) * (1 << bit)


def split_rows(count):
    first = (count // 2 + 15) // 16 * 16
    return ((0, first), (first, count - first))


class Gather:
    def __init__(self, bits, me, device_of, own, buf, stride, base, count, send_sems, recv_sems):
        self.stages = [[] for _ in range(bits)]
        self.arrived = [[] for _ in range(bits)]
        self.passed = [[] for _ in range(bits)]
        number = 0
        for half, (offset, size) in enumerate(split_rows(count)):
            held = [me]
            for stage in range(bits):
                bit = (stage + half) % bits
                for block in held:
                    rows = self.rows(block * stride + base + offset, size)
                    source = own.at[self.rows(base + offset, size)] if block is me else buf.at[rows]
                    self.passed[stage].append(block is not me)
                    self.stages[stage].append(
                        send(
                            source,
                            buf.at[rows],
                            send_sems.at[number],
                            recv_sems.at[number],
                            device_of(flip(me, bit)),
                        )
                    )
                    self.arrived[stage].append(
                        self.rows(flip(block, bit) * stride + base + offset, size)
                    )
                    number = number + 1
                held = held + [flip(block, bit) for block in held]

    @staticmethod
    def rows(start, size):
        return pl.ds(pl.multiple_of(start, 16), size)

    def start(self, stage):
        if stage == 0:
            for copies, passed in zip(self.stages, self.passed):
                for copy, later in zip(copies, passed):
                    if not later:
                        copy.start()
        else:
            for copy, later in zip(self.stages[stage], self.passed[stage]):
                if later:
                    copy.start()

    def wait(self, stage):
        for copy in self.stages[stage]:
            copy.wait_recv()

    def finish(self):
        for stage in self.stages:
            for copy in stage:
                copy.wait_send()


def turn(values, cosine, sinus):
    lane = lax.broadcasted_iota(jnp.int32, values.shape, 1)
    first = lax.rem(lane, HEAD_DIM) < HEAD_DIM // 2
    swapped = jnp.where(
        first,
        pltpu.roll(values, 128 - HEAD_DIM // 2, 1),
        pltpu.roll(values, HEAD_DIM // 2, 1),
    )
    return values * cosine + swapped * sinus


def two_parts(values):
    high = values.astype(jnp.bfloat16)
    low = (values - high.astype(jnp.float32)).astype(jnp.bfloat16)
    return jnp.concatenate([high, low], axis=1)


def normed(values, gain):
    scale = lax.rsqrt(jnp.mean(values * values, axis=-1, keepdims=True) + epsilon)
    return (values * scale * gain).astype(jnp.bfloat16)


def fill_bias(bias, hot_rows, reach_t, key_start, query_start):
    seen = nn_dot(hot_rows, reach_t)
    keys = key_start + lax.broadcasted_iota(jnp.int32, seen.shape, 0)
    queries = query_start + lax.broadcasted_iota(jnp.int32, seen.shape, 1)
    bias[...] = jnp.where((seen > 0.5) & (keys <= queries), 0.0, masked_score)


def head_half(shape, axis, odd):
    index = lax.broadcasted_iota(jnp.int32, shape, axis)
    return (index >= HEAD_DIM) if odd else (index < HEAD_DIM)


def tree_tables(parents, lengths, turns, context, rows, hot, reach_t, cosine, sinus):
    lane = lax.broadcasted_iota(jnp.int32, (1, 128), 1)
    far = jnp.full((1, 128), 1 << 30, jnp.int32)
    none = jnp.zeros((1, 128), jnp.int32)
    begins, ends, moves = far, far, none
    first, second = none - 1, none - 1
    start = jnp.int32(0)
    for s in range(parents.shape[1]):
        parent = parents[0, s]
        grand = parents[0, parent]
        here = lane == s
        above = jnp.where(parent != s, lengths[0, parent], 0) + jnp.where(
            (grand != s) & (grand != parent), lengths[0, grand], 0
        )
        begins = jnp.where(here, start, begins)
        moves = jnp.where(here, above - start, moves)
        first = jnp.where(here, parent, first)
        second = jnp.where(here, grand, second)
        start = start + lengths[0, s]
        ends = jnp.where(here, start, ends)
    over = lax.broadcasted_iota(jnp.int32, (128, 128), 0)
    under = lax.broadcasted_iota(jnp.int32, (128, 128), 1)
    ancestors = jnp.where((over == under) | (over == first) | (over == second), 1.0, 0.0).astype(
        jnp.bfloat16
    )

    def fill(chunk, carry):
        block = pl.ds(pl.multiple_of(chunk * rows, 16), rows)
        row = chunk * rows + lax.broadcasted_iota(jnp.int32, (rows, 128), 0)
        inside = (row >= begins) & (row < ends)
        hot[block, :] = jnp.where(inside, 1.0, 0.0).astype(jnp.bfloat16)
        moved = jnp.sum(jnp.where(inside, moves.astype(jnp.float32), 0.0), axis=1, keepdims=True)
        angle = (row.astype(jnp.float32) + moved) * turns[0:1, :]
        cosine[block, :] = jnp.cos(angle)
        sinus[block, :] = jnp.sin(angle) * turns[1:2, :]
        return carry

    lax.fori_loop(0, context + 1, fill, 0)
    own = pl.ds(pl.multiple_of(context * rows, 16), rows)
    reach_t[...] = nt_dot(ancestors, hot[own, :]).astype(jnp.bfloat16)


def choose(f, wanted, adapters, out):
    count = out.shape[0]
    own = adapters.shape[0] // count
    total = jnp.zeros((count, 128), jnp.float32)
    for a in range(own):
        block = adapters[a * count : (a + 1) * count, :].astype(jnp.float32)
        total = total + jnp.where(wanted == (f * own + a).astype(jnp.float32), block, 0.0)
    out[...] = total.astype(jnp.bfloat16)


def route_tables(f, table_all, place_row, place_col, weight_col, marks):
    fsdp, _, rows = table_all.shape
    own = EXPERTS // fsdp
    f32 = jnp.float32
    sub = lax.broadcasted_iota(jnp.int32, (8, rows), 0)
    expert = jnp.where(sub < own, f * own + sub, -1).astype(f32)
    before = lax.broadcasted_iota(jnp.int32, (rows, rows), 0)
    after = lax.broadcasted_iota(jnp.int32, (rows, rows), 1)
    upto = jnp.where(before <= after, 1.0, 0.0).astype(jnp.bfloat16)
    lane = lax.broadcasted_iota(jnp.int32, (8, 128), 1)
    base = jnp.zeros((8, 1), f32)
    found = jnp.zeros((8, 128), f32)
    more = jnp.zeros((120, rows), f32)
    for source in range(fsdp):
        table = table_all[source]
        one = table[0:1, :] == expert
        two = table[1:2, :] == expert
        hit = one | two
        weight = jnp.where(one, table[2:3, :], 0.0) + jnp.where(two, table[3:4, :], 0.0)
        count = nn_dot(jnp.where(hit, 1.0, 0.0).astype(jnp.bfloat16), upto) + base
        place = jnp.where(hit, count - 1.0, -1.0)
        block = slice(source * rows, (source + 1) * rows)
        place_row[:, block] = place
        place_col[block, :] = jnp.concatenate([place, more], axis=0).T
        weight_col[block, :] = jnp.concatenate([weight, more], axis=0).T.astype(jnp.bfloat16)
        for token in range(TOKEN_TILE - 1, fsdp * rows, TOKEN_TILE):
            if token // rows == source:
                at = token % rows
                found = jnp.where(lane == token // TOKEN_TILE + 1, count[:, at : at + 1], found)
        base = count[:, rows - 1 : rows]
    marks[...] = found.astype(jnp.int32)


def unpack_adapter(t, per_block, chosen, flat, wide, first, second):
    a_qkv, b_qkv2, a_qkv_t2, a_o, b_o2, a_o_t2 = first
    a_gu, b_gu2, a_gu_t2, a_dn, a_dn_t2, b_dn2 = second
    f32, bf = jnp.float32, jnp.bfloat16
    contexts = chosen.shape[1]
    width, units = a_o.shape[0], a_dn.shape[0]
    count = PARAMS // 128 // (2 * contexts)
    for context in range(contexts):
        for part in range(2):
            start = (2 * context + part) * count
            flat[start : start + count, :] = chosen[part, context, 0:count, :].astype(f32)

    def spread(start, groups, rank, out, out_t):
        total = groups * 128 // rank
        wide[...] = jnp.zeros_like(wide)
        lines = rank // math.gcd(rank, 128)
        each = lines * 128 // rank
        for i in range(each):
            row, at = divmod(i * rank, 128)
            def line(number):
                if lines == 1:
                    return flat[pl.ds(start, groups), :]
                return flat[pl.ds(start + number, groups // lines, stride=lines), :]

            piece = line(row)[:, at : min(at + rank, 128)]
            if at + rank > 128:
                piece = jnp.concatenate([piece, line(row + 1)[:, 0 : at + rank - 128]], axis=1)
            wide[pl.ds(i, groups // lines, stride=each), 0:rank] = piece
        out[...] = wide[0:total, :].astype(bf)
        if out_t is not None:
            for p in range(total // 128):
                turned = wide[128 * p : 128 * p + 128, :].T.astype(bf)
                out_t[0:128, 128 * p : 128 * p + 128] = turned
                out_t[128:256, 128 * p : 128 * p + 128] = turned

    def stack(start, lines, columns, out, row, column):
        for p, m in enumerate(columns):
            piece = (2.0 * flat[pl.ds(start + m, RANK, stride=lines), :]).astype(bf)
            lanes = slice(column + 128 * p, column + 128 * p + 128)
            out[row : row + RANK, lanes] = piece
            out[128 + row : 128 + row + RANK, lanes] = piece

    for ref in (b_qkv2, b_o2, b_gu2, b_dn2):
        ref[...] = jnp.zeros_like(ref)
    at = 0
    spread(at, 3 * RANK * D // 128, 3 * RANK, a_qkv, a_qkv_t2)
    at = at + 3 * RANK * D // 128
    lines = D // 128
    mine = [t * (width // 128) + p for p in range(width // 128)]
    for j in range(3):
        stack(at + j * RANK * lines, lines, mine, b_qkv2, j * RANK, j * width)
    at = at + 3 * RANK * lines
    spread(at + t * (width * RANK // 128), width * RANK // 128, RANK, a_o, a_o_t2)
    at = at + D * RANK // 128
    stack(at, lines, list(range(lines)), b_o2, 0, 0)
    at = at + RANK * lines
    spread(at, 2 * RANK * D // 128, 2 * RANK, a_gu, a_gu_t2)
    at = at + 2 * RANK * D // 128
    wide_lines = FF // 128
    mine = [t * (units // 128) + p for p in range(units // 128)]
    for j in range(2):
        stack(at + j * RANK * wide_lines, wide_lines, mine, b_gu2, j * RANK, j * units)
    at = at + 2 * RANK * wide_lines
    spread(at + t * (units * RANK // 128), units * RANK // 128, RANK, a_dn, a_dn_t2)
    at = at + FF * RANK // 128
    stack(at, lines, list(range(lines)), b_dn2, 0, 0)


def forward_kernel(
    sizes,
    x_in,
    g_in,
    wq_in,
    wo_in,
    gu_in,
    dn_in,
    adapters_in,
    gains_in,
    table_in,
    turns,
    parents,
    lengths,
    n1_all,
    k_all,
    v_all,
    wq_all,
    wo_all,
    n2_all,
    g_all,
    p_all,
    q_t_out,
    q_n_out,
    mixed_out,
    o_t_out,
    lse_out,
    resid_out,
    shared_out,
    dn2_out,
    da_gu,
    db_gu,
    da_dn,
    db_dn,
    gains_out,
    cosine_out,
    sinus_out,
    hot_out,
    reach_t_out,
    a_qkv_out,
    b_qkv2_out,
    a_qkv_t2_out,
    a_o_out,
    b_o2_out,
    a_o_t2_out,
    table_all_out,
    place_row_out,
    place_col_out,
    weight_col_out,
    marks,
    peaks,
    x_buf,
    wq,
    wo,
    gu,
    dn,
    g_own,
    n1_buf,
    k_buf,
    v_buf,
    v_t,
    peak,
    total,
    bias,
    part_out,
    part_in,
    n2_own,
    shared,
    dn2,
    adapters_all,
    picked,
    gains_all,
    chosen,
    flat,
    a_wide,
    a_gu,
    b_gu2,
    a_gu_t2,
    a_dn,
    a_dn_t2,
    b_dn2,
    fs_send,
    fs_recv,
    z_send,
    z_recv,
    core_send,
    core_recv,
    local_sems,
    chunk_sems,
    small_send,
    small_recv,
    lend_send,
    lend_recv,
    q_t,
    q_n,
    mixed,
    o_t,
    lse,
    resid,
    gains,
    cosine,
    sinus,
    hot,
    reach_t,
    a_qkv,
    b_qkv2,
    a_qkv_t2,
    a_o,
    b_o2,
    a_o_t2,
    table_all,
    place_row,
    place_col,
    weight_col,
    out_sems,
    p_buf,
    p_sems,
):
    fsdp, contexts, _ = sizes
    bits = fsdp.bit_length() - 1
    f, c, t = place_of()
    rows = x_in.shape[0]
    half = rows // 2
    heads = q_t.shape[0] // HEAD_DIM
    width = q_t.shape[0]
    units = dn_in.shape[1]
    own_n = wq_in.shape[0]
    sibling = (f, c, 1 - t)

    def peer(index):
        return (index, c, t)

    peers = [(lax.rem(f + k, fsdp), c, t) for k in range(1, fsdp)]
    stacked = [(f, lax.rem(c + k, contexts), t) for k in range(1, contexts)]
    greet(peers + stacked + [sibling])

    targets = (
        (q_t, q_t_out),
        (q_n, q_n_out),
        (mixed, mixed_out),
        (o_t, o_t_out),
        (lse, lse_out),
        (resid, resid_out),
        (shared, shared_out),
        (dn2, dn2_out),
        (gains, gains_out),
        (cosine, cosine_out),
        (sinus, sinus_out),
        (hot, hot_out),
        (reach_t, reach_t_out),
        (a_qkv, a_qkv_out),
        (b_qkv2, b_qkv2_out),
        (a_qkv_t2, a_qkv_t2_out),
        (a_o, a_o_out),
        (b_o2, b_o2_out),
        (a_o_t2, a_o_t2_out),
        (table_all, table_all_out),
        (place_row, place_row_out),
        (place_col, place_col_out),
        (weight_col, weight_col_out),
    )
    given = []

    def give_out(refs):
        for i, (ref, target) in enumerate(targets):
            if any(ref is other for other in refs):
                copy = pltpu.make_async_copy(ref, target, out_sems.at[i])
                copy.start()
                given.append(copy)

    def half_rows(chunk, part):
        return pl.ds(pl.multiple_of(chunk * rows + part * half, 16), half)

    def up(chunk, source):
        return send(
            source,
            x_buf.at[half_rows(chunk, t)],
            z_send.at[chunk],
            z_recv.at[chunk],
            (f, c + 1, t),
        )

    def across(chunk):
        block = x_buf.at[half_rows(chunk, t)]
        return send(block, block, core_send.at[chunk], core_recv.at[chunk], sibling)

    @pl.when(c < contexts - 1)
    def _():
        up(c, x_in.at[half_rows(0, t)]).start()

    gathers = []
    halved = (False, False, True, False)
    neighbour = (f, c + 1 - 2 * lax.rem(c, 2), t)
    own_half = own_n // 2
    for i, (own, buf) in enumerate(((wq_in, wq), (wo_in, wo), (gu_in, gu), (dn_in, dn))):
        base, count = (lax.rem(c, 2) * own_half, own_half) if halved[i] else (0, own_n)
        gathers.append(
            Gather(bits, f, peer, own, buf, own_n, base, count, fs_send.at[i], fs_recv.at[i])
        )

    def lent(gather, buf, which):
        copies, number = [], 0
        for stage in range(bits):
            group = []
            for block in gather.arrived[stage]:
                group.append(
                    send(
                        buf.at[block],
                        buf.at[block],
                        lend_send.at[which, number],
                        lend_recv.at[which, number],
                        neighbour,
                    )
                )
                number = number + 1
            copies.append(group)
        return copies

    gu_lent = lent(gathers[2], gu, 0)

    z_busy = (lax.rem(c, 2) == 0) & (c > 0)

    def lend(copies, stage):
        for copy in copies[stage]:
            copy.start()
    g_gather = Gather(
        bits, f, peer, g_in, g_all, rows, t * half, half, fs_send.at[4], fs_recv.at[4]
    )
    n2_gather = Gather(
        bits, f, peer, n2_own, n2_all, rows, t * half, half, fs_send.at[5], fs_recv.at[5]
    )
    wq_gather, wo_gather, gu_gather, dn_gather = gathers
    small, rows_sent = [], []
    for k, other in enumerate(peers):
        for j, (source, target) in enumerate(((table_in, table_all), (gains_in, gains_all))):
            copy = send(source, target.at[f], small_send.at[j, k], small_recv.at[j, k], other)
            copy.start()
            small.append(copy)
    wq_gather.start(0)
    locals_ = [pltpu.make_async_copy(x_in, x_buf.at[pl.ds(c * rows, rows)], local_sems.at[0])]
    for i, (own, buf) in enumerate(((wq_in, wq), (wo_in, wo), (gu_in, gu), (dn_in, dn))):
        locals_.append(
            pltpu.make_async_copy(own, buf.at[pl.ds(f * own_n, own_n)], local_sems.at[1 + i])
        )
    locals_.append(pltpu.make_async_copy(g_in, g_own, local_sems.at[5]))
    locals_.append(
        pltpu.make_async_copy(g_in, g_all.at[pl.ds(f * rows, rows)], local_sems.at[6])
    )
    for copy in locals_:
        copy.start()

    o_t[...] = jnp.zeros_like(o_t)
    peak[...] = jnp.full_like(peak, masked_score)
    total[...] = jnp.zeros_like(total)
    da_gu[...] = jnp.zeros_like(da_gu)
    db_gu[...] = jnp.zeros_like(db_gu)
    da_dn[...] = jnp.zeros_like(da_dn)
    db_dn[...] = jnp.zeros_like(db_dn)
    gains_all[f] = gains_in[...]
    table_all[f] = table_in[...]
    for copy in small:
        copy.wait_recv()
    for k, other in enumerate(peers):
        choose(f, table_all[lax.rem(f + k + 1, fsdp), 4:5, 0:1], adapters_in, picked.at[k])
        copy = send(
            picked.at[k], adapters_all.at[f], small_send.at[2, k], small_recv.at[2, k], other
        )
        copy.start()
        rows_sent.append(copy)
    choose(f, table_all[f, 4:5, 0:1], adapters_in, adapters_all.at[f])
    tree_tables(parents, lengths, turns, c, rows, hot, reach_t, cosine, sinus)

    def receive(step):
        chunk = c - step

        @pl.when(step <= c)
        def _():
            up(chunk, x_buf.at[half_rows(chunk, t)]).wait_recv()

            @pl.when(c < contexts - 1)
            def _():
                up(chunk, x_buf.at[half_rows(chunk, t)]).start()

            across(chunk).start()

    def chunk_rows(chunk):
        return pl.ds(pl.multiple_of(chunk * rows, 16), rows)

    def out_copies(chunk):
        block = chunk_rows(chunk)
        return [
            pltpu.make_async_copy(n1_buf.at[block], n1_all.at[block], chunk_sems.at[0, chunk]),
            pltpu.make_async_copy(k_buf.at[block], k_all.at[block], chunk_sems.at[1, chunk]),
            pltpu.make_async_copy(v_buf.at[block], v_all.at[block], chunk_sems.at[2, chunk]),
        ]

    def project(chunk, own):
        block = chunk_rows(chunk)
        n1 = normed(x_buf[block, :].astype(jnp.float32), gain_one)
        n1_buf[block, :] = n1
        rank = two_parts(nn_dot(n1, a_qkv[...]))
        cos_rows = cosine[block, :]
        sin_rows = sinus[block, :]
        start = 0 if own else width
        result = nn_dot(n1, wq[:, start:]) + nn_dot(rank, b_qkv2[:, start:])
        for p in range(width // 128):
            lanes = slice(128 * p, 128 * p + 128)
            cols = slice(width - start + 128 * p, width - start + 128 * p + 128)
            k_buf[block, lanes] = turn(result[:, cols], cos_rows, sin_rows).astype(jnp.bfloat16)
            cols = slice(2 * width - start + 128 * p, 2 * width - start + 128 * p + 128)
            value = result[:, cols]
            v_buf[block, lanes] = value.astype(jnp.bfloat16)
            v_t[lanes, :] = value.T.astype(jnp.bfloat16)
            if own:
                query = turn(result[:, lanes], cos_rows, sin_rows) * 0.125
                q_n[:, lanes] = query.astype(jnp.bfloat16)
                q_t[lanes, :] = query.T.astype(jnp.bfloat16)
        for copy in out_copies(chunk):
            copy.start()

    def weights_out(chunk, p):
        target = p_all.at[pl.ds(chunk * heads + 2 * p, 2)]
        return pltpu.make_async_copy(p_buf.at[pl.ds(2 * p, 2)], target, p_sems.at[p])

    def attend(chunk, first):
        block = chunk_rows(chunk)
        fill_bias(bias, hot[block, :], reach_t[...], chunk * rows, c * rows)

        def pair_step(p, carry):
            lanes = pl.ds(pl.multiple_of(p * 128, 128), 128)
            keys = k_buf[block, lanes]
            query = q_t[lanes, :]
            if not first:
                weights_out(chunk, p).wait()
            for odd in range(2):
                h = 2 * p + odd
                alone = jnp.where(
                    head_half(query.shape, 0, odd), query, jnp.zeros_like(query)
                )
                scores = nn_dot(keys, alone) + bias[...]
                before = peak[pl.ds(h, 1), :]
                now = jnp.maximum(before, jnp.max(scores, axis=0, keepdims=True))
                weights = jnp.exp(scores - now)
                shrink = jnp.exp(before - now)
                peak[pl.ds(h, 1), :] = now
                peaks[pl.ds(chunk * 8 + h, 1), :] = now
                low_weights = weights.astype(jnp.bfloat16)
                p_buf[h] = low_weights
                total[pl.ds(h, 1), :] = total[pl.ds(h, 1), :] * shrink + jnp.sum(
                    weights, axis=0, keepdims=True
                )
                head = pl.ds(pl.multiple_of(h * HEAD_DIM, HEAD_DIM), HEAD_DIM)
                o_t[head, :] = o_t[head, :] * shrink + nn_dot(
                    v_t[head, :], low_weights
                )
            weights_out(chunk, p).start()
            return carry

        lax.fori_loop(0, heads // 2, pair_step, 0)

    def advance(gather, following, copies=None):
        gather.wait(0)
        for stage in range(1, bits):
            gather.start(stage)
            if copies is not None:
                lend(copies, stage - 1)
            if stage < bits - 1:
                gather.wait(stage)
        following.start(0)

    for copy in rows_sent:
        copy.wait_recv()
    total_row = adapters_all[0].astype(jnp.float32)
    for b in range(1, fsdp):
        total_row = total_row + adapters_all[b].astype(jnp.float32)
    chosen[t, c] = total_row.astype(jnp.bfloat16)
    spread = []
    for k, other in enumerate(stacked):
        block = chosen.at[t, c]
        copy = send(block, block, small_send.at[3, k], small_recv.at[3, k], other)
        copy.start()
        spread.append(copy)
    gains[...] = jnp.zeros_like(gains)
    for i in range(2):
        pieces = [
            gains_all[b, 0:1, i * own_n : (i + 1) * own_n].astype(jnp.float32)
            for b in range(fsdp)
        ]
        gains[i : i + 1, :] = jnp.concatenate(pieces, axis=1)
    gain_one = gains[0:1, :]
    gain_two = gains[1:2, :]
    advance(wq_gather, wo_gather)
    receive(1)
    for copy in spread:
        copy.wait_recv()
    shared_copy = send(
        chosen.at[t], chosen.at[t], small_send.at[4, 0], small_recv.at[4, 0], sibling
    )
    shared_copy.start()
    route_tables(f, table_all, place_row, place_col, weight_col, marks)
    give_out(
        (table_all, place_row, place_col, weight_col, gains, cosine, sinus, hot, reach_t)
    )
    advance(wo_gather, gu_gather)
    shared_copy.wait_recv()
    unpack_adapter(
        t,
        adapters_in.shape[0] // (ADAPTERS // fsdp),
        chosen,
        flat,
        a_wide,
        (a_qkv, b_qkv2, a_qkv_t2, a_o, b_o2, a_o_t2),
        (a_gu, b_gu2, a_gu_t2, a_dn, a_dn_t2, b_dn2),
    )
    give_out((a_qkv, b_qkv2, a_qkv_t2, a_o, b_o2, a_o_t2))
    wq_gather.wait(bits - 1)
    locals_[0].wait()
    locals_[1].wait()
    wq_out = pltpu.make_async_copy(wq, wq_all, local_sems.at[10])
    wq_out.start()
    project(c, True)
    receive(2)
    attend(c, True)

    number = contexts

    def forwards(gather, buf, first):
        copies = []
        for stage in range(bits):
            group = []
            for block in gather.arrived[stage]:
                index = first + len(copies)
                copies.append(
                    send(
                        buf.at[block],
                        buf.at[block],
                        core_send.at[index],
                        core_recv.at[index],
                        sibling,
                    )
                )
        return copies

    per_stage = [len(stage) for stage in g_gather.arrived]
    g_forward = forwards(g_gather, g_all, number + 5)
    n2_forward = forwards(n2_gather, n2_all, number + 5 + sum(per_stage))

    def pass_on(copies, stage):
        start = sum(per_stage[:stage])
        for copy in copies[start : start + per_stage[stage]]:
            copy.start()

    def between(step):
        if step == 1:
            advance(gu_gather, dn_gather)

            @pl.when(jnp.logical_not(z_busy))
            def _():
                lend(gu_lent, 0)

        if step == 2:
            advance(dn_gather, g_gather)
            gu_gather.wait(bits - 1)

            @pl.when(z_busy)
            def _():
                lend(gu_lent, 0)

            for stage in range(1, bits):
                lend(gu_lent, stage)
        if step == 3:
            g_gather.wait(0)
            for stage in range(1, bits):
                g_gather.start(stage)
                pass_on(g_forward, stage - 1)
                if stage < bits - 1:
                    g_gather.wait(stage)

    def later(step):
        chunk = c - step

        @pl.when(step <= c)
        def _():
            across(chunk).wait_recv()
            project(chunk, False)
            receive(step + 2)
            attend(chunk, False)

    for step in range(1, 3):
        between(step)
        later(step)

    @pl.when(c >= 3)
    def _():
        between(3)
        later(3)

    def rest(step, carry):
        later(step)
        return carry

    lax.fori_loop(4, contexts, rest, 0)

    for h in range(heads):
        head = slice(h * HEAD_DIM, h * HEAD_DIM + HEAD_DIM)
        o_t[head, :] = o_t[head, :] / total[h : h + 1, :]
    lse[...] = peak[...] + jnp.log(total[...])
    for p in range(width // 128):
        mixed[:, 128 * p : 128 * p + 128] = o_t[128 * p : 128 * p + 128, :].T.astype(jnp.bfloat16)
    give_out((q_t, q_n, mixed, o_t, lse))
    wo_gather.wait(bits - 1)
    locals_[2].wait()
    wo_out = pltpu.make_async_copy(wo, wo_all, local_sems.at[11])
    wo_out.start()

    def local_rows(part):
        return pl.ds(pl.multiple_of(part * half, 16), half)

    mine = local_rows(t)
    theirs = local_rows(1 - t)

    def branch(block):
        values = mixed[block, :]
        rank = two_parts(nn_dot(values, a_o[...]))
        return nt_dot(values, wo[...]) + nn_dot(rank, b_o2[...])

    part_copies = []
    for i, block in enumerate((theirs, mine)):
        part_out[block, :] = branch(block).astype(jnp.bfloat16)
        copy = send(
            part_out.at[block],
            part_in.at[block],
            core_send.at[number + i],
            core_recv.at[number + i],
            sibling,
        )
        copy.start()
        part_copies.append(copy)

    def attended(block, copy):
        copy.wait_recv()
        resid[block, :] = x_rows(x_buf, c, rows, block) + (
            part_out[block, :].astype(jnp.float32) + part_in[block, :].astype(jnp.float32)
        )
        n2_own[block, :] = normed(resid[block, :], gain_two)

    attended(mine, part_copies[0])
    n2_gather.start(0)
    attended(theirs, part_copies[1])
    give_out((resid,))
    n2_out = pltpu.make_async_copy(n2_own, n2_all.at[pl.ds(f * rows, rows)], local_sems.at[12])
    n2_out.start()

    @pl.when(c < 3)
    def _():
        between(3)


    locals_[5].wait()
    for group in gu_lent:
        for copy in group:
            copy.wait_recv()
    locals_[3].wait()
    dn_gather.wait(bits - 1)
    locals_[4].wait()

    def shared_tile(block):
        inputs = n2_own[block, :]
        grads = g_own[block, :]
        rank = nn_dot(inputs, a_gu[...])
        rank2 = two_parts(rank)
        gate = nn_dot(inputs, gu[:, :units]) + nn_dot(rank2, b_gu2[:, :units])
        up_pre = nn_dot(inputs, gu[:, units:]) + nn_dot(rank2, b_gu2[:, units:])
        sigmoid_gate = jax.nn.sigmoid(gate)
        silu = gate * sigmoid_gate
        hidden = (silu * up_pre).astype(jnp.bfloat16)
        down_rank = nn_dot(hidden, a_dn[...])
        shared[block, :] = (
            nt_dot(hidden, dn[...]) + nn_dot(two_parts(down_rank), b_dn2[...])
        ).astype(jnp.bfloat16)
        down_back = nt_dot(grads, b_dn2[0:128, :])
        grad_hidden = nn_dot(grads, dn[...]) + nn_dot(two_parts(down_back), a_dn_t2[...])
        grad_gate = (
            grad_hidden * up_pre * sigmoid_gate * (1.0 + gate * (1.0 - sigmoid_gate))
        ).astype(jnp.bfloat16)
        grad_up = (grad_hidden * silu).astype(jnp.bfloat16)
        rank_back = nt_dot(grad_gate, b_gu2[0:128, :units]) + nt_dot(
            grad_up, b_gu2[0:128, units:]
        )
        dn2[block, :] = (
            nt_dot(grad_gate, gu[:, :units])
            + nt_dot(grad_up, gu[:, units:])
            + nn_dot(two_parts(rank_back), a_gu_t2[...])
        ).astype(jnp.bfloat16)
        rank_low = rank.astype(jnp.bfloat16)
        da_gu[...] += tn_dot(rank_back.astype(jnp.bfloat16), inputs)[0 : 2 * RANK]
        db_gu[0:RANK, :] += 2.0 * tn_dot(rank_low, grad_gate)[0:RANK]
        db_gu[RANK:, :] += 2.0 * tn_dot(rank_low, grad_up)[RANK : 2 * RANK]
        da_dn[...] += tn_dot(down_back.astype(jnp.bfloat16), hidden)[0:RANK]
        db_dn[...] += 2.0 * tn_dot(down_rank.astype(jnp.bfloat16), grads)[0:RANK]

    def pass_pieces(gather, copies, stage):
        start = sum(per_stage[:stage])
        for i, copy in enumerate(gather.stages[stage]):
            copy.wait_recv()
            copies[start + i].start()

    shared_tile(mine)
    n2_gather.wait(0)
    for stage in range(1, bits):
        n2_gather.start(stage)
        pass_on(n2_forward, stage - 1)
        if stage < bits - 1:
            n2_gather.wait(stage)
    shared_tile(theirs)
    give_out((shared, dn2))
    pass_pieces(g_gather, g_forward, bits - 1)
    pass_pieces(n2_gather, n2_forward, bits - 1)
    for copy in n2_forward + g_forward:
        copy.wait()
    for copy in small + rows_sent + spread + [shared_copy]:
        copy.wait_send()
    for group in gu_lent:
        for copy in group:
            copy.wait_send()
    for copy in given:
        copy.wait()
    for copy in part_copies:
        copy.wait_send()
    for gather in gathers + [g_gather, n2_gather]:
        gather.finish()
    n2_out.wait()
    wq_out.wait()
    wo_out.wait()
    locals_[6].wait()

    @pl.when(c < contexts - 1)
    def _():
        up(c, x_in.at[half_rows(0, t)]).wait_send()

    def drain(step, carry):
        chunk = c - step

        @pl.when(c < contexts - 1)
        def _():
            up(chunk, x_buf.at[half_rows(chunk, t)]).wait_send()

        across(chunk).wait_send()
        return carry

    lax.fori_loop(1, c + 1, drain, 0)

    def drain_out(step, carry):
        for copy in out_copies(c - step):
            copy.wait()
        return carry

    lax.fori_loop(0, c + 1, drain_out, 0)
    for p in range(heads // 2):
        weights_out(0, p).wait()


def x_rows(x_buf, chunk, rows, block):
    return x_buf[pl.ds(pl.multiple_of(chunk * rows, 16) + block.start, block.size), :].astype(
        jnp.float32
    )


def forward_call(sizes, sharded, local):
    fsdp, contexts, _ = sizes
    x, g, wq, wo, gu, dn = sharded
    adapters, gains, table = local[:3]
    rows = x.shape[0]
    tree = rows * contexts
    width = wo.shape[1]
    units = dn.shape[1]
    bf, f32 = jnp.bfloat16, jnp.float32
    vmem = pl.BlockSpec(memory_space=pltpu.VMEM)
    hbm = pl.BlockSpec(memory_space=pl.ANY)
    smem = pl.BlockSpec(memory_space=pltpu.SMEM)
    slots = max(fsdp, contexts)
    total = fsdp * rows
    per_adapter = adapters.shape[0] // (ADAPTERS // fsdp)

    def shape(kind, *dims):
        return jax.ShapeDtypeStruct(dims, kind)

    moves = 2 * (fsdp - 1)
    hops = contexts + 5 + 2 * moves
    return pl.pallas_call(
        functools.partial(forward_kernel, sizes),
        in_specs=[hbm] * 6 + [vmem] * 4 + [smem] * 2,
        out_specs=[hbm] * 8 + [hbm, hbm, hbm, hbm, hbm, hbm, hbm, hbm, vmem, vmem, vmem, vmem, hbm, hbm, hbm, hbm, hbm, hbm, hbm, hbm, hbm, hbm, hbm, hbm, hbm, hbm, hbm, vmem, vmem],
        out_shape=[
            shape(bf, tree, D),
            shape(bf, tree, width),
            shape(bf, tree, width),
            shape(bf, D, 3 * width),
            shape(bf, D, width),
            shape(bf, fsdp * rows, D),
            shape(bf, fsdp * rows, D),
            shape(bf, contexts * (width // HEAD_DIM), rows, rows),
            shape(bf, width, rows),
            shape(bf, rows, width),
            shape(bf, rows, width),
            shape(f32, width, rows),
            shape(f32, 8, rows),
            shape(f32, rows, D),
            shape(bf, rows, D),
            shape(bf, rows, D),
            shape(f32, 2 * RANK, D),
            shape(f32, 2 * RANK, units),
            shape(f32, RANK, units),
            shape(f32, RANK, D),
            shape(f32, 8, D),
            shape(f32, tree, 128),
            shape(f32, tree, 128),
            shape(bf, tree, 128),
            shape(bf, 128, rows),
            shape(bf, D, 128),
            shape(bf, 256, 3 * width),
            shape(bf, 256, D),
            shape(bf, width, 128),
            shape(bf, 256, D),
            shape(bf, 256, width),
            shape(f32, fsdp, 8, rows),
            shape(f32, 8, total),
            shape(f32, total, 128),
            shape(bf, total, 128),
            shape(jnp.int32, 8, 128),
            shape(f32, contexts * 8, rows),
        ],
        scratch_shapes=[
            pltpu.VMEM((tree, D), bf),
            pltpu.VMEM((D, 3 * width), bf),
            pltpu.VMEM((D, width), bf),
            pltpu.VMEM((D, 2 * units), bf),
            pltpu.VMEM((D, units), bf),
            pltpu.VMEM((rows, D), bf),
            pltpu.VMEM((tree, D), bf),
            pltpu.VMEM((tree, width), bf),
            pltpu.VMEM((tree, width), bf),
            pltpu.VMEM((width, rows), bf),
            pltpu.VMEM((8, rows), f32),
            pltpu.VMEM((8, rows), f32),
            pltpu.VMEM((rows, rows), f32),
            pltpu.VMEM((rows, D), bf),
            pltpu.VMEM((rows, D), bf),
            pltpu.VMEM((rows, D), bf),
            pltpu.VMEM((rows, D), bf),
            pltpu.VMEM((rows, D), bf),
            pltpu.VMEM((fsdp, per_adapter, 128), bf),
            pltpu.VMEM((fsdp - 1, per_adapter, 128), bf),
            pltpu.VMEM((fsdp,) + gains.shape, bf),
            pltpu.VMEM((2, contexts, per_adapter, 128), bf),
            pltpu.VMEM((PARAMS // 128, 128), f32),
            pltpu.VMEM((max(D, units), 128), f32),
            pltpu.VMEM((D, 128), bf),
            pltpu.VMEM((256, 2 * units), bf),
            pltpu.VMEM((256, D), bf),
            pltpu.VMEM((units, 128), bf),
            pltpu.VMEM((256, units), bf),
            pltpu.VMEM((256, D), bf),
            pltpu.SemaphoreType.DMA((6, moves)),
            pltpu.SemaphoreType.DMA((6, moves)),
            pltpu.SemaphoreType.DMA((contexts,)),
            pltpu.SemaphoreType.DMA((contexts,)),
            pltpu.SemaphoreType.DMA((hops,)),
            pltpu.SemaphoreType.DMA((hops,)),
            pltpu.SemaphoreType.DMA((13,)),
            pltpu.SemaphoreType.DMA((3, contexts)),
            pltpu.SemaphoreType.DMA((5, slots)),
            pltpu.SemaphoreType.DMA((5, slots)),
            pltpu.SemaphoreType.DMA((2, moves)),
            pltpu.SemaphoreType.DMA((2, moves)),
            pltpu.VMEM((width, rows), bf),
            pltpu.VMEM((rows, width), bf),
            pltpu.VMEM((rows, width), bf),
            pltpu.VMEM((width, rows), f32),
            pltpu.VMEM((8, rows), f32),
            pltpu.VMEM((rows, D), f32),
            pltpu.VMEM((8, D), f32),
            pltpu.VMEM((tree, 128), f32),
            pltpu.VMEM((tree, 128), f32),
            pltpu.VMEM((tree, 128), bf),
            pltpu.VMEM((128, rows), bf),
            pltpu.VMEM((D, 128), bf),
            pltpu.VMEM((256, 3 * width), bf),
            pltpu.VMEM((256, D), bf),
            pltpu.VMEM((width, 128), bf),
            pltpu.VMEM((256, D), bf),
            pltpu.VMEM((256, width), bf),
            pltpu.VMEM((fsdp, 8, rows), f32),
            pltpu.VMEM((8, total), f32),
            pltpu.VMEM((total, 128), f32),
            pltpu.VMEM((total, 128), bf),
            pltpu.SemaphoreType.DMA((23,)),
            pltpu.VMEM((width // HEAD_DIM, rows, rows), bf),
            pltpu.SemaphoreType.DMA((width // HEAD_DIM // 2,)),
        ],
        name="forward",
        compiler_params=pltpu.CompilerParams(
            collective_id=2, has_side_effects=True, vmem_limit_bytes=62 << 20
        ),
    )(*sharded, *local)


def flips(index, mask, bits):
    for bit in range(bits):
        if mask >> bit & 1:
            index = flip(index, bit)
    return index


class Scatter:
    def __init__(self, bits, me, device_of, work, inbox, count, send_sems, recv_sems):
        self.bits, self.work, self.inbox = bits, work, inbox
        self.copies = [[] for _ in range(bits)]
        self.masks = [[] for _ in range(bits)]
        self.adds = [[] for _ in range(bits)]
        number = 0
        for half, (offset, size) in enumerate(split_rows(count)):
            alive = list(range(1 << bits))
            slot = 0
            for stage in range(bits):
                bit = (stage + half) % bits
                for mask in alive:
                    if mask >> bit & 1:
                        source = Gather.rows(flips(me, mask, bits) * count + offset, size)
                        target = pl.ds(slot * count + offset, size)
                        kept = Gather.rows(flips(me, mask ^ (1 << bit), bits) * count + offset, size)
                        self.copies[stage].append(
                            send(
                                work.at[source],
                                inbox.at[target],
                                send_sems.at[number],
                                recv_sems.at[number],
                                device_of(flip(me, bit)),
                            )
                        )
                        self.adds[stage].append((kept, target, pl.ds(offset, size)))
                        self.masks[stage].append(mask)
                        number = number + 1
                        slot = slot + 1
                alive = [mask for mask in alive if not mask >> bit & 1]

    def start(self, stage):
        for copy in self.copies[stage]:
            copy.start()

    def start_mask(self, mask):
        for copy, number in zip(self.copies[0], self.masks[0]):
            if number == mask:
                copy.start()

    def add(self, stage):
        for copy in self.copies[stage]:
            copy.wait_recv()
        for kept, target, _ in self.adds[stage]:
            total = self.work[kept, :].astype(jnp.float32) + self.inbox[target, :].astype(
                jnp.float32
            )
            self.work[kept, :] = total.astype(jnp.bfloat16)

    def last(self, out):
        for copy in self.copies[self.bits - 1]:
            copy.wait_recv()
        for kept, target, rows in self.adds[self.bits - 1]:
            total = self.work[kept, :].astype(jnp.float32) + self.inbox[target, :].astype(
                jnp.float32
            )
            out[rows, :] = total.astype(jnp.bfloat16)

    def finish(self):
        for stage in self.copies:
            for copy in stage:
                copy.wait_send()


def pack_rows(grad_t, start, rank, flat, wide):
    total = grad_t.shape[1]
    more = jnp.zeros((128 - rank, 128), jnp.float32)
    for p in range(total // 128):
        piece = grad_t[:, 128 * p : 128 * p + 128]
        wide[128 * p : 128 * p + 128, :] = jnp.concatenate([piece, more], axis=0).T
    lines = rank // math.gcd(rank, 128)
    each = lines * 128 // rank
    count = total // each
    joined = jnp.concatenate(
        [wide[pl.ds(i, count, stride=each), :][:, 0:rank] for i in range(each)], axis=1
    )
    if lines == 1:
        flat[pl.ds(start, count), :] = joined
    else:
        for i in range(lines):
            flat[pl.ds(start + i, count, stride=lines), :] = joined[:, 128 * i : 128 * i + 128]


def pack_lines(grad, start, lines, columns, flat):
    for p, m in enumerate(columns):
        flat[pl.ds(start + m, grad.shape[0], stride=lines), :] = grad[:, 128 * p : 128 * p + 128]


def pack_first(t, flat, wide, da_qkv, db_qkv, da_o, db_o):
    width = da_o.shape[1]
    lines = D // 128
    mine = [t * (width // 128) + p for p in range(width // 128)]
    pack_rows(da_qkv[...], 0, 3 * RANK, flat, wide)
    at = 3 * RANK * D // 128
    for j in range(3):
        rows = slice(j * RANK, (j + 1) * RANK)
        pack_lines(db_qkv[rows, :], at + j * RANK * lines, lines, mine, flat)
    at = at + 3 * RANK * lines
    pack_rows(da_o[...], at + t * (width * RANK // 128), RANK, flat, wide)
    at = at + D * RANK // 128
    pack_lines(db_o[...], at, lines, list(range(lines)), flat)


def pack_second(t, flat, wide, da_gu, db_gu, da_dn, db_dn):
    units = da_dn.shape[1]
    lines = D // 128
    at = 8 * RANK * D // 128
    pack_rows(da_gu[...], at, 2 * RANK, flat, wide)
    at = at + 2 * RANK * D // 128
    wide_lines = FF // 128
    mine = [t * (units // 128) + p for p in range(units // 128)]
    for j in range(2):
        rows = slice(j * RANK, (j + 1) * RANK)
        pack_lines(db_gu[rows, :], at + j * RANK * wide_lines, wide_lines, mine, flat)
    at = at + 2 * RANK * wide_lines
    pack_rows(da_dn[...], at + t * (units * RANK // 128), RANK, flat, wide)
    at = at + FF * RANK // 128
    pack_lines(db_dn[...], at, lines, list(range(lines)), flat)


def backward_kernel(
    sizes,
    moe_out,
    moe_back,
    n1_hbm,
    k_hbm,
    v_hbm,
    wq_hbm,
    wo_hbm,
    cos_hbm,
    sin_hbm,
    p_hbm,
    x_in_hbm,
    g_in_hbm,
    gains,
    peaks,
    resid_hbm,
    shared_hbm,
    dn2_hbm,
    q_t_hbm,
    q_n_hbm,
    mixed_hbm,
    o_t_hbm,
    lse,
    a_qkv_hbm,
    b_qkv2_hbm,
    a_qkv_t2_hbm,
    a_o_hbm,
    a_o_t2_hbm,
    b_o2_hbm,
    da_gu,
    db_gu,
    da_dn,
    db_dn,
    table_all,
    block_out,
    input_grad,
    adapter_out,
    cosine,
    sinus,
    k_buf,
    v_buf,
    wq,
    wo,
    work_back,
    pair_back,
    inbox_back,
    work_out,
    pair_out,
    inbox_out,
    total_half,
    total_full,
    ffn_half,
    ffn_full,
    dy,
    do_n,
    do_t,
    delta,
    factor,
    k_t,
    dq_t,
    dq,
    part_in,
    z_in,
    dn1_full,
    fs_send,
    fs_recv,
    z_send,
    z_recv,
    core_send,
    core_recv,
    pair_send,
    pair_recv,
    local_sems,
    chunk_sems,
    x_in,
    g_in,
    resid,
    shared,
    dn2,
    q_t,
    q_n,
    mixed,
    o_t,
    a_qkv,
    b_qkv2,
    a_qkv_t2,
    a_o,
    a_o_t2,
    b_o2,
    da_qkv,
    db_qkv,
    da_o,
    db_o,
    flat,
    wide,
    packed,
    packed_in,
    up_out,
    up_in,
    own_sum,
    tree_sums,
    in_sems,
    sum_send,
    sum_recv,
    p_buf,
    p_sems,
    whole_back,
    whole_out,
):
    fsdp, contexts, _ = sizes
    bits = fsdp.bit_length() - 1
    f, c, t = place_of()
    rows = x_in.shape[0]
    half = rows // 2
    width = q_t.shape[0]
    inputs = []
    for i, (source, target) in enumerate(
        (
            (x_in_hbm, x_in),
            (g_in_hbm, g_in),
            (resid_hbm, resid),
            (shared_hbm, shared),
            (dn2_hbm, dn2),
            (q_t_hbm, q_t),
            (q_n_hbm, q_n),
            (mixed_hbm, mixed),
            (o_t_hbm, o_t),
            (a_qkv_hbm, a_qkv),
            (b_qkv2_hbm, b_qkv2),
            (a_qkv_t2_hbm, a_qkv_t2),
            (a_o_hbm, a_o),
            (a_o_t2_hbm, a_o_t2),
            (b_o2_hbm, b_o2),
        )
    ):
        inputs.append(pltpu.make_async_copy(source, target, in_sems.at[i]))
    heads = width // HEAD_DIM
    part_out, z_out, grad_kv = pair_back, work_back, inbox_back
    part, n1_buf = whole_back, whole_out
    kv_rows = pl.ds(0, rows)
    sibling = (f, c, 1 - t)
    f32, bf = jnp.float32, jnp.bfloat16

    def peer(index):
        return (index, c, t)

    def local_rows(part_index):
        return pl.ds(pl.multiple_of(part_index * half, 16), half)

    mine = local_rows(t)
    theirs = local_rows(1 - t)

    def block_rows(block, part_index):
        return pl.ds(pl.multiple_of(block * rows + part_index * half, 16), half)

    def work_rows(block):
        return pl.ds(pl.multiple_of(block * half, 16), half)

    masks = list(range(fsdp - 1, -1, -1))

    def exchange(source, work, inbox, which, whole):
        own, sent = [], []
        for mask in masks:
            block = flips(f, mask, bits)
            if mask == 0:
                own.append(
                    pltpu.make_async_copy(
                        source.at[pl.ds(pl.multiple_of(f * rows, 16), rows)],
                        whole,
                        local_sems.at[which, mask],
                    )
                )
                sent.append(
                    send(
                        whole.at[theirs],
                        inbox.at[work_rows(block)],
                        core_send.at[which, mask],
                        core_recv.at[which, mask],
                        sibling,
                    )
                )
                continue
            own.append(
                pltpu.make_async_copy(
                    source.at[block_rows(block, t)],
                    work.at[work_rows(block)],
                    local_sems.at[which, mask],
                )
            )
            sent.append(
                send(
                    source.at[block_rows(block, 1 - t)],
                    inbox.at[work_rows(block)],
                    core_send.at[which, mask],
                    core_recv.at[which, mask],
                    sibling,
                )
            )
        return own, sent

    back_own, back_sent = exchange(moe_back, work_back, pair_back, 0, whole_back)
    out_own, out_sent = exchange(moe_out, work_out, pair_out, 1, whole_out)
    for copy in back_own:
        copy.start()
    wo_copy = pltpu.make_async_copy(wo_hbm, wo, local_sems.at[2, 0])
    wq_copy = pltpu.make_async_copy(wq_hbm, wq, local_sems.at[2, 1])
    wo_copy.start()
    for copy in inputs:
        copy.start()
    peers = [(lax.rem(f + k, fsdp), c, t) for k in range(1, fsdp)]
    stacked = [(f, lax.rem(c + k, contexts), t) for k in range(1, contexts)]
    greet(peers + stacked + [sibling])
    for copy in back_sent[:-1]:
        copy.start()
    for copy in out_own:
        copy.start()
    wq_copy.start()

    lines = PARAMS // 128 // (2 * contexts)
    early = -(-(8 * RANK * D // 128) // (2 * lines))

    def fill_blocks(first, last):
        for context in range(first, last):
            for part_index in range(2):
                start = (2 * context + part_index) * lines
                packed[context, part_index, 0:lines, :] = flat[start : start + lines, :]

    def pair_block(block):
        return send(
            packed.at[block, 1 - t],
            packed_in.at[block],
            sum_send.at[0, block],
            sum_recv.at[0, block],
            sibling,
        )

    def to_owner(k):
        return send(
            up_out.at[k], up_in.at[k], sum_send.at[1, k], sum_recv.at[1, k], stacked[k]
        )

    def push_blocks(soon):
        for k in range(contexts - 1):
            owner = lax.rem(c + k + 1, contexts)

            @pl.when((owner >= early) if soon else (owner < early))
            def _(k=k, owner=owner):
                up_out[k] = (packed[owner, t] + packed_in[owner]).astype(bf)
                to_owner(k).start()

    def to_peer(k):
        return send(
            own_sum, tree_sums.at[k], sum_send.at[2, k], sum_recv.at[2, k], peers[k]
        )

    def sum_own():
        result = packed[c, t] + packed_in[c]
        for k in range(contexts - 1):
            to_owner(k).wait_recv()
            result = result + up_in[k].astype(f32)
        own_sum[...] = result.astype(bf)
        for k in range(fsdp - 1):
            to_peer(k).start()

    def chunk_rows(chunk):
        return pl.ds(pl.multiple_of(chunk * rows, 16), rows)

    def loads(chunk):
        block = chunk_rows(chunk)
        return [
            pltpu.make_async_copy(k_hbm.at[block], k_buf.at[block], chunk_sems.at[1, chunk]),
            pltpu.make_async_copy(v_hbm.at[block], v_buf.at[block], chunk_sems.at[2, chunk]),
        ]

    def n1_load(chunk):
        return pltpu.make_async_copy(
            n1_hbm.at[chunk_rows(chunk)], n1_buf, chunk_sems.at[0, chunk]
        )

    def table_loads(chunk):
        block = chunk_rows(chunk)
        return [
            pltpu.make_async_copy(cos_hbm.at[block], cosine, chunk_sems.at[3, chunk]),
            pltpu.make_async_copy(sin_hbm.at[block], sinus, chunk_sems.at[4, chunk]),
        ]

    def start_loads(chunk, carry):
        for copy in loads(chunk):
            copy.start()
        return carry

    lax.fori_loop(0, c + 1, start_loads, 0)

    def weights_in(chunk, p):
        source = p_hbm.at[pl.ds(chunk * heads + 2 * p, 2)]
        return pltpu.make_async_copy(source, p_buf.at[pl.ds(2 * p, 2)], p_sems.at[p])

    for p in range(heads // 2):
        weights_in(0, p).start()

    back = Scatter(
        bits, f, peer, work_back, inbox_back, half, fs_send.at[0], fs_recv.at[0]
    )
    out = Scatter(bits, f, peer, work_out, inbox_out, half, fs_send.at[1], fs_recv.at[1])

    def join(own, sent, whole, extra, work):
        own[-1].wait()
        whole[...] = (whole[...].astype(f32) + extra[...].astype(f32)).astype(bf)
        sent[-1].start()
        work[work_rows(f), :] = whole[mine, :]

    def pair_sum(own, sent, work, inbox, scatter):
        for i, mask in enumerate(masks):
            block = work_rows(flips(f, mask, bits))
            if mask != 0:
                own[i].wait()
            sent[i].wait_recv()
            work[block, :] = (
                work[block, :].astype(f32) + inbox[block, :].astype(f32)
            ).astype(bf)
            scatter.start_mask(mask)

    for copy in inputs:
        copy.wait()
    join(back_own, back_sent, whole_back, dn2, work_back)
    pair_sum(back_own, back_sent, work_back, pair_back, back)
    for copy in out_sent[:-1]:
        copy.start()
    join(out_own, out_sent, whole_out, shared, work_out)
    flat[...] = jnp.zeros_like(flat)
    pack_second(t, flat, wide, da_gu, db_gu, da_dn, db_dn)
    fill_blocks(early, contexts)
    for block in range(early, contexts):
        pair_block(block).start()
    for stage in range(1, bits):
        back.add(stage - 1)
        back.start(stage)
    dq_t[...] = jnp.zeros_like(dq_t)
    da_qkv[...] = jnp.zeros_like(da_qkv)
    db_qkv[...] = jnp.zeros_like(db_qkv)
    for block in range(early, contexts):
        pair_block(block).wait_recv()
    push_blocks(True)
    back.last(total_half)
    pair_sum(out_own, out_sent, work_out, pair_out, out)
    for copy in out_sent:
        copy.wait_send()
    total_full[mine, :] = total_half[...]
    full_copy = send(
        total_half, total_full.at[mine], core_send.at[2, 0], core_recv.at[2, 0], sibling
    )
    full_copy.start()
    back.finish()
    for copy in back_sent:
        copy.wait_send()
    gain_one = gains[0:1, :]
    gain_two = gains[1:2, :]
    wo_copy.wait()
    full_copy.wait_recv()

    def attn_tile(i, carry):
        block = local_rows(i)
        values = resid[block, :]
        gradient = g_in[block, :].astype(f32) + norm_back(
            values, rms_scale(values), gain_two, total_full[block, :].astype(f32)
        )
        dy[block, :] = gradient
        low_grad = gradient.astype(bf)
        rank_back = nt_dot(low_grad, b_o2[0:128, :])
        do_n[block, :] = (
            nn_dot(low_grad, wo[...]) + nn_dot(two_parts(rank_back), a_o_t2[...])
        ).astype(bf)
        values_o = mixed[block, :]
        rank = nn_dot(values_o, a_o[...])
        first = tn_dot(rank_back.astype(bf), values_o)[0:RANK]
        second = 2.0 * tn_dot(rank.astype(bf), low_grad)[0:RANK]

        @pl.when(i == 0)
        def _():
            da_o[...] = first
            db_o[...] = second

        @pl.when(i > 0)
        def _():
            da_o[...] += first
            db_o[...] += second

        return carry

    lax.fori_loop(0, 2, attn_tile, 0)
    for p in range(width // 128):
        lanes = slice(128 * p, 128 * p + 128)
        turned = do_n[:, lanes].astype(f32).T
        do_t[lanes, :] = turned.astype(bf)
        product = turned * o_t[lanes, :]
        for odd in range(2):
            delta[2 * p + odd : 2 * p + odd + 1, :] = jnp.sum(
                product[HEAD_DIM * odd : HEAD_DIM * odd + HEAD_DIM, :], axis=0, keepdims=True
            )
    wq_copy.wait()

    def attend_back(chunk):
        block = chunk_rows(chunk)
        n1_load(chunk).start()
        for copy in table_loads(chunk):
            copy.start()
        for copy in table_loads(chunk) + loads(chunk):
            copy.wait()
        scale = jnp.exp(peaks[pl.ds(pl.multiple_of(chunk * 8, 8), 8), :] - lse[...])
        factor[...] = scale
        cos_rows = cosine[...]
        sin_rows = -sinus[...]
        for p in range(width // 128):
            lanes = slice(128 * p, 128 * p + 128)
            k_t[lanes, :] = k_buf[block, lanes].astype(f32).T.astype(bf)

        def pair_step(p, carry):
            lanes = pl.ds(pl.multiple_of(p * 128, 128), 128)
            weights_in(chunk, p).wait()
            values = v_buf[block, lanes]
            grad_t = do_t[lanes, :]
            query = q_n[:, lanes]
            grad = do_n[:, lanes]
            grad_keys = jnp.zeros((rows, 128), f32)
            grad_values = jnp.zeros((rows, 128), f32)
            for odd in range(2):
                h = 2 * p + odd
                upper = head_half(grad_t.shape, 0, odd)
                side = head_half(query.shape, 1, odd)
                none_t = jnp.zeros_like(grad_t)
                none = jnp.zeros_like(query)
                weights = p_buf[h].astype(f32) * factor[pl.ds(h, 1), :]
                low_weights = weights.astype(bf)
                grad_weights = nn_dot(values, jnp.where(upper, grad_t, none_t))
                grad_scores = (weights * (grad_weights - delta[pl.ds(h, 1), :])).astype(bf)
                grad_values += nn_dot(low_weights, jnp.where(side, grad, none))
                grad_keys += nn_dot(grad_scores, jnp.where(side, query, none))
                head = pl.ds(pl.multiple_of(h * HEAD_DIM, HEAD_DIM), HEAD_DIM)
                dq_t[head, :] += nn_dot(k_t[head, :], grad_scores)
            grad_kv[kv_rows, lanes] = turn(grad_keys, cos_rows, sin_rows).astype(bf)
            grad_kv[kv_rows, pl.ds(pl.multiple_of(width + p * 128, 128), 128)] = grad_values.astype(bf)

            @pl.when(chunk < c)
            def _():
                weights_in(chunk + 1, p).start()

            return carry

        lax.fori_loop(0, heads // 2, pair_step, 0)

    def adapter_back(chunk, own):
        block = chunk_rows(chunk)
        grads = grad_kv[kv_rows, :]
        rank_back = nt_dot(grads, b_qkv2[0:128, width:])
        n1_load(chunk).wait()
        n1 = n1_buf[...]
        rank = nn_dot(n1, a_qkv[...]).astype(bf)
        both = 2.0 * tn_dot(rank, grads)
        db_qkv[RANK : 2 * RANK, :] += both[RANK : 2 * RANK, :width]
        db_qkv[2 * RANK :, :] += both[2 * RANK : 3 * RANK, width:]
        if own:
            for p in range(width // 128):
                lanes = slice(128 * p, 128 * p + 128)
                grad_query = (dq_t[lanes, :] * 0.125).T
                dq[:, lanes] = turn(grad_query, cosine[...], -sinus[...]).astype(bf)
            rank_back += nt_dot(dq[...], b_qkv2[0:128, :width])
            db_qkv[0:RANK, :] += 2.0 * tn_dot(rank, dq[...])[0:RANK, :]
        da_qkv[...] += tn_dot(rank_back.astype(bf), n1)[0 : 3 * RANK]
        return rank_back

    def project_back(chunk, own, rank_back):
        result = nt_dot(grad_kv[kv_rows, :], wq[:, width:])
        if own:
            result += nt_dot(dq[...], wq[:, :width])
        result += nn_dot(two_parts(rank_back), a_qkv_t2[...])
        part[...] = result.astype(bf)
        part_out[work_rows(chunk), :] = part[theirs, :]
        z_out[work_rows(chunk), :] = part[mine, :]

    def pair_copy(chunk):
        return send(
            part_out.at[work_rows(chunk)],
            part_in.at[work_rows(chunk)],
            pair_send.at[chunk],
            pair_recv.at[chunk],
            sibling,
        )

    pieces = split_rows(half)

    def down(chunk, piece):
        offset, size = pieces[piece]
        block = Gather.rows(chunk * half + offset, size)
        return send(
            z_out.at[block],
            z_in.at[block],
            z_send.at[chunk, piece],
            z_recv.at[chunk, piece],
            (f, c - 1, t),
        )

    def chain(chunk, onward):
        pair_copy(chunk).wait_recv()
        for piece, (offset, size) in enumerate(pieces):
            block = Gather.rows(chunk * half + offset, size)
            summed = z_out[block, :].astype(f32) + part_in[block, :].astype(f32)
            z_out[block, :] = summed.astype(bf)

            @pl.when(c < contexts - 1)
            def _(block=block, summed=summed, piece=piece):
                down(chunk, piece).wait_recv()
                z_out[block, :] = (summed + z_in[block, :].astype(f32)).astype(bf)

            if onward:
                down(chunk, piece).start()

    def pass_down(chunk):
        chain(chunk, True)

    def sum_moe():
        for stage in range(1, bits):
            out.add(stage - 1)
            out.start(stage)

    ffn_copy = send(ffn_half, ffn_full.at[mine], core_send.at[2, 1], core_recv.at[2, 1], sibling)

    def share_moe():
        out.last(ffn_half)
        ffn_full[mine, :] = ffn_half[...]
        ffn_copy.start()

    def step(chunk, carry):
        attend_back(chunk)
        project_back(chunk, False, adapter_back(chunk, False))
        pair_copy(chunk).start()

        @pl.when(c == contexts - 1)
        def _():
            pass_down(chunk)

        @pl.when((c < contexts - 1) & (chunk >= 1))
        def _():
            pass_down(chunk - 1)

        @pl.when(chunk == 0)
        def _():
            sum_moe()

        @pl.when(chunk == 1)
        def _():
            share_moe()

            @pl.when(c >= early)
            def _():
                sum_own()

        return carry

    lax.fori_loop(0, c, step, 0)
    attend_back(c)
    last_rank = adapter_back(c, True)
    pack_first(t, flat, wide, da_qkv, db_qkv, da_o, db_o)
    fill_blocks(0, early)
    for block in range(early):
        pair_block(block).start()
    project_back(c, True, last_rank)
    pair_copy(c).start()
    for block in range(early):
        pair_block(block).wait_recv()
    push_blocks(False)

    @pl.when((c < 2) & (c >= early))
    def _():
        sum_own()

    @pl.when(c == 0)
    def _():
        sum_moe()

    @pl.when((c < contexts - 1) & (c >= 1))
    def _():
        pass_down(c - 1)

    @pl.when(c < 2)
    def _():
        share_moe()

    chain(c, False)
    dn1_full[mine, :] = z_out[work_rows(c), :]
    dn1_copy = send(
        z_out.at[work_rows(c)],
        dn1_full.at[mine],
        core_send.at[2, 2],
        core_recv.at[2, 2],
        sibling,
    )
    dn1_copy.start()
    ffn_copy.wait_recv()
    resid[...] = resid[...] + ffn_full[...].astype(f32)
    block_copy = pltpu.make_async_copy(resid, block_out, in_sems.at[len(inputs)])
    block_copy.start()
    dn1_copy.wait_recv()

    def final_tile(i, carry):
        block = local_rows(i)
        values = x_in[block, :].astype(f32)
        dy[block, :] = dy[block, :] + norm_back(
            values, rms_scale(values), gain_one, dn1_full[block, :].astype(f32)
        )
        return carry

    lax.fori_loop(0, 2, final_tile, 0)
    grad_copy = pltpu.make_async_copy(dy, input_grad, in_sems.at[len(inputs) + 1])
    grad_copy.start()
    @pl.when(c < early)
    def _():
        sum_own()

    own = ADAPTERS // fsdp
    wanted = [(f * own + a).astype(f32) for a in range(own)]
    mine_sum = own_sum[...].astype(f32)
    sums = [jnp.where(table_all[f, 4:5, 0:1] == w, mine_sum, 0.0) for w in wanted]
    for k in range(fsdp - 1):
        to_peer(k).wait_recv()
        tree = table_all[lax.rem(f - k - 1 + fsdp, fsdp), 4:5, 0:1]
        block = tree_sums[k].astype(f32)
        sums = [total + jnp.where(tree == w, block, 0.0) for total, w in zip(sums, wanted)]
    for a in range(own):
        adapter_out[a] = sums[a]
    for copy in [full_copy, ffn_copy, dn1_copy]:
        copy.wait_send()
    block_copy.wait()
    grad_copy.wait()
    for block in range(contexts):
        pair_block(block).wait_send()
    for k in range(contexts - 1):
        to_owner(k).wait_send()
    for k in range(fsdp - 1):
        to_peer(k).wait_send()
    out.finish()

    def drain(chunk, carry):
        pair_copy(chunk).wait_send()

        @pl.when(chunk < c)
        def _():
            for piece in range(len(pieces)):
                down(chunk, piece).wait_send()

        return carry

    lax.fori_loop(0, c + 1, drain, 0)


def backward_call(sizes, remote, local):
    fsdp, contexts, _ = sizes
    rows = local[0].shape[0]
    padded = (PARAMS // 128 // (2 * contexts) + 15) // 16 * 16
    half = rows // 2
    tree = rows * contexts
    width = remote[6].shape[1]
    units = local[19].shape[1]
    bf, f32 = jnp.bfloat16, jnp.float32
    vmem = pl.BlockSpec(memory_space=pltpu.VMEM)
    hbm = pl.BlockSpec(memory_space=pl.ANY)

    def shape(kind, *dims):
        return jax.ShapeDtypeStruct(dims, kind)

    moves = 2 * (fsdp - 1)
    slots = max(fsdp, 4)
    dma = pltpu.SemaphoreType.DMA
    return pl.pallas_call(
        functools.partial(backward_kernel, sizes),
        in_specs=[hbm] * len(remote) + [hbm, hbm, vmem, vmem, hbm, hbm, hbm, hbm, hbm, hbm, hbm, vmem, hbm, hbm, hbm, hbm, hbm, hbm, vmem, vmem, vmem, vmem, vmem],
        out_specs=[hbm, hbm, vmem],
        out_shape=[
            shape(f32, rows, D),
            shape(f32, rows, D),
            shape(f32, ADAPTERS // fsdp, padded, 128),
        ],
        scratch_shapes=[
            pltpu.VMEM((rows, 128), f32),
            pltpu.VMEM((rows, 128), f32),
            pltpu.VMEM((tree, width), bf),
            pltpu.VMEM((tree, width), bf),
            pltpu.VMEM((D, 3 * width), bf),
            pltpu.VMEM((D, width), bf),
            pltpu.VMEM((max(fsdp, contexts) * half, D), bf),
            pltpu.VMEM((max(fsdp, contexts) * half, D), bf),
            pltpu.VMEM((max(fsdp - 1, 2) * half, D), bf),
            pltpu.VMEM((fsdp * half, D), bf),
            pltpu.VMEM((fsdp * half, D), bf),
            pltpu.VMEM(((fsdp - 1) * half, D), bf),
            pltpu.VMEM((half, D), bf),
            pltpu.VMEM((rows, D), bf),
            pltpu.VMEM((half, D), bf),
            pltpu.VMEM((rows, D), bf),
            pltpu.VMEM((rows, D), f32),
            pltpu.VMEM((rows, width), bf),
            pltpu.VMEM((width, rows), bf),
            pltpu.VMEM((8, rows), f32),
            pltpu.VMEM((8, rows), f32),
            pltpu.VMEM((width, rows), bf),
            pltpu.VMEM((width, rows), f32),
            pltpu.VMEM((rows, width), bf),
            pltpu.VMEM((contexts * half, D), bf),
            pltpu.VMEM((contexts * half, D), bf),
            pltpu.VMEM((rows, D), bf),
            dma((2, moves)),
            dma((2, moves)),
            dma((contexts, 2)),
            dma((contexts, 2)),
            dma((3, slots)),
            dma((3, slots)),
            dma((contexts,)),
            dma((contexts,)),
            dma((3, slots)),
            dma((5, contexts)),
            pltpu.VMEM((rows, D), bf),
            pltpu.VMEM((rows, D), bf),
            pltpu.VMEM((rows, D), f32),
            pltpu.VMEM((rows, D), bf),
            pltpu.VMEM((rows, D), bf),
            pltpu.VMEM((width, rows), bf),
            pltpu.VMEM((rows, width), bf),
            pltpu.VMEM((rows, width), bf),
            pltpu.VMEM((width, rows), f32),
            pltpu.VMEM((D, 128), bf),
            pltpu.VMEM((256, 3 * width), bf),
            pltpu.VMEM((256, D), bf),
            pltpu.VMEM((width, 128), bf),
            pltpu.VMEM((256, width), bf),
            pltpu.VMEM((256, D), bf),
            pltpu.VMEM((3 * RANK, D), f32),
            pltpu.VMEM((3 * RANK, width), f32),
            pltpu.VMEM((RANK, width), f32),
            pltpu.VMEM((RANK, D), f32),
            pltpu.VMEM((PARAMS // 128, 128), f32),
            pltpu.VMEM((max(D, units), 128), f32),
            pltpu.VMEM((contexts, 2, padded, 128), f32),
            pltpu.VMEM((contexts, padded, 128), f32),
            pltpu.VMEM((contexts - 1, padded, 128), bf),
            pltpu.VMEM((contexts - 1, padded, 128), bf),
            pltpu.VMEM((padded, 128), bf),
            pltpu.VMEM((fsdp - 1, padded, 128), bf),
            dma((17,)),
            dma((3, max(fsdp, contexts))),
            dma((3, max(fsdp, contexts))),
            pltpu.VMEM((width // HEAD_DIM, rows, rows), bf),
            dma((width // HEAD_DIM // 2,)),
            pltpu.VMEM((rows, D), bf),
            pltpu.VMEM((rows, D), bf),
        ],
        name="backward",
        compiler_params=pltpu.CompilerParams(
            collective_id=3, has_side_effects=True, vmem_limit_bytes=63 << 20
        ),
    )(*remote, *local)


def shards(
    tokens,
    attn_gain,
    w_qkv,
    w_out,
    ffn_gain,
    w_gu,
    w_dn,
    w_egu,
    w_edn,
    adapters,
    adapter_ids,
    parents,
    seg_lengths,
    routes,
    route_weights,
    cotangent,
):
    row_count = tokens.shape[1]
    contexts = lax.axis_size("context")
    tensors = lax.axis_size("tensor")
    fsdp_size = lax.axis_size("fsdp")
    sizes = (fsdp_size, contexts, tensors)
    local_width = w_qkv.shape[2]
    local_ff = w_dn.shape[0]
    own_adapters = adapters.shape[0]
    own_width = D // fsdp_size
    gains = jnp.broadcast_to(jnp.concatenate([attn_gain, ffn_gain])[None], (16, 2 * own_width))
    route_table = jnp.concatenate(
        [
            routes[0].astype(jnp.float32).T,
            route_weights[0].astype(jnp.float32).T,
            jnp.broadcast_to(adapter_ids.astype(jnp.float32)[:, None], (1, row_count)),
            jnp.zeros((3, row_count), jnp.float32),
        ]
    )
    lines = adapters.shape[1] // 128
    padded = (lines + 15) // 16 * 16
    adapter_rows = jnp.pad(
        adapters.reshape(own_adapters, lines, 128), ((0, 0), (0, padded - lines), (0, 0))
    ).reshape(own_adapters * padded, 128)
    half_dim = HEAD_DIM // 2
    exponents = -(np.arange(half_dim, dtype=np.float32) * np.float32(2.0)) / np.float32(HEAD_DIM)
    frequency = np.power(np.float32(rope_base), exponents).astype(np.float32)
    signs = np.repeat(np.array([-1.0, 1.0], np.float32), half_dim)
    turns = np.zeros((8, 128), np.float32)
    turns[0], turns[1] = np.tile(frequency, 4), np.tile(signs, 2)
    sharded = (
        tokens[0],
        cotangent[0],
        w_qkv.reshape(own_width, 3 * local_width),
        w_out.T,
        w_gu.reshape(own_width, 2 * local_ff),
        w_dn.T,
    )
    (
        n1_all,
        k_all,
        v_all,
        wq_all,
        wo_all,
        normed_all,
        cotangent_all,
        p_all,
        q_t,
        q_n,
        mixed_own,
        o_t,
        lse,
        resid,
        shared,
        dn2,
        da_gu_t,
        db_gu_own,
        da_dn_t,
        db_dn_own,
        gains_full,
        cosine,
        sinus,
        hot,
        reach_t,
        a_qkv,
        b_qkv2,
        a_qkv_t2,
        a_o,
        b_o2,
        a_o_t2,
        table_all,
        place_row,
        place_col,
        weight_col,
        marks,
        peaks,
    ) = forward_call(
        sizes,
        sharded,
        (adapter_rows, gains, route_table, turns, parents, seg_lengths),
    )
    moe_all, moe_back_all = moe_call(
        marks,
        place_row,
        place_col,
        weight_col,
        normed_all,
        cotangent_all,
        w_egu.transpose(0, 2, 1, 3),
        w_edn,
    )
    remote = (moe_all, moe_back_all, n1_all, k_all, v_all, wq_all, wo_all, cosine, sinus, p_all)
    block_out, input_grad, sums = backward_call(
        sizes,
        remote,
        (tokens[0], cotangent[0], gains_full, peaks)
        + (resid, shared, dn2, q_t, q_n, mixed_own, o_t, lse)
        + (a_qkv, b_qkv2, a_qkv_t2, a_o, a_o_t2, b_o2)
        + (da_gu_t, db_gu_own, da_dn_t, db_dn_own, table_all),
    )
    adapter_grads = sums[:, :lines].reshape(own_adapters, -1)
    return (block_out[None], input_grad[None], adapter_grads)


def solution(mesh):
    return jax.shard_map(
        shards,
        mesh=mesh,
        in_specs=(
            P("fsdp", "context", None),
            P("fsdp"),
            P("fsdp", None, "tensor"),
            P("tensor", "fsdp"),
            P("fsdp"),
            P("fsdp", None, "tensor"),
            P("tensor", "fsdp"),
            P("fsdp", None, None, "tensor"),
            P("fsdp", "tensor", None),
            P("fsdp", ("context", "tensor")),
            P("fsdp"),
            P("fsdp", None),
            P("fsdp", None),
            P("fsdp", "context", None),
            P("fsdp", "context", None),
            P("fsdp", "context", None),
        ),
        out_specs=(
            P("fsdp", "context", None),
            P("fsdp", "context", None),
            P("fsdp", ("context", "tensor")),
        ),
        check_vma=False,
    )
```

```python
import jax
import jax.numpy as jnp
import numpy as np
import functools
import math

from jax import lax
from jax.experimental import pallas as pl
from jax.experimental.pallas import tpu as pltpu
from jax.sharding import PartitionSpec as P

D = 768
HEADS = 12
HEAD_DIM = 64
FF = 2048
EXPERTS = 8
TOPK = 2
RANK = 16
ADAPTERS = 8
PARAMS = 233472


epsilon = 1e-06
adapter_scale = 2.0
rope_base = 10000.0
masked_score = -1e30
highest_precision = lax.Precision.HIGHEST


def rms_scale(values):
    return lax.rsqrt(jnp.mean(values * values, axis=-1, keepdims=True) + epsilon)


def norm_back(values, scaling, gain_values, gradient):
    weighted = gradient * gain_values
    inner_mean = jnp.mean(values * weighted, axis=-1, keepdims=True)
    return scaling * weighted - values * (scaling * scaling * scaling) * inner_mean


SLOT_TILE = 512
TOKEN_TILE = 256
SLOT_WINDOW = 128


def nt_dot(left, right):
    return lax.dot_general(left, right, (((1,), (1,)), ((), ())), preferred_element_type=jnp.float32)


def tn_dot(left, right):
    return lax.dot_general(left, right, (((0,), (0,)), ((), ())), preferred_element_type=jnp.float32)


def nn_dot(left, right):
    return jnp.dot(left, right, preferred_element_type=jnp.float32)


def moe_kernel(
    starts,
    place_row,
    place_hbm,
    weight_hbm,
    rows_hbm,
    grads_hbm,
    egu_hbm,
    edn_hbm,
    out_hbm,
    back_hbm,
    place_col,
    weight_col,
    rows_ref,
    grads_ref,
    egu_ref,
    edn_ref,
    out_ref,
    back_ref,
    taken,
    taken_grad,
    taken_weight,
    sems,
    block_sems,
):
    f32, bf = jnp.float32, jnp.bfloat16
    experts = egu_hbm.shape[0]
    blocks = rows_ref.shape[0] // TOKEN_TILE

    def block_rows(b):
        return pl.ds(pl.multiple_of(b * TOKEN_TILE, TOKEN_TILE), TOKEN_TILE)

    def loads(b):
        block = block_rows(b)
        return [
            pltpu.make_async_copy(source.at[block], target.at[block], block_sems.at[i, b])
            for i, (source, target) in enumerate(
                ((rows_hbm, rows_ref), (grads_hbm, grads_ref), (weight_hbm, weight_col))
            )
        ]

    def stores(b):
        block = block_rows(b)
        return [
            pltpu.make_async_copy(source.at[block], target.at[block], block_sems.at[3 + i, b])
            for i, (source, target) in enumerate(((out_ref, out_hbm), (back_ref, back_hbm)))
        ]

    def weights(e):
        return [
            pltpu.make_async_copy(egu_hbm.at[e], egu_ref.at[e], sems.at[0, e]),
            pltpu.make_async_copy(edn_hbm.at[e], edn_ref.at[e], sems.at[1, e]),
        ]

    def each(count, copies, action):
        def step(i, carry):
            for copy in copies(i):
                getattr(copy, action)()
            return carry

        lax.fori_loop(0, count, step, 0)

    each(blocks, loads, "start")
    each(experts, weights, "start")
    place_copy = pltpu.make_async_copy(place_hbm, place_col, sems.at[2, 0])
    place_copy.start()
    taken[...] = jnp.zeros_like(taken)
    taken_grad[...] = jnp.zeros_like(taken_grad)
    taken_weight[...] = jnp.zeros_like(taken_weight)
    slot_rows = lax.broadcasted_iota(jnp.int32, (SLOT_WINDOW, TOKEN_TILE), 0).astype(f32)
    slot_cols = lax.broadcasted_iota(jnp.int32, (TOKEN_TILE, SLOT_WINDOW), 1).astype(f32)

    def windows(e, b):
        begin = starts[e, b] // 16 * 16
        return begin, (starts[e, b + 1] - begin + SLOT_WINDOW - 1) // SLOT_WINDOW

    def window_rows(begin, i):
        return pl.ds(pl.multiple_of(begin + i * SLOT_WINDOW, 16), SLOT_WINDOW)

    def fetch(b, carry):
        block = block_rows(b)
        for copy in loads(b):
            copy.wait()

        def take(which):
            picks = []
            for e, first in which:
                hit = place_row[e : e + 1, block] == slot_rows + first.astype(f32)
                picks.append(jnp.where(hit, 1.0, 0.0).astype(bf))
            pick = picks[0] if len(picks) == 1 else jnp.concatenate(picks, axis=0)
            for source, target in (
                (rows_ref, taken),
                (grads_ref, taken_grad),
                (weight_col, taken_weight),
            ):
                got = nn_dot(pick, source[block, :]).astype(bf)
                for i, (e, first) in enumerate(which):
                    slots = window_rows(first, 0)
                    target[e, slots, :] += got[i * SLOT_WINDOW : (i + 1) * SLOT_WINDOW, :]

        spans = [windows(e, b) for e in range(experts)]
        take([(e, spans[e][0]) for e in range(experts)])
        for e in range(experts):

            def more(i, c, e=e):
                take([(e, spans[e][0] + i * SLOT_WINDOW)])
                return c

            lax.fori_loop(1, spans[e][1], more, 0)
        return carry

    lax.fori_loop(0, blocks, fetch, 0)

    def tile(e, start, size):
        slots = pl.ds(pl.multiple_of(start, 128), size)
        inputs = taken[e, slots, :]
        gate_pre = nn_dot(inputs, egu_ref[e, 0])
        up_pre = nn_dot(inputs, egu_ref[e, 1])
        sigmoid_gate = jax.nn.sigmoid(gate_pre)
        silu = gate_pre * sigmoid_gate
        active = (silu * up_pre).astype(bf)
        taken[e, slots, :] = nn_dot(active, edn_ref[e]).astype(bf)
        grad_active = nt_dot(taken_grad[e, slots, :], edn_ref[e])
        lane = lax.broadcasted_iota(jnp.int32, (size, 128), 1)
        scale = jnp.sum(
            jnp.where(lane == e, taken_weight[e, slots, :].astype(f32), 0.0), axis=1, keepdims=True
        )
        grad_active = grad_active * scale
        grad_gate = (
            grad_active * up_pre * sigmoid_gate * (1.0 + gate_pre * (1.0 - sigmoid_gate))
        ).astype(bf)
        grad_up = (grad_active * silu).astype(bf)
        taken_grad[e, slots, :] = (
            nt_dot(grad_gate, egu_ref[e, 0]) + nt_dot(grad_up, egu_ref[e, 1])
        ).astype(bf)

    def expert_step(e, carry):
        for copy in weights(e):
            copy.wait()
        count = starts[e, blocks]
        whole = count // SLOT_TILE
        rest = count - whole * SLOT_TILE

        def step(i, c):
            tile(e, i * SLOT_TILE, SLOT_TILE)
            return c

        lax.fori_loop(0, whole + jnp.where(rest > SLOT_TILE - 128, 1, 0), step, 0)
        for size in range(128, SLOT_TILE, 128):

            @pl.when((rest > size - 128) & (rest <= size))
            def _(size=size):
                tile(e, whole * SLOT_TILE, size)

        return carry

    lax.fori_loop(0, experts, expert_step, 0)
    place_copy.wait()

    def give(b, carry):
        block = block_rows(b)

        def hand(which):
            plain, scaled, values, values_grad = [], [], [], []
            for e, first in which:
                hit = place_col[block, e : e + 1] == slot_cols + first.astype(f32)
                plain.append(jnp.where(hit, 1.0, 0.0).astype(bf))
                weight = weight_col[block, e : e + 1].astype(f32)
                scaled.append(jnp.where(hit, weight, 0.0).astype(bf))
                values.append(taken[e, window_rows(first, 0), :])
                values_grad.append(taken_grad[e, window_rows(first, 0), :])

            def join(pieces, axis):
                return pieces[0] if len(pieces) == 1 else jnp.concatenate(pieces, axis=axis)

            return (
                nn_dot(join(scaled, 1), join(values, 0)),
                nn_dot(join(plain, 1), join(values_grad, 0)),
            )

        spans = [windows(e, b) for e in range(experts)]
        first, second = hand([(e, spans[e][0]) for e in range(experts)])
        out_ref[block, :] = first.astype(bf)
        back_ref[block, :] = second.astype(bf)
        for e in range(experts):

            def more(i, c, e=e):
                first, second = hand([(e, spans[e][0] + i * SLOT_WINDOW)])
                out_ref[block, :] = (out_ref[block, :].astype(f32) + first).astype(bf)
                back_ref[block, :] = (back_ref[block, :].astype(f32) + second).astype(bf)
                return c

            lax.fori_loop(1, spans[e][1], more, 0)
        for copy in stores(b):
            copy.start()
        return carry

    lax.fori_loop(0, blocks, give, 0)
    each(blocks, stores, "wait")


def moe_call(starts, place_row, place_col, weight_col, rows, grads, egu, edn):
    total, width = rows.shape
    experts = egu.shape[0]
    slots = total // 2 + SLOT_TILE
    blocks = total // TOKEN_TILE
    bf, f32 = jnp.bfloat16, jnp.float32
    vmem = pl.BlockSpec(memory_space=pltpu.VMEM)
    hbm = pl.BlockSpec(memory_space=pl.ANY)
    shape = jax.ShapeDtypeStruct((total, width), bf)
    return pl.pallas_call(
        moe_kernel,
        grid_spec=pltpu.PrefetchScalarGridSpec(
            num_scalar_prefetch=1,
            grid=(),
            in_specs=[vmem] + [hbm] * 6,
            out_specs=[hbm, hbm],
            scratch_shapes=[
                pltpu.VMEM((total, 128), f32),
                pltpu.VMEM((total, 128), bf),
                pltpu.VMEM((total, width), bf),
                pltpu.VMEM((total, width), bf),
                pltpu.VMEM(egu.shape, bf),
                pltpu.VMEM(edn.shape, bf),
                pltpu.VMEM((total, width), bf),
                pltpu.VMEM((total, width), bf),
                pltpu.VMEM((experts, slots, width), bf),
                pltpu.VMEM((experts, slots, width), bf),
                pltpu.VMEM((experts, slots, 128), bf),
                pltpu.SemaphoreType.DMA((3, experts)),
                pltpu.SemaphoreType.DMA((5, blocks)),
            ],
        ),
        out_shape=[shape, shape],
        name="experts",
        compiler_params=pltpu.CompilerParams(vmem_limit_bytes=62 << 20),
    )(starts, place_row, place_col, weight_col, rows, grads, egu, edn)


MESH = pl.DeviceIdType.MESH


def place_of():
    return lax.axis_index("fsdp"), lax.axis_index("context"), lax.axis_index("tensor")


def greet(devices):
    barrier = pltpu.get_barrier_semaphore()
    for device in devices:
        pl.semaphore_signal(barrier, inc=1, device_id=device, device_id_type=MESH)
    pl.semaphore_wait(barrier, len(devices))


def send(source, target, send_sem, recv_sem, device):
    return pltpu.make_async_remote_copy(
        src_ref=source,
        dst_ref=target,
        send_sem=send_sem,
        recv_sem=recv_sem,
        device_id=device,
        device_id_type=MESH,
    )


def flip(index, bit):
    return index + (1 - 2 * lax.rem(index // (1 << bit), 2)) * (1 << bit)


def split_rows(count):
    first = (count // 2 + 15) // 16 * 16
    return ((0, first), (first, count - first))


class Gather:
    def __init__(self, bits, me, device_of, own, buf, stride, base, count, send_sems, recv_sems):
        self.stages = [[] for _ in range(bits)]
        self.arrived = [[] for _ in range(bits)]
        self.passed = [[] for _ in range(bits)]
        number = 0
        for half, (offset, size) in enumerate(split_rows(count)):
            held = [me]
            for stage in range(bits):
                bit = (stage + half) % bits
                for block in held:
                    rows = self.rows(block * stride + base + offset, size)
                    source = own.at[self.rows(base + offset, size)] if block is me else buf.at[rows]
                    self.passed[stage].append(block is not me)
                    self.stages[stage].append(
                        send(
                            source,
                            buf.at[rows],
                            send_sems.at[number],
                            recv_sems.at[number],
                            device_of(flip(me, bit)),
                        )
                    )
                    self.arrived[stage].append(
                        self.rows(flip(block, bit) * stride + base + offset, size)
                    )
                    number = number + 1
                held = held + [flip(block, bit) for block in held]

    @staticmethod
    def rows(start, size):
        return pl.ds(pl.multiple_of(start, 16), size)

    def start(self, stage):
        if stage == 0:
            for copies, passed in zip(self.stages, self.passed):
                for copy, later in zip(copies, passed):
                    if not later:
                        copy.start()
        else:
            for copy, later in zip(self.stages[stage], self.passed[stage]):
                if later:
                    copy.start()

    def wait(self, stage):
        for copy in self.stages[stage]:
            copy.wait_recv()

    def finish(self):
        for stage in self.stages:
            for copy in stage:
                copy.wait_send()


def turn(values, cosine, sinus):
    lane = lax.broadcasted_iota(jnp.int32, values.shape, 1)
    first = lax.rem(lane, HEAD_DIM) < HEAD_DIM // 2
    swapped = jnp.where(
        first,
        pltpu.roll(values, 128 - HEAD_DIM // 2, 1),
        pltpu.roll(values, HEAD_DIM // 2, 1),
    )
    return values * cosine + swapped * sinus


def two_parts(values):
    high = values.astype(jnp.bfloat16)
    low = (values - high.astype(jnp.float32)).astype(jnp.bfloat16)
    return jnp.concatenate([high, low], axis=1)


def normed(values, gain):
    scale = lax.rsqrt(jnp.mean(values * values, axis=-1, keepdims=True) + epsilon)
    return (values * scale * gain).astype(jnp.bfloat16)


def fill_bias(bias, hot_rows, reach_t, key_start, query_start):
    seen = nn_dot(hot_rows, reach_t)
    keys = key_start + lax.broadcasted_iota(jnp.int32, seen.shape, 0)
    queries = query_start + lax.broadcasted_iota(jnp.int32, seen.shape, 1)
    bias[...] = jnp.where((seen > 0.5) & (keys <= queries), 0.0, masked_score)


def head_half(shape, axis, odd):
    index = lax.broadcasted_iota(jnp.int32, shape, axis)
    return (index >= HEAD_DIM) if odd else (index < HEAD_DIM)


def tree_tables(parents, lengths, turns, context, rows, hot, reach_t, cosine, sinus):
    lane = lax.broadcasted_iota(jnp.int32, (1, 128), 1)
    far = jnp.full((1, 128), 1 << 30, jnp.int32)
    none = jnp.zeros((1, 128), jnp.int32)
    begins, ends, moves = far, far, none
    first, second = none - 1, none - 1
    start = jnp.int32(0)
    for s in range(parents.shape[1]):
        parent = parents[0, s]
        grand = parents[0, parent]
        here = lane == s
        above = jnp.where(parent != s, lengths[0, parent], 0) + jnp.where(
            (grand != s) & (grand != parent), lengths[0, grand], 0
        )
        begins = jnp.where(here, start, begins)
        moves = jnp.where(here, above - start, moves)
        first = jnp.where(here, parent, first)
        second = jnp.where(here, grand, second)
        start = start + lengths[0, s]
        ends = jnp.where(here, start, ends)
    over = lax.broadcasted_iota(jnp.int32, (128, 128), 0)
    under = lax.broadcasted_iota(jnp.int32, (128, 128), 1)
    ancestors = jnp.where((over == under) | (over == first) | (over == second), 1.0, 0.0).astype(
        jnp.bfloat16
    )

    def fill(chunk, carry):
        block = pl.ds(pl.multiple_of(chunk * rows, 16), rows)
        row = chunk * rows + lax.broadcasted_iota(jnp.int32, (rows, 128), 0)
        inside = (row >= begins) & (row < ends)
        hot[block, :] = jnp.where(inside, 1.0, 0.0).astype(jnp.bfloat16)
        moved = jnp.sum(jnp.where(inside, moves.astype(jnp.float32), 0.0), axis=1, keepdims=True)
        angle = (row.astype(jnp.float32) + moved) * turns[0:1, :]
        cosine[block, :] = jnp.cos(angle)
        sinus[block, :] = jnp.sin(angle) * turns[1:2, :]
        return carry

    lax.fori_loop(0, context + 1, fill, 0)
    own = pl.ds(pl.multiple_of(context * rows, 16), rows)
    reach_t[...] = nt_dot(ancestors, hot[own, :]).astype(jnp.bfloat16)


def choose(f, wanted, adapters, out):
    count = out.shape[0]
    own = adapters.shape[0] // count
    total = jnp.zeros((count, 128), jnp.float32)
    for a in range(own):
        block = adapters[a * count : (a + 1) * count, :].astype(jnp.float32)
        total = total + jnp.where(wanted == (f * own + a).astype(jnp.float32), block, 0.0)
    out[...] = total.astype(jnp.bfloat16)


def route_tables(f, table_all, place_row, place_col, weight_col, marks):
    fsdp, _, rows = table_all.shape
    own = EXPERTS // fsdp
    f32 = jnp.float32
    sub = lax.broadcasted_iota(jnp.int32, (8, rows), 0)
    expert = jnp.where(sub < own, f * own + sub, -1).astype(f32)
    before = lax.broadcasted_iota(jnp.int32, (rows, rows), 0)
    after = lax.broadcasted_iota(jnp.int32, (rows, rows), 1)
    upto = jnp.where(before <= after, 1.0, 0.0).astype(jnp.bfloat16)
    lane = lax.broadcasted_iota(jnp.int32, (8, 128), 1)
    base = jnp.zeros((8, 1), f32)
    found = jnp.zeros((8, 128), f32)
    more = jnp.zeros((120, rows), f32)
    for source in range(fsdp):
        table = table_all[source]
        one = table[0:1, :] == expert
        two = table[1:2, :] == expert
        hit = one | two
        weight = jnp.where(one, table[2:3, :], 0.0) + jnp.where(two, table[3:4, :], 0.0)
        count = nn_dot(jnp.where(hit, 1.0, 0.0).astype(jnp.bfloat16), upto) + base
        place = jnp.where(hit, count - 1.0, -1.0)
        block = slice(source * rows, (source + 1) * rows)
        place_row[:, block] = place
        place_col[block, :] = jnp.concatenate([place, more], axis=0).T
        weight_col[block, :] = jnp.concatenate([weight, more], axis=0).T.astype(jnp.bfloat16)
        for token in range(TOKEN_TILE - 1, fsdp * rows, TOKEN_TILE):
            if token // rows == source:
                at = token % rows
                found = jnp.where(lane == token // TOKEN_TILE + 1, count[:, at : at + 1], found)
        base = count[:, rows - 1 : rows]
    marks[...] = found.astype(jnp.int32)


def unpack_adapter(t, per_block, chosen, flat, wide, first, second):
    a_qkv, b_qkv2, a_qkv_t2, a_o, b_o2, a_o_t2 = first
    a_gu, b_gu2, a_gu_t2, a_dn, a_dn_t2, b_dn2 = second
    f32, bf = jnp.float32, jnp.bfloat16
    contexts = chosen.shape[1]
    width, units = a_o.shape[0], a_dn.shape[0]
    count = PARAMS // 128 // (2 * contexts)
    for context in range(contexts):
        for part in range(2):
            start = (2 * context + part) * count
            flat[start : start + count, :] = chosen[part, context, 0:count, :].astype(f32)

    def spread(start, groups, rank, out, out_t):
        total = groups * 128 // rank
        wide[...] = jnp.zeros_like(wide)
        lines = rank // math.gcd(rank, 128)
        each = lines * 128 // rank
        for i in range(each):
            row, at = divmod(i * rank, 128)
            def line(number):
                if lines == 1:
                    return flat[pl.ds(start, groups), :]
                return flat[pl.ds(start + number, groups // lines, stride=lines), :]

            piece = line(row)[:, at : min(at + rank, 128)]
            if at + rank > 128:
                piece = jnp.concatenate([piece, line(row + 1)[:, 0 : at + rank - 128]], axis=1)
            wide[pl.ds(i, groups // lines, stride=each), 0:rank] = piece
        out[...] = wide[0:total, :].astype(bf)
        if out_t is not None:
            for p in range(total // 128):
                turned = wide[128 * p : 128 * p + 128, :].T.astype(bf)
                out_t[0:128, 128 * p : 128 * p + 128] = turned
                out_t[128:256, 128 * p : 128 * p + 128] = turned

    def stack(start, lines, columns, out, row, column):
        for p, m in enumerate(columns):
            piece = (2.0 * flat[pl.ds(start + m, RANK, stride=lines), :]).astype(bf)
            lanes = slice(column + 128 * p, column + 128 * p + 128)
            out[row : row + RANK, lanes] = piece
            out[128 + row : 128 + row + RANK, lanes] = piece

    for ref in (b_qkv2, b_o2, b_gu2, b_dn2):
        ref[...] = jnp.zeros_like(ref)
    at = 0
    spread(at, 3 * RANK * D // 128, 3 * RANK, a_qkv, a_qkv_t2)
    at = at + 3 * RANK * D // 128
    lines = D // 128
    mine = [t * (width // 128) + p for p in range(width // 128)]
    for j in range(3):
        stack(at + j * RANK * lines, lines, mine, b_qkv2, j * RANK, j * width)
    at = at + 3 * RANK * lines
    spread(at + t * (width * RANK // 128), width * RANK // 128, RANK, a_o, a_o_t2)
    at = at + D * RANK // 128
    stack(at, lines, list(range(lines)), b_o2, 0, 0)
    at = at + RANK * lines
    spread(at, 2 * RANK * D // 128, 2 * RANK, a_gu, a_gu_t2)
    at = at + 2 * RANK * D // 128
    wide_lines = FF // 128
    mine = [t * (units // 128) + p for p in range(units // 128)]
    for j in range(2):
        stack(at + j * RANK * wide_lines, wide_lines, mine, b_gu2, j * RANK, j * units)
    at = at + 2 * RANK * wide_lines
    spread(at + t * (units * RANK // 128), units * RANK // 128, RANK, a_dn, a_dn_t2)
    at = at + FF * RANK // 128
    stack(at, lines, list(range(lines)), b_dn2, 0, 0)


def forward_kernel(
    sizes,
    x_in,
    g_in,
    wq_in,
    wo_in,
    gu_in,
    dn_in,
    adapters_in,
    gains_in,
    table_in,
    turns,
    parents,
    lengths,
    n1_all,
    k_all,
    v_all,
    wq_all,
    wo_all,
    n2_all,
    g_all,
    p_all,
    q_t_out,
    q_n_out,
    mixed_out,
    o_t_out,
    lse_out,
    resid_out,
    shared_out,
    dn2_out,
    da_gu,
    db_gu,
    da_dn,
    db_dn,
    gains_out,
    cosine_out,
    sinus_out,
    hot_out,
    reach_t_out,
    a_qkv_out,
    b_qkv2_out,
    a_qkv_t2_out,
    a_o_out,
    b_o2_out,
    a_o_t2_out,
    table_all_out,
    place_row_out,
    place_col_out,
    weight_col_out,
    marks,
    peaks,
    x_buf,
    wq,
    wo,
    gu,
    dn,
    g_own,
    n1_buf,
    k_buf,
    v_buf,
    v_t,
    peak,
    total,
    bias,
    part_out,
    part_in,
    n2_own,
    shared,
    dn2,
    adapters_all,
    picked,
    gains_all,
    chosen,
    flat,
    a_wide,
    a_gu,
    b_gu2,
    a_gu_t2,
    a_dn,
    a_dn_t2,
    b_dn2,
    fs_send,
    fs_recv,
    z_send,
    z_recv,
    core_send,
    core_recv,
    local_sems,
    chunk_sems,
    small_send,
    small_recv,
    lend_send,
    lend_recv,
    q_t,
    q_n,
    mixed,
    o_t,
    lse,
    resid,
    gains,
    cosine,
    sinus,
    hot,
    reach_t,
    a_qkv,
    b_qkv2,
    a_qkv_t2,
    a_o,
    b_o2,
    a_o_t2,
    table_all,
    place_row,
    place_col,
    weight_col,
    out_sems,
    p_buf,
    p_sems,
):
    fsdp, contexts, _ = sizes
    bits = fsdp.bit_length() - 1
    f, c, t = place_of()
    rows = x_in.shape[0]
    half = rows // 2
    heads = q_t.shape[0] // HEAD_DIM
    width = q_t.shape[0]
    units = dn_in.shape[1]
    own_n = wq_in.shape[0]
    sibling = (f, c, 1 - t)

    def peer(index):
        return (index, c, t)

    peers = [(lax.rem(f + k, fsdp), c, t) for k in range(1, fsdp)]
    stacked = [(f, lax.rem(c + k, contexts), t) for k in range(1, contexts)]
    greet(peers + stacked + [sibling])

    targets = (
        (q_t, q_t_out),
        (q_n, q_n_out),
        (mixed, mixed_out),
        (o_t, o_t_out),
        (lse, lse_out),
        (resid, resid_out),
        (shared, shared_out),
        (dn2, dn2_out),
        (gains, gains_out),
        (cosine, cosine_out),
        (sinus, sinus_out),
        (hot, hot_out),
        (reach_t, reach_t_out),
        (a_qkv, a_qkv_out),
        (b_qkv2, b_qkv2_out),
        (a_qkv_t2, a_qkv_t2_out),
        (a_o, a_o_out),
        (b_o2, b_o2_out),
        (a_o_t2, a_o_t2_out),
        (table_all, table_all_out),
        (place_row, place_row_out),
        (place_col, place_col_out),
        (weight_col, weight_col_out),
    )
    given = []

    def give_out(refs):
        for i, (ref, target) in enumerate(targets):
            if any(ref is other for other in refs):
                copy = pltpu.make_async_copy(ref, target, out_sems.at[i])
                copy.start()
                given.append(copy)

    def half_rows(chunk, part):
        return pl.ds(pl.multiple_of(chunk * rows + part * half, 16), half)

    def up(chunk, source):
        return send(
            source,
            x_buf.at[half_rows(chunk, t)],
            z_send.at[chunk],
            z_recv.at[chunk],
            (f, c + 1, t),
        )

    def across(chunk):
        block = x_buf.at[half_rows(chunk, t)]
        return send(block, block, core_send.at[chunk], core_recv.at[chunk], sibling)

    @pl.when(c < contexts - 1)
    def _():
        up(c, x_in.at[half_rows(0, t)]).start()

    gathers = []
    halved = (False, False, True, False)
    neighbour = (f, c + 1 - 2 * lax.rem(c, 2), t)
    own_half = own_n // 2
    for i, (own, buf) in enumerate(((wq_in, wq), (wo_in, wo), (gu_in, gu), (dn_in, dn))):
        base, count = (lax.rem(c, 2) * own_half, own_half) if halved[i] else (0, own_n)
        gathers.append(
            Gather(bits, f, peer, own, buf, own_n, base, count, fs_send.at[i], fs_recv.at[i])
        )

    def lent(gather, buf, which):
        copies, number = [], 0
        for stage in range(bits):
            group = []
            for block in gather.arrived[stage]:
                group.append(
                    send(
                        buf.at[block],
                        buf.at[block],
                        lend_send.at[which, number],
                        lend_recv.at[which, number],
                        neighbour,
                    )
                )
                number = number + 1
            copies.append(group)
        return copies

    gu_lent = lent(gathers[2], gu, 0)

    z_busy = (lax.rem(c, 2) == 0) & (c > 0)

    def lend(copies, stage):
        for copy in copies[stage]:
            copy.start()
    g_gather = Gather(
        bits, f, peer, g_in, g_all, rows, t * half, half, fs_send.at[4], fs_recv.at[4]
    )
    n2_gather = Gather(
        bits, f, peer, n2_own, n2_all, rows, t * half, half, fs_send.at[5], fs_recv.at[5]
    )
    wq_gather, wo_gather, gu_gather, dn_gather = gathers
    small, rows_sent = [], []
    for k, other in enumerate(peers):
        for j, (source, target) in enumerate(((table_in, table_all), (gains_in, gains_all))):
            copy = send(source, target.at[f], small_send.at[j, k], small_recv.at[j, k], other)
            copy.start()
            small.append(copy)
    wq_gather.start(0)
    locals_ = [pltpu.make_async_copy(x_in, x_buf.at[pl.ds(c * rows, rows)], local_sems.at[0])]
    for i, (own, buf) in enumerate(((wq_in, wq), (wo_in, wo), (gu_in, gu), (dn_in, dn))):
        locals_.append(
            pltpu.make_async_copy(own, buf.at[pl.ds(f * own_n, own_n)], local_sems.at[1 + i])
        )
    locals_.append(pltpu.make_async_copy(g_in, g_own, local_sems.at[5]))
    locals_.append(
        pltpu.make_async_copy(g_in, g_all.at[pl.ds(f * rows, rows)], local_sems.at[6])
    )
    for copy in locals_:
        copy.start()

    o_t[...] = jnp.zeros_like(o_t)
    peak[...] = jnp.full_like(peak, masked_score)
    total[...] = jnp.zeros_like(total)
    da_gu[...] = jnp.zeros_like(da_gu)
    db_gu[...] = jnp.zeros_like(db_gu)
    da_dn[...] = jnp.zeros_like(da_dn)
    db_dn[...] = jnp.zeros_like(db_dn)
    gains_all[f] = gains_in[...]
    table_all[f] = table_in[...]
    for copy in small:
        copy.wait_recv()
    for k, other in enumerate(peers):
        choose(f, table_all[lax.rem(f + k + 1, fsdp), 4:5, 0:1], adapters_in, picked.at[k])
        copy = send(
            picked.at[k], adapters_all.at[f], small_send.at[2, k], small_recv.at[2, k], other
        )
        copy.start()
        rows_sent.append(copy)
    choose(f, table_all[f, 4:5, 0:1], adapters_in, adapters_all.at[f])
    tree_tables(parents, lengths, turns, c, rows, hot, reach_t, cosine, sinus)

    def receive(step):
        chunk = c - step

        @pl.when(step <= c)
        def _():
            up(chunk, x_buf.at[half_rows(chunk, t)]).wait_recv()

            @pl.when(c < contexts - 1)
            def _():
                up(chunk, x_buf.at[half_rows(chunk, t)]).start()

            across(chunk).start()

    def chunk_rows(chunk):
        return pl.ds(pl.multiple_of(chunk * rows, 16), rows)

    def out_copies(chunk):
        block = chunk_rows(chunk)
        return [
            pltpu.make_async_copy(n1_buf.at[block], n1_all.at[block], chunk_sems.at[0, chunk]),
            pltpu.make_async_copy(k_buf.at[block], k_all.at[block], chunk_sems.at[1, chunk]),
            pltpu.make_async_copy(v_buf.at[block], v_all.at[block], chunk_sems.at[2, chunk]),
        ]

    def project(chunk, own):
        block = chunk_rows(chunk)
        n1 = normed(x_buf[block, :].astype(jnp.float32), gain_one)
        n1_buf[block, :] = n1
        rank = two_parts(nn_dot(n1, a_qkv[...]))
        cos_rows = cosine[block, :]
        sin_rows = sinus[block, :]
        start = 0 if own else width
        result = nn_dot(n1, wq[:, start:]) + nn_dot(rank, b_qkv2[:, start:])
        for p in range(width // 128):
            lanes = slice(128 * p, 128 * p + 128)
            cols = slice(width - start + 128 * p, width - start + 128 * p + 128)
            k_buf[block, lanes] = turn(result[:, cols], cos_rows, sin_rows).astype(jnp.bfloat16)
            cols = slice(2 * width - start + 128 * p, 2 * width - start + 128 * p + 128)
            value = result[:, cols]
            v_buf[block, lanes] = value.astype(jnp.bfloat16)
            v_t[lanes, :] = value.T.astype(jnp.bfloat16)
            if own:
                query = turn(result[:, lanes], cos_rows, sin_rows) * 0.125
                q_n[:, lanes] = query.astype(jnp.bfloat16)
                q_t[lanes, :] = query.T.astype(jnp.bfloat16)
        for copy in out_copies(chunk):
            copy.start()

    def weights_out(chunk, p):
        target = p_all.at[pl.ds(chunk * heads + 2 * p, 2)]
        return pltpu.make_async_copy(p_buf.at[pl.ds(2 * p, 2)], target, p_sems.at[p])

    def attend(chunk, first):
        block = chunk_rows(chunk)
        fill_bias(bias, hot[block, :], reach_t[...], chunk * rows, c * rows)

        def pair_step(p, carry):
            lanes = pl.ds(pl.multiple_of(p * 128, 128), 128)
            keys = k_buf[block, lanes]
            query = q_t[lanes, :]
            if not first:
                weights_out(chunk, p).wait()
            for odd in range(2):
                h = 2 * p + odd
                alone = jnp.where(
                    head_half(query.shape, 0, odd), query, jnp.zeros_like(query)
                )
                scores = nn_dot(keys, alone) + bias[...]
                before = peak[pl.ds(h, 1), :]
                now = jnp.maximum(before, jnp.max(scores, axis=0, keepdims=True))
                weights = jnp.exp(scores - now)
                shrink = jnp.exp(before - now)
                peak[pl.ds(h, 1), :] = now
                peaks[pl.ds(chunk * 8 + h, 1), :] = now
                low_weights = weights.astype(jnp.bfloat16)
                p_buf[h] = low_weights
                total[pl.ds(h, 1), :] = total[pl.ds(h, 1), :] * shrink + jnp.sum(
                    weights, axis=0, keepdims=True
                )
                head = pl.ds(pl.multiple_of(h * HEAD_DIM, HEAD_DIM), HEAD_DIM)
                o_t[head, :] = o_t[head, :] * shrink + nn_dot(
                    v_t[head, :], low_weights
                )
            weights_out(chunk, p).start()
            return carry

        lax.fori_loop(0, heads // 2, pair_step, 0)

    def advance(gather, following, copies=None):
        gather.wait(0)
        for stage in range(1, bits):
            gather.start(stage)
            if copies is not None:
                lend(copies, stage - 1)
            if stage < bits - 1:
                gather.wait(stage)
        following.start(0)

    for copy in rows_sent:
        copy.wait_recv()
    total_row = adapters_all[0].astype(jnp.float32)
    for b in range(1, fsdp):
        total_row = total_row + adapters_all[b].astype(jnp.float32)
    chosen[t, c] = total_row.astype(jnp.bfloat16)
    spread = []
    for k, other in enumerate(stacked):
        block = chosen.at[t, c]
        copy = send(block, block, small_send.at[3, k], small_recv.at[3, k], other)
        copy.start()
        spread.append(copy)
    gains[...] = jnp.zeros_like(gains)
    for i in range(2):
        pieces = [
            gains_all[b, 0:1, i * own_n : (i + 1) * own_n].astype(jnp.float32)
            for b in range(fsdp)
        ]
        gains[i : i + 1, :] = jnp.concatenate(pieces, axis=1)
    gain_one = gains[0:1, :]
    gain_two = gains[1:2, :]
    advance(wq_gather, wo_gather)
    receive(1)
    for copy in spread:
        copy.wait_recv()
    shared_copy = send(
        chosen.at[t], chosen.at[t], small_send.at[4, 0], small_recv.at[4, 0], sibling
    )
    shared_copy.start()
    route_tables(f, table_all, place_row, place_col, weight_col, marks)
    give_out(
        (table_all, place_row, place_col, weight_col, gains, cosine, sinus, hot, reach_t)
    )
    advance(wo_gather, gu_gather)
    shared_copy.wait_recv()
    unpack_adapter(
        t,
        adapters_in.shape[0] // (ADAPTERS // fsdp),
        chosen,
        flat,
        a_wide,
        (a_qkv, b_qkv2, a_qkv_t2, a_o, b_o2, a_o_t2),
        (a_gu, b_gu2, a_gu_t2, a_dn, a_dn_t2, b_dn2),
    )
    give_out((a_qkv, b_qkv2, a_qkv_t2, a_o, b_o2, a_o_t2))
    wq_gather.wait(bits - 1)
    locals_[0].wait()
    locals_[1].wait()
    wq_out = pltpu.make_async_copy(wq, wq_all, local_sems.at[10])
    wq_out.start()
    project(c, True)
    receive(2)
    attend(c, True)

    number = contexts

    def forwards(gather, buf, first):
        copies = []
        for stage in range(bits):
            group = []
            for block in gather.arrived[stage]:
                index = first + len(copies)
                copies.append(
                    send(
                        buf.at[block],
                        buf.at[block],
                        core_send.at[index],
                        core_recv.at[index],
                        sibling,
                    )
                )
        return copies

    per_stage = [len(stage) for stage in g_gather.arrived]
    g_forward = forwards(g_gather, g_all, number + 5)
    n2_forward = forwards(n2_gather, n2_all, number + 5 + sum(per_stage))

    def pass_on(copies, stage):
        start = sum(per_stage[:stage])
        for copy in copies[start : start + per_stage[stage]]:
            copy.start()

    def between(step):
        if step == 1:
            advance(gu_gather, dn_gather)

            @pl.when(jnp.logical_not(z_busy))
            def _():
                lend(gu_lent, 0)

        if step == 2:
            advance(dn_gather, g_gather)
            gu_gather.wait(bits - 1)

            @pl.when(z_busy)
            def _():
                lend(gu_lent, 0)

            for stage in range(1, bits):
                lend(gu_lent, stage)
        if step == 3:
            g_gather.wait(0)
            for stage in range(1, bits):
                g_gather.start(stage)
                pass_on(g_forward, stage - 1)
                if stage < bits - 1:
                    g_gather.wait(stage)

    def later(step):
        chunk = c - step

        @pl.when(step <= c)
        def _():
            across(chunk).wait_recv()
            project(chunk, False)
            receive(step + 2)
            attend(chunk, False)

    for step in range(1, 3):
        between(step)
        later(step)

    @pl.when(c >= 3)
    def _():
        between(3)
        later(3)

    def rest(step, carry):
        later(step)
        return carry

    lax.fori_loop(4, contexts, rest, 0)

    for h in range(heads):
        head = slice(h * HEAD_DIM, h * HEAD_DIM + HEAD_DIM)
        o_t[head, :] = o_t[head, :] / total[h : h + 1, :]
    lse[...] = peak[...] + jnp.log(total[...])
    for p in range(width // 128):
        mixed[:, 128 * p : 128 * p + 128] = o_t[128 * p : 128 * p + 128, :].T.astype(jnp.bfloat16)
    give_out((q_t, q_n, mixed, o_t, lse))
    wo_gather.wait(bits - 1)
    locals_[2].wait()
    wo_out = pltpu.make_async_copy(wo, wo_all, local_sems.at[11])
    wo_out.start()

    def local_rows(part):
        return pl.ds(pl.multiple_of(part * half, 16), half)

    mine = local_rows(t)
    theirs = local_rows(1 - t)

    def branch(block):
        values = mixed[block, :]
        rank = two_parts(nn_dot(values, a_o[...]))
        return nt_dot(values, wo[...]) + nn_dot(rank, b_o2[...])

    part_copies = []
    for i, block in enumerate((theirs, mine)):
        part_out[block, :] = branch(block).astype(jnp.bfloat16)
        copy = send(
            part_out.at[block],
            part_in.at[block],
            core_send.at[number + i],
            core_recv.at[number + i],
            sibling,
        )
        copy.start()
        part_copies.append(copy)

    def attended(block, copy):
        copy.wait_recv()
        resid[block, :] = x_rows(x_buf, c, rows, block) + (
            part_out[block, :].astype(jnp.float32) + part_in[block, :].astype(jnp.float32)
        )
        n2_own[block, :] = normed(resid[block, :], gain_two)

    attended(mine, part_copies[0])
    n2_gather.start(0)
    attended(theirs, part_copies[1])
    give_out((resid,))
    n2_out = pltpu.make_async_copy(n2_own, n2_all.at[pl.ds(f * rows, rows)], local_sems.at[12])
    n2_out.start()

    @pl.when(c < 3)
    def _():
        between(3)


    locals_[5].wait()
    for group in gu_lent:
        for copy in group:
            copy.wait_recv()
    locals_[3].wait()
    dn_gather.wait(bits - 1)
    locals_[4].wait()

    def shared_tile(block):
        inputs = n2_own[block, :]
        grads = g_own[block, :]
        rank = nn_dot(inputs, a_gu[...])
        rank2 = two_parts(rank)
        gate = nn_dot(inputs, gu[:, :units]) + nn_dot(rank2, b_gu2[:, :units])
        up_pre = nn_dot(inputs, gu[:, units:]) + nn_dot(rank2, b_gu2[:, units:])
        sigmoid_gate = jax.nn.sigmoid(gate)
        silu = gate * sigmoid_gate
        hidden = (silu * up_pre).astype(jnp.bfloat16)
        down_rank = nn_dot(hidden, a_dn[...])
        shared[block, :] = (
            nt_dot(hidden, dn[...]) + nn_dot(two_parts(down_rank), b_dn2[...])
        ).astype(jnp.bfloat16)
        down_back = nt_dot(grads, b_dn2[0:128, :])
        grad_hidden = nn_dot(grads, dn[...]) + nn_dot(two_parts(down_back), a_dn_t2[...])
        grad_gate = (
            grad_hidden * up_pre * sigmoid_gate * (1.0 + gate * (1.0 - sigmoid_gate))
        ).astype(jnp.bfloat16)
        grad_up = (grad_hidden * silu).astype(jnp.bfloat16)
        rank_back = nt_dot(grad_gate, b_gu2[0:128, :units]) + nt_dot(
            grad_up, b_gu2[0:128, units:]
        )
        dn2[block, :] = (
            nt_dot(grad_gate, gu[:, :units])
            + nt_dot(grad_up, gu[:, units:])
            + nn_dot(two_parts(rank_back), a_gu_t2[...])
        ).astype(jnp.bfloat16)
        rank_low = rank.astype(jnp.bfloat16)
        da_gu[...] += tn_dot(rank_back.astype(jnp.bfloat16), inputs)[0 : 2 * RANK]
        db_gu[0:RANK, :] += 2.0 * tn_dot(rank_low, grad_gate)[0:RANK]
        db_gu[RANK:, :] += 2.0 * tn_dot(rank_low, grad_up)[RANK : 2 * RANK]
        da_dn[...] += tn_dot(down_back.astype(jnp.bfloat16), hidden)[0:RANK]
        db_dn[...] += 2.0 * tn_dot(down_rank.astype(jnp.bfloat16), grads)[0:RANK]

    def pass_pieces(gather, copies, stage):
        start = sum(per_stage[:stage])
        for i, copy in enumerate(gather.stages[stage]):
            copy.wait_recv()
            copies[start + i].start()

    shared_tile(mine)
    n2_gather.wait(0)
    for stage in range(1, bits):
        n2_gather.start(stage)
        pass_on(n2_forward, stage - 1)
        if stage < bits - 1:
            n2_gather.wait(stage)
    shared_tile(theirs)
    give_out((shared, dn2))
    pass_pieces(g_gather, g_forward, bits - 1)
    pass_pieces(n2_gather, n2_forward, bits - 1)
    for copy in n2_forward + g_forward:
        copy.wait()
    for copy in small + rows_sent + spread + [shared_copy]:
        copy.wait_send()
    for group in gu_lent:
        for copy in group:
            copy.wait_send()
    for copy in given:
        copy.wait()
    for copy in part_copies:
        copy.wait_send()
    for gather in gathers + [g_gather, n2_gather]:
        gather.finish()
    n2_out.wait()
    wq_out.wait()
    wo_out.wait()
    locals_[6].wait()

    @pl.when(c < contexts - 1)
    def _():
        up(c, x_in.at[half_rows(0, t)]).wait_send()

    def drain(step, carry):
        chunk = c - step

        @pl.when(c < contexts - 1)
        def _():
            up(chunk, x_buf.at[half_rows(chunk, t)]).wait_send()

        across(chunk).wait_send()
        return carry

    lax.fori_loop(1, c + 1, drain, 0)

    def drain_out(step, carry):
        for copy in out_copies(c - step):
            copy.wait()
        return carry

    lax.fori_loop(0, c + 1, drain_out, 0)
    for p in range(heads // 2):
        weights_out(0, p).wait()


def x_rows(x_buf, chunk, rows, block):
    return x_buf[pl.ds(pl.multiple_of(chunk * rows, 16) + block.start, block.size), :].astype(
        jnp.float32
    )


def forward_call(sizes, sharded, local):
    fsdp, contexts, _ = sizes
    x, g, wq, wo, gu, dn = sharded
    adapters, gains, table = local[:3]
    rows = x.shape[0]
    tree = rows * contexts
    width = wo.shape[1]
    units = dn.shape[1]
    bf, f32 = jnp.bfloat16, jnp.float32
    vmem = pl.BlockSpec(memory_space=pltpu.VMEM)
    hbm = pl.BlockSpec(memory_space=pl.ANY)
    smem = pl.BlockSpec(memory_space=pltpu.SMEM)
    slots = max(fsdp, contexts)
    total = fsdp * rows
    per_adapter = adapters.shape[0] // (ADAPTERS // fsdp)

    def shape(kind, *dims):
        return jax.ShapeDtypeStruct(dims, kind)

    moves = 2 * (fsdp - 1)
    hops = contexts + 5 + 2 * moves
    return pl.pallas_call(
        functools.partial(forward_kernel, sizes),
        in_specs=[hbm] * 6 + [vmem] * 4 + [smem] * 2,
        out_specs=[hbm] * 8 + [hbm, hbm, hbm, hbm, hbm, hbm, hbm, hbm, vmem, vmem, vmem, vmem, hbm, hbm, hbm, hbm, hbm, hbm, hbm, hbm, hbm, hbm, hbm, hbm, hbm, hbm, hbm, vmem, vmem],
        out_shape=[
            shape(bf, tree, D),
            shape(bf, tree, width),
            shape(bf, tree, width),
            shape(bf, D, 3 * width),
            shape(bf, D, width),
            shape(bf, fsdp * rows, D),
            shape(bf, fsdp * rows, D),
            shape(bf, contexts * (width // HEAD_DIM), rows, rows),
            shape(bf, width, rows),
            shape(bf, rows, width),
            shape(bf, rows, width),
            shape(f32, width, rows),
            shape(f32, 8, rows),
            shape(f32, rows, D),
            shape(bf, rows, D),
            shape(bf, rows, D),
            shape(f32, 2 * RANK, D),
            shape(f32, 2 * RANK, units),
            shape(f32, RANK, units),
            shape(f32, RANK, D),
            shape(f32, 8, D),
            shape(f32, tree, 128),
            shape(f32, tree, 128),
            shape(bf, tree, 128),
            shape(bf, 128, rows),
            shape(bf, D, 128),
            shape(bf, 256, 3 * width),
            shape(bf, 256, D),
            shape(bf, width, 128),
            shape(bf, 256, D),
            shape(bf, 256, width),
            shape(f32, fsdp, 8, rows),
            shape(f32, 8, total),
            shape(f32, total, 128),
            shape(bf, total, 128),
            shape(jnp.int32, 8, 128),
            shape(f32, contexts * 8, rows),
        ],
        scratch_shapes=[
            pltpu.VMEM((tree, D), bf),
            pltpu.VMEM((D, 3 * width), bf),
            pltpu.VMEM((D, width), bf),
            pltpu.VMEM((D, 2 * units), bf),
            pltpu.VMEM((D, units), bf),
            pltpu.VMEM((rows, D), bf),
            pltpu.VMEM((tree, D), bf),
            pltpu.VMEM((tree, width), bf),
            pltpu.VMEM((tree, width), bf),
            pltpu.VMEM((width, rows), bf),
            pltpu.VMEM((8, rows), f32),
            pltpu.VMEM((8, rows), f32),
            pltpu.VMEM((rows, rows), f32),
            pltpu.VMEM((rows, D), bf),
            pltpu.VMEM((rows, D), bf),
            pltpu.VMEM((rows, D), bf),
            pltpu.VMEM((rows, D), bf),
            pltpu.VMEM((rows, D), bf),
            pltpu.VMEM((fsdp, per_adapter, 128), bf),
            pltpu.VMEM((fsdp - 1, per_adapter, 128), bf),
            pltpu.VMEM((fsdp,) + gains.shape, bf),
            pltpu.VMEM((2, contexts, per_adapter, 128), bf),
            pltpu.VMEM((PARAMS // 128, 128), f32),
            pltpu.VMEM((max(D, units), 128), f32),
            pltpu.VMEM((D, 128), bf),
            pltpu.VMEM((256, 2 * units), bf),
            pltpu.VMEM((256, D), bf),
            pltpu.VMEM((units, 128), bf),
            pltpu.VMEM((256, units), bf),
            pltpu.VMEM((256, D), bf),
            pltpu.SemaphoreType.DMA((6, moves)),
            pltpu.SemaphoreType.DMA((6, moves)),
            pltpu.SemaphoreType.DMA((contexts,)),
            pltpu.SemaphoreType.DMA((contexts,)),
            pltpu.SemaphoreType.DMA((hops,)),
            pltpu.SemaphoreType.DMA((hops,)),
            pltpu.SemaphoreType.DMA((13,)),
            pltpu.SemaphoreType.DMA((3, contexts)),
            pltpu.SemaphoreType.DMA((5, slots)),
            pltpu.SemaphoreType.DMA((5, slots)),
            pltpu.SemaphoreType.DMA((2, moves)),
            pltpu.SemaphoreType.DMA((2, moves)),
            pltpu.VMEM((width, rows), bf),
            pltpu.VMEM((rows, width), bf),
            pltpu.VMEM((rows, width), bf),
            pltpu.VMEM((width, rows), f32),
            pltpu.VMEM((8, rows), f32),
            pltpu.VMEM((rows, D), f32),
            pltpu.VMEM((8, D), f32),
            pltpu.VMEM((tree, 128), f32),
            pltpu.VMEM((tree, 128), f32),
            pltpu.VMEM((tree, 128), bf),
            pltpu.VMEM((128, rows), bf),
            pltpu.VMEM((D, 128), bf),
            pltpu.VMEM((256, 3 * width), bf),
            pltpu.VMEM((256, D), bf),
            pltpu.VMEM((width, 128), bf),
            pltpu.VMEM((256, D), bf),
            pltpu.VMEM((256, width), bf),
            pltpu.VMEM((fsdp, 8, rows), f32),
            pltpu.VMEM((8, total), f32),
            pltpu.VMEM((total, 128), f32),
            pltpu.VMEM((total, 128), bf),
            pltpu.SemaphoreType.DMA((23,)),
            pltpu.VMEM((width // HEAD_DIM, rows, rows), bf),
            pltpu.SemaphoreType.DMA((width // HEAD_DIM // 2,)),
        ],
        name="forward",
        compiler_params=pltpu.CompilerParams(
            collective_id=2, has_side_effects=True, vmem_limit_bytes=62 << 20
        ),
    )(*sharded, *local)


def flips(index, mask, bits):
    for bit in range(bits):
        if mask >> bit & 1:
            index = flip(index, bit)
    return index


class Scatter:
    def __init__(self, bits, me, device_of, work, inbox, count, send_sems, recv_sems):
        self.bits, self.work, self.inbox = bits, work, inbox
        self.copies = [[] for _ in range(bits)]
        self.masks = [[] for _ in range(bits)]
        self.adds = [[] for _ in range(bits)]
        number = 0
        for half, (offset, size) in enumerate(split_rows(count)):
            alive = list(range(1 << bits))
            slot = 0
            for stage in range(bits):
                bit = (stage + half) % bits
                for mask in alive:
                    if mask >> bit & 1:
                        source = Gather.rows(flips(me, mask, bits) * count + offset, size)
                        target = pl.ds(slot * count + offset, size)
                        kept = Gather.rows(flips(me, mask ^ (1 << bit), bits) * count + offset, size)
                        self.copies[stage].append(
                            send(
                                work.at[source],
                                inbox.at[target],
                                send_sems.at[number],
                                recv_sems.at[number],
                                device_of(flip(me, bit)),
                            )
                        )
                        self.adds[stage].append((kept, target, pl.ds(offset, size)))
                        self.masks[stage].append(mask)
                        number = number + 1
                        slot = slot + 1
                alive = [mask for mask in alive if not mask >> bit & 1]

    def start(self, stage):
        for copy in self.copies[stage]:
            copy.start()

    def start_mask(self, mask):
        for copy, number in zip(self.copies[0], self.masks[0]):
            if number == mask:
                copy.start()

    def add(self, stage):
        for copy in self.copies[stage]:
            copy.wait_recv()
        for kept, target, _ in self.adds[stage]:
            total = self.work[kept, :].astype(jnp.float32) + self.inbox[target, :].astype(
                jnp.float32
            )
            self.work[kept, :] = total.astype(jnp.bfloat16)

    def last(self, out):
        for copy in self.copies[self.bits - 1]:
            copy.wait_recv()
        for kept, target, rows in self.adds[self.bits - 1]:
            total = self.work[kept, :].astype(jnp.float32) + self.inbox[target, :].astype(
                jnp.float32
            )
            out[rows, :] = total.astype(jnp.bfloat16)

    def finish(self):
        for stage in self.copies:
            for copy in stage:
                copy.wait_send()


def pack_rows(grad_t, start, rank, flat, wide):
    total = grad_t.shape[1]
    more = jnp.zeros((128 - rank, 128), jnp.float32)
    for p in range(total // 128):
        piece = grad_t[:, 128 * p : 128 * p + 128]
        wide[128 * p : 128 * p + 128, :] = jnp.concatenate([piece, more], axis=0).T
    lines = rank // math.gcd(rank, 128)
    each = lines * 128 // rank
    count = total // each
    joined = jnp.concatenate(
        [wide[pl.ds(i, count, stride=each), :][:, 0:rank] for i in range(each)], axis=1
    )
    if lines == 1:
        flat[pl.ds(start, count), :] = joined
    else:
        for i in range(lines):
            flat[pl.ds(start + i, count, stride=lines), :] = joined[:, 128 * i : 128 * i + 128]


def pack_lines(grad, start, lines, columns, flat):
    for p, m in enumerate(columns):
        flat[pl.ds(start + m, grad.shape[0], stride=lines), :] = grad[:, 128 * p : 128 * p + 128]


def pack_first(t, flat, wide, da_qkv, db_qkv, da_o, db_o):
    width = da_o.shape[1]
    lines = D // 128
    mine = [t * (width // 128) + p for p in range(width // 128)]
    pack_rows(da_qkv[...], 0, 3 * RANK, flat, wide)
    at = 3 * RANK * D // 128
    for j in range(3):
        rows = slice(j * RANK, (j + 1) * RANK)
        pack_lines(db_qkv[rows, :], at + j * RANK * lines, lines, mine, flat)
    at = at + 3 * RANK * lines
    pack_rows(da_o[...], at + t * (width * RANK // 128), RANK, flat, wide)
    at = at + D * RANK // 128
    pack_lines(db_o[...], at, lines, list(range(lines)), flat)


def pack_second(t, flat, wide, da_gu, db_gu, da_dn, db_dn):
    units = da_dn.shape[1]
    lines = D // 128
    at = 8 * RANK * D // 128
    pack_rows(da_gu[...], at, 2 * RANK, flat, wide)
    at = at + 2 * RANK * D // 128
    wide_lines = FF // 128
    mine = [t * (units // 128) + p for p in range(units // 128)]
    for j in range(2):
        rows = slice(j * RANK, (j + 1) * RANK)
        pack_lines(db_gu[rows, :], at + j * RANK * wide_lines, wide_lines, mine, flat)
    at = at + 2 * RANK * wide_lines
    pack_rows(da_dn[...], at + t * (units * RANK // 128), RANK, flat, wide)
    at = at + FF * RANK // 128
    pack_lines(db_dn[...], at, lines, list(range(lines)), flat)


def backward_kernel(
    sizes,
    moe_out,
    moe_back,
    n1_hbm,
    k_hbm,
    v_hbm,
    wq_hbm,
    wo_hbm,
    cos_hbm,
    sin_hbm,
    p_hbm,
    x_in_hbm,
    g_in_hbm,
    gains,
    peaks,
    resid_hbm,
    shared_hbm,
    dn2_hbm,
    q_t_hbm,
    q_n_hbm,
    mixed_hbm,
    o_t_hbm,
    lse,
    a_qkv_hbm,
    b_qkv2_hbm,
    a_qkv_t2_hbm,
    a_o_hbm,
    a_o_t2_hbm,
    b_o2_hbm,
    da_gu,
    db_gu,
    da_dn,
    db_dn,
    table_all,
    ffn_out,
    input_grad,
    adapter_out,
    cosine,
    sinus,
    k_buf,
    v_buf,
    wq,
    wo,
    work_back,
    pair_back,
    inbox_back,
    work_out,
    pair_out,
    inbox_out,
    total_half,
    total_full,
    ffn_half,
    ffn_full,
    dy,
    do_n,
    do_t,
    delta,
    factor,
    k_t,
    dq_t,
    dq,
    part_in,
    z_in,
    dn1_full,
    fs_send,
    fs_recv,
    z_send,
    z_recv,
    core_send,
    core_recv,
    pair_send,
    pair_recv,
    local_sems,
    chunk_sems,
    x_in,
    g_in,
    resid,
    shared,
    dn2,
    q_t,
    q_n,
    mixed,
    o_t,
    a_qkv,
    b_qkv2,
    a_qkv_t2,
    a_o,
    a_o_t2,
    b_o2,
    da_qkv,
    db_qkv,
    da_o,
    db_o,
    flat,
    wide,
    packed,
    packed_in,
    up_out,
    up_in,
    own_sum,
    tree_sums,
    in_sems,
    sum_send,
    sum_recv,
    p_buf,
    p_sems,
    whole_back,
    whole_out,
):
    fsdp, contexts, _ = sizes
    bits = fsdp.bit_length() - 1
    f, c, t = place_of()
    rows = x_in.shape[0]
    half = rows // 2
    width = q_t.shape[0]
    inputs = []
    for i, (source, target) in enumerate(
        (
            (x_in_hbm, x_in),
            (g_in_hbm, g_in),
            (resid_hbm, resid),
            (shared_hbm, shared),
            (dn2_hbm, dn2),
            (q_t_hbm, q_t),
            (q_n_hbm, q_n),
            (mixed_hbm, mixed),
            (o_t_hbm, o_t),
            (a_qkv_hbm, a_qkv),
            (b_qkv2_hbm, b_qkv2),
            (a_qkv_t2_hbm, a_qkv_t2),
            (a_o_hbm, a_o),
            (a_o_t2_hbm, a_o_t2),
            (b_o2_hbm, b_o2),
        )
    ):
        inputs.append(pltpu.make_async_copy(source, target, in_sems.at[i]))
    heads = width // HEAD_DIM
    part_out, z_out, grad_kv = pair_back, work_back, inbox_back
    part, n1_buf = whole_back, whole_out
    kv_rows = pl.ds(0, rows)
    sibling = (f, c, 1 - t)
    f32, bf = jnp.float32, jnp.bfloat16

    def peer(index):
        return (index, c, t)

    def local_rows(part_index):
        return pl.ds(pl.multiple_of(part_index * half, 16), half)

    mine = local_rows(t)
    theirs = local_rows(1 - t)

    def block_rows(block, part_index):
        return pl.ds(pl.multiple_of(block * rows + part_index * half, 16), half)

    def work_rows(block):
        return pl.ds(pl.multiple_of(block * half, 16), half)

    masks = list(range(fsdp - 1, -1, -1))

    def exchange(source, work, inbox, which, whole):
        own, sent = [], []
        for mask in masks:
            block = flips(f, mask, bits)
            if mask == 0:
                own.append(
                    pltpu.make_async_copy(
                        source.at[pl.ds(pl.multiple_of(f * rows, 16), rows)],
                        whole,
                        local_sems.at[which, mask],
                    )
                )
                sent.append(
                    send(
                        whole.at[theirs],
                        inbox.at[work_rows(block)],
                        core_send.at[which, mask],
                        core_recv.at[which, mask],
                        sibling,
                    )
                )
                continue
            own.append(
                pltpu.make_async_copy(
                    source.at[block_rows(block, t)],
                    work.at[work_rows(block)],
                    local_sems.at[which, mask],
                )
            )
            sent.append(
                send(
                    source.at[block_rows(block, 1 - t)],
                    inbox.at[work_rows(block)],
                    core_send.at[which, mask],
                    core_recv.at[which, mask],
                    sibling,
                )
            )
        return own, sent

    back_own, back_sent = exchange(moe_back, work_back, pair_back, 0, whole_back)
    out_own, out_sent = exchange(moe_out, work_out, pair_out, 1, whole_out)
    for copy in back_own:
        copy.start()
    wo_copy = pltpu.make_async_copy(wo_hbm, wo, local_sems.at[2, 0])
    wq_copy = pltpu.make_async_copy(wq_hbm, wq, local_sems.at[2, 1])
    wo_copy.start()
    for copy in inputs:
        copy.start()
    peers = [(lax.rem(f + k, fsdp), c, t) for k in range(1, fsdp)]
    stacked = [(f, lax.rem(c + k, contexts), t) for k in range(1, contexts)]
    greet(peers + stacked + [sibling])
    for copy in back_sent[:-1]:
        copy.start()
    for copy in out_own:
        copy.start()
    wq_copy.start()

    lines = PARAMS // 128 // (2 * contexts)
    early = -(-(8 * RANK * D // 128) // (2 * lines))

    def fill_blocks(first, last):
        for context in range(first, last):
            for part_index in range(2):
                start = (2 * context + part_index) * lines
                packed[context, part_index, 0:lines, :] = flat[start : start + lines, :]

    def pair_block(block):
        return send(
            packed.at[block, 1 - t],
            packed_in.at[block],
            sum_send.at[0, block],
            sum_recv.at[0, block],
            sibling,
        )

    def to_owner(k):
        return send(
            up_out.at[k], up_in.at[k], sum_send.at[1, k], sum_recv.at[1, k], stacked[k]
        )

    def push_blocks(soon):
        for k in range(contexts - 1):
            owner = lax.rem(c + k + 1, contexts)

            @pl.when((owner >= early) if soon else (owner < early))
            def _(k=k, owner=owner):
                up_out[k] = (packed[owner, t] + packed_in[owner]).astype(bf)
                to_owner(k).start()

    def to_peer(k):
        return send(
            own_sum, tree_sums.at[k], sum_send.at[2, k], sum_recv.at[2, k], peers[k]
        )

    def sum_own():
        result = packed[c, t] + packed_in[c]
        for k in range(contexts - 1):
            to_owner(k).wait_recv()
            result = result + up_in[k].astype(f32)
        own_sum[...] = result.astype(bf)
        for k in range(fsdp - 1):
            to_peer(k).start()

    def chunk_rows(chunk):
        return pl.ds(pl.multiple_of(chunk * rows, 16), rows)

    def loads(chunk):
        block = chunk_rows(chunk)
        return [
            pltpu.make_async_copy(k_hbm.at[block], k_buf.at[block], chunk_sems.at[1, chunk]),
            pltpu.make_async_copy(v_hbm.at[block], v_buf.at[block], chunk_sems.at[2, chunk]),
        ]

    def n1_load(chunk):
        return pltpu.make_async_copy(
            n1_hbm.at[chunk_rows(chunk)], n1_buf, chunk_sems.at[0, chunk]
        )

    def table_loads(chunk):
        block = chunk_rows(chunk)
        return [
            pltpu.make_async_copy(cos_hbm.at[block], cosine, chunk_sems.at[3, chunk]),
            pltpu.make_async_copy(sin_hbm.at[block], sinus, chunk_sems.at[4, chunk]),
        ]

    def start_loads(chunk, carry):
        for copy in loads(chunk):
            copy.start()
        return carry

    lax.fori_loop(0, c + 1, start_loads, 0)

    def weights_in(chunk, p):
        source = p_hbm.at[pl.ds(chunk * heads + 2 * p, 2)]
        return pltpu.make_async_copy(source, p_buf.at[pl.ds(2 * p, 2)], p_sems.at[p])

    for p in range(heads // 2):
        weights_in(0, p).start()

    back = Scatter(
        bits, f, peer, work_back, inbox_back, half, fs_send.at[0], fs_recv.at[0]
    )
    out = Scatter(bits, f, peer, work_out, inbox_out, half, fs_send.at[1], fs_recv.at[1])

    def join(own, sent, whole, extra, work):
        own[-1].wait()
        whole[...] = (whole[...].astype(f32) + extra[...].astype(f32)).astype(bf)
        sent[-1].start()
        work[work_rows(f), :] = whole[mine, :]

    def pair_sum(own, sent, work, inbox, scatter):
        for i, mask in enumerate(masks):
            block = work_rows(flips(f, mask, bits))
            if mask != 0:
                own[i].wait()
            sent[i].wait_recv()
            work[block, :] = (
                work[block, :].astype(f32) + inbox[block, :].astype(f32)
            ).astype(bf)
            scatter.start_mask(mask)

    for copy in inputs:
        copy.wait()
    join(back_own, back_sent, whole_back, dn2, work_back)
    pair_sum(back_own, back_sent, work_back, pair_back, back)
    for copy in out_sent[:-1]:
        copy.start()
    join(out_own, out_sent, whole_out, shared, work_out)
    flat[...] = jnp.zeros_like(flat)
    pack_second(t, flat, wide, da_gu, db_gu, da_dn, db_dn)
    fill_blocks(early, contexts)
    for block in range(early, contexts):
        pair_block(block).start()
    for stage in range(1, bits):
        back.add(stage - 1)
        back.start(stage)
    dq_t[...] = jnp.zeros_like(dq_t)
    da_qkv[...] = jnp.zeros_like(da_qkv)
    db_qkv[...] = jnp.zeros_like(db_qkv)
    for block in range(early, contexts):
        pair_block(block).wait_recv()
    push_blocks(True)
    back.last(total_half)
    pair_sum(out_own, out_sent, work_out, pair_out, out)
    for copy in out_sent:
        copy.wait_send()
    total_full[mine, :] = total_half[...]
    full_copy = send(
        total_half, total_full.at[mine], core_send.at[2, 0], core_recv.at[2, 0], sibling
    )
    full_copy.start()
    back.finish()
    for copy in back_sent:
        copy.wait_send()
    gain_one = gains[0:1, :]
    gain_two = gains[1:2, :]
    wo_copy.wait()
    full_copy.wait_recv()

    def attn_tile(i, carry):
        block = local_rows(i)
        values = resid[block, :]
        gradient = g_in[block, :].astype(f32) + norm_back(
            values, rms_scale(values), gain_two, total_full[block, :].astype(f32)
        )
        dy[block, :] = gradient
        low_grad = gradient.astype(bf)
        rank_back = nt_dot(low_grad, b_o2[0:128, :])
        do_n[block, :] = (
            nn_dot(low_grad, wo[...]) + nn_dot(two_parts(rank_back), a_o_t2[...])
        ).astype(bf)
        values_o = mixed[block, :]
        rank = nn_dot(values_o, a_o[...])
        first = tn_dot(rank_back.astype(bf), values_o)[0:RANK]
        second = 2.0 * tn_dot(rank.astype(bf), low_grad)[0:RANK]

        @pl.when(i == 0)
        def _():
            da_o[...] = first
            db_o[...] = second

        @pl.when(i > 0)
        def _():
            da_o[...] += first
            db_o[...] += second

        return carry

    lax.fori_loop(0, 2, attn_tile, 0)
    for p in range(width // 128):
        lanes = slice(128 * p, 128 * p + 128)
        turned = do_n[:, lanes].astype(f32).T
        do_t[lanes, :] = turned.astype(bf)
        product = turned * o_t[lanes, :]
        for odd in range(2):
            delta[2 * p + odd : 2 * p + odd + 1, :] = jnp.sum(
                product[HEAD_DIM * odd : HEAD_DIM * odd + HEAD_DIM, :], axis=0, keepdims=True
            )
    wq_copy.wait()

    def attend_back(chunk):
        block = chunk_rows(chunk)
        n1_load(chunk).start()
        for copy in table_loads(chunk):
            copy.start()
        for copy in table_loads(chunk) + loads(chunk):
            copy.wait()
        scale = jnp.exp(peaks[pl.ds(pl.multiple_of(chunk * 8, 8), 8), :] - lse[...])
        factor[...] = scale
        cos_rows = cosine[...]
        sin_rows = -sinus[...]
        for p in range(width // 128):
            lanes = slice(128 * p, 128 * p + 128)
            k_t[lanes, :] = k_buf[block, lanes].astype(f32).T.astype(bf)

        def pair_step(p, carry):
            lanes = pl.ds(pl.multiple_of(p * 128, 128), 128)
            weights_in(chunk, p).wait()
            values = v_buf[block, lanes]
            grad_t = do_t[lanes, :]
            query = q_n[:, lanes]
            grad = do_n[:, lanes]
            grad_keys = jnp.zeros((rows, 128), f32)
            grad_values = jnp.zeros((rows, 128), f32)
            for odd in range(2):
                h = 2 * p + odd
                upper = head_half(grad_t.shape, 0, odd)
                side = head_half(query.shape, 1, odd)
                none_t = jnp.zeros_like(grad_t)
                none = jnp.zeros_like(query)
                weights = p_buf[h].astype(f32) * factor[pl.ds(h, 1), :]
                low_weights = weights.astype(bf)
                grad_weights = nn_dot(values, jnp.where(upper, grad_t, none_t))
                grad_scores = (weights * (grad_weights - delta[pl.ds(h, 1), :])).astype(bf)
                grad_values += nn_dot(low_weights, jnp.where(side, grad, none))
                grad_keys += nn_dot(grad_scores, jnp.where(side, query, none))
                head = pl.ds(pl.multiple_of(h * HEAD_DIM, HEAD_DIM), HEAD_DIM)
                dq_t[head, :] += nn_dot(k_t[head, :], grad_scores)
            grad_kv[kv_rows, lanes] = turn(grad_keys, cos_rows, sin_rows).astype(bf)
            grad_kv[kv_rows, pl.ds(pl.multiple_of(width + p * 128, 128), 128)] = grad_values.astype(bf)

            @pl.when(chunk < c)
            def _():
                weights_in(chunk + 1, p).start()

            return carry

        lax.fori_loop(0, heads // 2, pair_step, 0)

    def ranks():
        return nt_dot(grad_kv[kv_rows, :], b_qkv2[0:128, width:])

    def adapter_back(chunk, own, rank_back):
        grads = grad_kv[kv_rows, :]
        n1_load(chunk).wait()
        n1 = n1_buf[...]
        rank = nn_dot(n1, a_qkv[...]).astype(bf)
        both = 2.0 * tn_dot(rank, grads)
        db_qkv[RANK : 2 * RANK, :] += both[RANK : 2 * RANK, :width]
        db_qkv[2 * RANK :, :] += both[2 * RANK : 3 * RANK, width:]
        if own:
            for p in range(width // 128):
                lanes = slice(128 * p, 128 * p + 128)
                grad_query = (dq_t[lanes, :] * 0.125).T
                dq[:, lanes] = turn(grad_query, cosine[...], -sinus[...]).astype(bf)
            rank_back += nt_dot(dq[...], b_qkv2[0:128, :width])
            db_qkv[0:RANK, :] += 2.0 * tn_dot(rank, dq[...])[0:RANK, :]
        da_qkv[...] += tn_dot(rank_back.astype(bf), n1)[0 : 3 * RANK]
        return rank_back

    def project_back(chunk, own, rank_back):
        result = nt_dot(grad_kv[kv_rows, :], wq[:, width:])
        if own:
            result += nt_dot(dq[...], wq[:, :width])
        result += nn_dot(two_parts(rank_back), a_qkv_t2[...])
        part[...] = result.astype(bf)
        part_out[work_rows(chunk), :] = part[theirs, :]
        z_out[work_rows(chunk), :] = part[mine, :]

    def pair_copy(chunk):
        return send(
            part_out.at[work_rows(chunk)],
            part_in.at[work_rows(chunk)],
            pair_send.at[chunk],
            pair_recv.at[chunk],
            sibling,
        )

    pieces = split_rows(half)

    def down(chunk, piece):
        offset, size = pieces[piece]
        block = Gather.rows(chunk * half + offset, size)
        return send(
            z_out.at[block],
            z_in.at[block],
            z_send.at[chunk, piece],
            z_recv.at[chunk, piece],
            (f, c - 1, t),
        )

    def chain(chunk, onward):
        pair_copy(chunk).wait_recv()
        for piece, (offset, size) in enumerate(pieces):
            block = Gather.rows(chunk * half + offset, size)
            summed = z_out[block, :].astype(f32) + part_in[block, :].astype(f32)
            z_out[block, :] = summed.astype(bf)

            @pl.when(c < contexts - 1)
            def _(block=block, summed=summed, piece=piece):
                down(chunk, piece).wait_recv()
                z_out[block, :] = (summed + z_in[block, :].astype(f32)).astype(bf)

            if onward:
                down(chunk, piece).start()

    def pass_down(chunk):
        chain(chunk, True)

    def sum_moe():
        for stage in range(1, bits):
            out.add(stage - 1)
            out.start(stage)

    ffn_copy = send(ffn_half, ffn_full.at[mine], core_send.at[2, 1], core_recv.at[2, 1], sibling)

    def share_moe():
        out.last(ffn_half)
        ffn_full[mine, :] = ffn_half[...]
        ffn_copy.start()

    def step(chunk, carry):
        attend_back(chunk)
        rank_back = ranks()
        project_back(chunk, False, rank_back)
        pair_copy(chunk).start()
        adapter_back(chunk, False, rank_back)

        @pl.when(c == contexts - 1)
        def _():
            pass_down(chunk)

        @pl.when((c < contexts - 1) & (chunk >= 1))
        def _():
            pass_down(chunk - 1)

        @pl.when(chunk == 0)
        def _():
            sum_moe()

        @pl.when(chunk == 1)
        def _():
            share_moe()

            @pl.when(c >= early)
            def _():
                sum_own()

        return carry

    lax.fori_loop(0, c, step, 0)
    attend_back(c)
    last_rank = adapter_back(c, True, ranks())
    pack_first(t, flat, wide, da_qkv, db_qkv, da_o, db_o)
    fill_blocks(0, early)
    for block in range(early):
        pair_block(block).start()
    project_back(c, True, last_rank)
    pair_copy(c).start()
    for block in range(early):
        pair_block(block).wait_recv()
    push_blocks(False)

    @pl.when((c < 2) & (c >= early))
    def _():
        sum_own()

    @pl.when(c == 0)
    def _():
        sum_moe()

    @pl.when((c < contexts - 1) & (c >= 1))
    def _():
        pass_down(c - 1)

    @pl.when(c < 2)
    def _():
        share_moe()

    chain(c, False)
    dn1_full[mine, :] = z_out[work_rows(c), :]
    dn1_copy = send(
        z_out.at[work_rows(c)],
        dn1_full.at[mine],
        core_send.at[2, 2],
        core_recv.at[2, 2],
        sibling,
    )
    dn1_copy.start()
    ffn_copy.wait_recv()
    block_copy = pltpu.make_async_copy(ffn_full, ffn_out, in_sems.at[len(inputs)])
    block_copy.start()

    @pl.when(c < early)
    def _():
        sum_own()

    dn1_copy.wait_recv()

    def final_tile(i, carry):
        block = local_rows(i)
        values = x_in[block, :].astype(f32)
        dy[block, :] = dy[block, :] + norm_back(
            values, rms_scale(values), gain_one, dn1_full[block, :].astype(f32)
        )
        return carry

    lax.fori_loop(0, 2, final_tile, 0)
    grad_copy = pltpu.make_async_copy(dy, input_grad, in_sems.at[len(inputs) + 1])
    grad_copy.start()
    own = ADAPTERS // fsdp
    wanted = [(f * own + a).astype(f32) for a in range(own)]
    mine_sum = own_sum[...].astype(f32)
    sums = [jnp.where(table_all[f, 4:5, 0:1] == w, mine_sum, 0.0) for w in wanted]
    for k in range(fsdp - 1):
        to_peer(k).wait_recv()
        tree = table_all[lax.rem(f - k - 1 + fsdp, fsdp), 4:5, 0:1]
        block = tree_sums[k].astype(f32)
        sums = [total + jnp.where(tree == w, block, 0.0) for total, w in zip(sums, wanted)]
    for a in range(own):
        adapter_out[a] = sums[a]
    for copy in [full_copy, ffn_copy, dn1_copy]:
        copy.wait_send()
    block_copy.wait()
    grad_copy.wait()
    for block in range(contexts):
        pair_block(block).wait_send()
    for k in range(contexts - 1):
        to_owner(k).wait_send()
    for k in range(fsdp - 1):
        to_peer(k).wait_send()
    out.finish()

    def drain(chunk, carry):
        pair_copy(chunk).wait_send()

        @pl.when(chunk < c)
        def _():
            for piece in range(len(pieces)):
                down(chunk, piece).wait_send()

        return carry

    lax.fori_loop(0, c + 1, drain, 0)


def backward_call(sizes, remote, local):
    fsdp, contexts, _ = sizes
    rows = local[0].shape[0]
    padded = (PARAMS // 128 // (2 * contexts) + 15) // 16 * 16
    half = rows // 2
    tree = rows * contexts
    width = remote[6].shape[1]
    units = local[19].shape[1]
    bf, f32 = jnp.bfloat16, jnp.float32
    vmem = pl.BlockSpec(memory_space=pltpu.VMEM)
    hbm = pl.BlockSpec(memory_space=pl.ANY)

    def shape(kind, *dims):
        return jax.ShapeDtypeStruct(dims, kind)

    moves = 2 * (fsdp - 1)
    slots = max(fsdp, 4)
    dma = pltpu.SemaphoreType.DMA
    return pl.pallas_call(
        functools.partial(backward_kernel, sizes),
        in_specs=[hbm] * len(remote) + [hbm, hbm, vmem, vmem, hbm, hbm, hbm, hbm, hbm, hbm, hbm, vmem, hbm, hbm, hbm, hbm, hbm, hbm, vmem, vmem, vmem, vmem, vmem],
        out_specs=[hbm, hbm, vmem],
        out_shape=[
            shape(bf, rows, D),
            shape(f32, rows, D),
            shape(f32, ADAPTERS // fsdp, padded, 128),
        ],
        scratch_shapes=[
            pltpu.VMEM((rows, 128), f32),
            pltpu.VMEM((rows, 128), f32),
            pltpu.VMEM((tree, width), bf),
            pltpu.VMEM((tree, width), bf),
            pltpu.VMEM((D, 3 * width), bf),
            pltpu.VMEM((D, width), bf),
            pltpu.VMEM((max(fsdp, contexts) * half, D), bf),
            pltpu.VMEM((max(fsdp, contexts) * half, D), bf),
            pltpu.VMEM((max(fsdp - 1, 2) * half, D), bf),
            pltpu.VMEM((fsdp * half, D), bf),
            pltpu.VMEM((fsdp * half, D), bf),
            pltpu.VMEM(((fsdp - 1) * half, D), bf),
            pltpu.VMEM((half, D), bf),
            pltpu.VMEM((rows, D), bf),
            pltpu.VMEM((half, D), bf),
            pltpu.VMEM((rows, D), bf),
            pltpu.VMEM((rows, D), f32),
            pltpu.VMEM((rows, width), bf),
            pltpu.VMEM((width, rows), bf),
            pltpu.VMEM((8, rows), f32),
            pltpu.VMEM((8, rows), f32),
            pltpu.VMEM((width, rows), bf),
            pltpu.VMEM((width, rows), f32),
            pltpu.VMEM((rows, width), bf),
            pltpu.VMEM((contexts * half, D), bf),
            pltpu.VMEM((contexts * half, D), bf),
            pltpu.VMEM((rows, D), bf),
            dma((2, moves)),
            dma((2, moves)),
            dma((contexts, 2)),
            dma((contexts, 2)),
            dma((3, slots)),
            dma((3, slots)),
            dma((contexts,)),
            dma((contexts,)),
            dma((3, slots)),
            dma((5, contexts)),
            pltpu.VMEM((rows, D), bf),
            pltpu.VMEM((rows, D), bf),
            pltpu.VMEM((rows, D), f32),
            pltpu.VMEM((rows, D), bf),
            pltpu.VMEM((rows, D), bf),
            pltpu.VMEM((width, rows), bf),
            pltpu.VMEM((rows, width), bf),
            pltpu.VMEM((rows, width), bf),
            pltpu.VMEM((width, rows), f32),
            pltpu.VMEM((D, 128), bf),
            pltpu.VMEM((256, 3 * width), bf),
            pltpu.VMEM((256, D), bf),
            pltpu.VMEM((width, 128), bf),
            pltpu.VMEM((256, width), bf),
            pltpu.VMEM((256, D), bf),
            pltpu.VMEM((3 * RANK, D), f32),
            pltpu.VMEM((3 * RANK, width), f32),
            pltpu.VMEM((RANK, width), f32),
            pltpu.VMEM((RANK, D), f32),
            pltpu.VMEM((PARAMS // 128, 128), f32),
            pltpu.VMEM((max(D, units), 128), f32),
            pltpu.VMEM((contexts, 2, padded, 128), f32),
            pltpu.VMEM((contexts, padded, 128), f32),
            pltpu.VMEM((contexts - 1, padded, 128), bf),
            pltpu.VMEM((contexts - 1, padded, 128), bf),
            pltpu.VMEM((padded, 128), bf),
            pltpu.VMEM((fsdp - 1, padded, 128), bf),
            dma((17,)),
            dma((3, max(fsdp, contexts))),
            dma((3, max(fsdp, contexts))),
            pltpu.VMEM((width // HEAD_DIM, rows, rows), bf),
            dma((width // HEAD_DIM // 2,)),
            pltpu.VMEM((rows, D), bf),
            pltpu.VMEM((rows, D), bf),
        ],
        name="backward",
        compiler_params=pltpu.CompilerParams(
            collective_id=3, has_side_effects=True, vmem_limit_bytes=63 << 20
        ),
    )(*remote, *local)


def shards(
    tokens,
    attn_gain,
    w_qkv,
    w_out,
    ffn_gain,
    w_gu,
    w_dn,
    w_egu,
    w_edn,
    adapters,
    adapter_ids,
    parents,
    seg_lengths,
    routes,
    route_weights,
    cotangent,
):
    row_count = tokens.shape[1]
    contexts = lax.axis_size("context")
    tensors = lax.axis_size("tensor")
    fsdp_size = lax.axis_size("fsdp")
    sizes = (fsdp_size, contexts, tensors)
    local_width = w_qkv.shape[2]
    local_ff = w_dn.shape[0]
    own_adapters = adapters.shape[0]
    own_width = D // fsdp_size
    gains = jnp.broadcast_to(jnp.concatenate([attn_gain, ffn_gain])[None], (16, 2 * own_width))
    route_table = jnp.concatenate(
        [
            routes[0].astype(jnp.float32).T,
            route_weights[0].astype(jnp.float32).T,
            jnp.broadcast_to(adapter_ids.astype(jnp.float32)[:, None], (1, row_count)),
            jnp.zeros((3, row_count), jnp.float32),
        ]
    )
    lines = adapters.shape[1] // 128
    padded = (lines + 15) // 16 * 16
    adapter_rows = jnp.pad(
        adapters.reshape(own_adapters, lines, 128), ((0, 0), (0, padded - lines), (0, 0))
    ).reshape(own_adapters * padded, 128)
    half_dim = HEAD_DIM // 2
    exponents = -(np.arange(half_dim, dtype=np.float32) * np.float32(2.0)) / np.float32(HEAD_DIM)
    frequency = np.power(np.float32(rope_base), exponents).astype(np.float32)
    signs = np.repeat(np.array([-1.0, 1.0], np.float32), half_dim)
    turns = np.zeros((8, 128), np.float32)
    turns[0], turns[1] = np.tile(frequency, 4), np.tile(signs, 2)
    sharded = (
        tokens[0],
        cotangent[0],
        w_qkv.reshape(own_width, 3 * local_width),
        w_out.T,
        w_gu.reshape(own_width, 2 * local_ff),
        w_dn.T,
    )
    (
        n1_all,
        k_all,
        v_all,
        wq_all,
        wo_all,
        normed_all,
        cotangent_all,
        p_all,
        q_t,
        q_n,
        mixed_own,
        o_t,
        lse,
        resid,
        shared,
        dn2,
        da_gu_t,
        db_gu_own,
        da_dn_t,
        db_dn_own,
        gains_full,
        cosine,
        sinus,
        hot,
        reach_t,
        a_qkv,
        b_qkv2,
        a_qkv_t2,
        a_o,
        b_o2,
        a_o_t2,
        table_all,
        place_row,
        place_col,
        weight_col,
        marks,
        peaks,
    ) = forward_call(
        sizes,
        sharded,
        (adapter_rows, gains, route_table, turns, parents, seg_lengths),
    )
    moe_all, moe_back_all = moe_call(
        marks,
        place_row,
        place_col,
        weight_col,
        normed_all,
        cotangent_all,
        w_egu.transpose(0, 2, 1, 3),
        w_edn,
    )
    remote = (moe_all, moe_back_all, n1_all, k_all, v_all, wq_all, wo_all, cosine, sinus, p_all)
    ffn_sum, input_grad, sums = backward_call(
        sizes,
        remote,
        (tokens[0], cotangent[0], gains_full, peaks)
        + (resid, shared, dn2, q_t, q_n, mixed_own, o_t, lse)
        + (a_qkv, b_qkv2, a_qkv_t2, a_o, a_o_t2, b_o2)
        + (da_gu_t, db_gu_own, da_dn_t, db_dn_own, table_all),
    )
    adapter_grads = sums[:, :lines].reshape(own_adapters, -1)
    block_out = resid + ffn_sum.astype(jnp.float32)
    return (block_out[None], input_grad[None], adapter_grads)


def solution(mesh):
    return jax.shard_map(
        shards,
        mesh=mesh,
        in_specs=(
            P("fsdp", "context", None),
            P("fsdp"),
            P("fsdp", None, "tensor"),
            P("tensor", "fsdp"),
            P("fsdp"),
            P("fsdp", None, "tensor"),
            P("tensor", "fsdp"),
            P("fsdp", None, None, "tensor"),
            P("fsdp", "tensor", None),
            P("fsdp", ("context", "tensor")),
            P("fsdp"),
            P("fsdp", None),
            P("fsdp", None),
            P("fsdp", "context", None),
            P("fsdp", "context", None),
            P("fsdp", "context", None),
        ),
        out_specs=(
            P("fsdp", "context", None),
            P("fsdp", "context", None),
            P("fsdp", ("context", "tensor")),
        ),
        check_vma=False,
    )
```

```python
import jax
import jax.numpy as jnp
import numpy as np
import functools
import math

from jax import lax
from jax.experimental import pallas as pl
from jax.experimental.pallas import tpu as pltpu
from jax.sharding import PartitionSpec as P

D = 768
HEADS = 12
HEAD_DIM = 64
FF = 2048
EXPERTS = 8
TOPK = 2
RANK = 16
ADAPTERS = 8
PARAMS = 233472


epsilon = 1e-06
adapter_scale = 2.0
rope_base = 10000.0
masked_score = -1e30
highest_precision = lax.Precision.HIGHEST


def rms_scale(values):
    return lax.rsqrt(jnp.mean(values * values, axis=-1, keepdims=True) + epsilon)


def norm_back(values, scaling, gain_values, gradient):
    weighted = gradient * gain_values
    inner_mean = jnp.mean(values * weighted, axis=-1, keepdims=True)
    return scaling * weighted - values * (scaling * scaling * scaling) * inner_mean


SLOT_TILE = 512
TOKEN_TILE = 256
SLOT_WINDOW = 128
TRUNK = 1024


def nt_dot(left, right):
    return lax.dot_general(left, right, (((1,), (1,)), ((), ())), preferred_element_type=jnp.float32)


def tn_dot(left, right):
    return lax.dot_general(left, right, (((0,), (0,)), ((), ())), preferred_element_type=jnp.float32)


def nn_dot(left, right):
    return jnp.dot(left, right, preferred_element_type=jnp.float32)


def moe_kernel(
    starts,
    place_row,
    place_hbm,
    weight_hbm,
    rows_hbm,
    grads_hbm,
    egu_hbm,
    edn_hbm,
    out_hbm,
    back_hbm,
    place_col,
    weight_col,
    rows_ref,
    grads_ref,
    egu_ref,
    edn_ref,
    out_ref,
    back_ref,
    taken,
    taken_grad,
    taken_weight,
    sems,
    block_sems,
):
    f32, bf = jnp.float32, jnp.bfloat16
    experts = egu_hbm.shape[0]
    blocks = rows_ref.shape[0] // TOKEN_TILE

    def block_rows(b):
        return pl.ds(pl.multiple_of(b * TOKEN_TILE, TOKEN_TILE), TOKEN_TILE)

    def loads(b):
        block = block_rows(b)
        return [
            pltpu.make_async_copy(source.at[block], target.at[block], block_sems.at[i, b])
            for i, (source, target) in enumerate(
                ((rows_hbm, rows_ref), (grads_hbm, grads_ref), (weight_hbm, weight_col))
            )
        ]

    def stores(b):
        block = block_rows(b)
        return [
            pltpu.make_async_copy(source.at[block], target.at[block], block_sems.at[3 + i, b])
            for i, (source, target) in enumerate(((out_ref, out_hbm), (back_ref, back_hbm)))
        ]

    def weights(e):
        return [
            pltpu.make_async_copy(egu_hbm.at[e], egu_ref.at[e], sems.at[0, e]),
            pltpu.make_async_copy(edn_hbm.at[e], edn_ref.at[e], sems.at[1, e]),
        ]

    def each(count, copies, action):
        def step(i, carry):
            for copy in copies(i):
                getattr(copy, action)()
            return carry

        lax.fori_loop(0, count, step, 0)

    each(blocks, loads, "start")
    each(experts, weights, "start")
    place_copy = pltpu.make_async_copy(place_hbm, place_col, sems.at[2, 0])
    place_copy.start()
    taken[...] = jnp.zeros_like(taken)
    taken_grad[...] = jnp.zeros_like(taken_grad)
    taken_weight[...] = jnp.zeros_like(taken_weight)
    slot_rows = lax.broadcasted_iota(jnp.int32, (SLOT_WINDOW, TOKEN_TILE), 0).astype(f32)
    slot_cols = lax.broadcasted_iota(jnp.int32, (TOKEN_TILE, SLOT_WINDOW), 1).astype(f32)

    def windows(e, b):
        begin = starts[e, b] // 16 * 16
        return begin, (starts[e, b + 1] - begin + SLOT_WINDOW - 1) // SLOT_WINDOW

    def window_rows(begin, i):
        return pl.ds(pl.multiple_of(begin + i * SLOT_WINDOW, 16), SLOT_WINDOW)

    def fetch(b, carry):
        block = block_rows(b)
        for copy in loads(b):
            copy.wait()

        def take(which):
            picks = []
            for e, first in which:
                hit = place_row[e : e + 1, block] == slot_rows + first.astype(f32)
                picks.append(jnp.where(hit, 1.0, 0.0).astype(bf))
            pick = picks[0] if len(picks) == 1 else jnp.concatenate(picks, axis=0)
            for source, target in (
                (rows_ref, taken),
                (grads_ref, taken_grad),
                (weight_col, taken_weight),
            ):
                got = nn_dot(pick, source[block, :]).astype(bf)
                for i, (e, first) in enumerate(which):
                    slots = window_rows(first, 0)
                    target[e, slots, :] += got[i * SLOT_WINDOW : (i + 1) * SLOT_WINDOW, :]

        spans = [windows(e, b) for e in range(experts)]
        take([(e, spans[e][0]) for e in range(experts)])
        for e in range(experts):

            def more(i, c, e=e):
                take([(e, spans[e][0] + i * SLOT_WINDOW)])
                return c

            lax.fori_loop(1, spans[e][1], more, 0)
        return carry

    lax.fori_loop(0, blocks, fetch, 0)

    def tile(e, start, size):
        slots = pl.ds(pl.multiple_of(start, 128), size)
        inputs = taken[e, slots, :]
        gate_pre = nn_dot(inputs, egu_ref[e, 0])
        up_pre = nn_dot(inputs, egu_ref[e, 1])
        sigmoid_gate = jax.nn.sigmoid(gate_pre)
        silu = gate_pre * sigmoid_gate
        active = (silu * up_pre).astype(bf)
        taken[e, slots, :] = nn_dot(active, edn_ref[e]).astype(bf)
        grad_active = nt_dot(taken_grad[e, slots, :], edn_ref[e])
        lane = lax.broadcasted_iota(jnp.int32, (size, 128), 1)
        scale = jnp.sum(
            jnp.where(lane == e, taken_weight[e, slots, :].astype(f32), 0.0), axis=1, keepdims=True
        )
        grad_active = grad_active * scale
        grad_gate = (
            grad_active * up_pre * sigmoid_gate * (1.0 + gate_pre * (1.0 - sigmoid_gate))
        ).astype(bf)
        grad_up = (grad_active * silu).astype(bf)
        taken_grad[e, slots, :] = (
            nt_dot(grad_gate, egu_ref[e, 0]) + nt_dot(grad_up, egu_ref[e, 1])
        ).astype(bf)

    def expert_step(e, carry):
        for copy in weights(e):
            copy.wait()
        count = starts[e, blocks]
        whole = count // SLOT_TILE
        rest = count - whole * SLOT_TILE

        def step(i, c):
            tile(e, i * SLOT_TILE, SLOT_TILE)
            return c

        lax.fori_loop(0, whole + jnp.where(rest > SLOT_TILE - 128, 1, 0), step, 0)
        for size in range(128, SLOT_TILE, 128):

            @pl.when((rest > size - 128) & (rest <= size))
            def _(size=size):
                tile(e, whole * SLOT_TILE, size)

        return carry

    lax.fori_loop(0, experts, expert_step, 0)
    place_copy.wait()

    def give(b, carry):
        block = block_rows(b)

        def hand(which):
            plain, scaled, values, values_grad = [], [], [], []
            for e, first in which:
                hit = place_col[block, e : e + 1] == slot_cols + first.astype(f32)
                plain.append(jnp.where(hit, 1.0, 0.0).astype(bf))
                weight = weight_col[block, e : e + 1].astype(f32)
                scaled.append(jnp.where(hit, weight, 0.0).astype(bf))
                values.append(taken[e, window_rows(first, 0), :])
                values_grad.append(taken_grad[e, window_rows(first, 0), :])

            def join(pieces, axis):
                return pieces[0] if len(pieces) == 1 else jnp.concatenate(pieces, axis=axis)

            return (
                nn_dot(join(scaled, 1), join(values, 0)),
                nn_dot(join(plain, 1), join(values_grad, 0)),
            )

        spans = [windows(e, b) for e in range(experts)]
        first, second = hand([(e, spans[e][0]) for e in range(experts)])
        out_ref[block, :] = first.astype(bf)
        back_ref[block, :] = second.astype(bf)
        for e in range(experts):

            def more(i, c, e=e):
                first, second = hand([(e, spans[e][0] + i * SLOT_WINDOW)])
                out_ref[block, :] = (out_ref[block, :].astype(f32) + first).astype(bf)
                back_ref[block, :] = (back_ref[block, :].astype(f32) + second).astype(bf)
                return c

            lax.fori_loop(1, spans[e][1], more, 0)
        for copy in stores(b):
            copy.start()
        return carry

    lax.fori_loop(0, blocks, give, 0)
    each(blocks, stores, "wait")


def moe_call(starts, place_row, place_col, weight_col, rows, grads, egu, edn):
    total, width = rows.shape
    experts = egu.shape[0]
    slots = total // 2 + SLOT_TILE
    blocks = total // TOKEN_TILE
    bf, f32 = jnp.bfloat16, jnp.float32
    vmem = pl.BlockSpec(memory_space=pltpu.VMEM)
    hbm = pl.BlockSpec(memory_space=pl.ANY)
    shape = jax.ShapeDtypeStruct((total, width), bf)
    return pl.pallas_call(
        moe_kernel,
        grid_spec=pltpu.PrefetchScalarGridSpec(
            num_scalar_prefetch=1,
            grid=(),
            in_specs=[vmem] + [hbm] * 6,
            out_specs=[hbm, hbm],
            scratch_shapes=[
                pltpu.VMEM((total, 128), f32),
                pltpu.VMEM((total, 128), bf),
                pltpu.VMEM((total, width), bf),
                pltpu.VMEM((total, width), bf),
                pltpu.VMEM(egu.shape, bf),
                pltpu.VMEM(edn.shape, bf),
                pltpu.VMEM((total, width), bf),
                pltpu.VMEM((total, width), bf),
                pltpu.VMEM((experts, slots, width), bf),
                pltpu.VMEM((experts, slots, width), bf),
                pltpu.VMEM((experts, slots, 128), bf),
                pltpu.SemaphoreType.DMA((3, experts)),
                pltpu.SemaphoreType.DMA((5, blocks)),
            ],
        ),
        out_shape=[shape, shape],
        name="experts",
        compiler_params=pltpu.CompilerParams(vmem_limit_bytes=62 << 20),
    )(starts, place_row, place_col, weight_col, rows, grads, egu, edn)


MESH = pl.DeviceIdType.MESH


def place_of():
    return lax.axis_index("fsdp"), lax.axis_index("context"), lax.axis_index("tensor")


def greet(devices):
    barrier = pltpu.get_barrier_semaphore()
    for device in devices:
        pl.semaphore_signal(barrier, inc=1, device_id=device, device_id_type=MESH)
    pl.semaphore_wait(barrier, len(devices))


def send(source, target, send_sem, recv_sem, device):
    return pltpu.make_async_remote_copy(
        src_ref=source,
        dst_ref=target,
        send_sem=send_sem,
        recv_sem=recv_sem,
        device_id=device,
        device_id_type=MESH,
    )


def flip(index, bit):
    return index + (1 - 2 * lax.rem(index // (1 << bit), 2)) * (1 << bit)


def split_rows(count):
    first = (count // 2 + 15) // 16 * 16
    return ((0, first), (first, count - first))


class Gather:
    def __init__(self, bits, me, device_of, own, buf, stride, base, count, send_sems, recv_sems):
        self.stages = [[] for _ in range(bits)]
        self.arrived = [[] for _ in range(bits)]
        self.passed = [[] for _ in range(bits)]
        number = 0
        for half, (offset, size) in enumerate(split_rows(count)):
            held = [me]
            for stage in range(bits):
                bit = (stage + half) % bits
                for block in held:
                    rows = self.rows(block * stride + base + offset, size)
                    source = own.at[self.rows(base + offset, size)] if block is me else buf.at[rows]
                    self.passed[stage].append(block is not me)
                    self.stages[stage].append(
                        send(
                            source,
                            buf.at[rows],
                            send_sems.at[number],
                            recv_sems.at[number],
                            device_of(flip(me, bit)),
                        )
                    )
                    self.arrived[stage].append(
                        self.rows(flip(block, bit) * stride + base + offset, size)
                    )
                    number = number + 1
                held = held + [flip(block, bit) for block in held]

    @staticmethod
    def rows(start, size):
        return pl.ds(pl.multiple_of(start, 16), size)

    def start(self, stage):
        if stage == 0:
            for copies, passed in zip(self.stages, self.passed):
                for copy, later in zip(copies, passed):
                    if not later:
                        copy.start()
        else:
            for copy, later in zip(self.stages[stage], self.passed[stage]):
                if later:
                    copy.start()

    def wait(self, stage):
        for copy in self.stages[stage]:
            copy.wait_recv()

    def finish(self):
        for stage in self.stages:
            for copy in stage:
                copy.wait_send()


def turn(values, cosine, sinus):
    lane = lax.broadcasted_iota(jnp.int32, values.shape, 1)
    first = lax.rem(lane, HEAD_DIM) < HEAD_DIM // 2
    swapped = jnp.where(
        first,
        pltpu.roll(values, 128 - HEAD_DIM // 2, 1),
        pltpu.roll(values, HEAD_DIM // 2, 1),
    )
    return values * cosine + swapped * sinus


def two_parts(values):
    high = values.astype(jnp.bfloat16)
    low = (values - high.astype(jnp.float32)).astype(jnp.bfloat16)
    return jnp.concatenate([high, low], axis=1)


def normed(values, gain):
    scale = lax.rsqrt(jnp.mean(values * values, axis=-1, keepdims=True) + epsilon)
    return (values * scale * gain).astype(jnp.bfloat16)


def fill_bias(bias, hot_rows, reach_t, key_start, query_start):
    seen = nn_dot(hot_rows, reach_t)
    keys = key_start + lax.broadcasted_iota(jnp.int32, seen.shape, 0)
    queries = query_start + lax.broadcasted_iota(jnp.int32, seen.shape, 1)
    bias[...] = jnp.where((seen > 0.5) & (keys <= queries), 0.0, masked_score)


def head_half(shape, axis, odd):
    index = lax.broadcasted_iota(jnp.int32, shape, axis)
    return (index >= HEAD_DIM) if odd else (index < HEAD_DIM)


def tree_tables(parents, lengths, turns, context, rows, hot, reach_t, cosine, sinus):
    lane = lax.broadcasted_iota(jnp.int32, (1, 128), 1)
    far = jnp.full((1, 128), 1 << 30, jnp.int32)
    none = jnp.zeros((1, 128), jnp.int32)
    begins, ends, moves = far, far, none
    first, second = none - 1, none - 1
    start = jnp.int32(0)
    for s in range(parents.shape[1]):
        parent = parents[0, s]
        grand = parents[0, parent]
        here = lane == s
        above = jnp.where(parent != s, lengths[0, parent], 0) + jnp.where(
            (grand != s) & (grand != parent), lengths[0, grand], 0
        )
        begins = jnp.where(here, start, begins)
        moves = jnp.where(here, above - start, moves)
        first = jnp.where(here, parent, first)
        second = jnp.where(here, grand, second)
        start = start + lengths[0, s]
        ends = jnp.where(here, start, ends)
    over = lax.broadcasted_iota(jnp.int32, (128, 128), 0)
    under = lax.broadcasted_iota(jnp.int32, (128, 128), 1)
    ancestors = jnp.where((over == under) | (over == first) | (over == second), 1.0, 0.0).astype(
        jnp.bfloat16
    )

    def fill(chunk, carry):
        block = pl.ds(pl.multiple_of(chunk * rows, 16), rows)
        row = chunk * rows + lax.broadcasted_iota(jnp.int32, (rows, 128), 0)
        inside = (row >= begins) & (row < ends)
        hot[block, :] = jnp.where(inside, 1.0, 0.0).astype(jnp.bfloat16)
        moved = jnp.sum(jnp.where(inside, moves.astype(jnp.float32), 0.0), axis=1, keepdims=True)
        angle = (row.astype(jnp.float32) + moved) * turns[0:1, :]
        cosine[block, :] = jnp.cos(angle)
        sinus[block, :] = jnp.sin(angle) * turns[1:2, :]
        return carry

    lax.fori_loop(0, context + 1, fill, 0)
    own = pl.ds(pl.multiple_of(context * rows, 16), rows)
    reach_t[...] = nt_dot(ancestors, hot[own, :]).astype(jnp.bfloat16)


def choose(f, wanted, adapters, out):
    count = out.shape[0]
    own = adapters.shape[0] // count
    total = jnp.zeros((count, 128), jnp.float32)
    for a in range(own):
        block = adapters[a * count : (a + 1) * count, :].astype(jnp.float32)
        total = total + jnp.where(wanted == (f * own + a).astype(jnp.float32), block, 0.0)
    out[...] = total.astype(jnp.bfloat16)


def route_tables(f, table_all, place_row, place_col, weight_col, marks):
    fsdp, _, rows = table_all.shape
    own = EXPERTS // fsdp
    f32 = jnp.float32
    sub = lax.broadcasted_iota(jnp.int32, (8, rows), 0)
    expert = jnp.where(sub < own, f * own + sub, -1).astype(f32)
    before = lax.broadcasted_iota(jnp.int32, (rows, rows), 0)
    after = lax.broadcasted_iota(jnp.int32, (rows, rows), 1)
    upto = jnp.where(before <= after, 1.0, 0.0).astype(jnp.bfloat16)
    lane = lax.broadcasted_iota(jnp.int32, (8, 128), 1)
    base = jnp.zeros((8, 1), f32)
    found = jnp.zeros((8, 128), f32)
    more = jnp.zeros((120, rows), f32)
    for source in range(fsdp):
        table = table_all[source]
        one = table[0:1, :] == expert
        two = table[1:2, :] == expert
        hit = one | two
        weight = jnp.where(one, table[2:3, :], 0.0) + jnp.where(two, table[3:4, :], 0.0)
        count = nn_dot(jnp.where(hit, 1.0, 0.0).astype(jnp.bfloat16), upto) + base
        place = jnp.where(hit, count - 1.0, -1.0)
        block = slice(source * rows, (source + 1) * rows)
        place_row[:, block] = place
        place_col[block, :] = jnp.concatenate([place, more], axis=0).T
        weight_col[block, :] = jnp.concatenate([weight, more], axis=0).T.astype(jnp.bfloat16)
        for token in range(TOKEN_TILE - 1, fsdp * rows, TOKEN_TILE):
            if token // rows == source:
                at = token % rows
                found = jnp.where(lane == token // TOKEN_TILE + 1, count[:, at : at + 1], found)
        base = count[:, rows - 1 : rows]
    marks[...] = found.astype(jnp.int32)


def unpack_adapter(t, per_block, chosen, flat, wide, first, second):
    a_qkv, b_qkv2, a_qkv_t2, a_o, b_o2, a_o_t2 = first
    a_gu, b_gu2, a_gu_t2, a_dn, a_dn_t2, b_dn2 = second
    f32, bf = jnp.float32, jnp.bfloat16
    contexts = chosen.shape[1]
    width, units = a_o.shape[0], a_dn.shape[0]
    count = PARAMS // 128 // (2 * contexts)
    for context in range(contexts):
        for part in range(2):
            start = (2 * context + part) * count
            flat[start : start + count, :] = chosen[part, context, 0:count, :].astype(f32)

    def spread(start, groups, rank, out, out_t):
        total = groups * 128 // rank
        wide[...] = jnp.zeros_like(wide)
        lines = rank // math.gcd(rank, 128)
        each = lines * 128 // rank
        for i in range(each):
            row, at = divmod(i * rank, 128)
            def line(number):
                if lines == 1:
                    return flat[pl.ds(start, groups), :]
                return flat[pl.ds(start + number, groups // lines, stride=lines), :]

            piece = line(row)[:, at : min(at + rank, 128)]
            if at + rank > 128:
                piece = jnp.concatenate([piece, line(row + 1)[:, 0 : at + rank - 128]], axis=1)
            wide[pl.ds(i, groups // lines, stride=each), 0:rank] = piece
        out[...] = wide[0:total, :].astype(bf)
        if out_t is not None:
            for p in range(total // 128):
                turned = wide[128 * p : 128 * p + 128, :].T.astype(bf)
                out_t[0:128, 128 * p : 128 * p + 128] = turned
                out_t[128:256, 128 * p : 128 * p + 128] = turned

    def stack(start, lines, columns, out, row, column):
        for p, m in enumerate(columns):
            piece = (2.0 * flat[pl.ds(start + m, RANK, stride=lines), :]).astype(bf)
            lanes = slice(column + 128 * p, column + 128 * p + 128)
            out[row : row + RANK, lanes] = piece
            out[128 + row : 128 + row + RANK, lanes] = piece

    for ref in (b_qkv2, b_o2, b_gu2, b_dn2):
        ref[...] = jnp.zeros_like(ref)
    at = 0
    spread(at, 3 * RANK * D // 128, 3 * RANK, a_qkv, a_qkv_t2)
    at = at + 3 * RANK * D // 128
    lines = D // 128
    mine = [t * (width // 128) + p for p in range(width // 128)]
    for j in range(3):
        stack(at + j * RANK * lines, lines, mine, b_qkv2, j * RANK, j * width)
    at = at + 3 * RANK * lines
    spread(at + t * (width * RANK // 128), width * RANK // 128, RANK, a_o, a_o_t2)
    at = at + D * RANK // 128
    stack(at, lines, list(range(lines)), b_o2, 0, 0)
    at = at + RANK * lines
    spread(at, 2 * RANK * D // 128, 2 * RANK, a_gu, a_gu_t2)
    at = at + 2 * RANK * D // 128
    wide_lines = FF // 128
    mine = [t * (units // 128) + p for p in range(units // 128)]
    for j in range(2):
        stack(at + j * RANK * wide_lines, wide_lines, mine, b_gu2, j * RANK, j * units)
    at = at + 2 * RANK * wide_lines
    spread(at + t * (units * RANK // 128), units * RANK // 128, RANK, a_dn, a_dn_t2)
    at = at + FF * RANK // 128
    stack(at, lines, list(range(lines)), b_dn2, 0, 0)


def forward_kernel(
    sizes,
    x_in,
    g_in,
    wq_in,
    wo_in,
    gu_in,
    dn_in,
    adapters_in,
    gains_in,
    table_in,
    turns,
    parents,
    lengths,
    n1_all,
    k_all,
    v_all,
    wq_all,
    wo_all,
    n2_all,
    g_all,
    p_all,
    q_t_out,
    q_n_out,
    mixed_out,
    o_t_out,
    lse_out,
    resid_out,
    shared_out,
    dn2_out,
    da_gu,
    db_gu,
    da_dn,
    db_dn,
    gains_out,
    cosine_out,
    sinus_out,
    hot_out,
    reach_t_out,
    a_qkv_out,
    b_qkv2_out,
    a_qkv_t2_out,
    a_o_out,
    b_o2_out,
    a_o_t2_out,
    table_all_out,
    place_row_out,
    place_col_out,
    weight_col_out,
    marks,
    peaks,
    x_buf,
    wq,
    wo,
    gu,
    dn,
    g_own,
    n1_buf,
    k_buf,
    v_buf,
    v_t,
    peak,
    total,
    bias,
    part_out,
    part_in,
    n2_own,
    shared,
    dn2,
    adapters_all,
    picked,
    gains_all,
    chosen,
    flat,
    a_wide,
    a_gu,
    b_gu2,
    a_gu_t2,
    a_dn,
    a_dn_t2,
    b_dn2,
    fs_send,
    fs_recv,
    z_send,
    z_recv,
    core_send,
    core_recv,
    local_sems,
    chunk_sems,
    small_send,
    small_recv,
    lend_send,
    lend_recv,
    q_t,
    q_n,
    mixed,
    o_t,
    lse,
    resid,
    gains,
    cosine,
    sinus,
    hot,
    reach_t,
    a_qkv,
    b_qkv2,
    a_qkv_t2,
    a_o,
    b_o2,
    a_o_t2,
    table_all,
    place_row,
    place_col,
    weight_col,
    out_sems,
    p_buf,
    p_sems,
):
    fsdp, contexts, _ = sizes
    bits = fsdp.bit_length() - 1
    f, c, t = place_of()
    rows = x_in.shape[0]
    half = rows // 2
    heads = q_t.shape[0] // HEAD_DIM
    width = q_t.shape[0]
    units = dn_in.shape[1]
    own_n = wq_in.shape[0]
    sibling = (f, c, 1 - t)

    def peer(index):
        return (index, c, t)

    peers = [(lax.rem(f + k, fsdp), c, t) for k in range(1, fsdp)]
    stacked = [(f, lax.rem(c + k, contexts), t) for k in range(1, contexts)]
    greet(peers + stacked + [sibling])

    targets = (
        (q_t, q_t_out),
        (q_n, q_n_out),
        (mixed, mixed_out),
        (o_t, o_t_out),
        (lse, lse_out),
        (resid, resid_out),
        (shared, shared_out),
        (dn2, dn2_out),
        (gains, gains_out),
        (cosine, cosine_out),
        (sinus, sinus_out),
        (hot, hot_out),
        (reach_t, reach_t_out),
        (a_qkv, a_qkv_out),
        (b_qkv2, b_qkv2_out),
        (a_qkv_t2, a_qkv_t2_out),
        (a_o, a_o_out),
        (b_o2, b_o2_out),
        (a_o_t2, a_o_t2_out),
        (table_all, table_all_out),
        (place_row, place_row_out),
        (place_col, place_col_out),
        (weight_col, weight_col_out),
    )
    given = []

    def give_out(refs):
        for i, (ref, target) in enumerate(targets):
            if any(ref is other for other in refs):
                copy = pltpu.make_async_copy(ref, target, out_sems.at[i])
                copy.start()
                given.append(copy)

    def half_rows(chunk, part):
        return pl.ds(pl.multiple_of(chunk * rows + part * half, 16), half)

    def up(chunk, source):
        return send(
            source,
            x_buf.at[half_rows(chunk, t)],
            z_send.at[chunk],
            z_recv.at[chunk],
            (f, c + 1, t),
        )

    def across(chunk):
        block = x_buf.at[half_rows(chunk, t)]
        return send(block, block, core_send.at[chunk], core_recv.at[chunk], sibling)

    @pl.when(c < contexts - 1)
    def _():
        up(c, x_in.at[half_rows(0, t)]).start()

    gathers = []
    halved = (False, False, True, False)
    neighbour = (f, c + 1 - 2 * lax.rem(c, 2), t)
    own_half = own_n // 2
    for i, (own, buf) in enumerate(((wq_in, wq), (wo_in, wo), (gu_in, gu), (dn_in, dn))):
        base, count = (lax.rem(c, 2) * own_half, own_half) if halved[i] else (0, own_n)
        gathers.append(
            Gather(bits, f, peer, own, buf, own_n, base, count, fs_send.at[i], fs_recv.at[i])
        )

    def lent(gather, buf, which):
        copies, number = [], 0
        for stage in range(bits):
            group = []
            for block in gather.arrived[stage]:
                group.append(
                    send(
                        buf.at[block],
                        buf.at[block],
                        lend_send.at[which, number],
                        lend_recv.at[which, number],
                        neighbour,
                    )
                )
                number = number + 1
            copies.append(group)
        return copies

    gu_lent = lent(gathers[2], gu, 0)

    z_busy = (lax.rem(c, 2) == 0) & (c > 0)

    def lend(copies, stage):
        for copy in copies[stage]:
            copy.start()
    g_gather = Gather(
        bits, f, peer, g_in, g_all, rows, t * half, half, fs_send.at[4], fs_recv.at[4]
    )
    n2_gather = Gather(
        bits, f, peer, n2_own, n2_all, rows, t * half, half, fs_send.at[5], fs_recv.at[5]
    )
    wq_gather, wo_gather, gu_gather, dn_gather = gathers
    small, rows_sent = [], []
    for k, other in enumerate(peers):
        for j, (source, target) in enumerate(((table_in, table_all), (gains_in, gains_all))):
            copy = send(source, target.at[f], small_send.at[j, k], small_recv.at[j, k], other)
            copy.start()
            small.append(copy)
    wq_gather.start(0)
    locals_ = [pltpu.make_async_copy(x_in, x_buf.at[pl.ds(c * rows, rows)], local_sems.at[0])]
    for i, (own, buf) in enumerate(((wq_in, wq), (wo_in, wo), (gu_in, gu), (dn_in, dn))):
        locals_.append(
            pltpu.make_async_copy(own, buf.at[pl.ds(f * own_n, own_n)], local_sems.at[1 + i])
        )
    locals_.append(pltpu.make_async_copy(g_in, g_own, local_sems.at[5]))
    locals_.append(
        pltpu.make_async_copy(g_in, g_all.at[pl.ds(f * rows, rows)], local_sems.at[6])
    )
    for copy in locals_:
        copy.start()

    o_t[...] = jnp.zeros_like(o_t)
    peak[...] = jnp.full_like(peak, masked_score)
    total[...] = jnp.zeros_like(total)
    da_gu[...] = jnp.zeros_like(da_gu)
    db_gu[...] = jnp.zeros_like(db_gu)
    da_dn[...] = jnp.zeros_like(da_dn)
    db_dn[...] = jnp.zeros_like(db_dn)
    gains_all[f] = gains_in[...]
    table_all[f] = table_in[...]
    for copy in small:
        copy.wait_recv()
    for k, other in enumerate(peers):
        choose(f, table_all[lax.rem(f + k + 1, fsdp), 4:5, 0:1], adapters_in, picked.at[k])
        copy = send(
            picked.at[k], adapters_all.at[f], small_send.at[2, k], small_recv.at[2, k], other
        )
        copy.start()
        rows_sent.append(copy)
    choose(f, table_all[f, 4:5, 0:1], adapters_in, adapters_all.at[f])
    tree_tables(parents, lengths, turns, c, rows, hot, reach_t, cosine, sinus)

    def receive(step):
        chunk = c - step

        @pl.when(step <= c)
        def _():
            up(chunk, x_buf.at[half_rows(chunk, t)]).wait_recv()

            @pl.when(c < contexts - 1)
            def _():
                up(chunk, x_buf.at[half_rows(chunk, t)]).start()

            across(chunk).start()

    def chunk_rows(chunk):
        return pl.ds(pl.multiple_of(chunk * rows, 16), rows)

    def out_copies(chunk):
        block = chunk_rows(chunk)
        return [
            pltpu.make_async_copy(n1_buf.at[block], n1_all.at[block], chunk_sems.at[0, chunk]),
            pltpu.make_async_copy(k_buf.at[block], k_all.at[block], chunk_sems.at[1, chunk]),
            pltpu.make_async_copy(v_buf.at[block], v_all.at[block], chunk_sems.at[2, chunk]),
        ]

    def project(chunk, own):
        block = chunk_rows(chunk)
        n1 = normed(x_buf[block, :].astype(jnp.float32), gain_one)
        n1_buf[block, :] = n1
        rank = two_parts(nn_dot(n1, a_qkv[...]))
        cos_rows = cosine[block, :]
        sin_rows = sinus[block, :]
        start = 0 if own else width
        result = nn_dot(n1, wq[:, start:]) + nn_dot(rank, b_qkv2[:, start:])
        for p in range(width // 128):
            lanes = slice(128 * p, 128 * p + 128)
            cols = slice(width - start + 128 * p, width - start + 128 * p + 128)
            k_buf[block, lanes] = turn(result[:, cols], cos_rows, sin_rows).astype(jnp.bfloat16)
            cols = slice(2 * width - start + 128 * p, 2 * width - start + 128 * p + 128)
            value = result[:, cols]
            v_buf[block, lanes] = value.astype(jnp.bfloat16)
            v_t[lanes, :] = value.T.astype(jnp.bfloat16)
            if own:
                query = turn(result[:, lanes], cos_rows, sin_rows) * 0.125
                q_n[:, lanes] = query.astype(jnp.bfloat16)
                q_t[lanes, :] = query.T.astype(jnp.bfloat16)
        for copy in out_copies(chunk):
            copy.start()

    def weights_out(chunk, p):
        target = p_all.at[pl.ds(chunk * heads + 2 * p, 2)]
        return pltpu.make_async_copy(p_buf.at[pl.ds(2 * p, 2)], target, p_sems.at[p])

    def attend(chunk, first):
        block = chunk_rows(chunk)
        trunk = ((chunk + 1) * rows <= TRUNK) & (c * rows >= TRUNK)

        @pl.when(trunk)
        def _():
            bias[...] = jnp.zeros_like(bias)

        @pl.when(jnp.logical_not(trunk))
        def _():
            fill_bias(bias, hot[block, :], reach_t[...], chunk * rows, c * rows)


        def pair_step(p, carry):
            lanes = pl.ds(pl.multiple_of(p * 128, 128), 128)
            keys = k_buf[block, lanes]
            query = q_t[lanes, :]
            if not first:
                weights_out(chunk, p).wait()
            for odd in range(2):
                h = 2 * p + odd
                alone = jnp.where(
                    head_half(query.shape, 0, odd), query, jnp.zeros_like(query)
                )
                scores = nn_dot(keys, alone) + bias[...]
                before = peak[pl.ds(h, 1), :]
                now = jnp.maximum(before, jnp.max(scores, axis=0, keepdims=True))
                weights = jnp.exp(scores - now)
                shrink = jnp.exp(before - now)
                peak[pl.ds(h, 1), :] = now
                peaks[pl.ds(chunk * 8 + h, 1), :] = now
                low_weights = weights.astype(jnp.bfloat16)
                p_buf[h] = low_weights
                total[pl.ds(h, 1), :] = total[pl.ds(h, 1), :] * shrink + jnp.sum(
                    weights, axis=0, keepdims=True
                )
                head = pl.ds(pl.multiple_of(h * HEAD_DIM, HEAD_DIM), HEAD_DIM)
                o_t[head, :] = o_t[head, :] * shrink + nn_dot(
                    v_t[head, :], low_weights
                )
            weights_out(chunk, p).start()
            return carry

        lax.fori_loop(0, heads // 2, pair_step, 0)

    def advance(gather, following, copies=None):
        gather.wait(0)
        for stage in range(1, bits):
            gather.start(stage)
            if copies is not None:
                lend(copies, stage - 1)
            if stage < bits - 1:
                gather.wait(stage)
        following.start(0)

    for copy in rows_sent:
        copy.wait_recv()
    total_row = adapters_all[0].astype(jnp.float32)
    for b in range(1, fsdp):
        total_row = total_row + adapters_all[b].astype(jnp.float32)
    chosen[t, c] = total_row.astype(jnp.bfloat16)
    spread = []
    for k, other in enumerate(stacked):
        block = chosen.at[t, c]
        copy = send(block, block, small_send.at[3, k], small_recv.at[3, k], other)
        copy.start()
        spread.append(copy)
    gains[...] = jnp.zeros_like(gains)
    for i in range(2):
        pieces = [
            gains_all[b, 0:1, i * own_n : (i + 1) * own_n].astype(jnp.float32)
            for b in range(fsdp)
        ]
        gains[i : i + 1, :] = jnp.concatenate(pieces, axis=1)
    gain_one = gains[0:1, :]
    gain_two = gains[1:2, :]
    advance(wq_gather, wo_gather)
    receive(1)
    for copy in spread:
        copy.wait_recv()
    shared_copy = send(
        chosen.at[t], chosen.at[t], small_send.at[4, 0], small_recv.at[4, 0], sibling
    )
    shared_copy.start()
    route_tables(f, table_all, place_row, place_col, weight_col, marks)
    give_out(
        (table_all, place_row, place_col, weight_col, gains, cosine, sinus, hot, reach_t)
    )
    advance(wo_gather, gu_gather)
    shared_copy.wait_recv()
    unpack_adapter(
        t,
        adapters_in.shape[0] // (ADAPTERS // fsdp),
        chosen,
        flat,
        a_wide,
        (a_qkv, b_qkv2, a_qkv_t2, a_o, b_o2, a_o_t2),
        (a_gu, b_gu2, a_gu_t2, a_dn, a_dn_t2, b_dn2),
    )
    give_out((a_qkv, b_qkv2, a_qkv_t2, a_o, b_o2, a_o_t2))
    wq_gather.wait(bits - 1)
    locals_[0].wait()
    locals_[1].wait()
    wq_out = pltpu.make_async_copy(wq, wq_all, local_sems.at[10])
    wq_out.start()
    project(c, True)
    receive(2)
    attend(c, True)

    number = contexts

    def forwards(gather, buf, first):
        copies = []
        for stage in range(bits):
            group = []
            for block in gather.arrived[stage]:
                index = first + len(copies)
                copies.append(
                    send(
                        buf.at[block],
                        buf.at[block],
                        core_send.at[index],
                        core_recv.at[index],
                        sibling,
                    )
                )
        return copies

    per_stage = [len(stage) for stage in g_gather.arrived]
    g_forward = forwards(g_gather, g_all, number + 5)
    n2_forward = forwards(n2_gather, n2_all, number + 5 + sum(per_stage))

    def pass_on(copies, stage):
        start = sum(per_stage[:stage])
        for copy in copies[start : start + per_stage[stage]]:
            copy.start()

    def between(step):
        if step == 1:
            advance(gu_gather, dn_gather)

            @pl.when(jnp.logical_not(z_busy))
            def _():
                lend(gu_lent, 0)

        if step == 2:
            advance(dn_gather, g_gather)
            gu_gather.wait(bits - 1)

            @pl.when(z_busy)
            def _():
                lend(gu_lent, 0)

            for stage in range(1, bits):
                lend(gu_lent, stage)
        if step == 3:
            g_gather.wait(0)
            for stage in range(1, bits):
                g_gather.start(stage)
                pass_on(g_forward, stage - 1)
                if stage < bits - 1:
                    g_gather.wait(stage)

    def later(step):
        chunk = c - step

        @pl.when(step <= c)
        def _():
            across(chunk).wait_recv()
            project(chunk, False)
            receive(step + 2)
            attend(chunk, False)

    for step in range(1, 3):
        between(step)
        later(step)

    @pl.when(c >= 3)
    def _():
        between(3)
        later(3)

    def rest(step, carry):
        later(step)
        return carry

    lax.fori_loop(4, contexts, rest, 0)

    for h in range(heads):
        head = slice(h * HEAD_DIM, h * HEAD_DIM + HEAD_DIM)
        o_t[head, :] = o_t[head, :] / total[h : h + 1, :]
    lse[...] = peak[...] + jnp.log(total[...])
    for p in range(width // 128):
        mixed[:, 128 * p : 128 * p + 128] = o_t[128 * p : 128 * p + 128, :].T.astype(jnp.bfloat16)
    give_out((q_t, q_n, mixed, o_t, lse))
    wo_gather.wait(bits - 1)
    locals_[2].wait()
    wo_out = pltpu.make_async_copy(wo, wo_all, local_sems.at[11])
    wo_out.start()

    def local_rows(part):
        return pl.ds(pl.multiple_of(part * half, 16), half)

    mine = local_rows(t)
    theirs = local_rows(1 - t)

    def branch(block):
        values = mixed[block, :]
        rank = two_parts(nn_dot(values, a_o[...]))
        return nt_dot(values, wo[...]) + nn_dot(rank, b_o2[...])

    part_copies = []
    for i, block in enumerate((theirs, mine)):
        part_out[block, :] = branch(block).astype(jnp.bfloat16)
        copy = send(
            part_out.at[block],
            part_in.at[block],
            core_send.at[number + i],
            core_recv.at[number + i],
            sibling,
        )
        copy.start()
        part_copies.append(copy)

    def attended(block, copy):
        copy.wait_recv()
        resid[block, :] = x_rows(x_buf, c, rows, block) + (
            part_out[block, :].astype(jnp.float32) + part_in[block, :].astype(jnp.float32)
        )
        n2_own[block, :] = normed(resid[block, :], gain_two)

    attended(mine, part_copies[0])
    n2_gather.start(0)
    attended(theirs, part_copies[1])
    give_out((resid,))
    n2_out = pltpu.make_async_copy(n2_own, n2_all.at[pl.ds(f * rows, rows)], local_sems.at[12])
    n2_out.start()

    @pl.when(c < 3)
    def _():
        between(3)


    locals_[5].wait()
    for group in gu_lent:
        for copy in group:
            copy.wait_recv()
    locals_[3].wait()
    dn_gather.wait(bits - 1)
    locals_[4].wait()

    def shared_tile(block):
        inputs = n2_own[block, :]
        grads = g_own[block, :]
        rank = nn_dot(inputs, a_gu[...])
        rank2 = two_parts(rank)
        gate = nn_dot(inputs, gu[:, :units]) + nn_dot(rank2, b_gu2[:, :units])
        up_pre = nn_dot(inputs, gu[:, units:]) + nn_dot(rank2, b_gu2[:, units:])
        sigmoid_gate = jax.nn.sigmoid(gate)
        silu = gate * sigmoid_gate
        hidden = (silu * up_pre).astype(jnp.bfloat16)
        down_rank = nn_dot(hidden, a_dn[...])
        shared[block, :] = (
            nt_dot(hidden, dn[...]) + nn_dot(two_parts(down_rank), b_dn2[...])
        ).astype(jnp.bfloat16)
        down_back = nt_dot(grads, b_dn2[0:128, :])
        grad_hidden = nn_dot(grads, dn[...]) + nn_dot(two_parts(down_back), a_dn_t2[...])
        grad_gate = (
            grad_hidden * up_pre * sigmoid_gate * (1.0 + gate * (1.0 - sigmoid_gate))
        ).astype(jnp.bfloat16)
        grad_up = (grad_hidden * silu).astype(jnp.bfloat16)
        rank_back = nt_dot(grad_gate, b_gu2[0:128, :units]) + nt_dot(
            grad_up, b_gu2[0:128, units:]
        )
        dn2[block, :] = (
            nt_dot(grad_gate, gu[:, :units])
            + nt_dot(grad_up, gu[:, units:])
            + nn_dot(two_parts(rank_back), a_gu_t2[...])
        ).astype(jnp.bfloat16)
        rank_low = rank.astype(jnp.bfloat16)
        da_gu[...] += tn_dot(rank_back.astype(jnp.bfloat16), inputs)[0 : 2 * RANK]
        db_gu[0:RANK, :] += 2.0 * tn_dot(rank_low, grad_gate)[0:RANK]
        db_gu[RANK:, :] += 2.0 * tn_dot(rank_low, grad_up)[RANK : 2 * RANK]
        da_dn[...] += tn_dot(down_back.astype(jnp.bfloat16), hidden)[0:RANK]
        db_dn[...] += 2.0 * tn_dot(down_rank.astype(jnp.bfloat16), grads)[0:RANK]

    def pass_pieces(gather, copies, stage):
        start = sum(per_stage[:stage])
        for i, copy in enumerate(gather.stages[stage]):
            copy.wait_recv()
            copies[start + i].start()

    shared_tile(mine)
    n2_gather.wait(0)
    for stage in range(1, bits):
        n2_gather.start(stage)
        pass_on(n2_forward, stage - 1)
        if stage < bits - 1:
            n2_gather.wait(stage)
    shared_tile(theirs)
    give_out((shared, dn2))
    pass_pieces(g_gather, g_forward, bits - 1)
    pass_pieces(n2_gather, n2_forward, bits - 1)
    for copy in n2_forward + g_forward:
        copy.wait()
    for copy in small + rows_sent + spread + [shared_copy]:
        copy.wait_send()
    for group in gu_lent:
        for copy in group:
            copy.wait_send()
    for copy in given:
        copy.wait()
    for copy in part_copies:
        copy.wait_send()
    for gather in gathers + [g_gather, n2_gather]:
        gather.finish()
    n2_out.wait()
    wq_out.wait()
    wo_out.wait()
    locals_[6].wait()

    @pl.when(c < contexts - 1)
    def _():
        up(c, x_in.at[half_rows(0, t)]).wait_send()

    def drain(step, carry):
        chunk = c - step

        @pl.when(c < contexts - 1)
        def _():
            up(chunk, x_buf.at[half_rows(chunk, t)]).wait_send()

        across(chunk).wait_send()
        return carry

    lax.fori_loop(1, c + 1, drain, 0)

    def drain_out(step, carry):
        for copy in out_copies(c - step):
            copy.wait()
        return carry

    lax.fori_loop(0, c + 1, drain_out, 0)
    for p in range(heads // 2):
        weights_out(0, p).wait()


def x_rows(x_buf, chunk, rows, block):
    return x_buf[pl.ds(pl.multiple_of(chunk * rows, 16) + block.start, block.size), :].astype(
        jnp.float32
    )


def forward_call(sizes, sharded, local):
    fsdp, contexts, _ = sizes
    x, g, wq, wo, gu, dn = sharded
    adapters, gains, table = local[:3]
    rows = x.shape[0]
    tree = rows * contexts
    width = wo.shape[1]
    units = dn.shape[1]
    bf, f32 = jnp.bfloat16, jnp.float32
    vmem = pl.BlockSpec(memory_space=pltpu.VMEM)
    hbm = pl.BlockSpec(memory_space=pl.ANY)
    smem = pl.BlockSpec(memory_space=pltpu.SMEM)
    slots = max(fsdp, contexts)
    total = fsdp * rows
    per_adapter = adapters.shape[0] // (ADAPTERS // fsdp)

    def shape(kind, *dims):
        return jax.ShapeDtypeStruct(dims, kind)

    moves = 2 * (fsdp - 1)
    hops = contexts + 5 + 2 * moves
    return pl.pallas_call(
        functools.partial(forward_kernel, sizes),
        in_specs=[hbm] * 6 + [vmem] * 4 + [smem] * 2,
        out_specs=[hbm] * 8 + [hbm, hbm, hbm, hbm, hbm, hbm, hbm, hbm, vmem, vmem, vmem, vmem, hbm, hbm, hbm, hbm, hbm, hbm, hbm, hbm, hbm, hbm, hbm, hbm, hbm, hbm, hbm, vmem, vmem],
        out_shape=[
            shape(bf, tree, D),
            shape(bf, tree, width),
            shape(bf, tree, width),
            shape(bf, D, 3 * width),
            shape(bf, D, width),
            shape(bf, fsdp * rows, D),
            shape(bf, fsdp * rows, D),
            shape(bf, contexts * (width // HEAD_DIM), rows, rows),
            shape(bf, width, rows),
            shape(bf, rows, width),
            shape(bf, rows, width),
            shape(f32, width, rows),
            shape(f32, 8, rows),
            shape(f32, rows, D),
            shape(bf, rows, D),
            shape(bf, rows, D),
            shape(f32, 2 * RANK, D),
            shape(f32, 2 * RANK, units),
            shape(f32, RANK, units),
            shape(f32, RANK, D),
            shape(f32, 8, D),
            shape(f32, tree, 128),
            shape(f32, tree, 128),
            shape(bf, tree, 128),
            shape(bf, 128, rows),
            shape(bf, D, 128),
            shape(bf, 256, 3 * width),
            shape(bf, 256, D),
            shape(bf, width, 128),
            shape(bf, 256, D),
            shape(bf, 256, width),
            shape(f32, fsdp, 8, rows),
            shape(f32, 8, total),
            shape(f32, total, 128),
            shape(bf, total, 128),
            shape(jnp.int32, 8, 128),
            shape(f32, contexts * 8, rows),
        ],
        scratch_shapes=[
            pltpu.VMEM((tree, D), bf),
            pltpu.VMEM((D, 3 * width), bf),
            pltpu.VMEM((D, width), bf),
            pltpu.VMEM((D, 2 * units), bf),
            pltpu.VMEM((D, units), bf),
            pltpu.VMEM((rows, D), bf),
            pltpu.VMEM((tree, D), bf),
            pltpu.VMEM((tree, width), bf),
            pltpu.VMEM((tree, width), bf),
            pltpu.VMEM((width, rows), bf),
            pltpu.VMEM((8, rows), f32),
            pltpu.VMEM((8, rows), f32),
            pltpu.VMEM((rows, rows), f32),
            pltpu.VMEM((rows, D), bf),
            pltpu.VMEM((rows, D), bf),
            pltpu.VMEM((rows, D), bf),
            pltpu.VMEM((rows, D), bf),
            pltpu.VMEM((rows, D), bf),
            pltpu.VMEM((fsdp, per_adapter, 128), bf),
            pltpu.VMEM((fsdp - 1, per_adapter, 128), bf),
            pltpu.VMEM((fsdp,) + gains.shape, bf),
            pltpu.VMEM((2, contexts, per_adapter, 128), bf),
            pltpu.VMEM((PARAMS // 128, 128), f32),
            pltpu.VMEM((max(D, units), 128), f32),
            pltpu.VMEM((D, 128), bf),
            pltpu.VMEM((256, 2 * units), bf),
            pltpu.VMEM((256, D), bf),
            pltpu.VMEM((units, 128), bf),
            pltpu.VMEM((256, units), bf),
            pltpu.VMEM((256, D), bf),
            pltpu.SemaphoreType.DMA((6, moves)),
            pltpu.SemaphoreType.DMA((6, moves)),
            pltpu.SemaphoreType.DMA((contexts,)),
            pltpu.SemaphoreType.DMA((contexts,)),
            pltpu.SemaphoreType.DMA((hops,)),
            pltpu.SemaphoreType.DMA((hops,)),
            pltpu.SemaphoreType.DMA((13,)),
            pltpu.SemaphoreType.DMA((3, contexts)),
            pltpu.SemaphoreType.DMA((5, slots)),
            pltpu.SemaphoreType.DMA((5, slots)),
            pltpu.SemaphoreType.DMA((2, moves)),
            pltpu.SemaphoreType.DMA((2, moves)),
            pltpu.VMEM((width, rows), bf),
            pltpu.VMEM((rows, width), bf),
            pltpu.VMEM((rows, width), bf),
            pltpu.VMEM((width, rows), f32),
            pltpu.VMEM((8, rows), f32),
            pltpu.VMEM((rows, D), f32),
            pltpu.VMEM((8, D), f32),
            pltpu.VMEM((tree, 128), f32),
            pltpu.VMEM((tree, 128), f32),
            pltpu.VMEM((tree, 128), bf),
            pltpu.VMEM((128, rows), bf),
            pltpu.VMEM((D, 128), bf),
            pltpu.VMEM((256, 3 * width), bf),
            pltpu.VMEM((256, D), bf),
            pltpu.VMEM((width, 128), bf),
            pltpu.VMEM((256, D), bf),
            pltpu.VMEM((256, width), bf),
            pltpu.VMEM((fsdp, 8, rows), f32),
            pltpu.VMEM((8, total), f32),
            pltpu.VMEM((total, 128), f32),
            pltpu.VMEM((total, 128), bf),
            pltpu.SemaphoreType.DMA((23,)),
            pltpu.VMEM((width // HEAD_DIM, rows, rows), bf),
            pltpu.SemaphoreType.DMA((width // HEAD_DIM // 2,)),
        ],
        name="forward",
        compiler_params=pltpu.CompilerParams(
            collective_id=2, has_side_effects=True, vmem_limit_bytes=62 << 20
        ),
    )(*sharded, *local)


def flips(index, mask, bits):
    for bit in range(bits):
        if mask >> bit & 1:
            index = flip(index, bit)
    return index


class Scatter:
    def __init__(self, bits, me, device_of, work, inbox, count, send_sems, recv_sems):
        self.bits, self.work, self.inbox = bits, work, inbox
        self.copies = [[] for _ in range(bits)]
        self.masks = [[] for _ in range(bits)]
        self.adds = [[] for _ in range(bits)]
        number = 0
        for half, (offset, size) in enumerate(split_rows(count)):
            alive = list(range(1 << bits))
            slot = 0
            for stage in range(bits):
                bit = (stage + half) % bits
                for mask in alive:
                    if mask >> bit & 1:
                        source = Gather.rows(flips(me, mask, bits) * count + offset, size)
                        target = pl.ds(slot * count + offset, size)
                        kept = Gather.rows(flips(me, mask ^ (1 << bit), bits) * count + offset, size)
                        self.copies[stage].append(
                            send(
                                work.at[source],
                                inbox.at[target],
                                send_sems.at[number],
                                recv_sems.at[number],
                                device_of(flip(me, bit)),
                            )
                        )
                        self.adds[stage].append((kept, target, pl.ds(offset, size)))
                        self.masks[stage].append(mask)
                        number = number + 1
                        slot = slot + 1
                alive = [mask for mask in alive if not mask >> bit & 1]

    def start(self, stage):
        for copy in self.copies[stage]:
            copy.start()

    def start_mask(self, mask):
        for copy, number in zip(self.copies[0], self.masks[0]):
            if number == mask:
                copy.start()

    def add(self, stage):
        for copy in self.copies[stage]:
            copy.wait_recv()
        for kept, target, _ in self.adds[stage]:
            total = self.work[kept, :].astype(jnp.float32) + self.inbox[target, :].astype(
                jnp.float32
            )
            self.work[kept, :] = total.astype(jnp.bfloat16)

    def last(self, out):
        for copy in self.copies[self.bits - 1]:
            copy.wait_recv()
        for kept, target, rows in self.adds[self.bits - 1]:
            total = self.work[kept, :].astype(jnp.float32) + self.inbox[target, :].astype(
                jnp.float32
            )
            out[rows, :] = total.astype(jnp.bfloat16)

    def finish(self):
        for stage in self.copies:
            for copy in stage:
                copy.wait_send()


def pack_rows(grad_t, start, rank, flat, wide):
    total = grad_t.shape[1]
    more = jnp.zeros((128 - rank, 128), jnp.float32)
    for p in range(total // 128):
        piece = grad_t[:, 128 * p : 128 * p + 128]
        wide[128 * p : 128 * p + 128, :] = jnp.concatenate([piece, more], axis=0).T
    lines = rank // math.gcd(rank, 128)
    each = lines * 128 // rank
    count = total // each
    joined = jnp.concatenate(
        [wide[pl.ds(i, count, stride=each), :][:, 0:rank] for i in range(each)], axis=1
    )
    if lines == 1:
        flat[pl.ds(start, count), :] = joined
    else:
        for i in range(lines):
            flat[pl.ds(start + i, count, stride=lines), :] = joined[:, 128 * i : 128 * i + 128]


def pack_lines(grad, start, lines, columns, flat):
    for p, m in enumerate(columns):
        flat[pl.ds(start + m, grad.shape[0], stride=lines), :] = grad[:, 128 * p : 128 * p + 128]


def pack_first(t, flat, wide, da_qkv, db_qkv, da_o, db_o):
    width = da_o.shape[1]
    lines = D // 128
    mine = [t * (width // 128) + p for p in range(width // 128)]
    pack_rows(da_qkv[...], 0, 3 * RANK, flat, wide)
    at = 3 * RANK * D // 128
    for j in range(3):
        rows = slice(j * RANK, (j + 1) * RANK)
        pack_lines(db_qkv[rows, :], at + j * RANK * lines, lines, mine, flat)
    at = at + 3 * RANK * lines
    pack_rows(da_o[...], at + t * (width * RANK // 128), RANK, flat, wide)
    at = at + D * RANK // 128
    pack_lines(db_o[...], at, lines, list(range(lines)), flat)


def pack_second(t, flat, wide, da_gu, db_gu, da_dn, db_dn):
    units = da_dn.shape[1]
    lines = D // 128
    at = 8 * RANK * D // 128
    pack_rows(da_gu[...], at, 2 * RANK, flat, wide)
    at = at + 2 * RANK * D // 128
    wide_lines = FF // 128
    mine = [t * (units // 128) + p for p in range(units // 128)]
    for j in range(2):
        rows = slice(j * RANK, (j + 1) * RANK)
        pack_lines(db_gu[rows, :], at + j * RANK * wide_lines, wide_lines, mine, flat)
    at = at + 2 * RANK * wide_lines
    pack_rows(da_dn[...], at + t * (units * RANK // 128), RANK, flat, wide)
    at = at + FF * RANK // 128
    pack_lines(db_dn[...], at, lines, list(range(lines)), flat)


def backward_kernel(
    sizes,
    moe_out,
    moe_back,
    n1_hbm,
    k_hbm,
    v_hbm,
    wq_hbm,
    wo_hbm,
    cos_hbm,
    sin_hbm,
    p_hbm,
    x_in_hbm,
    g_in_hbm,
    gains,
    peaks,
    resid_hbm,
    shared_hbm,
    dn2_hbm,
    q_t_hbm,
    q_n_hbm,
    mixed_hbm,
    o_t_hbm,
    lse,
    a_qkv_hbm,
    b_qkv2_hbm,
    a_qkv_t2_hbm,
    a_o_hbm,
    a_o_t2_hbm,
    b_o2_hbm,
    da_gu,
    db_gu,
    da_dn,
    db_dn,
    table_all,
    ffn_out,
    input_grad,
    adapter_out,
    cosine,
    sinus,
    k_buf,
    v_buf,
    wq,
    wo,
    work_back,
    pair_back,
    inbox_back,
    work_out,
    pair_out,
    inbox_out,
    total_half,
    total_full,
    ffn_half,
    ffn_full,
    dy,
    do_n,
    do_t,
    delta,
    factor,
    k_t,
    dq_t,
    dq,
    part_in,
    z_in,
    dn1_full,
    fs_send,
    fs_recv,
    z_send,
    z_recv,
    core_send,
    core_recv,
    pair_send,
    pair_recv,
    local_sems,
    chunk_sems,
    x_in,
    g_in,
    resid,
    shared,
    dn2,
    q_t,
    q_n,
    mixed,
    o_t,
    a_qkv,
    b_qkv2,
    a_qkv_t2,
    a_o,
    a_o_t2,
    b_o2,
    da_qkv,
    db_qkv,
    da_o,
    db_o,
    flat,
    wide,
    packed,
    packed_in,
    up_out,
    up_in,
    own_sum,
    tree_sums,
    in_sems,
    sum_send,
    sum_recv,
    p_buf,
    p_sems,
    whole_back,
    whole_out,
):
    fsdp, contexts, _ = sizes
    bits = fsdp.bit_length() - 1
    f, c, t = place_of()
    rows = x_in.shape[0]
    half = rows // 2
    width = q_t.shape[0]
    inputs = []
    for i, (source, target) in enumerate(
        (
            (x_in_hbm, x_in),
            (g_in_hbm, g_in),
            (resid_hbm, resid),
            (shared_hbm, shared),
            (dn2_hbm, dn2),
            (q_t_hbm, q_t),
            (q_n_hbm, q_n),
            (mixed_hbm, mixed),
            (o_t_hbm, o_t),
            (a_qkv_hbm, a_qkv),
            (b_qkv2_hbm, b_qkv2),
            (a_qkv_t2_hbm, a_qkv_t2),
            (a_o_hbm, a_o),
            (a_o_t2_hbm, a_o_t2),
            (b_o2_hbm, b_o2),
        )
    ):
        inputs.append(pltpu.make_async_copy(source, target, in_sems.at[i]))
    heads = width // HEAD_DIM
    part_out, z_out, grad_kv = pair_back, work_back, inbox_back
    part, n1_buf = whole_back, whole_out
    kv_rows = pl.ds(0, rows)
    sibling = (f, c, 1 - t)
    f32, bf = jnp.float32, jnp.bfloat16

    def peer(index):
        return (index, c, t)

    def local_rows(part_index):
        return pl.ds(pl.multiple_of(part_index * half, 16), half)

    mine = local_rows(t)
    theirs = local_rows(1 - t)

    def block_rows(block, part_index):
        return pl.ds(pl.multiple_of(block * rows + part_index * half, 16), half)

    def work_rows(block):
        return pl.ds(pl.multiple_of(block * half, 16), half)

    masks = list(range(fsdp - 1, -1, -1))

    def exchange(source, work, inbox, which, whole):
        own, sent = [], []
        for mask in masks:
            block = flips(f, mask, bits)
            if mask == 0:
                own.append(
                    pltpu.make_async_copy(
                        source.at[pl.ds(pl.multiple_of(f * rows, 16), rows)],
                        whole,
                        local_sems.at[which, mask],
                    )
                )
                sent.append(
                    send(
                        whole.at[theirs],
                        inbox.at[work_rows(block)],
                        core_send.at[which, mask],
                        core_recv.at[which, mask],
                        sibling,
                    )
                )
                continue
            own.append(
                pltpu.make_async_copy(
                    source.at[block_rows(block, t)],
                    work.at[work_rows(block)],
                    local_sems.at[which, mask],
                )
            )
            sent.append(
                send(
                    source.at[block_rows(block, 1 - t)],
                    inbox.at[work_rows(block)],
                    core_send.at[which, mask],
                    core_recv.at[which, mask],
                    sibling,
                )
            )
        return own, sent

    back_own, back_sent = exchange(moe_back, work_back, pair_back, 0, whole_back)
    out_own, out_sent = exchange(moe_out, work_out, pair_out, 1, whole_out)
    for copy in back_own:
        copy.start()
    wo_copy = pltpu.make_async_copy(wo_hbm, wo, local_sems.at[2, 0])
    wq_copy = pltpu.make_async_copy(wq_hbm, wq, local_sems.at[2, 1])
    wo_copy.start()
    for copy in inputs:
        copy.start()
    peers = [(lax.rem(f + k, fsdp), c, t) for k in range(1, fsdp)]
    stacked = [(f, lax.rem(c + k, contexts), t) for k in range(1, contexts)]
    greet(peers + stacked + [sibling])
    for copy in back_sent[:-1]:
        copy.start()
    for copy in out_own:
        copy.start()
    wq_copy.start()

    lines = PARAMS // 128 // (2 * contexts)
    early = -(-(8 * RANK * D // 128) // (2 * lines))

    def fill_blocks(first, last):
        for context in range(first, last):
            for part_index in range(2):
                start = (2 * context + part_index) * lines
                packed[context, part_index, 0:lines, :] = flat[start : start + lines, :]

    def pair_block(block):
        return send(
            packed.at[block, 1 - t],
            packed_in.at[block],
            sum_send.at[0, block],
            sum_recv.at[0, block],
            sibling,
        )

    def to_owner(k):
        return send(
            up_out.at[k], up_in.at[k], sum_send.at[1, k], sum_recv.at[1, k], stacked[k]
        )

    def push_blocks(soon):
        for k in range(contexts - 1):
            owner = lax.rem(c + k + 1, contexts)

            @pl.when((owner >= early) if soon else (owner < early))
            def _(k=k, owner=owner):
                up_out[k] = (packed[owner, t] + packed_in[owner]).astype(bf)
                to_owner(k).start()

    def to_peer(k):
        return send(
            own_sum, tree_sums.at[k], sum_send.at[2, k], sum_recv.at[2, k], peers[k]
        )

    def sum_own():
        result = packed[c, t] + packed_in[c]
        for k in range(contexts - 1):
            to_owner(k).wait_recv()
            result = result + up_in[k].astype(f32)
        own_sum[...] = result.astype(bf)
        for k in range(fsdp - 1):
            to_peer(k).start()

    def chunk_rows(chunk):
        return pl.ds(pl.multiple_of(chunk * rows, 16), rows)

    def loads(chunk):
        block = chunk_rows(chunk)
        return [
            pltpu.make_async_copy(k_hbm.at[block], k_buf.at[block], chunk_sems.at[1, chunk]),
            pltpu.make_async_copy(v_hbm.at[block], v_buf.at[block], chunk_sems.at[2, chunk]),
        ]

    def n1_load(chunk):
        return pltpu.make_async_copy(
            n1_hbm.at[chunk_rows(chunk)], n1_buf, chunk_sems.at[0, chunk]
        )

    def table_loads(chunk):
        block = chunk_rows(chunk)
        return [
            pltpu.make_async_copy(cos_hbm.at[block], cosine, chunk_sems.at[3, chunk]),
            pltpu.make_async_copy(sin_hbm.at[block], sinus, chunk_sems.at[4, chunk]),
        ]

    def start_loads(chunk, carry):
        for copy in loads(chunk):
            copy.start()
        return carry

    lax.fori_loop(0, c + 1, start_loads, 0)

    def weights_in(chunk, p):
        source = p_hbm.at[pl.ds(chunk * heads + 2 * p, 2)]
        return pltpu.make_async_copy(source, p_buf.at[pl.ds(2 * p, 2)], p_sems.at[p])

    for p in range(heads // 2):
        weights_in(0, p).start()

    back = Scatter(
        bits, f, peer, work_back, inbox_back, half, fs_send.at[0], fs_recv.at[0]
    )
    out = Scatter(bits, f, peer, work_out, inbox_out, half, fs_send.at[1], fs_recv.at[1])

    def join(own, sent, whole, extra, work):
        own[-1].wait()
        whole[...] = (whole[...].astype(f32) + extra[...].astype(f32)).astype(bf)
        sent[-1].start()
        work[work_rows(f), :] = whole[mine, :]

    def pair_sum(own, sent, work, inbox, scatter):
        for i, mask in enumerate(masks):
            block = work_rows(flips(f, mask, bits))
            if mask != 0:
                own[i].wait()
            sent[i].wait_recv()
            work[block, :] = (
                work[block, :].astype(f32) + inbox[block, :].astype(f32)
            ).astype(bf)
            scatter.start_mask(mask)

    for copy in inputs:
        copy.wait()
    join(back_own, back_sent, whole_back, dn2, work_back)
    pair_sum(back_own, back_sent, work_back, pair_back, back)
    for copy in out_sent[:-1]:
        copy.start()
    join(out_own, out_sent, whole_out, shared, work_out)
    flat[...] = jnp.zeros_like(flat)
    pack_second(t, flat, wide, da_gu, db_gu, da_dn, db_dn)
    fill_blocks(early, contexts)
    for block in range(early, contexts):
        pair_block(block).start()
    for stage in range(1, bits):
        back.add(stage - 1)
        back.start(stage)
    dq_t[...] = jnp.zeros_like(dq_t)
    da_qkv[...] = jnp.zeros_like(da_qkv)
    db_qkv[...] = jnp.zeros_like(db_qkv)
    for block in range(early, contexts):
        pair_block(block).wait_recv()
    push_blocks(True)
    back.last(total_half)
    pair_sum(out_own, out_sent, work_out, pair_out, out)
    for copy in out_sent:
        copy.wait_send()
    total_full[mine, :] = total_half[...]
    full_copy = send(
        total_half, total_full.at[mine], core_send.at[2, 0], core_recv.at[2, 0], sibling
    )
    full_copy.start()
    back.finish()
    for copy in back_sent:
        copy.wait_send()
    gain_one = gains[0:1, :]
    gain_two = gains[1:2, :]
    wo_copy.wait()
    full_copy.wait_recv()

    def attn_tile(i, carry):
        block = local_rows(i)
        values = resid[block, :]
        gradient = g_in[block, :].astype(f32) + norm_back(
            values, rms_scale(values), gain_two, total_full[block, :].astype(f32)
        )
        dy[block, :] = gradient
        low_grad = gradient.astype(bf)
        rank_back = nt_dot(low_grad, b_o2[0:128, :])
        do_n[block, :] = (
            nn_dot(low_grad, wo[...]) + nn_dot(two_parts(rank_back), a_o_t2[...])
        ).astype(bf)
        values_o = mixed[block, :]
        rank = nn_dot(values_o, a_o[...])
        first = tn_dot(rank_back.astype(bf), values_o)[0:RANK]
        second = 2.0 * tn_dot(rank.astype(bf), low_grad)[0:RANK]

        @pl.when(i == 0)
        def _():
            da_o[...] = first
            db_o[...] = second

        @pl.when(i > 0)
        def _():
            da_o[...] += first
            db_o[...] += second

        return carry

    lax.fori_loop(0, 2, attn_tile, 0)
    for p in range(width // 128):
        lanes = slice(128 * p, 128 * p + 128)
        turned = do_n[:, lanes].astype(f32).T
        do_t[lanes, :] = turned.astype(bf)
        product = turned * o_t[lanes, :]
        for odd in range(2):
            delta[2 * p + odd : 2 * p + odd + 1, :] = jnp.sum(
                product[HEAD_DIM * odd : HEAD_DIM * odd + HEAD_DIM, :], axis=0, keepdims=True
            )
    wq_copy.wait()

    def attend_back(chunk):
        block = chunk_rows(chunk)
        n1_load(chunk).start()
        for copy in table_loads(chunk):
            copy.start()
        for copy in table_loads(chunk) + loads(chunk):
            copy.wait()
        scale = jnp.exp(peaks[pl.ds(pl.multiple_of(chunk * 8, 8), 8), :] - lse[...])
        factor[...] = scale
        cos_rows = cosine[...]
        sin_rows = -sinus[...]
        for p in range(width // 128):
            lanes = slice(128 * p, 128 * p + 128)
            k_t[lanes, :] = k_buf[block, lanes].astype(f32).T.astype(bf)

        def pair_step(p, carry):
            lanes = pl.ds(pl.multiple_of(p * 128, 128), 128)
            weights_in(chunk, p).wait()
            values = v_buf[block, lanes]
            grad_t = do_t[lanes, :]
            query = q_n[:, lanes]
            grad = do_n[:, lanes]
            grad_keys = jnp.zeros((rows, 128), f32)
            grad_values = jnp.zeros((rows, 128), f32)
            for odd in range(2):
                h = 2 * p + odd
                upper = head_half(grad_t.shape, 0, odd)
                side = head_half(query.shape, 1, odd)
                none_t = jnp.zeros_like(grad_t)
                none = jnp.zeros_like(query)
                weights = p_buf[h].astype(f32) * factor[pl.ds(h, 1), :]
                low_weights = weights.astype(bf)
                grad_weights = nn_dot(values, jnp.where(upper, grad_t, none_t))
                grad_scores = (weights * (grad_weights - delta[pl.ds(h, 1), :])).astype(bf)
                grad_values += nn_dot(low_weights, jnp.where(side, grad, none))
                grad_keys += nn_dot(grad_scores, jnp.where(side, query, none))
                head = pl.ds(pl.multiple_of(h * HEAD_DIM, HEAD_DIM), HEAD_DIM)
                dq_t[head, :] += nn_dot(k_t[head, :], grad_scores)
            grad_kv[kv_rows, lanes] = turn(grad_keys, cos_rows, sin_rows).astype(bf)
            grad_kv[kv_rows, pl.ds(pl.multiple_of(width + p * 128, 128), 128)] = grad_values.astype(bf)

            @pl.when(chunk < c)
            def _():
                weights_in(chunk + 1, p).start()

            return carry

        lax.fori_loop(0, heads // 2, pair_step, 0)

    def ranks():
        return nt_dot(grad_kv[kv_rows, :], b_qkv2[0:128, width:])

    def adapter_back(chunk, own, rank_back):
        grads = grad_kv[kv_rows, :]
        n1_load(chunk).wait()
        n1 = n1_buf[...]
        rank = nn_dot(n1, a_qkv[...]).astype(bf)
        both = 2.0 * tn_dot(rank, grads)
        db_qkv[RANK : 2 * RANK, :] += both[RANK : 2 * RANK, :width]
        db_qkv[2 * RANK :, :] += both[2 * RANK : 3 * RANK, width:]
        if own:
            for p in range(width // 128):
                lanes = slice(128 * p, 128 * p + 128)
                grad_query = (dq_t[lanes, :] * 0.125).T
                dq[:, lanes] = turn(grad_query, cosine[...], -sinus[...]).astype(bf)
            rank_back += nt_dot(dq[...], b_qkv2[0:128, :width])
            db_qkv[0:RANK, :] += 2.0 * tn_dot(rank, dq[...])[0:RANK, :]
        da_qkv[...] += tn_dot(rank_back.astype(bf), n1)[0 : 3 * RANK]
        return rank_back

    def project_back(chunk, own, rank_back):
        result = nt_dot(grad_kv[kv_rows, :], wq[:, width:])
        if own:
            result += nt_dot(dq[...], wq[:, :width])
        result += nn_dot(two_parts(rank_back), a_qkv_t2[...])
        part[...] = result.astype(bf)
        part_out[work_rows(chunk), :] = part[theirs, :]
        z_out[work_rows(chunk), :] = part[mine, :]

    def pair_copy(chunk):
        return send(
            part_out.at[work_rows(chunk)],
            part_in.at[work_rows(chunk)],
            pair_send.at[chunk],
            pair_recv.at[chunk],
            sibling,
        )

    pieces = split_rows(half)

    def down(chunk, piece):
        offset, size = pieces[piece]
        block = Gather.rows(chunk * half + offset, size)
        return send(
            z_out.at[block],
            z_in.at[block],
            z_send.at[chunk, piece],
            z_recv.at[chunk, piece],
            (f, c - 1, t),
        )

    def chain(chunk, onward):
        pair_copy(chunk).wait_recv()
        for piece, (offset, size) in enumerate(pieces):
            block = Gather.rows(chunk * half + offset, size)
            summed = z_out[block, :].astype(f32) + part_in[block, :].astype(f32)
            z_out[block, :] = summed.astype(bf)

            @pl.when(c < contexts - 1)
            def _(block=block, summed=summed, piece=piece):
                down(chunk, piece).wait_recv()
                z_out[block, :] = (summed + z_in[block, :].astype(f32)).astype(bf)

            if onward:
                down(chunk, piece).start()

    def pass_down(chunk):
        chain(chunk, True)

    def sum_moe():
        for stage in range(1, bits):
            out.add(stage - 1)
            out.start(stage)

    ffn_copy = send(ffn_half, ffn_full.at[mine], core_send.at[2, 1], core_recv.at[2, 1], sibling)

    def share_moe():
        out.last(ffn_half)
        ffn_full[mine, :] = ffn_half[...]
        ffn_copy.start()

    def step(chunk, carry):
        attend_back(chunk)
        rank_back = ranks()
        project_back(chunk, False, rank_back)
        pair_copy(chunk).start()
        adapter_back(chunk, False, rank_back)

        @pl.when(c == contexts - 1)
        def _():
            pass_down(chunk)

        @pl.when((c < contexts - 1) & (chunk >= 1))
        def _():
            pass_down(chunk - 1)

        @pl.when(chunk == 0)
        def _():
            sum_moe()

        @pl.when(chunk == 1)
        def _():
            share_moe()

            @pl.when(c >= early)
            def _():
                sum_own()

        return carry

    lax.fori_loop(0, c, step, 0)
    attend_back(c)
    last_rank = adapter_back(c, True, ranks())
    pack_first(t, flat, wide, da_qkv, db_qkv, da_o, db_o)
    fill_blocks(0, early)
    for block in range(early):
        pair_block(block).start()
    project_back(c, True, last_rank)
    pair_copy(c).start()
    for block in range(early):
        pair_block(block).wait_recv()
    push_blocks(False)

    @pl.when((c < 2) & (c >= early))
    def _():
        sum_own()

    @pl.when(c == 0)
    def _():
        sum_moe()

    @pl.when((c < contexts - 1) & (c >= 1))
    def _():
        pass_down(c - 1)

    @pl.when(c < 2)
    def _():
        share_moe()

    chain(c, False)
    dn1_full[mine, :] = z_out[work_rows(c), :]
    dn1_copy = send(
        z_out.at[work_rows(c)],
        dn1_full.at[mine],
        core_send.at[2, 2],
        core_recv.at[2, 2],
        sibling,
    )
    dn1_copy.start()
    ffn_copy.wait_recv()
    block_copy = pltpu.make_async_copy(ffn_full, ffn_out, in_sems.at[len(inputs)])
    block_copy.start()

    @pl.when(c < early)
    def _():
        sum_own()

    dn1_copy.wait_recv()

    def final_tile(i, carry):
        block = local_rows(i)
        values = x_in[block, :].astype(f32)
        dy[block, :] = dy[block, :] + norm_back(
            values, rms_scale(values), gain_one, dn1_full[block, :].astype(f32)
        )
        return carry

    lax.fori_loop(0, 2, final_tile, 0)
    grad_copy = pltpu.make_async_copy(dy, input_grad, in_sems.at[len(inputs) + 1])
    grad_copy.start()
    own = ADAPTERS // fsdp
    wanted = [(f * own + a).astype(f32) for a in range(own)]
    mine_sum = own_sum[...].astype(f32)
    sums = [jnp.where(table_all[f, 4:5, 0:1] == w, mine_sum, 0.0) for w in wanted]
    for k in range(fsdp - 1):
        to_peer(k).wait_recv()
        tree = table_all[lax.rem(f - k - 1 + fsdp, fsdp), 4:5, 0:1]
        block = tree_sums[k].astype(f32)
        sums = [total + jnp.where(tree == w, block, 0.0) for total, w in zip(sums, wanted)]
    for a in range(own):
        adapter_out[a] = sums[a]
    for copy in [full_copy, ffn_copy, dn1_copy]:
        copy.wait_send()
    block_copy.wait()
    grad_copy.wait()
    for block in range(contexts):
        pair_block(block).wait_send()
    for k in range(contexts - 1):
        to_owner(k).wait_send()
    for k in range(fsdp - 1):
        to_peer(k).wait_send()
    out.finish()

    def drain(chunk, carry):
        pair_copy(chunk).wait_send()

        @pl.when(chunk < c)
        def _():
            for piece in range(len(pieces)):
                down(chunk, piece).wait_send()

        return carry

    lax.fori_loop(0, c + 1, drain, 0)


def backward_call(sizes, remote, local):
    fsdp, contexts, _ = sizes
    rows = local[0].shape[0]
    padded = (PARAMS // 128 // (2 * contexts) + 15) // 16 * 16
    half = rows // 2
    tree = rows * contexts
    width = remote[6].shape[1]
    units = local[19].shape[1]
    bf, f32 = jnp.bfloat16, jnp.float32
    vmem = pl.BlockSpec(memory_space=pltpu.VMEM)
    hbm = pl.BlockSpec(memory_space=pl.ANY)

    def shape(kind, *dims):
        return jax.ShapeDtypeStruct(dims, kind)

    moves = 2 * (fsdp - 1)
    slots = max(fsdp, 4)
    dma = pltpu.SemaphoreType.DMA
    return pl.pallas_call(
        functools.partial(backward_kernel, sizes),
        in_specs=[hbm] * len(remote) + [hbm, hbm, vmem, vmem, hbm, hbm, hbm, hbm, hbm, hbm, hbm, vmem, hbm, hbm, hbm, hbm, hbm, hbm, vmem, vmem, vmem, vmem, vmem],
        out_specs=[hbm, hbm, vmem],
        out_shape=[
            shape(bf, rows, D),
            shape(f32, rows, D),
            shape(f32, ADAPTERS // fsdp, padded, 128),
        ],
        scratch_shapes=[
            pltpu.VMEM((rows, 128), f32),
            pltpu.VMEM((rows, 128), f32),
            pltpu.VMEM((tree, width), bf),
            pltpu.VMEM((tree, width), bf),
            pltpu.VMEM((D, 3 * width), bf),
            pltpu.VMEM((D, width), bf),
            pltpu.VMEM((max(fsdp, contexts) * half, D), bf),
            pltpu.VMEM((max(fsdp, contexts) * half, D), bf),
            pltpu.VMEM((max(fsdp - 1, 2) * half, D), bf),
            pltpu.VMEM((fsdp * half, D), bf),
            pltpu.VMEM((fsdp * half, D), bf),
            pltpu.VMEM(((fsdp - 1) * half, D), bf),
            pltpu.VMEM((half, D), bf),
            pltpu.VMEM((rows, D), bf),
            pltpu.VMEM((half, D), bf),
            pltpu.VMEM((rows, D), bf),
            pltpu.VMEM((rows, D), f32),
            pltpu.VMEM((rows, width), bf),
            pltpu.VMEM((width, rows), bf),
            pltpu.VMEM((8, rows), f32),
            pltpu.VMEM((8, rows), f32),
            pltpu.VMEM((width, rows), bf),
            pltpu.VMEM((width, rows), f32),
            pltpu.VMEM((rows, width), bf),
            pltpu.VMEM((contexts * half, D), bf),
            pltpu.VMEM((contexts * half, D), bf),
            pltpu.VMEM((rows, D), bf),
            dma((2, moves)),
            dma((2, moves)),
            dma((contexts, 2)),
            dma((contexts, 2)),
            dma((3, slots)),
            dma((3, slots)),
            dma((contexts,)),
            dma((contexts,)),
            dma((3, slots)),
            dma((5, contexts)),
            pltpu.VMEM((rows, D), bf),
            pltpu.VMEM((rows, D), bf),
            pltpu.VMEM((rows, D), f32),
            pltpu.VMEM((rows, D), bf),
            pltpu.VMEM((rows, D), bf),
            pltpu.VMEM((width, rows), bf),
            pltpu.VMEM((rows, width), bf),
            pltpu.VMEM((rows, width), bf),
            pltpu.VMEM((width, rows), f32),
            pltpu.VMEM((D, 128), bf),
            pltpu.VMEM((256, 3 * width), bf),
            pltpu.VMEM((256, D), bf),
            pltpu.VMEM((width, 128), bf),
            pltpu.VMEM((256, width), bf),
            pltpu.VMEM((256, D), bf),
            pltpu.VMEM((3 * RANK, D), f32),
            pltpu.VMEM((3 * RANK, width), f32),
            pltpu.VMEM((RANK, width), f32),
            pltpu.VMEM((RANK, D), f32),
            pltpu.VMEM((PARAMS // 128, 128), f32),
            pltpu.VMEM((max(D, units), 128), f32),
            pltpu.VMEM((contexts, 2, padded, 128), f32),
            pltpu.VMEM((contexts, padded, 128), f32),
            pltpu.VMEM((contexts - 1, padded, 128), bf),
            pltpu.VMEM((contexts - 1, padded, 128), bf),
            pltpu.VMEM((padded, 128), bf),
            pltpu.VMEM((fsdp - 1, padded, 128), bf),
            dma((17,)),
            dma((3, max(fsdp, contexts))),
            dma((3, max(fsdp, contexts))),
            pltpu.VMEM((width // HEAD_DIM, rows, rows), bf),
            dma((width // HEAD_DIM // 2,)),
            pltpu.VMEM((rows, D), bf),
            pltpu.VMEM((rows, D), bf),
        ],
        name="backward",
        compiler_params=pltpu.CompilerParams(
            collective_id=3, has_side_effects=True, vmem_limit_bytes=63 << 20
        ),
    )(*remote, *local)


def shards(
    tokens,
    attn_gain,
    w_qkv,
    w_out,
    ffn_gain,
    w_gu,
    w_dn,
    w_egu,
    w_edn,
    adapters,
    adapter_ids,
    parents,
    seg_lengths,
    routes,
    route_weights,
    cotangent,
):
    row_count = tokens.shape[1]
    contexts = lax.axis_size("context")
    tensors = lax.axis_size("tensor")
    fsdp_size = lax.axis_size("fsdp")
    sizes = (fsdp_size, contexts, tensors)
    local_width = w_qkv.shape[2]
    local_ff = w_dn.shape[0]
    own_adapters = adapters.shape[0]
    own_width = D // fsdp_size
    gains = jnp.broadcast_to(jnp.concatenate([attn_gain, ffn_gain])[None], (16, 2 * own_width))
    route_table = jnp.concatenate(
        [
            routes[0].astype(jnp.float32).T,
            route_weights[0].astype(jnp.float32).T,
            jnp.broadcast_to(adapter_ids.astype(jnp.float32)[:, None], (1, row_count)),
            jnp.zeros((3, row_count), jnp.float32),
        ]
    )
    lines = adapters.shape[1] // 128
    padded = (lines + 15) // 16 * 16
    adapter_rows = jnp.pad(
        adapters.reshape(own_adapters, lines, 128), ((0, 0), (0, padded - lines), (0, 0))
    ).reshape(own_adapters * padded, 128)
    half_dim = HEAD_DIM // 2
    exponents = -(np.arange(half_dim, dtype=np.float32) * np.float32(2.0)) / np.float32(HEAD_DIM)
    frequency = np.power(np.float32(rope_base), exponents).astype(np.float32)
    signs = np.repeat(np.array([-1.0, 1.0], np.float32), half_dim)
    turns = np.zeros((8, 128), np.float32)
    turns[0], turns[1] = np.tile(frequency, 4), np.tile(signs, 2)
    sharded = (
        tokens[0],
        cotangent[0],
        w_qkv.reshape(own_width, 3 * local_width),
        w_out.T,
        w_gu.reshape(own_width, 2 * local_ff),
        w_dn.T,
    )
    (
        n1_all,
        k_all,
        v_all,
        wq_all,
        wo_all,
        normed_all,
        cotangent_all,
        p_all,
        q_t,
        q_n,
        mixed_own,
        o_t,
        lse,
        resid,
        shared,
        dn2,
        da_gu_t,
        db_gu_own,
        da_dn_t,
        db_dn_own,
        gains_full,
        cosine,
        sinus,
        hot,
        reach_t,
        a_qkv,
        b_qkv2,
        a_qkv_t2,
        a_o,
        b_o2,
        a_o_t2,
        table_all,
        place_row,
        place_col,
        weight_col,
        marks,
        peaks,
    ) = forward_call(
        sizes,
        sharded,
        (adapter_rows, gains, route_table, turns, parents, seg_lengths),
    )
    moe_all, moe_back_all = moe_call(
        marks,
        place_row,
        place_col,
        weight_col,
        normed_all,
        cotangent_all,
        w_egu.transpose(0, 2, 1, 3),
        w_edn,
    )
    remote = (moe_all, moe_back_all, n1_all, k_all, v_all, wq_all, wo_all, cosine, sinus, p_all)
    ffn_sum, input_grad, sums = backward_call(
        sizes,
        remote,
        (tokens[0], cotangent[0], gains_full, peaks)
        + (resid, shared, dn2, q_t, q_n, mixed_own, o_t, lse)
        + (a_qkv, b_qkv2, a_qkv_t2, a_o, a_o_t2, b_o2)
        + (da_gu_t, db_gu_own, da_dn_t, db_dn_own, table_all),
    )
    adapter_grads = sums[:, :lines].reshape(own_adapters, -1)
    block_out = resid + ffn_sum.astype(jnp.float32)
    return (block_out[None], input_grad[None], adapter_grads)


def solution(mesh):
    return jax.shard_map(
        shards,
        mesh=mesh,
        in_specs=(
            P("fsdp", "context", None),
            P("fsdp"),
            P("fsdp", None, "tensor"),
            P("tensor", "fsdp"),
            P("fsdp"),
            P("fsdp", None, "tensor"),
            P("tensor", "fsdp"),
            P("fsdp", None, None, "tensor"),
            P("fsdp", "tensor", None),
            P("fsdp", ("context", "tensor")),
            P("fsdp"),
            P("fsdp", None),
            P("fsdp", None),
            P("fsdp", "context", None),
            P("fsdp", "context", None),
            P("fsdp", "context", None),
        ),
        out_specs=(
            P("fsdp", "context", None),
            P("fsdp", "context", None),
            P("fsdp", ("context", "tensor")),
        ),
        check_vma=False,
    )
```
